32 devices in a mesh: wide: 8 (over z, y), narrow: 4 (over x, core).
Axes of the slice: x: 2, y: 2, z: 4, core: 2. Of those that a mesh axis runs over, the one named last changes fastest.
Arguments:
- ends: bfloat16 [16384, 1024], P(('wide', 'narrow')), may hold values from -6 to 6
- lengths: int32 [4, 2, 3], replicated, may hold values from 1 to 896, 1024 in all within a row
- w_qkv: bfloat16 [2, 1024, 3072], P(None, None, 'narrow'), may hold values from -0.1875 to 0.1875
- w_out: bfloat16 [2, 1024, 1024], P(None, None, 'narrow'), may hold values from -0.1875 to 0.1875
- w_up: bfloat16 [2, 1024, 4096], P(None, None, 'narrow'), may hold values from -0.1875 to 0.1875
- b_up: bfloat16 [2, 4096], P(None, 'narrow'), may hold values from -3 to 3
- w_down: bfloat16 [2, 4096, 1024], P(None, None, 'narrow'), may hold values from -0.09375 to 0.09375
- norm_gain: bfloat16 [2, 4, 1024], P(None, None, 'narrow'), may hold values from 0.5 to 1.5
- norm_bias: bfloat16 [2, 4, 1024], P(None, None, 'narrow'), may hold values from -1.75 to 1.75
Outputs:
- ends_out: bfloat16 [16384, 1024], P(('wide', 'narrow'))
- grad_qkv: float32 [2, 1024, 3072], P(None, None, 'narrow')
- grad_out: float32 [2, 1024, 1024], P(None, None, 'narrow')
- grad_up: float32 [2, 1024, 4096], P(None, None, 'narrow')
- grad_up_bias: float32 [2, 4096], P(None, 'narrow')
- grad_down: float32 [2, 4096, 1024], P(None, None, 'narrow')
- grad_gain: float32 [2, 4, 1024], P(None, None, 'narrow')
- grad_bias: float32 [2, 4, 1024], P(None, None, 'narrow')
The draws below stay inside these ranges and needn't reach their ends.
Inputs may be any that keep to these rules, and one draw needn't show every extreme that they name: Each row of 3 document lengths sums to 1024; its longest is exactly 896, at a position drawn from the seed.
All inputs are finite; a program needn't handle non-finite values.
Results may differ from the reference program's by a relative error of at most 0.018.
Values may be sent and summed in bfloat16 or wider, within the bound.
A program may use at most 640 MiB of HBM per device.

```python
import math
import jax
import jax.numpy as jnp
import numpy as np
from jax import lax

D = 1024
H = 16
HD = 64
FF = 4096
SEG = 256
MICRO = 2
DOCS = 3
GROUPS = 4
STREAM = 1024
LONGEST = 896
TOKENS = 8192
N_NARROW = 4


def block_levels(stream_key, shape, pieces, smallest, high):
    def one(position, blocks):
        draws = jax.random.uniform(jax.random.fold_in(jax.random.fold_in(stream_key, 6), position), (blocks,), jnp.float32, smallest / len(pieces), high / len(pieces))
        return jnp.repeat(jnp.exp(draws), shape[position] // blocks).reshape((-1,) + (1,) * (len(shape) - position - 1))

    level = one(*pieces[0])
    for cut in pieces[1:]:
        level = level * one(*cut)
    return level


def split_up(amount, total, reach, skew):
    weights = [(1 << 20) // math.isqrt(grade ** skew) + 1 for grade in range(2, amount + 1)]
    spare, holding = total - reach - (amount - 1), [1] * (amount - 1)
    while spare > 0:
        movable = [i for i in range(amount - 1) if holding[i] < reach]
        pool, budget = sum([weights[i] for i in movable]), spare
        for i in movable:
            more = min(reach - holding[i], max(1, budget * weights[i] // pool), spare)
            holding[i] = holding[i] + more
            spare = spare - more
    return np.array([reach] + holding)


def ragged_sizes(stream_key, number_of, total, most, slope):
    if number_of == 2:
        one = jax.random.randint(stream_key, (), max(1, total - most), min(most, total - 1) + 1)
        return jnp.stack([one, total - one])
    sizes = jnp.asarray(split_up(number_of, total, most, slope), jnp.int32)
    twos = (number_of - 1) // 2
    source_of, taker = sizes[1:1 + 2 * twos:2], sizes[2:2 + 2 * twos:2]
    margin = jnp.minimum(source_of - 1, most - taker)
    shifted = jax.random.randint(jax.random.fold_in(stream_key, 1), (twos,), 0, 1 << 20) % (margin + 1)
    sizes = sizes.at[1:1 + 2 * twos:2].set(source_of - shifted).at[2:2 + 2 * twos:2].set(taker + shifted)
    return sizes[jax.random.permutation(jax.random.fold_in(stream_key, 2), number_of)]


def scatter_about(key, shape, width, most, shards=(), held_as=jnp.bfloat16):
    entries = jax.random.normal(key, shape, jnp.float32) * width
    if len(shards) > 0:
        entries = block_levels(key, shape, shards, -0.22, 0.18) * entries
    return jnp.clip(entries, min=-most, max=most).astype(held_as)


def setup_inputs(seed: int = 0) -> dict:
    streams_of = jax.random.split(jax.random.key(seed), 10)
    return {
        "ends": scatter_about(streams_of[0], (2 * TOKENS, D), 1.0, 6.0, ((0, 32),)),
        "lengths": jax.vmap(lambda own: ragged_sizes(own, DOCS, STREAM, LONGEST, 0))(jax.random.split(streams_of[1], GROUPS * MICRO)).reshape((GROUPS, MICRO, DOCS)).astype(jnp.int32),
        "w_qkv": scatter_about(streams_of[2], (2, D, 3 * D), D ** -0.5, 0.1875, ((2, 4),)),
        "w_out": scatter_about(streams_of[3], (2, D, D), D ** -0.5, 0.1875, ((2, 4),)),
        "w_up": scatter_about(streams_of[4], (2, D, FF), D ** -0.5, 0.1875, ((2, 4),)),
        "b_up": scatter_about(streams_of[5], (2, FF), 0.5, 3.0, ((1, 4),)),
        "w_down": scatter_about(streams_of[6], (2, FF, D), FF ** -0.5, 0.09375, ((2, 4),)),
        "norm_gain": jnp.clip(1.0 + 0.1 * jax.random.normal(streams_of[7], (2, 4, D), jnp.float32), 0.5, 1.5).astype(jnp.bfloat16),
        "norm_bias": scatter_about(streams_of[8], (2, 4, D), 0.3, 1.75, ((2, 4),)),
    }


EPSILON = 1e-05
MASKED = -1e+30

@jax.custom_vjp
def low(v):
    return lax.optimization_barrier(v.astype(jnp.bfloat16)).astype(jnp.float32)

@jax.custom_vjp
def low_back(v):
    return v

def low_keep(v):
    return (low(v), None)

def low_pass(kept, grad):
    return (grad,)

def back_keep(v):
    return (v, None)

def back_low(kept, grad):
    return (low(grad),)
low.defvjp(low_keep, low_pass)
low_back.defvjp(back_keep, back_low)

def product(left, right):
    return jnp.dot(left, right, precision=lax.Precision.HIGHEST)

def layer_norm(values, gain_row, shift_row):
    center = lax.optimization_barrier(jnp.mean(values, axis=-1, keepdims=True))
    centred = values - center
    spread = lax.optimization_barrier(jnp.mean(centred * centred, axis=-1, keepdims=True))
    return centred * lax.rsqrt(spread + EPSILON) * gain_row + shift_row

def rotate(field, places):
    halfway = field.shape[-1] // 2
    ladder = jnp.arange(halfway, dtype=jnp.float32) * (2.0 / field.shape[-1])
    inverse = jnp.exp(-math.log(10000.0) * ladder)
    angles = places[:, None] * inverse[None, :]
    cosine = jnp.cos(angles)[:, None, :]
    sine_value = jnp.sin(angles)[:, None, :]
    first = field[..., :halfway]
    second = field[..., halfway:]
    return jnp.concatenate([first * cosine - second * sine_value, second * cosine + first * sine_value], axis=-1)

def doc_tables(lengths_row, places):
    closing = jnp.cumsum(lengths_row)
    passed = (places[:, None] >= closing[None, :]).astype(jnp.int32)
    doc_number = lax.optimization_barrier(jnp.sum(passed, axis=1))
    opening = lax.optimization_barrier(jnp.sum(passed * lengths_row[None, :], axis=1))
    return (doc_number, places - opening)

def layer(resid, allowed, offsets, w_qkv, w_out, w_up, b_up, w_down, gains, shifts):
    length = resid.shape[0]
    normed = low(layer_norm(resid, gains[0], shifts[0]))
    projected = low_back(product(normed, w_qkv))
    query, keys_all, values_all = jnp.split(projected, 3, axis=1)
    query = low(rotate(query.reshape(length, H, HD), offsets))
    keys_all = low(rotate(keys_all.reshape(length, H, HD), offsets))
    values_all = low(values_all.reshape(length, H, HD))

    def one_head(triple):
        q_head, k_head, v_head = triple
        scores = low_back(product(q_head, k_head.T) * HD ** (-0.5))
        scores = jnp.where(allowed, scores, MASKED)
        summit = lax.optimization_barrier(jnp.max(scores, axis=1, keepdims=True))
        weights = jnp.exp(scores - summit)
        chances = weights / lax.optimization_barrier(jnp.sum(weights, axis=1, keepdims=True))
        return product(low(chances), v_head)
    mixture = lax.map(jax.checkpoint(one_head), (query.transpose(1, 0, 2), keys_all.transpose(1, 0, 2), values_all.transpose(1, 0, 2)))
    mixture = low_back(low(mixture.transpose(1, 0, 2).reshape(length, H * HD)))
    branch = low_back(product(mixture, w_out))
    middle = resid + layer_norm(branch, gains[1], shifts[1])
    normed = low(layer_norm(middle, gains[2], shifts[2]))
    hidden = low_back(product(normed, w_up) + b_up)
    activated = low(jax.nn.gelu(hidden, approximate=False))
    second = low_back(product(activated, w_down))
    return middle + layer_norm(second, gains[3], shifts[3])

def to_streams(block):
    shaped = block.astype(jnp.float32).reshape(GROUPS, N_NARROW, MICRO, SEG, D)
    return shaped.transpose(0, 2, 1, 3, 4).reshape(GROUPS * MICRO, N_NARROW * SEG, D)

def from_streams(stack):
    shaped = stack.reshape(GROUPS, MICRO, N_NARROW, SEG, D)
    return shaped.transpose(0, 2, 1, 3, 4).reshape(GROUPS * N_NARROW * MICRO * SEG, D)

def reference(ends, lengths, w_qkv, w_out, w_up, b_up, w_down, norm_gain, norm_bias):
    inputs = to_streams(ends[:TOKENS])
    upstream = to_streams(ends[TOKENS:])
    doc_rows = lengths.reshape(GROUPS * MICRO, DOCS)
    params = (w_qkv.astype(jnp.float32), w_out.astype(jnp.float32), w_up.astype(jnp.float32), b_up.astype(jnp.float32), w_down.astype(jnp.float32), norm_gain.astype(jnp.float32), norm_bias.astype(jnp.float32))
    places = jnp.arange(N_NARROW * SEG, dtype=jnp.int32)

    def one_stream(totals, bundle):
        resid, cotangent, lengths_row = bundle
        doc_number, offset_int = doc_tables(lengths_row, places)
        allowed = (places[None, :] <= places[:, None]) & (doc_number[None, :] == doc_number[:, None])
        offsets = offset_int.astype(jnp.float32)

        def stacked(start, p_qkv, p_out, p_up, p_bias, p_down, p_gain, p_shift):
            middle = layer(start, allowed, offsets, p_qkv[0], p_out[0], p_up[0], p_bias[0], p_down[0], p_gain[0], p_shift[0])
            middle = low_back(low(middle))
            return layer(middle, allowed, offsets, p_qkv[1], p_out[1], p_up[1], p_bias[1], p_down[1], p_gain[1], p_shift[1])
        result, pull = jax.vjp(stacked, resid, *params)
        grads = pull(cotangent)
        totals = tuple((total + grad for total, grad in zip(totals, grads[1:])))
        return (totals, (result, grads[0]))
    zero_totals = tuple((jnp.zeros_like(param) for param in params))
    totals, (results, input_grads) = lax.scan(one_stream, zero_totals, (inputs, upstream, doc_rows))
    ends_out = jnp.concatenate([from_streams(input_grads), from_streams(results)], axis=0).astype(jnp.bfloat16)
    return (ends_out, totals[0], totals[1], totals[2], totals[3], totals[4], totals[5], totals[6])
```

```python
import functools
import math

import jax
import jax.numpy as jnp
from jax import lax
from jax.experimental import pallas as pl
from jax.experimental.pallas import tpu as pltpu
from jax.sharding import PartitionSpec as P

HD = 64
EPSILON = 1e-05
MASKED = -1e30
SCALE = HD ** (-0.5)
F32 = jnp.float32
BF16 = jnp.bfloat16


def layer_norm(values, gain_row, shift_row):
    center = jnp.mean(values, axis=-1, keepdims=True)
    centred = values - center
    spread = jnp.mean(centred * centred, axis=-1, keepdims=True)
    return centred * lax.rsqrt(spread + EPSILON) * gain_row + shift_row


def smooth(values):
    return jax.nn.gelu(values, approximate=False)


def rope_tables(offsets):
    halfway = HD // 2
    ladder = jnp.arange(halfway, dtype=F32) * (2.0 / HD)
    inverse = jnp.exp(-math.log(10000.0) * ladder)
    angles = offsets.astype(F32)[:, None] * inverse[None, :]
    return jnp.cos(angles), jnp.sin(angles)


def rotate(matrix, cosine, sine):
    rows, width = matrix.shape
    field = matrix.reshape(rows, width // HD, 2, HD // 2)
    first, second = field[:, :, 0], field[:, :, 1]
    cosine, sine = cosine[:, None], sine[:, None]
    turned = jnp.stack([first * cosine - second * sine, second * cosine + first * sine], axis=2)
    return turned.reshape(rows, width)


def dot(left, right):
    return jnp.dot(left, right, preferred_element_type=F32)


def dot_t(left, right):
    return lax.dot_general(left, right, (((1,), (1,)), ((), ())), preferred_element_type=F32)


def t_dot(left, right):
    return lax.dot_general(left, right, (((0,), (0,)), ((), ())), preferred_element_type=F32)


BLOCK = 256


def attend_kernel(q_ref, k_ref, v_ref, start_ref, o_ref, lse_ref):
    length = q_ref.shape[0]
    for at in range(length // BLOCK):
        rows = slice(at * BLOCK, (at + 1) * BLOCK)
        reach = (at + 1) * BLOCK
        key = lax.broadcasted_iota(jnp.int32, (BLOCK, reach), 1)
        query = lax.broadcasted_iota(jnp.int32, (BLOCK, reach), 0) + at * BLOCK
        allowed = (key >= start_ref[rows, :]) & (key <= query)
        mixed, logs = [], []
        for head in range(q_ref.shape[1] // HD):
            lanes = slice(head * HD, (head + 1) * HD)
            scores = dot_t(q_ref[rows, lanes] * SCALE, k_ref[:reach, lanes])
            scores = jnp.where(allowed, scores, MASKED)
            summit = jnp.max(scores, axis=1, keepdims=True)
            weights = jnp.exp(scores - summit)
            total = jnp.sum(weights, axis=1, keepdims=True)
            chances = (weights * (1.0 / total)).astype(BF16)
            mixed.append(dot(chances, v_ref[:reach, lanes]))
            logs.append(summit + jnp.log(total))
        o_ref[rows, :] = jnp.concatenate(mixed, axis=1).astype(BF16)
        lse_ref[0, rows, :] = jnp.concatenate(logs, axis=1)


def attend(query, keys, values, start):
    length, width = query.shape
    pairs = width // 128
    block = pl.BlockSpec((length, 128), lambda i: (0, i))
    return pl.pallas_call(
        attend_kernel,
        grid=(pairs,),
        in_specs=[block, block, block, pl.BlockSpec((length, 1), lambda i: (0, 0))],
        out_specs=[block, pl.BlockSpec((1, length, 2), lambda i: (i, 0, 0))],
        out_shape=[
            jax.ShapeDtypeStruct((length, width), BF16),
            jax.ShapeDtypeStruct((pairs, length, 2), F32),
        ],
        compiler_params=pltpu.CompilerParams(vmem_limit_bytes=48 * 2**20),
        cost_estimate=pl.CostEstimate(
            flops=4 * length * length * width, bytes_accessed=8 * length * width,
            transcendentals=length * length * width // HD,
        ),
        name="attend",
    )(query, keys, values, start)


def attend_back_kernel(
    q_ref, k_ref, v_ref, g_ref, start_ref, lse_ref, inner_ref, dq_ref, dk_ref, dv_ref
):
    length = q_ref.shape[0]
    dk_ref[...] = jnp.zeros_like(dk_ref)
    dv_ref[...] = jnp.zeros_like(dv_ref)
    for at in range(length // BLOCK):
        rows = slice(at * BLOCK, (at + 1) * BLOCK)
        reach = (at + 1) * BLOCK
        key = lax.broadcasted_iota(jnp.int32, (reach, BLOCK), 0)
        query = lax.broadcasted_iota(jnp.int32, (reach, BLOCK), 1) + at * BLOCK
        allowed = (key >= start_ref[:, rows]) & (key <= query)
        dqs, dks, dvs = [], [], []
        for head in range(q_ref.shape[1] // HD):
            lanes = slice(head * HD, (head + 1) * HD)
            k_head, g_head = k_ref[:reach, lanes], g_ref[rows, lanes]
            q_head = q_ref[rows, lanes] * SCALE
            scores = dot_t(k_head, q_head) - lse_ref[0, head : head + 1, rows]
            chances = jnp.exp(jnp.where(allowed, scores, MASKED))
            grad_prob = dot_t(v_ref[:reach, lanes], g_head)
            grad_score = chances * (grad_prob - inner_ref[0, head : head + 1, rows])
            grad_score = grad_score.astype(BF16)
            dvs.append(dot(chances.astype(BF16), g_head))
            dks.append(dot(grad_score, q_head))
            dqs.append(t_dot(grad_score, k_head) * SCALE)
        dq_ref[rows, :] = jnp.concatenate(dqs, axis=1)
        dk_ref[:reach, :] += jnp.concatenate(dks, axis=1)
        dv_ref[:reach, :] += jnp.concatenate(dvs, axis=1)


def attend_back(query, keys, values, grad, start, logs, inner):
    length, width = query.shape
    pairs = width // 128
    block = pl.BlockSpec((length, 128), lambda i: (0, i))
    line = pl.BlockSpec((1, 2, length), lambda i: (i, 0, 0))
    return pl.pallas_call(
        attend_back_kernel,
        grid=(pairs,),
        in_specs=[block] * 4 + [pl.BlockSpec((1, length), lambda i: (0, 0)), line, line],
        out_specs=[block] * 3,
        out_shape=[jax.ShapeDtypeStruct((length, width), F32)] * 3,
        compiler_params=pltpu.CompilerParams(vmem_limit_bytes=48 * 2**20),
        cost_estimate=pl.CostEstimate(
            flops=10 * length * length * width, bytes_accessed=20 * length * width,
            transcendentals=length * length * width // HD,
        ),
        name="attend_back",
    )(query, keys, values, grad, start, logs, inner)


def swap(block, distance):
    count = lax.axis_size("narrow")
    return lax.ppermute(block, "narrow", [(i, i ^ distance) for i in range(count)])


def pick(stack, table, at):
    return lax.dynamic_index_in_dim(stack, jnp.asarray(table)[at], 0, keepdims=False)


def by_heads(block, at):
    parts = jnp.stack(jnp.split(block, 3, axis=1))
    own = pick(parts, [0, 2, 0, 2], at)
    near = swap(parts[1], 1)
    far = swap(pick(parts, [2, 0, 2, 0], at), 2)
    parts = jnp.stack([own, near, far])
    order = jnp.asarray([[0, 1, 2], [1, 0, 2], [2, 0, 1], [2, 1, 0]])[at]
    return jnp.concatenate(
        [lax.dynamic_index_in_dim(parts, order[i], 0, keepdims=False) for i in range(3)], axis=1
    )


def from_heads(block, at):
    parts = jnp.stack(jnp.split(block, 3, axis=1))
    own = pick(parts, [0, 1, 1, 2], at)
    near = swap(pick(parts, [1, 0, 2, 1], at), 1)
    far = swap(pick(parts, [2, 2, 0, 0], at), 2)
    parts = jnp.stack([own, near, far])
    order = jnp.asarray([[0, 1, 2], [2, 1, 0], [0, 1, 2], [2, 1, 0]])[at]
    return jnp.concatenate(
        [lax.dynamic_index_in_dim(parts, order[i], 0, keepdims=False) for i in range(3)], axis=1
    )


def to_rows(block):
    return lax.all_to_all(block, "narrow", split_axis=0, concat_axis=1, tiled=True)


def to_columns(block):
    return lax.all_to_all(block, "narrow", split_axis=1, concat_axis=0, tiled=True)


def gather(block):
    return lax.all_gather(block, "narrow", axis=0, tiled=True)


def scatter(block):
    return lax.psum_scatter(
        block.astype(BF16), "narrow", scatter_dimension=0, tiled=True
    ).astype(F32)


def layer_forward(resid, weights, start, tables):
    w_qkv, w_out, w_up, b_up, w_down, gains, shifts = weights
    normed = gather(layer_norm(resid, gains[0], shifts[0]).astype(BF16))
    query, keys, values = jnp.split(dot(normed, w_qkv), 3, axis=1)
    query = rotate(query, *tables).astype(BF16)
    keys = rotate(keys, *tables).astype(BF16)
    values = values.astype(BF16)
    mixture, logs = attend(query, keys, values, start[:, None])
    branch = scatter(dot(mixture, w_out))
    middle = resid + layer_norm(branch, gains[1], shifts[1])
    inner = gather(layer_norm(middle, gains[2], shifts[2]).astype(BF16))
    hidden = dot(inner, w_up) + b_up
    second = scatter(dot(smooth(hidden).astype(BF16), w_down))
    result = middle + layer_norm(second, gains[3], shifts[3])
    return result, (resid, normed, query, keys, values, mixture, logs, branch, middle, inner, hidden, second)


def layer_backward(grad, saved, weights, start, tables):
    w_qkv, w_out, w_up, b_up, w_down, gains, shifts = weights
    resid, normed, query, keys, values, mixture, logs, branch, middle, inner, hidden, second = saved
    grad_second, gain_3, shift_3 = jax.vjp(layer_norm, second, gains[3], shifts[3])[1](grad)
    grad_second = gather(grad_second.astype(BF16))
    grad_down = t_dot(smooth(hidden).astype(BF16), grad_second)
    grad_hidden = jax.vjp(smooth, hidden)[1](dot_t(grad_second, w_down))[0].astype(BF16)
    grad_b_up = jnp.sum(grad_hidden.astype(F32), axis=0)
    grad_up = t_dot(inner, grad_hidden)
    grad_inner = scatter(dot_t(grad_hidden, w_up))
    grad_middle, gain_2, shift_2 = jax.vjp(layer_norm, middle, gains[2], shifts[2])[1](grad_inner)
    grad_middle = grad + grad_middle
    grad_branch, gain_1, shift_1 = jax.vjp(layer_norm, branch, gains[1], shifts[1])[1](grad_middle)
    grad_branch = gather(grad_branch.astype(BF16))
    grad_out = t_dot(mixture, grad_branch)
    grad_mixture = dot_t(grad_branch, w_out).astype(BF16)
    length = grad_mixture.shape[0]
    inner_sums = jnp.sum(
        (grad_mixture.astype(F32) * mixture.astype(F32)).reshape(length, -1, 2, HD), axis=-1
    ).transpose(1, 2, 0)
    dq, dk, dv = attend_back(
        query, keys, values, grad_mixture, start[None], logs.transpose(0, 2, 1), inner_sums
    )
    cosine, sine = tables
    grad_projected = jnp.concatenate(
        [rotate(dq, cosine, -sine), rotate(dk, cosine, -sine), dv], axis=1
    ).astype(BF16)
    grad_qkv = t_dot(normed, grad_projected)
    grad_normed = scatter(dot_t(grad_projected, w_qkv))
    grad_resid, gain_0, shift_0 = jax.vjp(layer_norm, resid, gains[0], shifts[0])[1](grad_normed)
    grads = (
        grad_qkv,
        grad_out,
        grad_up,
        grad_b_up,
        grad_down,
        jnp.stack([gain_0, gain_1, gain_2, gain_3]),
        jnp.stack([shift_0, shift_1, shift_2, shift_3]),
    )
    return grad_middle + grad_resid, grads


def reduce_grads(grads, at):
    def fold(block):
        return lax.psum_scatter(block.astype(BF16), "wide", scatter_dimension=0, tiled=True)

    def spread(block):
        return lax.all_gather(block, "wide", axis=0, tiled=True)

    def spread_rows(block):
        wide, narrow = lax.axis_size("wide"), lax.axis_size("narrow")
        rows, width = block.shape
        full = spread(block).reshape(wide, narrow, rows // narrow, width)
        return full.transpose(1, 0, 2, 3).reshape(wide * rows, width)

    qkv, out, up, b_up, down, gains, shifts = grads
    qkv = spread(from_heads(fold(qkv), at))
    out = spread_rows(to_columns(fold(out)))
    up = spread(fold(up))
    down = spread_rows(to_columns(fold(down)))
    b_up = lax.psum(b_up, "wide")
    norms = lax.psum(jnp.concatenate([gains, shifts]), ("wide", "narrow"))
    part = norms.shape[1] // lax.axis_size("narrow")
    norms = lax.dynamic_slice_in_dim(norms, at * part, part, 1)
    return qkv, out, up, b_up, down, norms[:4], norms[4:]


def on_device(ends, lengths, w_qkv, w_out, w_up, b_up, w_down, norm_gain, norm_bias):
    wide = lax.axis_size("wide")
    narrow = lax.axis_size("narrow")
    halfway = wide // 2
    flip = wide - 2
    wide_at = lax.axis_index("wide")
    at = lax.axis_index("narrow")
    first = wide_at < halfway
    row_count = ends.shape[0] // 2
    width = ends.shape[1]
    length = row_count * narrow
    blocks = ends.reshape(2, row_count, width)

    def route(block, pairs):
        return lax.ppermute(block, "wide", pairs)

    groups = range(halfway)
    x_came = route(blocks[1], [(g, g ^ flip) for g in groups])
    dy_first = route(blocks[0], [(g + halfway, g) for g in groups])
    dy_second = route(blocks[1], [(g + halfway, g ^ flip) for g in groups])
    resid = jnp.where(first, blocks[0], x_came).astype(F32)
    upstream = jnp.where(first, dy_first, dy_second).astype(F32)
    group_at = jnp.where(first, wide_at, wide_at ^ flip)
    micro_at = jnp.where(first, 0, 1)

    own_lengths = lengths[group_at, micro_at]
    places = jnp.arange(length, dtype=jnp.int32)
    passed = (places[:, None] >= jnp.cumsum(own_lengths)[None, :]).astype(jnp.int32)
    start = jnp.sum(passed * own_lengths[None, :], axis=1)
    tables = rope_tables(places - start)

    def weights_of(layer):
        return (
            by_heads(w_qkv[layer], at),
            to_rows(w_out[layer]),
            w_up[layer],
            b_up[layer].astype(F32),
            to_rows(w_down[layer]),
            lax.all_gather(norm_gain[layer], "narrow", axis=1, tiled=True).astype(F32),
            lax.all_gather(norm_bias[layer], "narrow", axis=1, tiled=True).astype(F32),
        )

    weights = [weights_of(layer) for layer in range(2)]
    middle, saved_first = layer_forward(resid, weights[0], start, tables)
    middle = middle.astype(BF16).astype(F32)
    result, saved_second = layer_forward(middle, weights[1], start, tables)
    result = result.astype(BF16)
    grad, grads_second = layer_backward(upstream, saved_second, weights[1], start, tables)
    totals_second = reduce_grads(grads_second, at)
    grad = grad.astype(BF16).astype(F32)
    grad, grads_first = layer_backward(grad, saved_first, weights[0], start, tables)
    totals_first = reduce_grads(grads_first, at)
    grad = grad.astype(BF16)

    grad_came = route(grad, [(g ^ flip, g) for g in groups])
    result_first = route(result, [(g, g + halfway) for g in groups])
    result_second = route(result, [(g ^ flip, g + halfway) for g in groups])
    ends_out = jnp.where(
        first,
        jnp.concatenate([grad, grad_came]),
        jnp.concatenate([result_first, result_second]),
    )
    totals = [jnp.stack([a.astype(F32), b.astype(F32)]) for a, b in zip(totals_first, totals_second)]
    return (ends_out,) + tuple(totals)


def solution(mesh):
    placed = (
        P(("wide", "narrow"), None),
        P(),
        P(None, None, "narrow"),
        P(None, None, "narrow"),
        P(None, None, "narrow"),
        P(None, "narrow"),
        P(None, None, "narrow"),
        P(None, None, "narrow"),
        P(None, None, "narrow"),
    )
    return jax.shard_map(
        on_device,
        mesh=mesh,
        in_specs=placed,
        out_specs=(P(("wide", "narrow"), None),) + placed[2:],
        check_vma=False,
    )
```

```python
import functools
import math

import jax
import jax.numpy as jnp
from jax import lax
from jax.experimental import pallas as pl
from jax.experimental.pallas import tpu as pltpu
from jax.sharding import PartitionSpec as P

HD = 64
EPSILON = 1e-05
MASKED = -1e30
SCALE = HD ** (-0.5)
F32 = jnp.float32
BF16 = jnp.bfloat16


def layer_norm(values, gain_row, shift_row):
    center = jnp.mean(values, axis=-1, keepdims=True)
    centred = values - center
    spread = jnp.mean(centred * centred, axis=-1, keepdims=True)
    return centred * lax.rsqrt(spread + EPSILON) * gain_row + shift_row


def rope_tables(offsets):
    halfway = HD // 2
    ladder = jnp.arange(halfway, dtype=F32) * (2.0 / HD)
    inverse = jnp.exp(-math.log(10000.0) * ladder)
    angles = offsets.astype(F32)[:, None] * inverse[None, :]
    cosine, sine = jnp.cos(angles), jnp.sin(angles)
    return (
        jnp.concatenate([cosine, cosine] * 2, axis=1),
        jnp.concatenate([-sine, sine] * 2, axis=1),
    )


def dot(left, right):
    return jnp.dot(left, right, preferred_element_type=F32)


def dot_t(left, right):
    return lax.dot_general(left, right, (((1,), (1,)), ((), ())), preferred_element_type=F32)


def t_dot(left, right):
    return lax.dot_general(left, right, (((0,), (0,)), ((), ())), preferred_element_type=F32)


MESH = pl.DeviceIdType.MESH
SEMAPHORES = 160


def layer_norm_back(values, grad, gain_row):
    center = jnp.mean(values, axis=-1, keepdims=True)
    centred = values - center
    scale = lax.rsqrt(jnp.mean(centred * centred, axis=-1, keepdims=True) + EPSILON)
    unit = centred * scale
    inner = grad * gain_row
    mean = jnp.mean(inner, axis=-1, keepdims=True)
    slope = jnp.mean(inner * unit, axis=-1, keepdims=True)
    grad_values = scale * (inner - mean - unit * slope)
    return (
        grad_values,
        jnp.sum(grad * unit, axis=0, keepdims=True),
        jnp.sum(grad, axis=0, keepdims=True),
    )


class Wire:
    def __init__(self, sems):
        self.sems, self.used, self.made = sems, 0, []
        self.at = lax.axis_index("narrow")
        self.near = self.at + 1 - 2 * lax.rem(self.at, 2)
        self.far = lax.rem(self.at + 2, 4)
        self.diagonal = lax.rem(self.near + 2, 4)

    def barrier(self):
        barrier = pltpu.get_barrier_semaphore()
        for peer in (self.near, self.far):
            pl.semaphore_signal(barrier, inc=1, device_id={"narrow": peer}, device_id_type=MESH)
        pl.semaphore_wait(barrier, 2)

    def copy(self, source, target, peer):
        made = pltpu.make_async_remote_copy(
            src_ref=source,
            dst_ref=target,
            send_sem=self.sems.at[self.used],
            recv_sem=self.sems.at[self.used + 1],
            device_id=peer if isinstance(peer, dict) else {"narrow": peer},
            device_id_type=MESH,
        )
        self.used += 2
        self.made.append(made)
        return made

    def send(self, source, target, peer):
        made = self.copy(source, target, peer)
        made.start()
        return made

    def finish(self):
        for made in self.made:
            made.wait_send()


def block_rows(block, size, part=0, parts=1):
    step = size // parts
    return pl.ds(pl.multiple_of(block * size + part * step, step), step)


class Gather:
    def __init__(self, wire, full, size):
        self.wire, self.full, self.size = wire, full, size
        self.to_near, self.to_far, self.relayed = [], [], []

    def rows(self, block, part):
        return self.full.at[block_rows(block, self.size, part, 2)]

    def push(self, part):
        own = self.rows(self.wire.at, part)
        self.to_near.append(self.wire.send(own, own, self.wire.near))
        self.to_far.append(self.wire.send(own, own, self.wire.far))

    def wait_near(self):
        for made in self.to_near:
            made.wait_recv()

    def relay(self, part):
        self.to_far[part].wait_recv()
        held = self.rows(self.wire.far, part)
        self.relayed.append(self.wire.send(held, held, self.wire.near))

    def wait_diagonal(self, part):
        self.relayed[part].wait_recv()


class Scatter:
    def __init__(self, wire, held, own, parts):
        self.held, self.own = held, own
        self.size = own.shape[0]
        step = self.size // parts
        self.cuts = [pl.ds(i * step, step) for i in range(parts)]

        def copies(out, into, peer, cuts):
            return [wire.copy(held.at[out, cut], held.at[into, cut], peer) for cut in cuts]

        self.side = copies(0, 1, wire.near, self.cuts)
        self.cross = copies(2, 3, wire.far, self.cuts)
        self.home = copies(4, 5, wire.near, [pl.ds(0, self.size)])[0]

    def put_diagonal(self, partial, part):
        self.held[0, self.cuts[part]] = partial.astype(BF16)
        self.side[part].start()

    def put_far(self, partial, part):
        cut = self.cuts[part]
        self.side[part].wait_recv()
        self.held[2, cut] = (partial + self.held[1, cut].astype(F32)).astype(BF16)
        self.cross[part].start()

    def put_near(self, partial):
        self.held[4] = partial.astype(BF16)
        self.home.start()

    def total(self):
        self.home.wait_recv()
        for made in self.cross:
            made.wait_recv()
        return self.own[...] + self.held[5].astype(F32) + self.held[3].astype(F32)


def turn(field, cosine, sine):
    lane = lax.broadcasted_iota(jnp.int32, cosine.shape, 1)
    first = lax.rem(lane, HD) < HD // 2
    turned = []
    for at in range(0, field.shape[1], 128):
        part = field[:, at : at + 128]
        swapped = jnp.where(
            first, pltpu.roll(part, 128 - HD // 2, 1), pltpu.roll(part, HD // 2, 1)
        )
        turned.append(part * cosine + swapped * sine)
    return jnp.concatenate(turned, axis=1)


def vmem(count):
    return [pl.BlockSpec(memory_space=pltpu.VMEM)] * count


def shaped(*entries):
    return [jax.ShapeDtypeStruct(shape, kind) for shape, kind in entries]


def call(kernel, number, outs, scratch, flops, *operands):
    return pl.pallas_call(
        kernel,
        in_specs=vmem(len(operands)),
        out_specs=vmem(len(outs)),
        out_shape=shaped(*outs),
        scratch_shapes=scratch + [pltpu.SemaphoreType.DMA((SEMAPHORES,))],
        compiler_params=pltpu.CompilerParams(
            collective_id=number, has_side_effects=True, vmem_limit_bytes=52 * 2**20
        ),
        cost_estimate=pl.CostEstimate(flops=flops, bytes_accessed=2**24, transcendentals=0),
        name=kernel.__name__,
    )(*operands)


def attend_half_kernel(
    x_ref, gain_ref, shift_ref, cos_ref, sin_ref, start_ref, w_qkv_ref, w_out_ref,
    a_ref, q_ref, k_ref, v_ref, o_ref, lse_ref, z_ref, h_ref, c_ref,
    held, own, sems,
):
    size = x_ref.shape[0]
    wire = Wire(sems)
    wire.barrier()
    gather = Gather(wire, a_ref, size)
    for part in range(2):
        rows = pl.ds(part * (size // 2), size // 2)
        normed = layer_norm(x_ref[rows], gain_ref[0:1], shift_ref[0:1])
        a_ref[block_rows(wire.at, size, part, 2)] = normed.astype(BF16)
        gather.push(part)
    width = q_ref.shape[1]

    def project(block):
        rows = block_rows(block, size)
        projected = dot(a_ref[rows], w_qkv_ref[...])
        cosine, sine = cos_ref[rows], sin_ref[rows]
        q_ref[rows] = turn(projected[:, :width], cosine, sine).astype(BF16)
        k_ref[rows] = turn(projected[:, width : 2 * width], cosine, sine).astype(BF16)
        v_ref[rows] = projected[:, 2 * width :].astype(BF16)

    project(wire.at)
    gather.wait_near()
    project(wire.near)
    gather.relay(0)
    gather.relay(1)
    project(wire.far)
    gather.wait_diagonal(0)
    gather.wait_diagonal(1)
    project(wire.diagonal)

    scatter = Scatter(wire, held, own, 1)
    for block in (3, 1, 2, 0):
        rows = slice(block * size, (block + 1) * size)
        reach = (block + 1) * size
        key = lax.broadcasted_iota(jnp.int32, (size, reach), 1)
        query = lax.broadcasted_iota(jnp.int32, (size, reach), 0) + block * size
        allowed = (key >= start_ref[rows, :]) & (key <= query)
        mixed, logs = [], jnp.zeros((size, 128), F32)
        lane = lax.broadcasted_iota(jnp.int32, (size, 128), 1)
        for head in range(width // HD):
            lanes = slice(head * HD, (head + 1) * HD)
            scores = dot_t(q_ref[rows, lanes] * SCALE, k_ref[:reach, lanes])
            scores = jnp.where(allowed, scores, MASKED)
            summit = jnp.max(scores, axis=1, keepdims=True)
            weights = jnp.exp(scores - summit)
            total = jnp.sum(weights, axis=1, keepdims=True)
            chances = (weights * (1.0 / total)).astype(BF16)
            mixed.append(dot(chances, v_ref[:reach, lanes]))
            logs = jnp.where(lane == head, summit + jnp.log(total), logs)
        o_ref[rows, :] = jnp.concatenate(mixed, axis=1).astype(BF16)
        lse_ref[:, rows] = logs.T[: lse_ref.shape[0]]
        partial = dot(o_ref[rows, :], w_out_ref[...])

        @pl.when(wire.diagonal == block)
        def _():
            scatter.put_diagonal(partial, 0)

        @pl.when(wire.far == block)
        def _():
            scatter.put_far(partial, 0)

        @pl.when(wire.near == block)
        def _():
            scatter.put_near(partial)

        @pl.when(wire.at == block)
        def _():
            own[...] = partial

    branch = scatter.total()
    z_ref[...] = branch
    middle = x_ref[...] + layer_norm(branch, gain_ref[1:2], shift_ref[1:2])
    h_ref[...] = middle
    c_ref[...] = layer_norm(middle, gain_ref[2:3], shift_ref[2:3]).astype(BF16)
    wire.finish()


def attend_half(resid, gains, shifts, cosine, sine, start, w_qkv, w_out):
    size, width = resid.shape
    length, part = cosine.shape[0], w_out.shape[0]
    return call(
        attend_half_kernel,
        1,
        [((length, width), BF16)]
        + [((length, part), BF16)] * 4
        + [((8, length), F32), ((size, width), F32), ((size, width), F32), ((size, width), BF16)],
        [pltpu.VMEM((6, size, width), BF16), pltpu.VMEM((size, width), F32)],
        8 * length * width * part + 4 * length * length * part,
        resid, gains, shifts, cosine, sine, start, w_qkv, w_out,
    )


def feed_half_kernel(
    c_ref, h_ref, gain_ref, shift_ref, w_up_ref, b_up_ref, w_down_ref,
    inner_ref, e_ref, d_ref, w_ref, y_ref,
    held, own, sems,
):
    size = c_ref.shape[0]
    half = size // 2
    wire = Wire(sems)
    wire.barrier()
    gather = Gather(wire, inner_ref, size)
    for part in range(2):
        inner_ref[block_rows(wire.at, size, part, 2)] = c_ref[pl.ds(part * half, half)]
        gather.push(part)
    scatter = Scatter(wire, held, own, 2)

    def feed(cuts):
        inner = jnp.concatenate([inner_ref[cut] for cut in cuts])
        hidden = dot(inner, w_up_ref[...]) + b_up_ref[...]
        below = 0.5 + 0.5 * lax.erf(hidden * (0.5**0.5))
        density = jnp.exp(-0.5 * hidden * hidden) * ((2.0 * math.pi) ** -0.5)
        active = (hidden * below).astype(BF16)
        slope = (below + hidden * density).astype(BF16)
        for at, cut in enumerate(cuts):
            step = inner.shape[0] // len(cuts)
            e_ref[cut] = active[at * step : (at + 1) * step]
            d_ref[cut] = slope[at * step : (at + 1) * step]
        return dot(active, w_down_ref[...])

    own[...] = feed([block_rows(wire.at, size)])
    gather.wait_near()
    scatter.put_near(feed([block_rows(wire.near, size)]))
    for part in range(2):
        gather.relay(part)
        gather.wait_diagonal(part)
        partial = feed(
            [block_rows(wire.diagonal, size, part, 2), block_rows(wire.far, size, part, 2)]
        )
        scatter.put_diagonal(partial[:half], part)
        scatter.put_far(partial[half:], part)
    second = scatter.total()
    w_ref[...] = second
    y_ref[...] = h_ref[...] + layer_norm(second, gain_ref[3:4], shift_ref[3:4])
    wire.finish()


def feed_half(inner, middle, gains, shifts, w_up, b_up, w_down):
    size, width = inner.shape
    length, hidden = 4 * size, w_up.shape[1]
    return call(
        feed_half_kernel,
        2,
        [((length, width), BF16)]
        + [((length, hidden), BF16)] * 2
        + [((size, width), F32)] * 2,
        [pltpu.VMEM((6, size, width), BF16), pltpu.VMEM((size, width), F32)],
        4 * length * width * hidden,
        inner, middle, gains, shifts, w_up, b_up, w_down,
    )


def feed_back_kernel(
    g_ref, w_ref, h_ref, z_ref, gain_ref, inner_ref, e_ref, d_ref, w_up_ref, w_down_ref,
    grad_down_ref, grad_up_ref, grad_b_ref, norms_ref, dh_ref, dz_ref,
    second, hidden, held, own, sems,
):
    size = g_ref.shape[0]
    half = size // 2
    wire = Wire(sems)
    wire.barrier()
    gather = Gather(wire, second, size)
    norms = [jnp.zeros((1, g_ref.shape[1]), F32)] * 2
    for part in range(2):
        rows = pl.ds(part * half, half)
        grad, gain, shift = layer_norm_back(w_ref[rows], g_ref[rows], gain_ref[3:4])
        second[block_rows(wire.at, size, part, 2)] = grad.astype(BF16)
        gather.push(part)
        norms = [norms[0] + gain, norms[1] + shift]
    norms_ref[3:4] = norms[0]
    norms_ref[7:8] = norms[1]
    norms_ref[0:1] = jnp.zeros_like(norms[0])
    norms_ref[4:5] = jnp.zeros_like(norms[0])
    scatter = Scatter(wire, held, own, 2)

    def feed(cuts, first=False):
        grad = jnp.concatenate([second[cut] for cut in cuts])
        slope = jnp.concatenate([d_ref[cut] for cut in cuts]).astype(F32)
        grad = (slope * dot_t(grad, w_down_ref[...])).astype(BF16)
        for at, cut in enumerate(cuts):
            step = grad.shape[0] // len(cuts)
            hidden[cut] = grad[at * step : (at + 1) * step]
        bias = jnp.sum(grad.astype(F32), axis=0, keepdims=True)
        grad_b_ref[...] = bias if first else grad_b_ref[...] + bias
        return dot_t(grad, w_up_ref[...])

    own[...] = feed([block_rows(wire.at, size)], True)
    gather.wait_near()
    scatter.put_near(feed([block_rows(wire.near, size)]))
    for part in range(2):
        gather.relay(part)
        gather.wait_diagonal(part)
        partial = feed(
            [block_rows(wire.diagonal, size, part, 2), block_rows(wire.far, size, part, 2)]
        )
        scatter.put_diagonal(partial[:half], part)
        scatter.put_far(partial[half:], part)
    for at in range(0, e_ref.shape[1], 256):
        cut = slice(at, at + 256)
        grad_down_ref[cut, :] = t_dot(e_ref[:, cut], second[...]).astype(BF16)
    for at in range(0, inner_ref.shape[1], 256):
        cut = slice(at, at + 256)
        grad_up_ref[cut, :] = t_dot(inner_ref[:, cut], hidden[...]).astype(BF16)
    grad, gain, shift = layer_norm_back(h_ref[...], scatter.total(), gain_ref[2:3])
    norms_ref[2:3] = gain
    norms_ref[6:7] = shift
    grad = g_ref[...] + grad
    dh_ref[...] = grad
    grad, gain, shift = layer_norm_back(z_ref[...], grad, gain_ref[1:2])
    norms_ref[1:2] = gain
    norms_ref[5:6] = shift
    dz_ref[...] = grad.astype(BF16)
    wire.finish()


def feed_back(grad, second, middle, branch, gains, inner, active, slope, w_up, w_down):
    size, width = grad.shape
    length, hidden = 4 * size, w_up.shape[1]
    return call(
        feed_back_kernel,
        3,
        [
            ((hidden, width), BF16),
            ((width, hidden), BF16),
            ((1, hidden), F32),
            ((8, width), F32),
            ((size, width), F32),
            ((size, width), BF16),
        ],
        [
            pltpu.VMEM((length, width), BF16),
            pltpu.VMEM((length, hidden), BF16),
            pltpu.VMEM((6, size, width), BF16),
            pltpu.VMEM((size, width), F32),
        ],
        8 * length * width * hidden,
        grad, second, middle, branch, gains, inner, active, slope, w_up, w_down,
    )


def attend_back_kernel(
    dz_ref, dh_ref, x_ref, gain_ref, a_ref, q_ref, k_ref, v_ref, o_ref, lse_ref, start_ref,
    cos_ref, sin_ref, w_qkv_ref, w_out_ref,
    grad_qkv_ref, grad_out_ref, norms_ref, dx_ref,
    branch, mixture, projected, dk, dv, held, own, sems,
):
    size = dz_ref.shape[0]
    length, width = q_ref.shape
    half = size // 2
    wire = Wire(sems)
    wire.barrier()
    gather = Gather(wire, branch, size)
    for part in range(2):
        branch[block_rows(wire.at, size, part, 2)] = dz_ref[pl.ds(part * half, half)]
        gather.push(part)

    def unmix(block):
        rows = block_rows(block, size)
        mixture[rows] = dot_t(branch[rows], w_out_ref[...]).astype(BF16)

    dk[...] = jnp.zeros_like(dk)
    dv[...] = jnp.zeros_like(dv)
    unmix(wire.at)
    gather.wait_near()
    unmix(wire.near)
    gather.relay(0)
    gather.relay(1)
    unmix(wire.far)
    gather.wait_diagonal(0)
    gather.wait_diagonal(1)
    unmix(wire.diagonal)
    grad_out_ref[...] = t_dot(o_ref[...], branch[...]).astype(BF16)

    pick_head = (
        lax.broadcasted_iota(jnp.int32, (8, width), 1) // HD
        == lax.broadcasted_iota(jnp.int32, (8, width), 0)
    ).astype(F32)
    for block in range(length // size):
        rows = slice(block * size, (block + 1) * size)
        reach = (block + 1) * size
        key = lax.broadcasted_iota(jnp.int32, (reach, size), 0)
        query = lax.broadcasted_iota(jnp.int32, (reach, size), 1) + block * size
        allowed = (key >= start_ref[:, rows]) & (key <= query)
        inner = lax.dot_general(
            pick_head,
            mixture[rows].astype(F32) * o_ref[rows].astype(F32),
            (((1,), (1,)), ((), ())),
            precision=lax.Precision.HIGHEST,
            preferred_element_type=F32,
        )
        dqs, dks, dvs = [], [], []
        for head in range(width // HD):
            lanes = slice(head * HD, (head + 1) * HD)
            k_head, g_head = k_ref[:reach, lanes], mixture[rows, lanes]
            q_head = q_ref[rows, lanes] * SCALE
            scores = dot_t(k_head, q_head) - lse_ref[head : head + 1, rows]
            chances = jnp.exp(jnp.where(allowed, scores, MASKED))
            grad_prob = dot_t(v_ref[:reach, lanes], g_head)
            grad_score = (chances * (grad_prob - inner[head : head + 1])).astype(BF16)
            dvs.append(dot(chances.astype(BF16), g_head))
            dks.append(dot(grad_score, q_head))
            dqs.append(t_dot(grad_score, k_head) * SCALE)
        dq = jnp.concatenate(dqs, axis=1)
        projected[rows, :width] = turn(dq, cos_ref[rows], -sin_ref[rows]).astype(BF16)
        dk[:reach, :] += jnp.concatenate(dks, axis=1)
        dv[:reach, :] += jnp.concatenate(dvs, axis=1)
    for block in range(length // size):
        rows = slice(block * size, (block + 1) * size)
        turned = turn(dk[rows], cos_ref[rows], -sin_ref[rows])
        projected[rows, width : 2 * width] = turned.astype(BF16)
        projected[rows, 2 * width :] = dv[rows].astype(BF16)

    scatter = Scatter(wire, held, own, 2)

    def unproject(cut):
        return dot_t(projected[cut], w_qkv_ref[...])

    partial = unproject(block_rows(wire.diagonal, size))
    scatter.put_diagonal(partial[:half], 0)
    scatter.put_diagonal(partial[half:], 1)
    partial = unproject(block_rows(wire.far, size))
    scatter.put_far(partial[:half], 0)
    scatter.put_far(partial[half:], 1)
    scatter.put_near(unproject(block_rows(wire.near, size)))
    own[...] = unproject(block_rows(wire.at, size))
    for at in range(0, a_ref.shape[1], 256):
        cut = slice(at, at + 256)
        grad_qkv_ref[cut, :] = t_dot(a_ref[:, cut], projected[...]).astype(BF16)
    grad, gain, shift = layer_norm_back(x_ref[...], scatter.total(), gain_ref[0:1])
    norms_ref[...] = jnp.zeros_like(norms_ref)
    norms_ref[0:1] = gain
    norms_ref[4:5] = shift
    dx_ref[...] = (dh_ref[...] + grad).astype(BF16)
    wire.finish()


def attend_back(
    grad_branch, grad_middle, resid, gains, normed, query, keys, values, mixture, logs, start,
    cosine, sine, w_qkv, w_out,
):
    size, width = resid.shape
    length, part = query.shape
    return call(
        attend_back_kernel,
        4,
        [
            ((width, 3 * part), BF16),
            ((part, width), BF16),
            ((8, width), F32),
            ((size, width), BF16),
        ],
        [
            pltpu.VMEM((length, width), BF16),
            pltpu.VMEM((length, part), BF16),
            pltpu.VMEM((length, 3 * part), BF16),
            pltpu.VMEM((length, part), F32),
            pltpu.VMEM((length, part), F32),
            pltpu.VMEM((6, size, width), BF16),
            pltpu.VMEM((size, width), F32),
        ],
        16 * length * width * part + 10 * length * length * part,
        grad_branch, grad_middle, resid, gains, normed, query, keys, values, mixture, logs,
        start, cosine, sine, w_qkv, w_out,
    )


class Ring:
    def __init__(self):
        at = lax.axis_index("wide")
        self.pair = lax.rem(at, 2)
        self.turn = at // 2
        self.up = {"wide": lax.rem(self.turn + 1, 4) * 2 + self.pair}
        self.down = {"wide": lax.rem(self.turn + 3, 4) * 2 + self.pair}
        self.side = {"wide": at + 1 - 2 * self.pair}


def span(start, size):
    return pl.ds(pl.multiple_of(start, 16), size)


class Piece:
    def __init__(self, view, rows, by_side, ring):
        self.view, self.rows, self.by_side = view, rows, by_side
        self.eighth = rows // 8
        pair, turn = ring.pair, ring.turn
        if by_side:
            self.mine = pair * (rows // 2) + turn * self.eighth
            self.joined, self.joined_size = pair * (rows // 2), rows // 2
        else:
            self.mine = turn * (rows // 4) + pair * self.eighth
            self.joined, self.joined_size = turn * (rows // 4), rows // 4

    def own(self):
        return self.view(span(self.mine, self.eighth))

    def whole(self):
        return self.view(span(self.joined, self.joined_size))

    def around(self, ring, step, half):
        size = self.eighth if self.by_side else self.joined_size
        start = self.joined if self.by_side else 0
        other = lax.rem(ring.turn + step, 4) * size + start
        return self.view(span(other + half * (size // 2), size // 2))


def spread_steps(wire, ring, pieces):
    def both_ways(piece, part):
        return (
            wire.send(part, part, ring.up),
            wire.send(part, part, ring.down),
        )

    def onwards(piece, sent):
        sent[0].wait_recv()
        first = piece.around(ring, 3, 0)
        up = wire.send(first, first, ring.up)
        sent[1].wait_recv()
        second = piece.around(ring, 1, 1)
        return up, wire.send(second, second, ring.down)

    by_side = [piece for piece in pieces if piece.by_side]
    others = [piece for piece in pieces if not piece.by_side]
    sent = [both_ways(piece, piece.own()) for piece in by_side]
    across = [wire.send(piece.own(), piece.own(), ring.side) for piece in others]
    yield
    relayed = [onwards(piece, pair) for piece, pair in zip(by_side, sent)]
    for made in across:
        made.wait_recv()
    sent = [both_ways(piece, piece.whole()) for piece in others]
    yield
    for pair in relayed:
        for made in pair:
            made.wait_recv()
    across = [wire.send(piece.whole(), piece.whole(), ring.side) for piece in by_side]
    relayed = [onwards(piece, pair) for piece, pair in zip(others, sent)]
    yield
    for made in across:
        made.wait_recv()
    for pair in relayed:
        for made in pair:
            made.wait_recv()


def add_rows(target, rows, *sources):
    step = min(rows, 128)
    for at in range(0, rows, step):
        cut = pl.ds(at, step)
        total = sources[0](at, step).astype(F32)
        for source in sources[1:]:
            total = total + source(at, step).astype(F32)
        target[cut] = total.astype(BF16)


def part_of(ref, start=0):
    return lambda at, step: ref[span(start + at, step)]


def slot_of(ref, slot, start=0):
    return lambda at, step: ref[slot, span(start + at, step)]


class Fold:
    def __init__(self, wire, ring, ref, by_side, scratch):
        self.wire, self.ring, self.ref, self.by_side = wire, ring, ref, by_side
        self.joined, self.across, self.early, self.out, self.into, self.final = scratch
        self.rows = ref.shape[0]
        self.size = self.rows // 8 if by_side else self.rows // 4

    @staticmethod
    def scratch(rows, columns, by_side):
        size = rows // 8 if by_side else rows // 4
        joined = rows // 2 if by_side else rows // 4
        across = rows // 2 if by_side else rows // 8
        return [
            pltpu.VMEM((joined, columns), BF16),
            pltpu.VMEM((across, columns), BF16),
            pltpu.VMEM((2, size // 2, columns), BF16),
            pltpu.VMEM((2, size, columns), BF16),
            pltpu.VMEM((2, size, columns), BF16),
            pltpu.VMEM((rows // 8, columns), BF16),
        ]

    def source(self):
        return self.joined if self.by_side else self.ref

    def part(self, step):
        return lax.rem(self.ring.turn + step, 4) * self.size

    def start_side(self):
        pair = self.ring.pair
        if self.by_side:
            half = self.rows // 2
            source = self.ref.at[span((1 - pair) * half, half)]
        else:
            half = self.rows // 8
            source = self.joined.at[span((1 - pair) * half, half)]
        self.side = self.wire.send(source, self.across, self.ring.side)

    def end_side(self):
        self.side.wait_recv()
        pair = self.ring.pair
        if self.by_side:
            half = self.rows // 2
            add_rows(self.joined, half, part_of(self.ref, pair * half), part_of(self.across))
        else:
            half = self.rows // 8
            add_rows(self.final, half, part_of(self.joined, pair * half), part_of(self.across))

    def start_early(self):
        half = self.size // 2
        opposite = self.part(2)
        source = self.source()
        self.first = [
            self.wire.send(source.at[span(opposite, half)], self.early.at[0], self.ring.up),
            self.wire.send(source.at[span(opposite + half, half)], self.early.at[1], self.ring.down),
        ]

    def start_late(self):
        half = self.size // 2
        source = self.source()
        self.second = []
        for way, (step, peer) in enumerate([(1, self.ring.up), (3, self.ring.down)]):
            self.first[way].wait_recv()
            start = self.part(step)
            out = self.out.at[way]
            for at in (0, 1):
                cut = out.at[pl.ds(at * half, half)]
                if at == way:
                    add_rows(
                        cut, half, part_of(source, start + at * half), slot_of(self.early, way)
                    )
                else:
                    cut[...] = source[span(start + at * half, half)]
            self.second.append(self.wire.send(out, self.into.at[way], peer))

    def end_late(self):
        for made in self.second:
            made.wait_recv()
        target = self.final if self.by_side else self.joined
        start = self.part(0)
        add_rows(
            target,
            self.size,
            part_of(self.source(), start),
            slot_of(self.into, 0),
            slot_of(self.into, 1),
        )


def fold_steps(folds):
    by_side = [fold for fold in folds if fold.by_side]
    others = [fold for fold in folds if not fold.by_side]
    for fold in others:
        fold.start_early()
    for fold in by_side:
        fold.start_side()
    yield
    for fold in others:
        fold.start_late()
    yield
    for fold in by_side:
        fold.end_side()
        fold.start_early()
    yield
    for fold in others:
        fold.end_late()
        fold.start_side()
    for fold in by_side:
        fold.start_late()
    yield
    for fold in others:
        fold.end_side()
    for fold in by_side:
        fold.end_late()


def small_steps(wire, ring, norms_ref, bias_ref, narrow_in, sums, side_in, turn_in, total_ref):
    part = total_ref.shape[1]
    made = []

    def columns(device):
        return pl.ds(pl.multiple_of(device * part, part), part)

    for peer in (wire.near, wire.far, wire.diagonal):
        made.append(
            wire.send(norms_ref.at[:, columns(peer)], narrow_in.at[wire.at], {"narrow": peer})
        )
    narrow_in[wire.at] = norms_ref[:, columns(wire.at)]
    yield
    for copy in made:
        copy.wait_recv()
    total = narrow_in[0] + narrow_in[1] + narrow_in[2] + narrow_in[3]
    lines = [bias_ref[:, at * part : (at + 1) * part] for at in range(4)]
    sums[...] = jnp.concatenate([total] + lines + [jnp.zeros((4, part), F32)], axis=0)
    side = wire.send(sums, side_in, ring.side)
    yield
    side.wait_recv()
    turn_in[ring.turn] = sums[...] + side_in[...]
    own = turn_in.at[ring.turn]
    up, down = wire.send(own, own, ring.up), wire.send(own, own, ring.down)
    yield
    up.wait_recv()
    down.wait_recv()
    below = turn_in.at[lax.rem(ring.turn + 3, 4)]
    last = wire.send(below, below, ring.up)
    yield
    last.wait_recv()
    total_ref[...] = turn_in[0] + turn_in[1] + turn_in[2] + turn_in[3]


def wide_barrier(wire, ring):
    barrier = pltpu.get_barrier_semaphore()
    peers = [ring.up, ring.down, ring.side]
    peers += [{"narrow": peer} for peer in (wire.near, wire.far, wire.diagonal)]
    for peer in peers:
        pl.semaphore_signal(barrier, inc=1, device_id=peer, device_id_type=MESH)
    pl.semaphore_wait(barrier, len(peers))


def run(*steps):
    steps = list(steps)
    while steps:
        for at in list(steps):
            if next(at, "end") == "end":
                steps.remove(at)


def sum_gradients_kernel(
    qkv_ref, out_ref, up_ref, down_ref, norms_ref, bias_ref,
    full_qkv, full_out, full_up, full_down, total_ref,
    *scratch,
):
    narrow_in, sums, side_in, turn_in, sems = scratch[24:]
    wire, ring = Wire(sems), Ring()
    wide_barrier(wire, ring)
    down = Fold(wire, ring, down_ref, True, scratch[0:6])
    out = Fold(wire, ring, out_ref, True, scratch[6:12])
    up = Fold(wire, ring, up_ref, False, scratch[12:18])
    qkv = Fold(wire, ring, qkv_ref, False, scratch[18:24])
    run(
        fold_steps([down, out, up, qkv]),
        small_steps(
            wire, ring, norms_ref, bias_ref, narrow_in, sums, side_in, turn_in, total_ref
        ),
    )
    part = total_ref.shape[1]

    def columns(device):
        return pl.ds(pl.multiple_of(device * part, part), part)

    pieces = [
        Piece(lambda rows: full_down.at[:, rows], down_ref.shape[0], True, ring),
        Piece(lambda rows: full_out.at[:, rows], out_ref.shape[0], True, ring),
        Piece(lambda rows: full_up.at[rows], up_ref.shape[0], False, ring),
        Piece(lambda rows: full_qkv.at[rows], qkv_ref.shape[0], False, ring),
    ]
    made = []
    at = wire.at
    for fold, piece, full in ((down, pieces[0], full_down), (out, pieces[1], full_out)):
        slot = full.at[at, span(piece.mine, piece.eighth)]
        for peer in (wire.diagonal, wire.far, wire.near):
            made.append(wire.send(fold.final.at[:, columns(peer)], slot, {"narrow": peer}))
        slot[...] = fold.final[:, columns(at)]
    pieces[2].own()[...] = up.final[...]
    rows = span(pieces[3].mine, pieces[3].eighth)
    odd, upper = lax.rem(at, 2), at // 2
    made.append(
        wire.send(
            qkv.final.at[:, columns(2 - 2 * upper)],
            full_qkv.at[rows, columns(2 - 2 * odd)],
            {"narrow": wire.far},
        )
    )
    made.append(
        wire.send(
            qkv.final.at[:, columns(1 - odd + upper)],
            full_qkv.at[rows, columns(1)],
            {"narrow": wire.near},
        )
    )
    full_qkv[rows, columns(2 * odd)] = qkv.final[:, columns((at + 1) // 2)]
    for copy in made:
        copy.wait_recv()
    run(spread_steps(wire, ring, pieces))
    wire.finish()


def sum_gradients(qkv, out, up, down, norms, bias):
    narrow = lax.axis_size("narrow")
    part = norms.shape[1] // narrow
    items = ((down, True), (out, True), (up, False), (qkv, False))
    scratch = [entry for item, kind in items for entry in Fold.scratch(*item.shape, kind)]
    scratch += [
        pltpu.VMEM((narrow, 8, part), F32),
        pltpu.VMEM((16, part), F32),
        pltpu.VMEM((16, part), F32),
        pltpu.VMEM((4, 16, part), F32),
    ]
    return call(
        sum_gradients_kernel,
        5,
        [
            (qkv.shape, BF16),
            ((narrow, out.shape[0], part), BF16),
            (up.shape, BF16),
            ((narrow, down.shape[0], part), BF16),
            ((16, part), F32),
        ],
        scratch,
        0,
        qkv, out, up, down, norms, bias,
    )


def swap(block, distance):
    count = lax.axis_size("narrow")
    return lax.ppermute(block, "narrow", [(i, i ^ distance) for i in range(count)])


def pick(stack, table, at):
    return lax.dynamic_index_in_dim(stack, jnp.asarray(table)[at], 0, keepdims=False)


def by_heads(block, at):
    parts = jnp.stack(jnp.split(block, 3, axis=1))
    own = pick(parts, [0, 2, 0, 2], at)
    near = swap(parts[1], 1)
    far = swap(pick(parts, [2, 0, 2, 0], at), 2)
    parts = jnp.stack([own, near, far])
    order = jnp.asarray([[0, 1, 2], [1, 0, 2], [2, 0, 1], [2, 1, 0]])[at]
    return jnp.concatenate(
        [lax.dynamic_index_in_dim(parts, order[i], 0, keepdims=False) for i in range(3)], axis=1
    )


def from_heads(block, at):
    parts = jnp.stack(jnp.split(block, 3, axis=1))
    own = pick(parts, [0, 1, 1, 2], at)
    near = swap(pick(parts, [1, 0, 2, 1], at), 1)
    far = swap(pick(parts, [2, 2, 0, 0], at), 2)
    parts = jnp.stack([own, near, far])
    order = jnp.asarray([[0, 1, 2], [2, 1, 0], [0, 1, 2], [2, 1, 0]])[at]
    return jnp.concatenate(
        [lax.dynamic_index_in_dim(parts, order[i], 0, keepdims=False) for i in range(3)], axis=1
    )


def to_rows(block):
    return lax.all_to_all(block, "narrow", split_axis=0, concat_axis=1, tiled=True)


def to_columns(block):
    return lax.all_to_all(block, "narrow", split_axis=1, concat_axis=0, tiled=True)


def layer_forward(resid, weights, start, tables):
    w_qkv, w_out, w_up, b_up, w_down, gains, shifts = weights
    normed, query, keys, values, mixture, logs, branch, middle, inner = attend_half(
        resid, gains, shifts, *tables, start[:, None], w_qkv, w_out
    )
    inner, active, slope, second, result = feed_half(
        inner, middle, gains, shifts, w_up, b_up, w_down
    )
    return result, (
        resid, normed, query, keys, values, mixture, logs, branch, middle, inner, active, slope, second
    )


def layer_backward(grad, saved, weights, start, tables):
    w_qkv, w_out, w_up, b_up, w_down, gains, shifts = weights
    resid, normed, query, keys, values, mixture, logs, branch, middle, inner, active, slope, second = saved
    grad_down, grad_up, grad_b_up, norms, grad_middle, grad_branch = feed_back(
        grad, second, middle, branch, gains, inner, active, slope, w_up, w_down
    )
    grad_qkv, grad_out, norms_too, grad = attend_back(
        grad_branch, grad_middle, resid, gains, normed, query, keys, values, mixture, logs,
        start[None], *tables, w_qkv, w_out,
    )
    return grad, (grad_qkv, grad_out, grad_up, grad_b_up, grad_down, norms + norms_too)


def reduce_grads(grads, at):
    def fold(block):
        return lax.psum_scatter(block, "wide", scatter_dimension=0, tiled=True)

    def spread(block):
        return lax.all_gather(block, "wide", axis=0, tiled=True)

    def spread_rows(block):
        wide, narrow = lax.axis_size("wide"), lax.axis_size("narrow")
        rows, width = block.shape
        full = spread(block).reshape(wide, narrow, rows // narrow, width)
        return full.transpose(1, 0, 2, 3).reshape(wide * rows, width)

    qkv, out, up, b_up, down, norms = grads
    if lax.axis_size("wide") == 8:
        qkv, out, up, down, total = sum_gradients(qkv, out, up, down, norms, b_up)
        out, down = (block.reshape(-1, block.shape[2]) for block in (out, down))
        return qkv, out, up, total[8:12].reshape(-1), down, total[:4], total[4:8]
    qkv = spread(from_heads(fold(qkv), at))
    out = spread_rows(to_columns(fold(out)))
    up = spread(fold(up))
    down = spread_rows(to_columns(fold(down)))
    b_up = lax.psum(b_up[0], "wide")
    norms = lax.psum(norms, ("wide", "narrow"))
    part = norms.shape[1] // lax.axis_size("narrow")
    norms = lax.dynamic_slice_in_dim(norms, at * part, part, 1)
    return qkv, out, up, b_up, down, norms[:4], norms[4:]


def on_device(ends, lengths, w_qkv, w_out, w_up, b_up, w_down, norm_gain, norm_bias):
    wide = lax.axis_size("wide")
    narrow = lax.axis_size("narrow")
    halfway = wide // 2
    flip = wide - 2
    wide_at = lax.axis_index("wide")
    at = lax.axis_index("narrow")
    first = wide_at < halfway
    row_count = ends.shape[0] // 2
    width = ends.shape[1]
    length = row_count * narrow
    blocks = ends.reshape(2, row_count, width)

    def route(block, pairs):
        return lax.ppermute(block, "wide", pairs)

    groups = range(halfway)
    x_came = route(blocks[1], [(g, g ^ flip) for g in groups])
    dy_first = route(blocks[0], [(g + halfway, g) for g in groups])
    dy_second = route(blocks[1], [(g + halfway, g ^ flip) for g in groups])
    resid = jnp.where(first, blocks[0], x_came).astype(F32)
    upstream = jnp.where(first, dy_first, dy_second).astype(F32)
    group_at = jnp.where(first, wide_at, wide_at ^ flip)
    micro_at = jnp.where(first, 0, 1)

    own_lengths = lengths[group_at, micro_at]
    places = jnp.arange(length, dtype=jnp.int32)
    passed = (places[:, None] >= jnp.cumsum(own_lengths)[None, :]).astype(jnp.int32)
    start = jnp.sum(passed * own_lengths[None, :], axis=1)
    tables = rope_tables(places - start)

    def weights_of(layer):
        return (
            by_heads(w_qkv[layer], at),
            to_rows(w_out[layer]),
            w_up[layer],
            b_up[layer].astype(F32)[None],
            to_rows(w_down[layer]),
            lax.all_gather(norm_gain[layer], "narrow", axis=1, tiled=True).astype(F32),
            lax.all_gather(norm_bias[layer], "narrow", axis=1, tiled=True).astype(F32),
        )

    weights = [weights_of(layer) for layer in range(2)]
    middle, saved_first = layer_forward(resid, weights[0], start, tables)
    middle = middle.astype(BF16).astype(F32)
    result, saved_second = layer_forward(middle, weights[1], start, tables)
    result = result.astype(BF16)
    grad, grads_second = layer_backward(upstream, saved_second, weights[1], start, tables)
    totals_second = reduce_grads(grads_second, at)
    grad, grads_first = layer_backward(grad.astype(F32), saved_first, weights[0], start, tables)
    totals_first = reduce_grads(grads_first, at)

    grad_came = route(grad, [(g ^ flip, g) for g in groups])
    result_first = route(result, [(g, g + halfway) for g in groups])
    result_second = route(result, [(g ^ flip, g + halfway) for g in groups])
    ends_out = jnp.where(
        first,
        jnp.concatenate([grad, grad_came]),
        jnp.concatenate([result_first, result_second]),
    )
    totals = [jnp.stack([a.astype(F32), b.astype(F32)]) for a, b in zip(totals_first, totals_second)]
    return (ends_out,) + tuple(totals)


def solution(mesh):
    placed = (
        P(("wide", "narrow"), None),
        P(),
        P(None, None, "narrow"),
        P(None, None, "narrow"),
        P(None, None, "narrow"),
        P(None, "narrow"),
        P(None, None, "narrow"),
        P(None, None, "narrow"),
        P(None, None, "narrow"),
    )
    return jax.shard_map(
        on_device,
        mesh=mesh,
        in_specs=placed,
        out_specs=(P(("wide", "narrow"), None),) + placed[2:],
        check_vma=False,
    )
```

```python
import functools
import math

import jax
import jax.numpy as jnp
from jax import lax
from jax.experimental import pallas as pl
from jax.experimental.pallas import tpu as pltpu
from jax.sharding import PartitionSpec as P

HD = 64
EPSILON = 1e-05
MASKED = -1e30
SCALE = HD ** (-0.5)
F32 = jnp.float32
BF16 = jnp.bfloat16


def layer_norm(values, gain_row, shift_row):
    center = jnp.mean(values, axis=-1, keepdims=True)
    centred = values - center
    spread = jnp.mean(centred * centred, axis=-1, keepdims=True)
    return centred * lax.rsqrt(spread + EPSILON) * gain_row + shift_row


def rope_tables(offsets):
    halfway = HD // 2
    ladder = jnp.arange(halfway, dtype=F32) * (2.0 / HD)
    inverse = jnp.exp(-math.log(10000.0) * ladder)
    angles = offsets.astype(F32)[:, None] * inverse[None, :]
    cosine, sine = jnp.cos(angles), jnp.sin(angles)
    return (
        jnp.concatenate([cosine, cosine] * 2, axis=1),
        jnp.concatenate([-sine, sine] * 2, axis=1),
    )


def dot(left, right):
    return jnp.dot(left, right, preferred_element_type=F32)


def dot_t(left, right):
    return lax.dot_general(left, right, (((1,), (1,)), ((), ())), preferred_element_type=F32)


def t_dot(left, right):
    return lax.dot_general(left, right, (((0,), (0,)), ((), ())), preferred_element_type=F32)


MESH = pl.DeviceIdType.MESH
SEMAPHORES = 400


def layer_norm_back(values, grad, gain_row):
    center = jnp.mean(values, axis=-1, keepdims=True)
    centred = values - center
    scale = lax.rsqrt(jnp.mean(centred * centred, axis=-1, keepdims=True) + EPSILON)
    unit = centred * scale
    inner = grad * gain_row
    mean = jnp.mean(inner, axis=-1, keepdims=True)
    slope = jnp.mean(inner * unit, axis=-1, keepdims=True)
    grad_values = scale * (inner - mean - unit * slope)
    return (
        grad_values,
        jnp.sum(grad * unit, axis=0, keepdims=True),
        jnp.sum(grad, axis=0, keepdims=True),
    )


class Copy:
    def __init__(self, wire, source, target, peer, when):
        self.when = when
        self.pieces = (source, target, wire.sems.at[wire.used], wire.sems.at[wire.used + 1], peer)
        wire.used += 2
        wire.made.append(self)

    def remote(self, source=None):
        own, target, send_sem, recv_sem, peer = self.pieces
        return pltpu.make_async_remote_copy(
            src_ref=own if source is None else source,
            dst_ref=target,
            send_sem=send_sem,
            recv_sem=recv_sem,
            device_id=peer if isinstance(peer, dict) else {"narrow": peer},
            device_id_type=MESH,
        )

    def start(self):
        self.remote().start()

    def start_from(self, source):
        self.remote(source).start()

    def wait_recv(self):
        self.remote().wait_recv()

    def wait_send_early(self, others):
        self.when = others
        self.remote().wait_send()

    def wait_send(self):
        if self.when is None:
            self.remote().wait_send()
        else:

            @pl.when(self.when)
            def _():
                self.remote().wait_send()


class Wire:
    def __init__(self, sems):
        self.sems, self.used, self.made = sems, 0, []
        self.at = lax.axis_index("narrow")
        self.near = self.at + 1 - 2 * lax.rem(self.at, 2)
        self.far = lax.rem(self.at + 2, 4)
        self.diagonal = lax.rem(self.near + 2, 4)

    def barrier(self):
        barrier = pltpu.get_barrier_semaphore()
        for peer in (self.near, self.far):
            pl.semaphore_signal(barrier, inc=1, device_id={"narrow": peer}, device_id_type=MESH)
        pl.semaphore_wait(barrier, 2)

    def copy(self, source, target, peer, when=None):
        return Copy(self, source, target, peer, when)

    def send(self, source, target, peer):
        made = self.copy(source, target, peer)
        made.start()
        return made

    def finish(self):
        for made in self.made:
            made.wait_send()


def block_rows(block, size, part=0, parts=1):
    step = size // parts
    return pl.ds(pl.multiple_of(block * size + part * step, step), step)


class Gather:
    def __init__(self, wire, full, size):
        self.wire, self.full, self.size = wire, full, size
        self.to_near, self.to_far, self.relayed = [], [], []

    def rows(self, block, part):
        return self.full.at[block_rows(block, self.size, part, 2)]

    def push(self, part):
        own = self.rows(self.wire.at, part)
        self.to_near.append(self.wire.send(own, own, self.wire.near))
        self.to_far.append(self.wire.send(own, own, self.wire.far))

    def wait_near(self):
        for made in self.to_near:
            made.wait_recv()

    def relay(self, part):
        self.to_far[part].wait_recv()
        held = self.rows(self.wire.far, part)
        self.relayed.append(self.wire.send(held, held, self.wire.near))

    def wait_diagonal(self, part):
        self.relayed[part].wait_recv()


class Scatter:
    def __init__(self, wire, held, own, parts):
        self.held, self.own = held, own
        self.size = own.shape[0]
        step = self.size // parts
        self.cuts = [pl.ds(i * step, step) for i in range(parts)]

        def copies(out, into, peer, cuts):
            return [wire.copy(held.at[out, cut], held.at[into, cut], peer) for cut in cuts]

        self.side = copies(0, 1, wire.near, self.cuts)
        self.cross = copies(2, 3, wire.far, self.cuts)
        self.home = copies(4, 5, wire.near, [pl.ds(0, self.size)])[0]

    def put_diagonal(self, partial, part):
        self.held[0, self.cuts[part]] = partial.astype(BF16)
        self.side[part].start()

    def put_far(self, partial, part):
        cut = self.cuts[part]
        self.side[part].wait_recv()
        self.held[2, cut] = (partial + self.held[1, cut].astype(F32)).astype(BF16)
        self.cross[part].start()

    def put_near(self, partial):
        self.held[4] = partial.astype(BF16)
        self.home.start()

    def total(self):
        self.home.wait_recv()
        for made in self.cross:
            made.wait_recv()
        return self.own[...] + self.held[5].astype(F32) + self.held[3].astype(F32)


def turn(field, cosine, sine):
    lane = lax.broadcasted_iota(jnp.int32, cosine.shape, 1)
    first = lax.rem(lane, HD) < HD // 2
    turned = []
    for at in range(0, field.shape[1], 128):
        part = field[:, at : at + 128]
        swapped = jnp.where(
            first, pltpu.roll(part, 128 - HD // 2, 1), pltpu.roll(part, HD // 2, 1)
        )
        turned.append(part * cosine + swapped * sine)
    return jnp.concatenate(turned, axis=1)


def vmem(count):
    return [pl.BlockSpec(memory_space=pltpu.VMEM)] * count


def shaped(*entries):
    return [jax.ShapeDtypeStruct(shape, kind) for shape, kind in entries]


def call(kernel, number, outs, scratch, flops, *operands):
    return pl.pallas_call(
        kernel,
        in_specs=vmem(len(operands)),
        out_specs=vmem(len(outs)),
        out_shape=shaped(*outs),
        scratch_shapes=scratch + [pltpu.SemaphoreType.DMA((SEMAPHORES,))],
        compiler_params=pltpu.CompilerParams(
            collective_id=number, has_side_effects=True, vmem_limit_bytes=52 * 2**20
        ),
        cost_estimate=pl.CostEstimate(flops=flops, bytes_accessed=2**24, transcendentals=0),
        name=kernel.__name__,
    )(*operands)


class Background:
    def __init__(self, number=None, operands=(), outs=(), scratch=(), steps=None, quad=False, across=False):
        self.number, self.operands, self.outs = number, list(operands), list(outs)
        self.scratch, self.steps, self.quad, self.across = list(scratch), steps, quad, across


def call_with(body, background, outs, scratch, flops, *operands):
    counts = [
        len(operands), len(background.operands), len(outs), len(background.outs),
        len(scratch), len(background.scratch),
    ]

    def kernel(*refs):
        refs, groups = list(refs), []
        for count in counts:
            groups.append(refs[:count])
            refs = refs[count:]
        wire = Wire(refs[0])
        steps = []
        if background.steps is None:
            wire.barrier()
        else:
            if background.quad:
                place = Quad()
                quad_barrier(wire, place, *([place.across] if background.across else []))
            else:
                place = Line()
                wide_barrier(wire, place)
            steps = [background.steps(wire, place, groups[1], groups[3], groups[5])]

        def poll(times=1):
            for _ in range(times):
                for step in list(steps):
                    if next(step, "end") == "end":
                        steps.remove(step)

        body(wire, poll, *groups[0], *groups[2], *groups[4])
        while steps:
            poll()
        wire.finish()

    kernel.__name__ = body.__name__ if background.steps is None else body.__name__ + "_wide"
    place = anywhere if background.quad else vmem
    results = pl.pallas_call(
        kernel,
        in_specs=vmem(len(operands)) + place(len(background.operands)),
        out_specs=vmem(len(outs)) + place(len(background.outs)),
        out_shape=shaped(*outs, *background.outs),
        scratch_shapes=list(scratch)
        + background.scratch
        + [pltpu.SemaphoreType.DMA((SEMAPHORES,))],
        compiler_params=pltpu.CompilerParams(
            collective_id=background.number, has_side_effects=True, vmem_limit_bytes=52 * 2**20
        ),
        cost_estimate=pl.CostEstimate(flops=flops, bytes_accessed=2**24, transcendentals=0),
        name=kernel.__name__,
    )(*operands, *background.operands)
    return results[: len(outs)], results[len(outs) :]


def attend_half_body(
    wire, poll,
    x_ref, gain_ref, shift_ref, cos_ref, sin_ref, start_ref, w_qkv_ref, w_out_ref,
    a_ref, q_ref, k_ref, v_ref, o_ref, lse_ref, z_ref, h_ref, c_ref,
    held, own,
):
    size = x_ref.shape[0]
    gather = Gather(wire, a_ref, size)
    for part in range(2):
        rows = pl.ds(part * (size // 2), size // 2)
        normed = layer_norm(x_ref[rows], gain_ref[0:1], shift_ref[0:1])
        a_ref[block_rows(wire.at, size, part, 2)] = normed.astype(BF16)
        gather.push(part)
    width = q_ref.shape[1]

    def project(block):
        rows = block_rows(block, size)
        projected = dot(a_ref[rows], w_qkv_ref[...])
        cosine, sine = cos_ref[rows], sin_ref[rows]
        q_ref[rows] = turn(projected[:, :width], cosine, sine).astype(BF16)
        k_ref[rows] = turn(projected[:, width : 2 * width], cosine, sine).astype(BF16)
        v_ref[rows] = projected[:, 2 * width :].astype(BF16)

    poll()
    project(wire.at)
    gather.wait_near()
    project(wire.near)
    gather.relay(0)
    gather.relay(1)
    project(wire.far)
    gather.wait_diagonal(0)
    gather.wait_diagonal(1)
    project(wire.diagonal)

    poll()
    scatter = Scatter(wire, held, own, 1)
    for block in (3, 1, 2, 0):
        rows = slice(block * size, (block + 1) * size)
        reach = (block + 1) * size
        key = lax.broadcasted_iota(jnp.int32, (size, reach), 1)
        query = lax.broadcasted_iota(jnp.int32, (size, reach), 0) + block * size
        allowed = (key >= start_ref[rows, :]) & (key <= query)
        mixed, logs = [], jnp.zeros((size, 128), F32)
        lane = lax.broadcasted_iota(jnp.int32, (size, 128), 1)
        for head in range(width // HD):
            lanes = slice(head * HD, (head + 1) * HD)
            scores = dot_t(q_ref[rows, lanes] * SCALE, k_ref[:reach, lanes])
            scores = jnp.where(allowed, scores, MASKED)
            summit = jnp.max(scores, axis=1, keepdims=True)
            weights = jnp.exp(scores - summit)
            total = jnp.sum(weights, axis=1, keepdims=True)
            chances = (weights * (1.0 / total)).astype(BF16)
            mixed.append(dot(chances, v_ref[:reach, lanes]))
            logs = jnp.where(lane == head, summit + jnp.log(total), logs)
        o_ref[rows, :] = jnp.concatenate(mixed, axis=1).astype(BF16)
        lse_ref[:, rows] = logs.T[: lse_ref.shape[0]]
        partial = dot(o_ref[rows, :], w_out_ref[...])

        if block in (1, 2):
            poll()

        @pl.when(wire.diagonal == block)
        def _():
            scatter.put_diagonal(partial, 0)

        @pl.when(wire.far == block)
        def _():
            scatter.put_far(partial, 0)

        @pl.when(wire.near == block)
        def _():
            scatter.put_near(partial)

        @pl.when(wire.at == block)
        def _():
            own[...] = partial

    branch = scatter.total()
    z_ref[...] = branch
    middle = x_ref[...] + layer_norm(branch, gain_ref[1:2], shift_ref[1:2])
    h_ref[...] = middle
    c_ref[...] = layer_norm(middle, gain_ref[2:3], shift_ref[2:3]).astype(BF16)


def attend_half(background, resid, gains, shifts, cosine, sine, start, w_qkv, w_out):
    size, width = resid.shape
    length, part = cosine.shape[0], w_out.shape[0]
    return call_with(
        attend_half_body,
        background,
        [((length, width), BF16)]
        + [((length, part), BF16)] * 4
        + [((8, length), F32), ((size, width), F32), ((size, width), F32), ((size, width), BF16)],
        [pltpu.VMEM((6, size, width), BF16), pltpu.VMEM((size, width), F32)],
        8 * length * width * part + 4 * length * length * part,
        resid, gains, shifts, cosine, sine, start, w_qkv, w_out,
    )


def feed_half_kernel(
    c_ref, h_ref, gain_ref, shift_ref, w_up_ref, b_up_ref, w_down_ref,
    inner_ref, e_ref, d_ref, w_ref, y_ref,
    held, own, sems,
):
    size = c_ref.shape[0]
    half = size // 2
    wire = Wire(sems)
    wire.barrier()
    gather = Gather(wire, inner_ref, size)
    for part in range(2):
        inner_ref[block_rows(wire.at, size, part, 2)] = c_ref[pl.ds(part * half, half)]
        gather.push(part)
    scatter = Scatter(wire, held, own, 2)

    def feed(cuts):
        inner = jnp.concatenate([inner_ref[cut] for cut in cuts])
        hidden = dot(inner, w_up_ref[...]) + b_up_ref[...]
        below = 0.5 + 0.5 * lax.erf(hidden * (0.5**0.5))
        density = jnp.exp(-0.5 * hidden * hidden) * ((2.0 * math.pi) ** -0.5)
        active = (hidden * below).astype(BF16)
        slope = (below + hidden * density).astype(BF16)
        for at, cut in enumerate(cuts):
            step = inner.shape[0] // len(cuts)
            e_ref[cut] = active[at * step : (at + 1) * step]
            d_ref[cut] = slope[at * step : (at + 1) * step]
        return dot(active, w_down_ref[...])

    own[...] = feed([block_rows(wire.at, size)])
    gather.wait_near()
    scatter.put_near(feed([block_rows(wire.near, size)]))
    for part in range(2):
        gather.relay(part)
        gather.wait_diagonal(part)
        partial = feed(
            [block_rows(wire.diagonal, size, part, 2), block_rows(wire.far, size, part, 2)]
        )
        scatter.put_diagonal(partial[:half], part)
        scatter.put_far(partial[half:], part)
    second = scatter.total()
    w_ref[...] = second
    y_ref[...] = h_ref[...] + layer_norm(second, gain_ref[3:4], shift_ref[3:4])
    wire.finish()


def feed_half(inner, middle, gains, shifts, w_up, b_up, w_down):
    size, width = inner.shape
    length, hidden = 4 * size, w_up.shape[1]
    return call(
        feed_half_kernel,
        2,
        [((length, width), BF16)]
        + [((length, hidden), BF16)] * 2
        + [((size, width), F32)] * 2,
        [pltpu.VMEM((6, size, width), BF16), pltpu.VMEM((size, width), F32)],
        4 * length * width * hidden,
        inner, middle, gains, shifts, w_up, b_up, w_down,
    )


def feed_back_body(
    wire, poll,
    g_ref, w_ref, h_ref, z_ref, gain_ref, inner_ref, e_ref, d_ref, w_up_ref, w_down_ref,
    grad_down_ref, grad_up_ref, grad_b_ref, norms_ref, dh_ref, dz_ref,
    second, hidden, held, own,
):
    size = g_ref.shape[0]
    half = size // 2
    gather = Gather(wire, second, size)
    norms = [jnp.zeros((1, g_ref.shape[1]), F32)] * 2
    for part in range(2):
        rows = pl.ds(part * half, half)
        grad, gain, shift = layer_norm_back(w_ref[rows], g_ref[rows], gain_ref[3:4])
        second[block_rows(wire.at, size, part, 2)] = grad.astype(BF16)
        gather.push(part)
        norms = [norms[0] + gain, norms[1] + shift]
    norms_ref[3:4] = norms[0]
    norms_ref[7:8] = norms[1]
    norms_ref[0:1] = jnp.zeros_like(norms[0])
    norms_ref[4:5] = jnp.zeros_like(norms[0])
    scatter = Scatter(wire, held, own, 2)
    poll()

    def feed(cuts, first=False):
        grad = jnp.concatenate([second[cut] for cut in cuts])
        slope = jnp.concatenate([d_ref[cut] for cut in cuts]).astype(F32)
        grad = (slope * dot_t(grad, w_down_ref[...])).astype(BF16)
        for at, cut in enumerate(cuts):
            step = grad.shape[0] // len(cuts)
            hidden[cut] = grad[at * step : (at + 1) * step]
        bias = jnp.sum(grad.astype(F32), axis=0, keepdims=True)
        grad_b_ref[...] = bias if first else grad_b_ref[...] + bias
        return dot_t(grad, w_up_ref[...])

    own[...] = feed([block_rows(wire.at, size)], True)
    poll()
    gather.wait_near()
    scatter.put_near(feed([block_rows(wire.near, size)]))
    poll()
    for part in range(2):
        poll(2)
        gather.relay(part)
        gather.wait_diagonal(part)
        partial = feed(
            [block_rows(wire.diagonal, size, part, 2), block_rows(wire.far, size, part, 2)]
        )
        scatter.put_diagonal(partial[:half], part)
        scatter.put_far(partial[half:], part)
        poll()
    for at in range(0, e_ref.shape[1], 256):
        cut = slice(at, at + 256)
        grad_down_ref[cut, :] = t_dot(e_ref[:, cut], second[...]).astype(BF16)
        poll()
    for at in range(0, inner_ref.shape[1], 256):
        cut = slice(at, at + 256)
        grad_up_ref[cut, :] = t_dot(inner_ref[:, cut], hidden[...]).astype(BF16)
        poll()
    poll(3)
    grad, gain, shift = layer_norm_back(h_ref[...], scatter.total(), gain_ref[2:3])
    norms_ref[2:3] = gain
    norms_ref[6:7] = shift
    grad = g_ref[...] + grad
    dh_ref[...] = grad
    grad, gain, shift = layer_norm_back(z_ref[...], grad, gain_ref[1:2])
    norms_ref[1:2] = gain
    norms_ref[5:6] = shift
    dz_ref[...] = grad.astype(BF16)


def feed_back(background, grad, second, middle, branch, gains, inner, active, slope, w_up, w_down):
    size, width = grad.shape
    length, hidden = 4 * size, w_up.shape[1]
    return call_with(
        feed_back_body,
        background,
        [
            ((hidden, width), BF16),
            ((width, hidden), BF16),
            ((1, hidden), F32),
            ((8, width), F32),
            ((size, width), F32),
            ((size, width), BF16),
        ],
        [
            pltpu.VMEM((length, width), BF16),
            pltpu.VMEM((length, hidden), BF16),
            pltpu.VMEM((6, size, width), BF16),
            pltpu.VMEM((size, width), F32),
        ],
        8 * length * width * hidden,
        grad, second, middle, branch, gains, inner, active, slope, w_up, w_down,
    )


def attend_back_body(
    wire, poll,
    dz_ref, dh_ref, x_ref, gain_ref, a_ref, q_ref, k_ref, v_ref, o_ref, lse_ref, start_ref,
    cos_ref, sin_ref, w_qkv_ref, w_out_ref,
    grad_qkv_ref, grad_out_ref, norms_ref, dx_ref,
    branch, mixture, projected, dk, dv, held, own,
):
    size = dz_ref.shape[0]
    length, width = q_ref.shape
    half = size // 2
    gather = Gather(wire, branch, size)
    for part in range(2):
        branch[block_rows(wire.at, size, part, 2)] = dz_ref[pl.ds(part * half, half)]
        gather.push(part)

    def unmix(block):
        rows = block_rows(block, size)
        mixture[rows] = dot_t(branch[rows], w_out_ref[...]).astype(BF16)

    dk[...] = jnp.zeros_like(dk)
    dv[...] = jnp.zeros_like(dv)
    poll()
    unmix(wire.at)
    gather.wait_near()
    unmix(wire.near)
    poll()
    poll(2)
    gather.relay(0)
    poll(2)
    gather.relay(1)
    unmix(wire.far)
    gather.wait_diagonal(0)
    gather.wait_diagonal(1)
    unmix(wire.diagonal)
    grad_out_ref[...] = t_dot(o_ref[...], branch[...]).astype(BF16)
    poll()

    pick_head = (
        lax.broadcasted_iota(jnp.int32, (8, width), 1) // HD
        == lax.broadcasted_iota(jnp.int32, (8, width), 0)
    ).astype(F32)
    for block in range(length // size):
        rows = slice(block * size, (block + 1) * size)
        reach = (block + 1) * size
        key = lax.broadcasted_iota(jnp.int32, (reach, size), 0)
        query = lax.broadcasted_iota(jnp.int32, (reach, size), 1) + block * size
        allowed = (key >= start_ref[:, rows]) & (key <= query)
        inner = lax.dot_general(
            pick_head,
            mixture[rows].astype(F32) * o_ref[rows].astype(F32),
            (((1,), (1,)), ((), ())),
            precision=lax.Precision.HIGHEST,
            preferred_element_type=F32,
        )
        dqs, dks, dvs = [], [], []
        for head in range(width // HD):
            lanes = slice(head * HD, (head + 1) * HD)
            k_head, g_head = k_ref[:reach, lanes], mixture[rows, lanes]
            q_head = q_ref[rows, lanes] * SCALE
            scores = dot_t(k_head, q_head) - lse_ref[head : head + 1, rows]
            chances = jnp.exp(jnp.where(allowed, scores, MASKED))
            grad_prob = dot_t(v_ref[:reach, lanes], g_head)
            grad_score = (chances * (grad_prob - inner[head : head + 1])).astype(BF16)
            dvs.append(dot(chances.astype(BF16), g_head))
            dks.append(dot(grad_score, q_head))
            dqs.append(t_dot(grad_score, k_head) * SCALE)
            if block > 0 and head % 2 == 1:
                poll()
        dq = jnp.concatenate(dqs, axis=1)
        projected[rows, :width] = turn(dq, cos_ref[rows], -sin_ref[rows]).astype(BF16)
        dk[:reach, :] += jnp.concatenate(dks, axis=1)
        dv[:reach, :] += jnp.concatenate(dvs, axis=1)
    for block in range(length // size):
        rows = slice(block * size, (block + 1) * size)
        turned = turn(dk[rows], cos_ref[rows], -sin_ref[rows])
        projected[rows, width : 2 * width] = turned.astype(BF16)
        projected[rows, 2 * width :] = dv[rows].astype(BF16)

    scatter = Scatter(wire, held, own, 2)

    def unproject(cut):
        return dot_t(projected[cut], w_qkv_ref[...])

    partial = unproject(block_rows(wire.diagonal, size))
    scatter.put_diagonal(partial[:half], 0)
    scatter.put_diagonal(partial[half:], 1)
    poll()
    partial = unproject(block_rows(wire.far, size))
    scatter.put_far(partial[:half], 0)
    scatter.put_far(partial[half:], 1)
    poll()
    scatter.put_near(unproject(block_rows(wire.near, size)))
    own[...] = unproject(block_rows(wire.at, size))
    for at in range(0, a_ref.shape[1], 256):
        cut = slice(at, at + 256)
        grad_qkv_ref[cut, :] = t_dot(a_ref[:, cut], projected[...]).astype(BF16)
        poll()
    poll(3)
    grad, gain, shift = layer_norm_back(x_ref[...], scatter.total(), gain_ref[0:1])
    norms_ref[...] = jnp.zeros_like(norms_ref)
    norms_ref[0:1] = gain
    norms_ref[4:5] = shift
    dx_ref[...] = (dh_ref[...] + grad).astype(BF16)


def attend_back(
    background,
    grad_branch, grad_middle, resid, gains, normed, query, keys, values, mixture, logs, start,
    cosine, sine, w_qkv, w_out,
):
    size, width = resid.shape
    length, part = query.shape
    return call_with(
        attend_back_body,
        background,
        [
            ((width, 3 * part), BF16),
            ((part, width), BF16),
            ((8, width), F32),
            ((size, width), BF16),
        ],
        [
            pltpu.VMEM((length, width), BF16),
            pltpu.VMEM((length, part), BF16),
            pltpu.VMEM((length, 3 * part), BF16),
            pltpu.VMEM((length, part), F32),
            pltpu.VMEM((length, part), F32),
            pltpu.VMEM((6, size, width), BF16),
            pltpu.VMEM((size, width), F32),
        ],
        16 * length * width * part + 10 * length * length * part,
        grad_branch, grad_middle, resid, gains, normed, query, keys, values, mixture, logs,
        start, cosine, sine, w_qkv, w_out,
    )


CHUNK = 64
LATE = 2


class Line:
    def __init__(self):
        at = lax.axis_index("wide")
        self.pair = lax.rem(at, 2)
        self.turn = at // 2
        self.upper = self.turn // 3
        self.up = {"wide": lax.rem(self.turn + 1, 4) * 2 + self.pair}
        self.down = {"wide": lax.rem(self.turn + 3, 4) * 2 + self.pair}
        self.side = {"wide": at + 1 - 2 * self.pair}
        self.bottom, self.top = self.turn == 0, self.turn == 3
        self.at_end = self.upper * 3 == self.turn
        self.inside = jnp.logical_not(self.at_end)
        not_bottom, not_top = self.turn > 0, self.turn < 3
        self.ways = (
            (self.up, self.bottom, self.top, not_bottom, not_top),
            (self.down, self.top, self.bottom, not_top, not_bottom),
        )

    def steps(self, chunks):
        for at in range(len(chunks) + 3 * LATE):
            for turn in range(4):

                @pl.when(self.turn == turn)
                def _():
                    for way, hops in sorted(((0, turn), (1, 3 - turn)), key=lambda item: item[1]):
                        chunk = at - hops * LATE
                        if not 0 <= chunk < len(chunks):
                            continue
                        if hops == 0:
                            if chunk >= 2:
                                chunks[chunk - 2](way, "sent")
                            chunks[chunk](way, "first")
                        else:
                            chunks[chunk](way, "last" if hops == 3 else "inner")

            yield


def span(start, size):
    return pl.ds(pl.multiple_of(start, 16), size)


class Fold:
    def __init__(self, wire, line, ref, by_side, into, across, final):
        self.wire, self.line, self.ref, self.by_side = wire, line, ref, by_side
        self.into, self.across, self.final = into, across, final
        rows = ref.shape[0]
        self.length = rows // 4 if by_side else rows // 2
        self.base = line.pair * (rows // 2) if by_side else 0
        self.count = self.length // CHUNK
        self.copies, self.sides = [], []
        for way, (peer, _, _, _, inner) in enumerate(line.ways):
            cuts = [into.at[way, pl.ds(c * CHUNK, CHUNK)] for c in range(self.count)]
            self.copies.append([wire.copy(cut, cut, peer, inner) for cut in cuts])

    @staticmethod
    def scratch(rows, columns, by_side):
        return [
            pltpu.VMEM((2, rows // 4 if by_side else rows // 2, columns), BF16),
            pltpu.VMEM((rows // 2 if by_side else rows // 4, columns), BF16),
        ]

    def place(self, way, chunk):
        return (self.length if way == 0 else 0) + chunk * CHUNK

    def start(self):
        line = self.line
        if self.by_side:
            away = (1 - line.pair) * (self.ref.shape[0] // 2)
            for chunk in range(self.count):
                pair = []
                for way in (0, 1):
                    place = self.place(way, chunk)
                    pair.append(
                        self.wire.send(
                            self.ref.at[span(away + place, CHUNK)],
                            self.across.at[pl.ds(place, CHUNK)],
                            line.side,
                        )
                    )
                self.sides.append(pair)

    def step(self, chunk, way, role):
        place = self.place(way, chunk)
        cut = pl.ds(chunk * CHUNK, CHUNK)
        made = self.copies[way][chunk]
        if role == "sent":
            made.wait_send_early(self.line.inside)
            return
        if self.by_side:
            self.sides[chunk][way].wait_recv()

        def own():
            total = self.ref[span(self.base + place, CHUNK)].astype(F32)
            if self.by_side:
                total = total + self.across[pl.ds(place, CHUNK)].astype(F32)
            return total

        if role == "first":
            if self.by_side:
                self.into[way, cut] = own().astype(BF16)
                made.start()
            else:
                made.start_from(self.ref.at[pl.ds(place, CHUNK)])
            return
        made.wait_recv()
        self.into[way, cut] = (own() + self.into[way, cut].astype(F32)).astype(BF16)
        if role == "inner":
            made.start()

    def chunks(self):
        return [functools.partial(self.step, chunk) for chunk in range(self.count)]

    def start_side(self):
        line = self.line
        half = self.length // 2
        source = self.into.at[1 - line.upper, span((1 - line.pair) * half, half)]
        self.side = self.wire.copy(source, self.across, line.side, line.at_end)

        @pl.when(line.at_end)
        def _():
            self.side.start()

    def end(self):
        line = self.line
        size = self.final.shape[0]

        @pl.when(line.at_end)
        def _():
            if not self.by_side:
                self.side.wait_recv()
            for at in range(0, size, CHUNK):
                if self.by_side:
                    self.final[pl.ds(at, CHUNK)] = self.into[1 - line.upper, pl.ds(at, CHUNK)]
                else:
                    own = self.into[1 - line.upper, span(line.pair * size + at, CHUNK)]
                    total = own.astype(F32) + self.across[pl.ds(at, CHUNK)].astype(F32)
                    self.final[pl.ds(at, CHUNK)] = total.astype(BF16)


class Spread:
    def __init__(self, wire, line, view, rows, by_side):
        self.wire, self.line, self.view, self.by_side = wire, line, view, by_side
        pair, upper = line.pair, line.upper
        self.quarter = rows // 4
        if by_side:
            self.length, self.base = rows // 4, pair * (rows // 2)
            self.mine = self.base + upper * self.quarter
        else:
            self.length, self.base = rows // 2, 0
            self.mine = upper * (rows // 2) + pair * self.quarter
        self.count = self.length // CHUNK
        self.copies = []
        for way, (peer, _, _, _, inner) in enumerate(line.ways):
            cuts = [self.chunk(way, c) for c in range(self.count)]
            self.copies.append([wire.copy(cut, cut, peer, inner) for cut in cuts])
        self.sides = []
        if not by_side:
            self.side = wire.copy(self.own(), self.own(), line.side, line.at_end)

    def own(self):
        return self.view(span(self.mine, self.quarter))

    def chunk(self, way, chunk):
        start = self.base + (0 if way == 0 else self.length) + chunk * CHUNK
        return self.view(span(start, CHUNK))

    def start(self):
        if not self.by_side:

            @pl.when(self.line.at_end)
            def _():
                self.side.start()

    def step(self, chunk, way, role):
        made = self.copies[way][chunk]
        if role == "sent":
            made.wait_send_early(self.line.inside)
            return
        if role == "first":
            if not self.by_side and chunk == 0:
                self.side.wait_recv()
            made.start()
        else:
            made.wait_recv()
            if role == "inner":
                made.start()
        if self.by_side:
            self.sides[chunk][way].start()

    def chunks(self):
        if self.by_side:
            self.sides = []
            for chunk in range(self.count):
                cuts = [self.chunk(way, chunk) for way in (0, 1)]
                self.sides.append([self.wire.copy(cut, cut, self.line.side) for cut in cuts])
        return [functools.partial(self.step, chunk) for chunk in range(self.count)]

    def end(self):
        for pair in self.sides:
            for made in pair:
                made.wait_recv()


class Sequence:
    def __init__(self, line):
        self.line, self.chunks, self.actions = line, [], {}

    def add(self, *lists):
        total = max(len(chunks) for chunks in lists)
        placed = [
            ((at + 0.5) * total / len(chunks), which, chunk)
            for which, chunks in enumerate(lists)
            for at, chunk in enumerate(chunks)
        ]
        self.chunks += [chunk for _, _, chunk in sorted(placed, key=lambda item: item[:2])]
        return self

    def before_next(self, *actions):
        self.actions.setdefault(len(self.chunks) - 1, []).extend(actions)

    def after(self, chunk, *actions):
        self.actions.setdefault(self.chunks.index(chunk) + 3 * LATE, []).extend(actions)

    def steps(self):
        for action in self.actions.get(-1, []):
            action()
        for at, _ in enumerate(self.line.steps(self.chunks)):
            for action in self.actions.get(at, []):
                action()
            yield


def small_steps(wire, line, norms_ref, bias_ref, narrow_in, sums, side_in, slots, total_ref):
    part = total_ref.shape[1]
    made = []

    def columns(device):
        return pl.ds(pl.multiple_of(device * part, part), part)

    for peer in (wire.near, wire.far, wire.diagonal):
        made.append(
            wire.send(norms_ref.at[:, columns(peer)], narrow_in.at[wire.at], {"narrow": peer})
        )
    narrow_in[wire.at] = norms_ref[:, columns(wire.at)]
    yield
    for copy in made:
        copy.wait_recv()
    total = narrow_in[0] + narrow_in[1] + narrow_in[2] + narrow_in[3]
    lines = [bias_ref[:, at * part : (at + 1) * part] for at in range(4)]
    sums[...] = jnp.concatenate([total] + lines + [jnp.zeros((4, part), F32)], axis=0)
    side = wire.send(sums, side_in, line.side)
    yield
    side.wait_recv()
    slots[line.turn] = sums[...] + side_in[...]
    for step in range(3):
        sends = []
        for way, peer in enumerate((line.up, line.down)):
            place = line.turn if way == 0 else 3 - line.turn
            goes = (place >= step) & (place < 3)
            comes = place > step
            slot = slots.at[lax.rem(line.turn + (4 - step if way == 0 else step), 4)]
            copy = wire.copy(slot, slot, peer, goes)
            sends.append((copy, goes, comes))

            @pl.when(goes)
            def _():
                copy.start()

        yield
        for copy, goes, comes in sends:

            @pl.when(comes)
            def _():
                copy.wait_recv()

    total_ref[...] = slots[0] + slots[1] + slots[2] + slots[3]


def home(wire, line, down, out, qkv, full_down, full_out, full_qkv):
    part = (full_out if full_down is None else full_down).shape[2]
    made = []
    at = wire.at

    def columns(device):
        return pl.ds(pl.multiple_of(device * part, part), part)

    for final, full, by_side in ((down, full_down, True), (out, full_out, False)):
        if final is None:
            continue
        quarter = final.shape[0]
        if by_side:
            mine = line.pair * (2 * quarter) + line.upper * quarter
        else:
            mine = line.upper * (2 * quarter) + line.pair * quarter
        slot = full.at[at, span(mine, quarter)]
        for peer in (wire.diagonal, wire.far, wire.near):
            made.append(
                wire.copy(final.at[:, columns(peer)], slot, {"narrow": peer}, line.at_end)
            )

        @pl.when(line.at_end)
        def _():
            slot[...] = final[:, columns(at)]

    if qkv is not None:
        quarter = qkv.shape[0]
        rows = span(line.pair * (2 * quarter) + line.upper * quarter, quarter)
        odd, upper = lax.rem(at, 2), at // 2
        far_slot = columns(2 - 2 * odd)
        made.append(
            wire.copy(
                qkv.at[:, columns(2 - 2 * upper)], full_qkv.at[rows, far_slot],
                {"narrow": wire.far}, line.at_end,
            )
        )
        made.append(
            wire.copy(
                qkv.at[:, columns(1 - odd + upper)], full_qkv.at[rows, columns(1)],
                {"narrow": wire.near}, line.at_end,
            )
        )

        @pl.when(line.at_end)
        def _():
            full_qkv[rows, columns(2 * odd)] = qkv[:, columns((at + 1) // 2)]

    @pl.when(line.at_end)
    def _():
        for copy in made:
            copy.start()

    def wait():
        @pl.when(line.at_end)
        def _():
            for copy in made:
                copy.wait_recv()

    return wait


def wide_barrier(wire, line, *others):
    barrier = pltpu.get_barrier_semaphore()

    def greet(peer):
        pl.semaphore_signal(barrier, inc=1, device_id=peer, device_id_type=MESH)

    for peer in (line.side,) + others:
        greet(peer)
    for peer in (wire.near, wire.far, wire.diagonal):
        greet({"narrow": peer})

    @pl.when(line.turn < 3)
    def _():
        greet(line.up)

    @pl.when(line.turn > 0)
    def _():
        greet(line.down)

    @pl.when(line.at_end)
    def _():
        pl.semaphore_wait(barrier, 5 + len(others))

    @pl.when(line.inside)
    def _():
        pl.semaphore_wait(barrier, 6 + len(others))


def run(*steps):
    steps = list(steps)
    while steps:
        for at in list(steps):
            if next(at, "end") == "end":
                steps.remove(at)


def fold_pair(wire, line, refs, finals, scratch):
    return (
        Fold(wire, line, refs[0], False, *scratch[0:2], finals[0]),
        Fold(wire, line, refs[1], True, *scratch[2:4], finals[1]),
    )


def spread_feed(wire, line, full_up, full_down):
    return (
        Spread(wire, line, lambda rows: full_up.at[rows], full_up.shape[0], False),
        Spread(wire, line, lambda rows: full_down.at[:, rows], full_down.shape[1], True),
    )


def spread_attend(wire, line, full_out, full_qkv):
    return (
        Spread(wire, line, lambda rows: full_out.at[:, rows], full_out.shape[1], False),
        Spread(wire, line, lambda rows: full_qkv.at[rows], full_qkv.shape[0], True),
    )


def place_own(line, spread, final):
    @pl.when(line.at_end)
    def _():
        spread.own()[...] = final[...]


def fold_feed_steps(wire, line, refs, outs, scratch):
    up, down = fold_pair(wire, line, refs, outs, scratch)
    down.start()
    sequence = Sequence(line)
    chunks = up.chunks()
    sequence.add(chunks).add(down.chunks())
    sequence.after(chunks[-1], up.start_side)
    yield from sequence.steps()
    up.end()
    down.end()


def fold_attend_spread_feed_steps(wire, line, refs, outs, scratch):
    out, qkv = fold_pair(wire, line, refs[0:2], outs[0:2], scratch)
    up, down = spread_feed(wire, line, *outs[2:4])
    place_own(line, up, refs[2])
    home_wait = home(wire, line, refs[3], None, None, outs[3], None, None)
    qkv.start()
    up.start()
    sequence = Sequence(line)
    chunks = out.chunks()
    sequence.add(chunks).before_next(home_wait)
    sequence.add(down.chunks()).add(up.chunks(), qkv.chunks())
    sequence.after(chunks[-1], out.start_side)
    yield from sequence.steps()
    out.end()
    qkv.end()
    down.end()


def spread_attend_fold_feed_steps(wire, line, refs, outs, scratch):
    out, qkv = spread_attend(wire, line, *outs[0:2])
    up, down = fold_pair(wire, line, refs[2:4], outs[2:4], scratch)
    home_wait = home(wire, line, None, refs[0], refs[1], None, *outs[0:2])
    down.start()
    sequence = Sequence(line)
    chunks = up.chunks()
    sequence.add(chunks[:2]).before_next(home_wait, out.start)
    sequence.add(chunks[2:6], qkv.chunks()).add(chunks[6:], out.chunks()).add(down.chunks())
    sequence.after(chunks[-1], up.start_side)
    yield from sequence.steps()
    up.end()
    down.end()
    qkv.end()


def tail_steps(wire, line, grads, finals, full_feed, full_attend, own, scratch):
    out, qkv = fold_pair(wire, line, grads, own, scratch)
    up, down = spread_feed(wire, line, *full_feed)
    full_out, full_qkv = spread_attend(wire, line, *full_attend)
    place_own(line, up, finals[0])
    home_wait = home(wire, line, finals[1], None, None, full_feed[1], None, None)
    qkv.start()
    up.start()
    waits = []

    def go_home():
        out.end()
        qkv.end()
        waits.append(home(wire, line, None, *own, None, *full_attend))

    sequence = Sequence(line)
    out_chunks, qkv_chunks = out.chunks(), qkv.chunks()
    sequence.add(out_chunks).before_next(home_wait)
    sequence.add(down.chunks()).add(qkv_chunks).add(up.chunks())
    sequence.before_next(lambda: waits[0](), full_out.start)
    sequence.add(full_qkv.chunks()).add(full_out.chunks())
    sequence.after(out_chunks[-1], out.start_side)
    sequence.after(qkv_chunks[-1], go_home)
    yield from sequence.steps()
    down.end()
    full_qkv.end()


def fold_outs(blocks):
    return [((block.shape[0] // 4, block.shape[1]), BF16) for block in blocks]


def fold_scratch(blocks):
    kinds = zip(blocks, (False, True))
    return [entry for block, kind in kinds for entry in Fold.scratch(*block.shape, kind)]


def feed_full(grads):
    up, down = grads
    return [(up.shape, BF16), ((4, down.shape[0], down.shape[1] // 4), BF16)]


def attend_full(grads):
    out, qkv = grads
    return [((4, out.shape[0], out.shape[1] // 4), BF16), (qkv.shape, BF16)]


def swap_across(wire, source, target, first_sends):
    quad = Quad()
    second = jnp.logical_not(quad.first)
    sends, takes = (quad.first, second) if first_sends else (second, quad.first)
    made = wire.copy(source, target, quad.across, sends)

    @pl.when(sends)
    def _():
        made.start()

    yield

    @pl.when(takes)
    def _():
        made.wait_recv()


def tail_kernel(*refs):
    sems, refs = refs[-1], refs[:-1]
    grads, finals, small_refs, away, refs = refs[0:2], refs[2:4], refs[4:8], refs[8], refs[9:]
    full_feed, full_attend, totals, came = refs[0:2], refs[2:4], refs[4:6], refs[6]
    scratch = refs[7:]
    wire, line = Wire(sems), Line()
    wide_barrier(wire, line, Quad().across)
    swap = swap_across(wire, away, came, False)
    next(swap)
    smalls = [
        small_steps(wire, line, *small_refs[2 * at : 2 * at + 2], *scratch[4 * at : 4 * at + 4], totals[at])
        for at in range(2)
    ]
    own = scratch[12:14]
    steps = tail_steps(wire, line, grads, finals, full_feed, full_attend, own, scratch[8:12])
    run(steps, *smalls)
    next(swap, None)
    wire.finish()


def tail(attend, feed_finals, feed, norms, biases, away):
    part = norms[0].shape[1] // 4
    small = [
        pltpu.VMEM((4, 8, part), F32),
        pltpu.VMEM((16, part), F32),
        pltpu.VMEM((16, part), F32),
        pltpu.VMEM((4, 16, part), F32),
    ]
    return call(
        tail_kernel,
        9,
        feed_full(feed)
        + attend_full(attend)
        + [((16, part), F32)] * 2
        + [(away.shape, away.dtype)],
        small * 2
        + fold_scratch(attend)
        + [pltpu.VMEM(shape, kind) for shape, kind in fold_outs(attend)],
        0,
        *attend, *feed_finals, norms[0], biases[0], norms[1], biases[1], away,
    )


def backward_wide(grad, result, saved, weights, start, tables):
    (grad_feed_1, norms_1, bias_1, grad_middle, grad_branch), (result_came,) = feed_backward(
        Background(
            3, [result], [(result.shape, result.dtype)], [],
            lambda wire, quad, refs, outs, scratch: swap_across(wire, refs[0], outs[0], True),
            quad=True, across=True,
        ),
        grad, saved[1], weights[1],
    )
    (grad_attend_1, norms, grad), finals_1 = attend_backward(
        Background(
            4, grad_feed_1, fold_outs(grad_feed_1), fold_scratch(grad_feed_1),
            fold_feed_steps,
        ),
        grad_branch, grad_middle, saved[1], weights[1], start, tables,
    )
    norms_1 = norms_1 + norms

    (grad_feed_0, norms_0, bias_0, grad_middle, grad_branch), results = feed_backward(
        Background(
            6, list(grad_attend_1) + list(finals_1),
            fold_outs(grad_attend_1) + feed_full(grad_feed_1), fold_scratch(grad_attend_1),
            fold_attend_spread_feed_steps,
        ),
        grad.astype(F32), saved[0], weights[0],
    )
    finals_1, full_feed_1 = results[:2], results[2:]

    (grad_attend_0, norms, grad), results = attend_backward(
        Background(
            7, list(finals_1) + list(grad_feed_0),
            attend_full(grad_attend_1) + fold_outs(grad_feed_0), fold_scratch(grad_feed_0),
            spread_attend_fold_feed_steps,
        ),
        grad_branch, grad_middle, saved[0], weights[0], start, tables,
    )
    norms_0 = norms_0 + norms
    full_attend_1, finals_0 = results[:2], results[2:]
    results = tail(
        grad_attend_0, finals_0, grad_feed_0, (norms_0, norms_1), (bias_0, bias_1), grad
    )
    full_feed_0, full_attend_0, totals = results[:2], results[2:4], results[4:6]
    grad_came = results[6]

    def shards(feed, attend, total):
        up, down = feed
        out, qkv = attend
        out, down = (block.reshape(-1, block.shape[2]) for block in (out, down))
        return qkv, out, up, total[8:12].reshape(-1), down, total[:4], total[4:8]

    return grad, grad_came, result_came, (
        shards(full_feed_0, full_attend_0, totals[0]),
        shards(full_feed_1, full_attend_1, totals[1]),
    )


class Quad:
    def __init__(self):
        at = lax.axis_index("wide")
        pair, turn = lax.rem(at, 2), at // 2
        odd = lax.rem(turn, 2)
        self.side = {"wide": at + 1 - 2 * pair}
        self.mate = {"wide": (turn + 1 - 2 * odd) * 2 + pair}
        self.mine = odd * 2 + pair
        self.from_side = odd * 2 + 1 - pair
        self.from_mate = (1 - odd) * 2 + pair
        halfway = lax.axis_size("wide") // 2
        self.first = at < halfway
        self.across = {"wide": lax.rem(at + halfway, 2 * halfway)}


class Fetch:
    def __init__(self, wire, shard, full, by_heads):
        self.wire, self.full, self.rows = wire, full, full.shape[0]
        at, odd, upper = wire.at, lax.rem(wire.at, 2), wire.at // 2
        part = shard.shape[1]

        def columns(block, count=1):
            return pl.ds(pl.multiple_of(block * 256, 256), 256 * count)

        if by_heads:
            self.far = [
                (
                    lambda rows: shard.at[rows, columns(2 - 2 * odd)],
                    lambda rows: full.at[rows, columns(2 * upper)],
                    wire.far,
                )
            ]
            self.relay = lambda rows: full.at[rows, columns(2 - 2 * upper)]
            self.near = (shard.at[:, columns(1)], full.at[:, columns(odd + upper)])
            self.own = (shard.at[:, columns(2 * odd)], full.at[:, columns((at + 1) // 2)])
        else:
            block = self.rows

            def away(peer):
                return (
                    lambda rows: shard.at[span(peer * block + rows.start, rows.size)],
                    lambda rows: full.at[rows, columns(at)],
                    peer,
                )

            self.far = [away(wire.far), away(wire.diagonal)]
            self.relay = lambda rows: full.at[rows, columns(2 - 2 * upper, 2)]
            self.near = (shard.at[span(wire.near * block, block)], full.at[:, columns(at)])
            self.own = (shard.at[span(at * block, block)], full.at[:, columns(at)])

    def quarter(self, which, half=0, halves=1):
        size = self.rows // 4
        return span(which * size + half * (size // halves), size // halves)


def fetch_steps(wire, quad, fetches, local):
    copies, sent, nears = [], [], []
    for at, fetch in enumerate(fetches):
        rows = fetch.quarter(quad.mine)
        for source, target, peer in fetch.far:
            sent.append(wire.send(source(rows), target(rows), {"narrow": peer}))
        nears.append(wire.send(*fetch.near, {"narrow": wire.near}))
        copies.append(pltpu.make_async_copy(*fetch.own, local.at[at]))
        copies[-1].start()
    yield
    for made in sent:
        made.wait_recv()
    sides, mates = [], []
    for fetch in fetches:
        held = fetch.relay(fetch.quarter(quad.mine))
        sides.append(wire.send(held, held, quad.side))
        mates.append(wire.send(held, held, quad.mate))
    yield
    last = []
    for fetch, side, mate in zip(fetches, sides, mates):
        side.wait_recv()
        held = fetch.relay(fetch.quarter(quad.from_side, 0, 2))
        last.append(wire.send(held, held, quad.mate))
        mate.wait_recv()
        held = fetch.relay(fetch.quarter(quad.from_mate, 1, 2))
        last.append(wire.send(held, held, quad.side))
    yield
    for made in last + nears:
        made.wait_recv()
    for copy in copies:
        copy.wait()


def greet(peers):
    barrier = pltpu.get_barrier_semaphore()
    for peer in peers:
        pl.semaphore_signal(barrier, inc=1, device_id=peer, device_id_type=MESH)
    pl.semaphore_wait(barrier, len(peers))


def quad_barrier(wire, quad, *others):
    narrow = [{"narrow": peer} for peer in (wire.near, wire.far, wire.diagonal)]
    greet(narrow + [quad.side, quad.mate] + list(others))


def begin_kernel(
    blocks_ref, w_qkv_ref, w_out_ref, norms_ref,
    qkv_ref, out_ref, full_norms_ref, came_ref,
    local, sems,
):
    wire, quad = Wire(sems), Quad()
    quad_barrier(wire, quad, quad.across)
    size = came_ref.shape[0]
    away = blocks_ref.at[span(quad.first.astype(jnp.int32) * size, size)]
    swap = wire.send(away, came_ref, quad.across)
    fetches = [
        Fetch(wire, w_qkv_ref.at[0], qkv_ref, True),
        Fetch(wire, w_out_ref.at[0], out_ref, False),
    ]
    part = norms_ref.shape[1]
    slot = full_norms_ref.at[:, pl.ds(pl.multiple_of(wire.at * part, part), part)]
    sent = [
        wire.send(norms_ref, slot, {"narrow": peer})
        for peer in (wire.diagonal, wire.far, wire.near)
    ]
    own = pltpu.make_async_copy(norms_ref, slot, local.at[len(fetches)])
    own.start()
    run(fetch_steps(wire, quad, fetches, local))
    for made in sent:
        made.wait_recv()
    own.wait()
    swap.wait_recv()
    wire.finish()


def anywhere(count):
    return [pl.BlockSpec(memory_space=pl.ANY)] * count


def begin(blocks, w_qkv, w_out, norms):
    width = blocks.shape[1]
    shapes = [
        (w_qkv.shape[1:], BF16),
        ((w_out.shape[2], width), BF16),
        ((norms.shape[0], width), BF16),
        ((blocks.shape[0] // 2, width), BF16),
    ]
    return pl.pallas_call(
        begin_kernel,
        in_specs=anywhere(4),
        out_specs=anywhere(4),
        out_shape=shaped(*shapes),
        scratch_shapes=[pltpu.SemaphoreType.DMA((8,)), pltpu.SemaphoreType.DMA((SEMAPHORES,))],
        compiler_params=pltpu.CompilerParams(collective_id=10, has_side_effects=True),
        name="begin",
    )(blocks, w_qkv, w_out, norms)


def fetch_rest_steps(wire, quad, refs, outs, scratch):
    w_qkv, w_out, w_down = refs
    down_0, qkv_1, out_1, down_1 = outs
    first = fetch_steps(wire, quad, [Fetch(wire, w_down.at[0], down_0, False)], scratch[0])
    rest = [
        Fetch(wire, w_qkv.at[1], qkv_1, True),
        Fetch(wire, w_out.at[1], out_1, False),
        Fetch(wire, w_down.at[1], down_1, False),
    ]
    second = fetch_steps(wire, quad, rest, scratch[1])
    next(first)
    yield
    next(first)
    next(second)
    yield
    next(first)
    next(second)
    yield
    next(first, None)
    next(second)
    yield
    next(second, None)


def swap(block, distance):
    count = lax.axis_size("narrow")
    return lax.ppermute(block, "narrow", [(i, i ^ distance) for i in range(count)])


def pick(stack, table, at):
    return lax.dynamic_index_in_dim(stack, jnp.asarray(table)[at], 0, keepdims=False)


def by_heads(block, at):
    parts = jnp.stack(jnp.split(block, 3, axis=1))
    own = pick(parts, [0, 2, 0, 2], at)
    near = swap(parts[1], 1)
    far = swap(pick(parts, [2, 0, 2, 0], at), 2)
    parts = jnp.stack([own, near, far])
    order = jnp.asarray([[0, 1, 2], [1, 0, 2], [2, 0, 1], [2, 1, 0]])[at]
    return jnp.concatenate(
        [lax.dynamic_index_in_dim(parts, order[i], 0, keepdims=False) for i in range(3)], axis=1
    )


def from_heads(block, at):
    parts = jnp.stack(jnp.split(block, 3, axis=1))
    own = pick(parts, [0, 1, 1, 2], at)
    near = swap(pick(parts, [1, 0, 2, 1], at), 1)
    far = swap(pick(parts, [2, 2, 0, 0], at), 2)
    parts = jnp.stack([own, near, far])
    order = jnp.asarray([[0, 1, 2], [2, 1, 0], [0, 1, 2], [2, 1, 0]])[at]
    return jnp.concatenate(
        [lax.dynamic_index_in_dim(parts, order[i], 0, keepdims=False) for i in range(3)], axis=1
    )


def to_rows(block):
    return lax.all_to_all(block, "narrow", split_axis=0, concat_axis=1, tiled=True)


def to_columns(block):
    return lax.all_to_all(block, "narrow", split_axis=1, concat_axis=0, tiled=True)


def layer_forward(resid, weights, start, tables, background=None):
    w_qkv, w_out, w_up, b_up, w_down, gains, shifts = weights
    (normed, query, keys, values, mixture, logs, branch, middle, inner), more = attend_half(
        background or Background(1), resid, gains, shifts, *tables, start[:, None], w_qkv, w_out
    )
    if background is not None:
        w_down = more[0]
    inner, active, slope, second, result = feed_half(
        inner, middle, gains, shifts, w_up, b_up, w_down
    )
    return result, more, (
        resid, normed, query, keys, values, mixture, logs, branch, middle, inner, active, slope, second
    )


def feed_backward(background, grad, saved, weights):
    w_qkv, w_out, w_up, b_up, w_down, gains, shifts = weights
    _, _, _, _, _, _, _, branch, middle, inner, active, slope, second = saved
    (grad_down, grad_up, grad_b_up, norms, grad_middle, grad_branch), results = feed_back(
        background, grad, second, middle, branch, gains, inner, active, slope, w_up, w_down
    )
    return ((grad_up, grad_down), norms, grad_b_up, grad_middle, grad_branch), results


def attend_backward(background, grad_branch, grad_middle, saved, weights, start, tables):
    w_qkv, w_out, w_up, b_up, w_down, gains, shifts = weights
    resid, normed, query, keys, values, mixture, logs, _, _, _, _, _, _ = saved
    (grad_qkv, grad_out, norms, grad), results = attend_back(
        background, grad_branch, grad_middle, resid, gains, normed, query, keys, values, mixture,
        logs, start[None], *tables, w_qkv, w_out,
    )
    return ((grad_out, grad_qkv), norms, grad), results


def layer_backward(grad, saved, weights, start, tables):
    ((grad_up, grad_down), norms, grad_b_up, grad_middle, grad_branch), _ = feed_backward(
        Background(3), grad, saved, weights
    )
    ((grad_out, grad_qkv), norms_too, grad), _ = attend_backward(
        Background(4), grad_branch, grad_middle, saved, weights, start, tables
    )
    return grad, (grad_qkv, grad_out, grad_up, grad_b_up, grad_down, norms + norms_too)


def reduce_grads(grads, at):
    def fold(block):
        return lax.psum_scatter(block, "wide", scatter_dimension=0, tiled=True)

    def spread(block):
        return lax.all_gather(block, "wide", axis=0, tiled=True)

    def spread_rows(block):
        wide, narrow = lax.axis_size("wide"), lax.axis_size("narrow")
        rows, width = block.shape
        full = spread(block).reshape(wide, narrow, rows // narrow, width)
        return full.transpose(1, 0, 2, 3).reshape(wide * rows, width)

    qkv, out, up, b_up, down, norms = grads
    qkv = spread(from_heads(fold(qkv), at))
    out = spread_rows(to_columns(fold(out)))
    up = spread(fold(up))
    down = spread_rows(to_columns(fold(down)))
    b_up = lax.psum(b_up[0], "wide")
    norms = lax.psum(norms, ("wide", "narrow"))
    part = norms.shape[1] // lax.axis_size("narrow")
    norms = lax.dynamic_slice_in_dim(norms, at * part, part, 1)
    return qkv, out, up, b_up, down, norms[:4], norms[4:]


def on_device(ends, lengths, w_qkv, w_out, w_up, b_up, w_down, norm_gain, norm_bias):
    wide = lax.axis_size("wide")
    narrow = lax.axis_size("narrow")
    halfway = wide // 2
    wide_at = lax.axis_index("wide")
    at = lax.axis_index("narrow")
    first = wide_at < halfway
    row_count = ends.shape[0] // 2
    length = row_count * narrow

    def route(block):
        pairs = [(i, (i + halfway) % wide) for i in range(wide)]
        return lax.ppermute(block, "wide", pairs)

    own_lengths = lengths[lax.rem(wide_at, halfway), wide_at // halfway]
    places = jnp.arange(length, dtype=jnp.int32)
    passed = (places[:, None] >= jnp.cumsum(own_lengths)[None, :]).astype(jnp.int32)
    start = jnp.sum(passed * own_lengths[None, :], axis=1)
    tables = rope_tables(places - start)
    b_up = b_up.astype(F32)[:, None]
    norms = jnp.concatenate([norm_gain, norm_bias]).reshape(16, -1)

    if wide == 8:
        qkv_0, out_0, norms, came = begin(ends, w_qkv, w_out, norms)
    else:
        came = route(jnp.where(first, ends[row_count:], ends[:row_count]))
        norms = lax.all_gather(norms, "narrow", axis=1, tiled=True)
        qkv_0, out_0 = by_heads(w_qkv[0], at), to_rows(w_out[0])
        down_0, down_1 = to_rows(w_down[0]), to_rows(w_down[1])
        qkv_1, out_1 = by_heads(w_qkv[1], at), to_rows(w_out[1])
    norms = norms.astype(F32)
    resid = jnp.where(first, ends[:row_count], came).astype(F32)
    upstream = jnp.where(first, came, ends[row_count:]).astype(F32)

    if wide == 8:
        width = ends.shape[1]
        part = w_out.shape[2]
        background = Background(
            11, [w_qkv, w_out, w_down],
            [
                ((w_up.shape[2], width), BF16),
                (w_qkv.shape[1:], BF16),
                ((part, width), BF16),
                ((w_up.shape[2], width), BF16),
            ],
            [pltpu.SemaphoreType.DMA((4,))] * 2, fetch_rest_steps, quad=True,
        )
        weights_0 = (qkv_0, out_0, w_up[0], b_up[0], None, norms[0:4], norms[8:12])
        middle, more, saved_first = layer_forward(resid, weights_0, start, tables, background)
        down_0, qkv_1, out_1, down_1 = more
        weights_0 = weights_0[:4] + (down_0,) + weights_0[5:]
    else:
        weights_0 = (qkv_0, out_0, w_up[0], b_up[0], down_0, norms[0:4], norms[8:12])
        middle, _, saved_first = layer_forward(resid, weights_0, start, tables)
    weights_1 = (qkv_1, out_1, w_up[1], b_up[1], down_1, norms[4:8], norms[12:16])
    weights = (weights_0, weights_1)
    middle = middle.astype(BF16).astype(F32)
    result, _, saved_second = layer_forward(middle, weights_1, start, tables)
    result = result.astype(BF16)
    if wide == 8:
        grad, grad_came, result_came, (totals_first, totals_second) = backward_wide(
            upstream, result, (saved_first, saved_second), weights, start, tables
        )
    else:
        result_came = route(result)
        grad, grads_second = layer_backward(upstream, saved_second, weights_1, start, tables)
        totals_second = reduce_grads(grads_second, at)
        grad, grads_first = layer_backward(grad.astype(F32), saved_first, weights_0, start, tables)
        totals_first = reduce_grads(grads_first, at)
        grad_came = route(grad)

    ends_out = jnp.where(
        first, jnp.concatenate([grad, grad_came]), jnp.concatenate([result_came, result])
    )
    totals = [jnp.stack([a.astype(F32), b.astype(F32)]) for a, b in zip(totals_first, totals_second)]
    return (ends_out,) + tuple(totals)


def solution(mesh):
    placed = (
        P(("wide", "narrow"), None),
        P(),
        P(None, None, "narrow"),
        P(None, None, "narrow"),
        P(None, None, "narrow"),
        P(None, "narrow"),
        P(None, None, "narrow"),
        P(None, None, "narrow"),
        P(None, None, "narrow"),
    )
    return jax.shard_map(
        on_device,
        mesh=mesh,
        in_specs=placed,
        out_specs=(P(("wide", "narrow"), None),) + placed[2:],
        check_vma=False,
    )
```

```python
import functools
import math

import jax
import jax.numpy as jnp
from jax import lax
from jax.experimental import pallas as pl
from jax.experimental.pallas import tpu as pltpu
from jax.sharding import PartitionSpec as P

HD = 64
EPSILON = 1e-05
MASKED = -1e30
SCALE = HD ** (-0.5)
F32 = jnp.float32
BF16 = jnp.bfloat16


def layer_norm(values, gain_row, shift_row):
    center = jnp.mean(values, axis=-1, keepdims=True)
    centred = values - center
    spread = jnp.mean(centred * centred, axis=-1, keepdims=True)
    return centred * lax.rsqrt(spread + EPSILON) * gain_row + shift_row


def rope_tables(offsets):
    halfway = HD // 2
    ladder = jnp.arange(halfway, dtype=F32) * (2.0 / HD)
    inverse = jnp.exp(-math.log(10000.0) * ladder)
    angles = offsets.astype(F32)[:, None] * inverse[None, :]
    cosine, sine = jnp.cos(angles), jnp.sin(angles)
    return (
        jnp.concatenate([cosine, cosine] * 2, axis=1),
        jnp.concatenate([-sine, sine] * 2, axis=1),
    )


def dot(left, right):
    return jnp.dot(left, right, preferred_element_type=F32)


def dot_t(left, right):
    return lax.dot_general(left, right, (((1,), (1,)), ((), ())), preferred_element_type=F32)


def t_dot(left, right):
    return lax.dot_general(left, right, (((0,), (0,)), ((), ())), preferred_element_type=F32)


MESH = pl.DeviceIdType.MESH


def layer_norm_back(values, grad, gain_row):
    center = jnp.mean(values, axis=-1, keepdims=True)
    centred = values - center
    scale = lax.rsqrt(jnp.mean(centred * centred, axis=-1, keepdims=True) + EPSILON)
    unit = centred * scale
    inner = grad * gain_row
    mean = jnp.mean(inner, axis=-1, keepdims=True)
    slope = jnp.mean(inner * unit, axis=-1, keepdims=True)
    grad_values = scale * (inner - mean - unit * slope)
    return (
        grad_values,
        jnp.sum(grad * unit, axis=0, keepdims=True),
        jnp.sum(grad, axis=0, keepdims=True),
    )


class Copy:
    def __init__(self, wire, source, target, peer, when):
        self.when, self.settled = when, False
        source, target = (item.ref if isinstance(item, Staged) else item for item in (source, target))
        self.pieces = (source, target, wire.sems.at[wire.used], wire.sems.at[wire.used + 1], peer)
        wire.used += 2
        wire.made.append(self)

    def remote(self, source=None):
        own, target, send_sem, recv_sem, peer = self.pieces
        return pltpu.make_async_remote_copy(
            src_ref=own if source is None else source,
            dst_ref=target,
            send_sem=send_sem,
            recv_sem=recv_sem,
            device_id=peer if isinstance(peer, dict) else {"narrow": peer},
            device_id_type=MESH,
        )

    def start(self):
        self.remote().start()

    def start_from(self, source):
        self.remote(source).start()

    def wait_recv(self):
        self.remote().wait_recv()

    def wait_send_early(self, others):
        self.when = others
        self.remote().wait_send()

    def settle(self):
        if not self.settled:
            self.settled = True
            self.wait_send()

    def wait_send(self):
        if self.when is None:
            self.remote().wait_send()
        else:

            @pl.when(self.when)
            def _():
                self.remote().wait_send()


class Wire:
    def __init__(self, sems):
        self.sems, self.used, self.made = sems, 0, []
        self.at = lax.axis_index("narrow")
        self.near = self.at + 1 - 2 * lax.rem(self.at, 2)
        self.far = lax.rem(self.at + 2, 4)
        self.diagonal = lax.rem(self.near + 2, 4)

    def barrier(self):
        barrier = pltpu.get_barrier_semaphore()
        for peer in (self.near, self.far):
            pl.semaphore_signal(barrier, inc=1, device_id={"narrow": peer}, device_id_type=MESH)
        pl.semaphore_wait(barrier, 2)

    def copy(self, source, target, peer, when=None):
        return Copy(self, source, target, peer, when)

    def send(self, source, target, peer):
        made = self.copy(source, target, peer)
        made.start()
        return made

    def move(self, source, target):
        source = source.ref if isinstance(source, Staged) else source
        copy = pltpu.make_async_copy(source, target, self.sems.at[self.used])
        self.used += 1
        copy.start()
        copy.wait()

    def finish(self):
        for made in self.made:
            made.settle()


def block_rows(block, size, part=0, parts=1):
    step = size // parts
    return pl.ds(pl.multiple_of(block * size + part * step, step), step)


class Gather:
    def __init__(self, wire, full, size):
        self.wire, self.full, self.size = wire, full, size
        self.to_near, self.to_far, self.relayed = [], [], []

    def rows(self, block, part):
        return self.full.at[block_rows(block, self.size, part, 2)]

    def push(self, part):
        own = self.rows(self.wire.at, part)
        self.to_near.append(self.wire.send(own, own, self.wire.near))
        self.to_far.append(self.wire.send(own, own, self.wire.far))

    def wait_near(self):
        for made in self.to_near:
            made.wait_recv()

    def relay(self, part):
        self.to_far[part].wait_recv()
        held = self.rows(self.wire.far, part)
        self.relayed.append(self.wire.send(held, held, self.wire.near))

    def wait_diagonal(self, part):
        self.relayed[part].wait_recv()


class Scatter:
    def __init__(self, wire, held, own, parts):
        self.held, self.own = held, own
        self.size = own.shape[0]
        step = self.size // parts
        self.cuts = [pl.ds(i * step, step) for i in range(parts)]

        def copies(out, into, peer, cuts):
            return [wire.copy(held.at[out, cut], held.at[into, cut], peer) for cut in cuts]

        self.side = copies(0, 1, wire.near, self.cuts)
        self.cross = copies(2, 3, wire.far, self.cuts)
        self.home = copies(4, 5, wire.near, [pl.ds(0, self.size)])[0]

    def put_diagonal(self, partial, part):
        self.held[0, self.cuts[part]] = partial.astype(BF16)
        self.side[part].start()

    def put_far(self, partial, part):
        cut = self.cuts[part]
        self.side[part].wait_recv()
        self.held[2, cut] = (partial + self.held[1, cut].astype(F32)).astype(BF16)
        self.cross[part].start()

    def put_near(self, partial):
        self.held[4] = partial.astype(BF16)
        self.home.start()

    def total(self):
        self.home.wait_recv()
        for made in self.cross:
            made.wait_recv()
        return self.own[...] + self.held[5].astype(F32) + self.held[3].astype(F32)


def turn(field, cosine, sine):
    lane = lax.broadcasted_iota(jnp.int32, cosine.shape, 1)
    first = lax.rem(lane, HD) < HD // 2
    turned = []
    for at in range(0, field.shape[1], 128):
        part = field[:, at : at + 128]
        swapped = jnp.where(
            first, pltpu.roll(part, 128 - HD // 2, 1), pltpu.roll(part, HD // 2, 1)
        )
        turned.append(part * cosine + swapped * sine)
    return jnp.concatenate(turned, axis=1)


def vmem(count):
    return [pl.BlockSpec(memory_space=pltpu.VMEM)] * count


def shaped(*entries):
    return [jax.ShapeDtypeStruct(shape, kind) for shape, kind in entries]


class Poll:
    def __init__(self, steps):
        self.steps = steps

    def __call__(self, times=1):
        for _ in range(times):
            for step in list(self.steps):
                if next(step, "end") == "end":
                    self.steps.remove(step)

    def enter(self):
        pass

    def leave(self):
        pass

    def before(self, what):
        pass


SMALL = 2**16


class Staged:
    def __init__(self, ref, copy, is_result):
        self.ref, self.copy, self.is_result = ref, copy, is_result
        self.begun = self.ended = False
        self.shape, self.dtype = ref.shape, ref.dtype

    def begin(self):
        self.begun = True
        self.copy.start()

    def wait(self):
        if not self.ended:
            self.ended = True
            self.copy.wait()

    def check(self):
        assert self.is_result or self.ended

    @property
    def at(self):
        self.check()
        return self.ref.at

    def __getitem__(self, index):
        self.check()
        return self.ref[index]

    def __setitem__(self, index, value):
        self.ref[index] = value


def ready(*refs):
    for ref in refs:
        if isinstance(ref, Staged):
            ref.wait()


def done(*refs):
    for ref in refs:
        if isinstance(ref, Staged):
            ref.begin()


class Background:
    def __init__(
        self, number, operands=(), outs=(), scratch=(), steps=None, staged=0, quad=False,
        across=False, semaphores=24,
    ):
        self.semaphores = semaphores
        self.staged = staged
        self.number, self.operands, self.outs = number, list(operands), list(outs)
        self.scratch, self.steps, self.quad, self.across = list(scratch), steps, quad, across


def is_large(shape, kind):
    return math.prod(shape) * jnp.dtype(kind).itemsize > SMALL


def call_with(body, background, outs, scratch, flops, *operands):
    placed = len(operands)
    everything = list(operands) + background.operands
    arrays = [item[0] if isinstance(item, tuple) else item for item in everything]
    shapes = [
        (array.shape[1:] if isinstance(item, tuple) else array.shape, array.dtype)
        for array, item in zip(arrays, everything)
    ]
    results = list(outs) + background.outs
    copies_in = [
        is_large(*shape) and not (background.quad and at >= placed)
        for at, shape in enumerate(shapes)
    ]
    raw_in = [background.quad and at >= placed for at in range(len(shapes))]
    raw_out = [at >= len(outs) + background.staged for at in range(len(results))]
    copies_out = [is_large(*shape) and not raw for shape, raw in zip(results, raw_out)]
    staged = [shape for shape, copied in zip(shapes + results, copies_in + copies_out) if copied]

    def kernel(*refs):
        refs = list(refs)

        def take(count):
            taken = refs[:count]
            del refs[:count]
            return taken

        sources, targets = take(len(shapes)), take(len(results))
        body_scratch, more_scratch = take(len(scratch)), take(len(background.scratch))
        held = take(len(staged))
        sems, local = take(2)
        wire = Wire(sems)
        number = 0
        for at, item in enumerate(everything):
            if copies_in[at]:
                source = sources[at].at[item[1]] if isinstance(item, tuple) else sources[at]
                ref = held[number]
                copy = pltpu.make_async_copy(source, ref, local.at[number])
                sources[at] = Staged(ref, copy, False)
                sources[at].begin()
                number += 1
        for at in range(len(results)):
            if copies_out[at]:
                ref = held[number]
                copy = pltpu.make_async_copy(ref, targets[at], local.at[number])
                targets[at] = Staged(ref, copy, True)
                number += 1
        steps = []
        if background.steps is None:
            wire.barrier()
        else:
            if background.quad:
                place = Quad()
                quad_barrier(wire, place, *([place.across] if background.across else []))
            else:
                place = Line()
                wide_barrier(wire, place, *([Quad().across] if background.across else []))
            steps = [
                background.steps(
                    wire, place, sources[placed:], targets[len(outs) :], more_scratch
                )
            ]

        poll = Poll(steps)
        body(wire, poll, *sources[:placed], *targets[: len(outs)], *body_scratch)
        while steps:
            poll()
        for ref in sources:
            ready(ref)
        for ref in targets:
            if isinstance(ref, Staged) and not ref.begun:
                ref.begin()
        wire.finish()
        for ref in targets:
            ready(ref)

    kernel.__name__ = body.__name__ if background.steps is None else body.__name__ + "_wide"

    def spec(apart):
        return pl.BlockSpec(memory_space=pl.ANY if apart else pltpu.VMEM)

    found = pl.pallas_call(
        kernel,
        in_specs=[spec(raw or copied) for raw, copied in zip(raw_in, copies_in)],
        out_specs=[spec(raw or copied) for raw, copied in zip(raw_out, copies_out)],
        out_shape=shaped(*results),
        scratch_shapes=list(scratch)
        + background.scratch
        + [pltpu.VMEM(*shape) for shape in staged]
        + [pltpu.SemaphoreType.DMA((background.semaphores,))]
        + [pltpu.SemaphoreType.DMA((max(len(staged), 1),))],
        compiler_params=pltpu.CompilerParams(
            collective_id=background.number, has_side_effects=True, vmem_limit_bytes=56 * 2**20
        ),
        cost_estimate=pl.CostEstimate(flops=flops, bytes_accessed=2**24, transcendentals=0),
        name=kernel.__name__,
    )(*arrays)
    return found[: len(outs)], found[len(outs) :]


def attend_half_body(
    wire, poll,
    x_ref, gain_ref, shift_ref, cos_ref, sin_ref, start_ref, w_qkv_ref, w_out_ref,
    a_ref, q_ref, k_ref, v_ref, o_ref, lse_ref, z_ref, h_ref, c_ref,
    held, own,
):
    size = x_ref.shape[0]
    ready(x_ref)
    gather = Gather(wire, a_ref, size)
    for part in range(2):
        rows = pl.ds(part * (size // 2), size // 2)
        normed = layer_norm(x_ref[rows].astype(F32), gain_ref[0:1], shift_ref[0:1])
        a_ref[block_rows(wire.at, size, part, 2)] = normed.astype(BF16)
        gather.push(part)
    width = q_ref.shape[1]

    def project(block):
        rows = block_rows(block, size)
        projected = dot(a_ref[rows], w_qkv_ref[...])
        cosine, sine = cos_ref[rows], sin_ref[rows]
        q_ref[rows] = turn(projected[:, :width], cosine, sine).astype(BF16)
        k_ref[rows] = turn(projected[:, width : 2 * width], cosine, sine).astype(BF16)
        v_ref[rows] = projected[:, 2 * width :].astype(BF16)

    poll()
    ready(w_qkv_ref, cos_ref, sin_ref)
    project(wire.at)
    gather.wait_near()
    project(wire.near)
    gather.relay(0)
    gather.relay(1)
    project(wire.far)
    gather.wait_diagonal(0)
    gather.wait_diagonal(1)
    project(wire.diagonal)

    done(a_ref, q_ref, k_ref, v_ref)
    poll()
    ready(start_ref, w_out_ref)
    scatter = Scatter(wire, held, own, 1)
    for block in (3, 1, 2, 0):
        rows = slice(block * size, (block + 1) * size)
        reach = (block + 1) * size
        key = lax.broadcasted_iota(jnp.int32, (size, reach), 1)
        query = lax.broadcasted_iota(jnp.int32, (size, reach), 0) + block * size
        allowed = (key >= start_ref[rows, :]) & (key <= query)
        mixed, logs = [], jnp.zeros((size, 128), F32)
        lane = lax.broadcasted_iota(jnp.int32, (size, 128), 1)
        for head in range(width // HD):
            lanes = slice(head * HD, (head + 1) * HD)
            scores = dot_t(q_ref[rows, lanes] * SCALE, k_ref[:reach, lanes])
            scores = jnp.where(allowed, scores, MASKED)
            summit = jnp.max(scores, axis=1, keepdims=True)
            weights = jnp.exp(scores - summit)
            total = jnp.sum(weights, axis=1, keepdims=True)
            chances = (weights * (1.0 / total)).astype(BF16)
            mixed.append(dot(chances, v_ref[:reach, lanes]))
            logs = jnp.where(lane == head, summit + jnp.log(total), logs)
        o_ref[rows, :] = jnp.concatenate(mixed, axis=1).astype(BF16)
        lse_ref[:, rows] = logs.T[: lse_ref.shape[0]]
        partial = dot(o_ref[rows, :], w_out_ref[...])

        if block in (1, 2):
            poll()

        @pl.when(wire.diagonal == block)
        def _():
            scatter.put_diagonal(partial, 0)

        @pl.when(wire.far == block)
        def _():
            scatter.put_far(partial, 0)

        @pl.when(wire.near == block)
        def _():
            scatter.put_near(partial)

        @pl.when(wire.at == block)
        def _():
            own[...] = partial

    done(o_ref, lse_ref)
    branch = scatter.total()
    z_ref[...] = branch
    middle = x_ref[...].astype(F32) + layer_norm(branch, gain_ref[1:2], shift_ref[1:2])
    h_ref[...] = middle
    c_ref[...] = layer_norm(middle, gain_ref[2:3], shift_ref[2:3]).astype(BF16)


def attend_half(background, resid, gains, shifts, cosine, sine, start, w_qkv, w_out):
    size, width = resid.shape
    length, part = cosine.shape[0], w_out.shape[0]
    return call_with(
        attend_half_body,
        background,
        [((length, width), BF16)]
        + [((length, part), BF16)] * 4
        + [((8, length), F32), ((size, width), F32), ((size, width), F32), ((size, width), BF16)],
        [pltpu.VMEM((6, size, width), BF16), pltpu.VMEM((size, width), F32)],
        8 * length * width * part + 4 * length * length * part,
        resid, gains, shifts, cosine, sine, start, w_qkv, w_out,
    )


def feed_half_body(
    wire, poll,
    c_ref, h_ref, gain_ref, shift_ref, w_up_ref, b_up_ref, w_down_ref,
    inner_ref, e_ref, d_ref, w_ref, y_ref,
    held, own,
):
    size = c_ref.shape[0]
    half = size // 2
    ready(c_ref)
    gather = Gather(wire, inner_ref, size)
    for part in range(2):
        inner_ref[block_rows(wire.at, size, part, 2)] = c_ref[pl.ds(part * half, half)]
        gather.push(part)
    scatter = Scatter(wire, held, own, 2)

    def feed(cuts):
        inner = jnp.concatenate([inner_ref[cut] for cut in cuts])
        hidden = dot(inner, w_up_ref[...]) + b_up_ref[...]
        below = 0.5 + 0.5 * lax.erf(hidden * (0.5**0.5))
        density = jnp.exp(-0.5 * hidden * hidden) * ((2.0 * math.pi) ** -0.5)
        active = (hidden * below).astype(BF16)
        slope = (below + hidden * density).astype(BF16)
        for at, cut in enumerate(cuts):
            step = inner.shape[0] // len(cuts)
            e_ref[cut] = active[at * step : (at + 1) * step]
            d_ref[cut] = slope[at * step : (at + 1) * step]
        return dot(active, w_down_ref[...])

    ready(w_up_ref, b_up_ref, w_down_ref)
    own[...] = feed([block_rows(wire.at, size)])
    gather.wait_near()
    scatter.put_near(feed([block_rows(wire.near, size)]))
    for part in range(2):
        gather.relay(part)
        gather.wait_diagonal(part)
        partial = feed(
            [block_rows(wire.diagonal, size, part, 2), block_rows(wire.far, size, part, 2)]
        )
        scatter.put_diagonal(partial[:half], part)
        scatter.put_far(partial[half:], part)
    done(inner_ref, e_ref, d_ref)
    ready(h_ref)
    second = scatter.total()
    w_ref[...] = second
    result = h_ref[...] + layer_norm(second, gain_ref[3:4], shift_ref[3:4])
    y_ref[...] = result.astype(BF16)


def feed_half(number, inner, middle, gains, shifts, w_up, b_up, w_down):
    size, width = inner.shape
    length, hidden = 4 * size, b_up.shape[1]
    return call_with(
        feed_half_body,
        Background(number),
        [((length, width), BF16)]
        + [((length, hidden), BF16)] * 2
        + [((size, width), F32), ((size, width), BF16)],
        [pltpu.VMEM((6, size, width), BF16), pltpu.VMEM((size, width), F32)],
        4 * length * width * hidden,
        inner, middle, gains, shifts, w_up, b_up, w_down,
    )[0]


def feed_back_body(
    wire, poll,
    g_ref, w_ref, h_ref, z_ref, gain_ref, inner_ref, e_ref, d_ref, w_up_ref, w_down_ref,
    grad_down_ref, grad_up_ref, grad_b_ref, norms_ref, dh_ref, dz_ref,
    second, hidden, held, own,
):
    size = g_ref.shape[0]
    half = size // 2
    ready(g_ref, w_ref)
    gather = Gather(wire, second, size)
    norms = [jnp.zeros((1, g_ref.shape[1]), F32)] * 2
    for part in range(2):
        rows = pl.ds(part * half, half)
        grad, gain, shift = layer_norm_back(w_ref[rows], g_ref[rows].astype(F32), gain_ref[3:4])
        if part == 0:
            poll.enter()
        second[block_rows(wire.at, size, part, 2)] = grad.astype(BF16)
        gather.push(part)
        norms = [norms[0] + gain, norms[1] + shift]
    norms_ref[3:4] = norms[0]
    norms_ref[7:8] = norms[1]
    norms_ref[0:1] = jnp.zeros_like(norms[0])
    norms_ref[4:5] = jnp.zeros_like(norms[0])
    scatter = Scatter(wire, held, own, 2)
    poll()

    def feed(cuts, first=False):
        grad = jnp.concatenate([second[cut] for cut in cuts])
        slope = jnp.concatenate([d_ref[cut] for cut in cuts]).astype(F32)
        grad = (slope * dot_t(grad, w_down_ref[...])).astype(BF16)
        for at, cut in enumerate(cuts):
            step = grad.shape[0] // len(cuts)
            hidden[cut] = grad[at * step : (at + 1) * step]
        bias = jnp.sum(grad.astype(F32), axis=0, keepdims=True)
        grad_b_ref[...] = bias if first else grad_b_ref[...] + bias
        return dot_t(grad, w_up_ref[...])

    ready(d_ref, w_down_ref, w_up_ref)
    own[...] = feed([block_rows(wire.at, size)], True)
    poll()
    gather.wait_near()
    scatter.put_near(feed([block_rows(wire.near, size)]))
    poll()
    for part in range(2):
        poll(2)
        gather.relay(part)
        gather.wait_diagonal(part)
        partial = feed(
            [block_rows(wire.diagonal, size, part, 2), block_rows(wire.far, size, part, 2)]
        )
        scatter.put_diagonal(partial[:half], part)
        scatter.put_far(partial[half:], part)
        poll()
    poll.before("feed")
    ready(e_ref, inner_ref)
    for at in range(0, e_ref.shape[1], 256):
        cut = slice(at, at + 256)
        grad_down_ref[cut, :] = t_dot(e_ref[:, cut], second[...]).astype(BF16)
        poll()
    done(grad_down_ref)
    for at in range(0, inner_ref.shape[1], 256):
        cut = slice(at, at + 256)
        grad_up_ref[cut, :] = t_dot(inner_ref[:, cut], hidden[...]).astype(BF16)
        poll()
    done(grad_up_ref)
    poll(3)
    ready(h_ref, z_ref)
    grad, gain, shift = layer_norm_back(h_ref[...], scatter.total(), gain_ref[2:3])
    norms_ref[2:3] = gain
    norms_ref[6:7] = shift
    grad = g_ref[...].astype(F32) + grad
    dh_ref[...] = grad
    grad, gain, shift = layer_norm_back(z_ref[...], grad, gain_ref[1:2])
    norms_ref[1:2] = gain
    norms_ref[5:6] = shift
    dz_ref[...] = grad.astype(BF16)
    poll.leave()


def feed_back(background, grad, second, middle, branch, gains, inner, active, slope, w_up, w_down):
    size, width = grad.shape
    length, hidden = 4 * size, active.shape[1]
    return call_with(
        feed_back_body,
        background,
        [
            ((hidden, width), BF16),
            ((width, hidden), BF16),
            ((1, hidden), F32),
            ((8, width), F32),
            ((size, width), F32),
            ((size, width), BF16),
        ],
        [
            pltpu.VMEM((length, width), BF16),
            pltpu.VMEM((length, hidden), BF16),
            pltpu.VMEM((6, size, width), BF16),
            pltpu.VMEM((size, width), F32),
        ],
        8 * length * width * hidden,
        grad, second, middle, branch, gains, inner, active, slope, w_up, w_down,
    )


def attend_back_body(
    wire, poll,
    dz_ref, dh_ref, x_ref, gain_ref, a_ref, q_ref, k_ref, v_ref, o_ref, lse_ref, start_ref,
    cos_ref, sin_ref, w_qkv_ref, w_out_ref,
    grad_qkv_ref, grad_out_ref, norms_ref, dx_ref,
    branch, mixture, projected, dk, dv, held, own,
):
    size = dz_ref.shape[0]
    length, width = q_ref.shape
    half = size // 2
    ready(dz_ref)
    gather = Gather(wire, branch, size)
    poll.enter()
    for part in range(2):
        branch[block_rows(wire.at, size, part, 2)] = dz_ref[pl.ds(part * half, half)]
        gather.push(part)

    def unmix(block):
        rows = block_rows(block, size)
        mixture[rows] = dot_t(branch[rows], w_out_ref[...]).astype(BF16)

    dk[...] = jnp.zeros_like(dk)
    dv[...] = jnp.zeros_like(dv)
    poll()
    ready(w_out_ref)
    unmix(wire.at)
    gather.wait_near()
    unmix(wire.near)
    poll()
    poll(2)
    gather.relay(0)
    poll(2)
    gather.relay(1)
    unmix(wire.far)
    gather.wait_diagonal(0)
    gather.wait_diagonal(1)
    unmix(wire.diagonal)
    ready(o_ref, q_ref, k_ref, v_ref, lse_ref, start_ref, cos_ref, sin_ref, w_qkv_ref)
    poll.before("attend")
    grad_out_ref[...] = t_dot(o_ref[...], branch[...]).astype(BF16)
    done(grad_out_ref)
    poll()

    pick_head = (
        lax.broadcasted_iota(jnp.int32, (8, width), 1) // HD
        == lax.broadcasted_iota(jnp.int32, (8, width), 0)
    ).astype(F32)
    for block in range(length // size):
        rows = slice(block * size, (block + 1) * size)
        reach = (block + 1) * size
        key = lax.broadcasted_iota(jnp.int32, (reach, size), 0)
        query = lax.broadcasted_iota(jnp.int32, (reach, size), 1) + block * size
        allowed = (key >= start_ref[:, rows]) & (key <= query)
        inner = lax.dot_general(
            pick_head,
            mixture[rows].astype(F32) * o_ref[rows].astype(F32),
            (((1,), (1,)), ((), ())),
            precision=lax.Precision.HIGHEST,
            preferred_element_type=F32,
        )
        dqs, dks, dvs = [], [], []
        for head in range(width // HD):
            lanes = slice(head * HD, (head + 1) * HD)
            k_head, g_head = k_ref[:reach, lanes], mixture[rows, lanes]
            q_head = q_ref[rows, lanes] * SCALE
            scores = dot_t(k_head, q_head) - lse_ref[head : head + 1, rows]
            chances = jnp.exp(jnp.where(allowed, scores, MASKED))
            grad_prob = dot_t(v_ref[:reach, lanes], g_head)
            grad_score = (chances * (grad_prob - inner[head : head + 1])).astype(BF16)
            dvs.append(dot(chances.astype(BF16), g_head))
            dks.append(dot(grad_score, q_head))
            dqs.append(t_dot(grad_score, k_head) * SCALE)
            if block > 0 and head % 2 == 1:
                poll()
        dq = jnp.concatenate(dqs, axis=1)
        projected[rows, :width] = turn(dq, cos_ref[rows], -sin_ref[rows]).astype(BF16)
        dk[:reach, :] += jnp.concatenate(dks, axis=1)
        dv[:reach, :] += jnp.concatenate(dvs, axis=1)
    for block in range(length // size):
        rows = slice(block * size, (block + 1) * size)
        turned = turn(dk[rows], cos_ref[rows], -sin_ref[rows])
        projected[rows, width : 2 * width] = turned.astype(BF16)
        projected[rows, 2 * width :] = dv[rows].astype(BF16)

    scatter = Scatter(wire, held, own, 2)

    def unproject(cut):
        return dot_t(projected[cut], w_qkv_ref[...])

    partial = unproject(block_rows(wire.diagonal, size))
    scatter.put_diagonal(partial[:half], 0)
    scatter.put_diagonal(partial[half:], 1)
    poll()
    partial = unproject(block_rows(wire.far, size))
    scatter.put_far(partial[:half], 0)
    scatter.put_far(partial[half:], 1)
    poll()
    scatter.put_near(unproject(block_rows(wire.near, size)))
    own[...] = unproject(block_rows(wire.at, size))
    ready(a_ref)
    for at in range(0, a_ref.shape[1], 256):
        cut = slice(at, at + 256)
        grad_qkv_ref[cut, :] = t_dot(a_ref[:, cut], projected[...]).astype(BF16)
        poll()
    done(grad_qkv_ref)
    poll(3)
    ready(x_ref, dh_ref)
    grad, gain, shift = layer_norm_back(x_ref[...].astype(F32), scatter.total(), gain_ref[0:1])
    norms_ref[...] = jnp.zeros_like(norms_ref)
    norms_ref[0:1] = gain
    norms_ref[4:5] = shift
    dx_ref[...] = (dh_ref[...] + grad).astype(BF16)
    poll.leave()


def attend_back(
    background,
    grad_branch, grad_middle, resid, gains, normed, query, keys, values, mixture, logs, start,
    cosine, sine, w_qkv, w_out,
):
    size, width = resid.shape
    length, part = query.shape
    return call_with(
        attend_back_body,
        background,
        [
            ((width, 3 * part), BF16),
            ((part, width), BF16),
            ((8, width), F32),
            ((size, width), BF16),
        ],
        [
            pltpu.VMEM((length, width), BF16),
            pltpu.VMEM((length, part), BF16),
            pltpu.VMEM((length, 3 * part), BF16),
            pltpu.VMEM((length, part), F32),
            pltpu.VMEM((length, part), F32),
            pltpu.VMEM((6, size, width), BF16),
            pltpu.VMEM((size, width), F32),
        ],
        16 * length * width * part + 10 * length * length * part,
        grad_branch, grad_middle, resid, gains, normed, query, keys, values, mixture, logs,
        start, cosine, sine, w_qkv, w_out,
    )


CHUNK = 64
LATE = 2


class Line:
    def __init__(self):
        at = lax.axis_index("wide")
        self.pair = lax.rem(at, 2)
        self.turn = at // 2
        self.upper = self.turn // 3
        self.up = {"wide": lax.rem(self.turn + 1, 4) * 2 + self.pair}
        self.down = {"wide": lax.rem(self.turn + 3, 4) * 2 + self.pair}
        self.side = {"wide": at + 1 - 2 * self.pair}
        self.bottom, self.top = self.turn == 0, self.turn == 3
        self.at_end = self.upper * 3 == self.turn
        self.inside = jnp.logical_not(self.at_end)
        not_bottom, not_top = self.turn > 0, self.turn < 3
        self.ways = (
            (self.up, self.bottom, self.top, not_bottom, not_top),
            (self.down, self.top, self.bottom, not_top, not_bottom),
        )

    def steps(self, chunks):
        for at in range(len(chunks) + 3 * LATE):
            for turn in range(4):

                @pl.when(self.turn == turn)
                def _():
                    for way, hops in sorted(((0, turn), (1, 3 - turn)), key=lambda item: item[1]):
                        chunk = at - hops * LATE
                        if not 0 <= chunk < len(chunks):
                            continue
                        if hops == 0:
                            if chunk >= 2:
                                chunks[chunk - 2](way, "sent")
                            chunks[chunk](way, "first")
                        else:
                            chunks[chunk](way, "last" if hops == 3 else "inner")

            yield


def span(start, size):
    return pl.ds(pl.multiple_of(start, 16), size)


class Fold:
    def __init__(self, wire, line, ref, by_side, into, across, final):
        self.wire, self.line, self.ref, self.by_side = wire, line, ref, by_side
        self.into, self.across, self.final = into, across, final
        rows = ref.shape[0]
        self.length = rows // 4 if by_side else rows // 2
        self.base = line.pair * (rows // 2) if by_side else 0
        self.count = self.length // CHUNK
        self.copies, self.sides = [], []
        for way, (peer, _, _, _, inner) in enumerate(line.ways):
            cuts = [into.at[way, pl.ds(c * CHUNK, CHUNK)] for c in range(self.count)]
            self.copies.append([wire.copy(cut, cut, peer, inner) for cut in cuts])

    @staticmethod
    def scratch(rows, columns, by_side):
        return [
            pltpu.VMEM((2, rows // 4 if by_side else rows // 2, columns), BF16),
            pltpu.VMEM((rows // 2 if by_side else rows // 4, columns), BF16),
        ]

    def place(self, way, chunk):
        return (self.length if way == 0 else 0) + chunk * CHUNK

    def start(self):
        line = self.line
        if self.by_side:
            away = (1 - line.pair) * (self.ref.shape[0] // 2)
            for chunk in range(self.count):
                pair = []
                for way in (0, 1):
                    place = self.place(way, chunk)
                    pair.append(
                        self.wire.send(
                            self.ref.at[span(away + place, CHUNK)],
                            self.across.at[pl.ds(place, CHUNK)],
                            line.side,
                        )
                    )
                self.sides.append(pair)

    def step(self, chunk, way, role):
        place = self.place(way, chunk)
        cut = pl.ds(chunk * CHUNK, CHUNK)
        made = self.copies[way][chunk]
        if role == "sent":
            made.wait_send_early(self.line.inside)
            return
        if self.by_side:
            self.sides[chunk][way].wait_recv()

        def own():
            total = self.ref[span(self.base + place, CHUNK)].astype(F32)
            if self.by_side:
                total = total + self.across[pl.ds(place, CHUNK)].astype(F32)
            return total

        if role == "first":
            if self.by_side:
                self.into[way, cut] = own().astype(BF16)
                made.start()
            else:
                made.start_from(self.ref.at[pl.ds(place, CHUNK)])
            return
        made.wait_recv()
        self.into[way, cut] = (own() + self.into[way, cut].astype(F32)).astype(BF16)
        if role == "inner":
            made.start()

    def chunks(self):
        return [functools.partial(self.step, chunk) for chunk in range(self.count)]

    def start_side(self):
        line = self.line
        half = self.length // 2
        source = self.into.at[1 - line.upper, span((1 - line.pair) * half, half)]
        self.side = self.wire.copy(source, self.across, line.side, line.at_end)

        @pl.when(line.at_end)
        def _():
            self.side.start()

    def end(self):
        line = self.line
        size = self.final.shape[0]

        @pl.when(line.at_end)
        def _():
            if not self.by_side:
                self.side.wait_recv()
            for at in range(0, size, CHUNK):
                if self.by_side:
                    self.final[pl.ds(at, CHUNK)] = self.into[1 - line.upper, pl.ds(at, CHUNK)]
                else:
                    own = self.into[1 - line.upper, span(line.pair * size + at, CHUNK)]
                    total = own.astype(F32) + self.across[pl.ds(at, CHUNK)].astype(F32)
                    self.final[pl.ds(at, CHUNK)] = total.astype(BF16)

        for made in sum(self.copies + self.sides, []):
            made.settle()
        if not self.by_side:
            self.side.settle()


class Spread:
    def __init__(self, wire, line, view, rows, by_side):
        self.wire, self.line, self.view, self.by_side = wire, line, view, by_side
        pair, upper = line.pair, line.upper
        self.quarter = rows // 4
        if by_side:
            self.length, self.base = rows // 4, pair * (rows // 2)
            self.mine = self.base + upper * self.quarter
        else:
            self.length, self.base = rows // 2, 0
            self.mine = upper * (rows // 2) + pair * self.quarter
        self.count = self.length // CHUNK
        self.copies = []
        for way, (peer, _, _, _, inner) in enumerate(line.ways):
            cuts = [self.chunk(way, c) for c in range(self.count)]
            self.copies.append([wire.copy(cut, cut, peer, inner) for cut in cuts])
        self.sides = []
        if not by_side:
            self.side = wire.copy(self.own(), self.own(), line.side, line.at_end)

    def own(self):
        return self.view(span(self.mine, self.quarter))

    def chunk(self, way, chunk):
        start = self.base + (0 if way == 0 else self.length) + chunk * CHUNK
        return self.view(span(start, CHUNK))

    def start(self):
        if not self.by_side:

            @pl.when(self.line.at_end)
            def _():
                self.side.start()

    def step(self, chunk, way, role):
        made = self.copies[way][chunk]
        if role == "sent":
            made.wait_send_early(self.line.inside)
            return
        if role == "first":
            if not self.by_side and chunk == 0:
                self.side.wait_recv()
            made.start()
        else:
            made.wait_recv()
            if role == "inner":
                made.start()
        if self.by_side:
            self.sides[chunk][way].start()

    def chunks(self):
        if self.by_side:
            self.sides = []
            for chunk in range(self.count):
                cuts = [self.chunk(way, chunk) for way in (0, 1)]
                self.sides.append([self.wire.copy(cut, cut, self.line.side) for cut in cuts])
        return [functools.partial(self.step, chunk) for chunk in range(self.count)]

    def end(self):
        for pair in self.sides:
            for made in pair:
                made.wait_recv()


class Sequence:
    def __init__(self, line):
        self.line, self.chunks, self.actions = line, [], {}

    def add(self, *lists):
        total = max(len(chunks) for chunks in lists)
        placed = [
            ((at + 0.5) * total / len(chunks), which, chunk)
            for which, chunks in enumerate(lists)
            for at, chunk in enumerate(chunks)
        ]
        self.chunks += [chunk for _, _, chunk in sorted(placed, key=lambda item: item[:2])]
        return self

    def before_next(self, *actions):
        self.actions.setdefault(len(self.chunks) - 1, []).extend(actions)

    def after(self, chunk, *actions):
        self.actions.setdefault(self.chunks.index(chunk) + 3 * LATE, []).extend(actions)

    def steps(self):
        for action in self.actions.get(-1, []):
            action()
        for at, _ in enumerate(self.line.steps(self.chunks)):
            for action in self.actions.get(at, []):
                action()
            yield


def small_steps(wire, line, norms_ref, bias_ref, narrow_in, sums, side_in, slots, total_ref):
    part = total_ref.shape[1]
    made = []

    def columns(device):
        return pl.ds(pl.multiple_of(device * part, part), part)

    for peer in (wire.near, wire.far, wire.diagonal):
        made.append(
            wire.send(norms_ref.at[:, columns(peer)], narrow_in.at[wire.at], {"narrow": peer})
        )
    narrow_in[wire.at] = norms_ref[:, columns(wire.at)]
    yield
    for copy in made:
        copy.wait_recv()
    total = narrow_in[0] + narrow_in[1] + narrow_in[2] + narrow_in[3]
    lines = [bias_ref[:, at * part : (at + 1) * part] for at in range(4)]
    sums[...] = jnp.concatenate([total] + lines + [jnp.zeros((4, part), F32)], axis=0)
    side = wire.send(sums, side_in, line.side)
    yield
    side.wait_recv()
    slots[line.turn] = sums[...] + side_in[...]
    for step in range(3):
        sends = []
        for way, peer in enumerate((line.up, line.down)):
            place = line.turn if way == 0 else 3 - line.turn
            goes = (place >= step) & (place < 3)
            comes = place > step
            slot = slots.at[lax.rem(line.turn + (4 - step if way == 0 else step), 4)]
            copy = wire.copy(slot, slot, peer, goes)
            sends.append((copy, goes, comes))

            @pl.when(goes)
            def _():
                copy.start()

        yield
        for copy, goes, comes in sends:

            @pl.when(comes)
            def _():
                copy.wait_recv()

    total_ref[...] = slots[0] + slots[1] + slots[2] + slots[3]


def home(wire, line, down, out, qkv, full_down, full_out, full_qkv):
    part = (full_out if full_down is None else full_down).shape[2]
    made = []
    at = wire.at

    def columns(device):
        return pl.ds(pl.multiple_of(device * part, part), part)

    for final, full, by_side in ((down, full_down, True), (out, full_out, False)):
        if final is None:
            continue
        quarter = final.shape[0]
        if by_side:
            mine = line.pair * (2 * quarter) + line.upper * quarter
        else:
            mine = line.upper * (2 * quarter) + line.pair * quarter
        slot = full.at[at, span(mine, quarter)]
        for peer in (wire.diagonal, wire.far, wire.near):
            made.append(
                wire.copy(final.at[:, columns(peer)], slot, {"narrow": peer}, line.at_end)
            )

        @pl.when(line.at_end)
        def _():
            wire.move(final.at[:, columns(at)], slot)

    if qkv is not None:
        quarter = qkv.shape[0]
        rows = span(line.pair * (2 * quarter) + line.upper * quarter, quarter)
        odd, upper = lax.rem(at, 2), at // 2
        far_slot = columns(2 - 2 * odd)
        made.append(
            wire.copy(
                qkv.at[:, columns(2 - 2 * upper)], full_qkv.at[rows, far_slot],
                {"narrow": wire.far}, line.at_end,
            )
        )
        made.append(
            wire.copy(
                qkv.at[:, columns(1 - odd + upper)], full_qkv.at[rows, columns(1)],
                {"narrow": wire.near}, line.at_end,
            )
        )

        @pl.when(line.at_end)
        def _():
            wire.move(qkv.at[:, columns((at + 1) // 2)], full_qkv.at[rows, columns(2 * odd)])

    @pl.when(line.at_end)
    def _():
        for copy in made:
            copy.start()

    def wait():
        @pl.when(line.at_end)
        def _():
            for copy in made:
                copy.wait_recv()

    return wait


def wide_barrier(wire, line, *others):
    barrier = pltpu.get_barrier_semaphore()

    def greet(peer):
        pl.semaphore_signal(barrier, inc=1, device_id=peer, device_id_type=MESH)

    for peer in (line.side,) + others:
        greet(peer)
    for peer in (wire.near, wire.far, wire.diagonal):
        greet({"narrow": peer})

    @pl.when(line.turn < 3)
    def _():
        greet(line.up)

    @pl.when(line.turn > 0)
    def _():
        greet(line.down)

    @pl.when(line.at_end)
    def _():
        pl.semaphore_wait(barrier, 5 + len(others))

    @pl.when(line.inside)
    def _():
        pl.semaphore_wait(barrier, 6 + len(others))


def run(*steps):
    steps = list(steps)
    while steps:
        for at in list(steps):
            if next(at, "end") == "end":
                steps.remove(at)


def fold_pair(wire, line, refs, finals, scratch):
    return (
        Fold(wire, line, refs[0], False, *scratch[0:2], finals[0]),
        Fold(wire, line, refs[1], True, *scratch[2:4], finals[1]),
    )


def spread_feed(wire, line, full_up, full_down):
    return (
        Spread(wire, line, lambda rows: full_up.at[rows], full_up.shape[0], False),
        Spread(wire, line, lambda rows: full_down.at[:, rows], full_down.shape[1], True),
    )


def spread_attend(wire, line, full_out, full_qkv):
    return (
        Spread(wire, line, lambda rows: full_out.at[:, rows], full_out.shape[1], False),
        Spread(wire, line, lambda rows: full_qkv.at[rows], full_qkv.shape[0], True),
    )


def place_own(wire, line, spread, final):
    @pl.when(line.at_end)
    def _():
        wire.move(final, spread.own())


def swap_across(wire, source, target, first_sends):
    quad = Quad()
    second = jnp.logical_not(quad.first)
    sends, takes = (quad.first, second) if first_sends else (second, quad.first)
    made = wire.copy(source, target, quad.across, sends)

    @pl.when(sends)
    def _():
        made.start()

    yield

    @pl.when(takes)
    def _():
        made.wait_recv()


class Flow(Poll):
    def __init__(self, wire, wide_wire, line, free):
        super().__init__([])
        self.wire, self.wide_wire, self.line, self.free = wire, wide_wire, line, free
        self.sequence, self.done, self.limit, self.limits = Sequence(line), 0, 0, {}
        self.entered = self.last = False
        self.walk = None

    def __call__(self, times=1):
        for _ in range(times):
            if self.walk is not None and self.done < self.limit:
                self.done += 1
                if next(self.walk, "end") == "end":
                    self.walk = None

    def until(self, count):
        while self.walk is not None and self.done < min(count, self.limit):
            self()

    def open(self, limit):
        self.limit = limit

    def before(self, what):
        self.until(self.limits.get(what, 0))

    def enter(self):
        if self.entered:
            pl.semaphore_wait(self.free.at[0], 1)
            pl.semaphore_wait(self.free.at[1], 1)
        self.entered = True

    def leave(self):
        self.wire.finish()
        self.wire.made = []
        if self.last:
            return
        for at, peer in enumerate((self.wire.near, self.wire.far)):
            pl.semaphore_signal(
                self.free.at[at], inc=1, device_id={"narrow": peer}, device_id_type=MESH
            )

    def peers(self):
        line = self.line
        not_bottom, not_top = line.ways[0][3], line.ways[1][3]
        return (
            (2, line.up, not_top, not_bottom),
            (3, line.down, not_bottom, not_top),
            (4, line.side, None, None),
        )

    def greet(self):
        for at, peer, sends, _ in self.peers():
            signal = functools.partial(
                pl.semaphore_signal, self.free.at[at], inc=1, device_id=peer, device_id_type=MESH
            )
            signal() if sends is None else pl.when(sends)(lambda signal=signal: signal())

    def greeted(self):
        for at, _, _, comes in self.peers():
            wait = functools.partial(pl.semaphore_wait, self.free.at[at], 1)
            wait() if comes is None else pl.when(comes)(lambda wait=wait: wait())


FEED_NAMES = ("w", "h", "z", "inner", "e", "d", "down")
ATTEND_NAMES = ("x", "a", "q", "k", "v", "o", "qkv", "out")


def backward_kernel(shape, *refs):
    size, length, width, hidden_count, part = shape
    refs = list(refs)

    def take(count):
        taken = refs[:count]
        del refs[:count]
        return taken

    dy, result, up, cosine, sine, start = take(6)
    gains, logs, large = [], [], []
    for _ in range(2):
        gain, log = take(2)
        gains.append(gain)
        logs.append(log)
        large.append(dict(zip(FEED_NAMES + ATTEND_NAMES, take(15))))
    dx_out, grad_came, result_came = take(3)
    totals = take(2)
    fulls = [dict(zip(("up", "down", "out", "qkv"), take(4))) for _ in range(2)]
    held_names = ("g", "up", "cos", "sin") + FEED_NAMES + ATTEND_NAMES
    buffers = dict(zip(held_names, take(len(held_names))))
    second, hidden, mixture, projected, dk, dv, held, own, dh, dz, dx = take(11)
    grad_up, grad_down, grad_out, grad_qkv = take(4)
    feed_scratch, attend_scratch = take(4), take(4)
    finals = [dict(zip(("up", "down", "out", "qkv"), take(4))) for _ in range(2)]
    small = [take(4) for _ in range(2)]
    norms = [take(2) for _ in range(2)]
    biases = take(2)
    sems, wide_sems, local, free = take(4)

    loads = {}

    def load(layer, name, source):
        at = held_names.index(name)
        copy = pltpu.make_async_copy(source, buffers[name], local.at[at])
        loads[layer, name] = Staged(buffers[name], copy, False)
        loads[layer, name].begin()

    def load_feed(layer):
        load(layer, "up", up.at[layer])
        for name in ("w", "d", "down", "e", "inner", "h", "z"):
            load(layer, name, large[layer][name])

    def load_attend(layer):
        for name in ("out", "o", "q", "k", "v", "qkv", "a", "x"):
            load(layer, name, large[layer][name])

    load(1, "g", dy)
    load_feed(1)
    load_attend(1)
    load(1, "cos", cosine)
    load(1, "sin", sine)
    wire, wide_wire, line = Wire(sems), Wire(wide_sems), Line()
    wide_barrier(wide_wire, line, Quad().across)
    result_swap = swap_across(wide_wire, result, result_came, True)
    next(result_swap)

    flow = Flow(wire, wide_wire, line, free)
    sequence = flow.sequence
    folds, spreads, waits = {}, {}, {}

    def fold_feed(layer):
        folds[layer, "up"], folds[layer, "down"] = fold_pair(
            wide_wire, line, (grad_up, grad_down),
            (finals[layer]["up"], finals[layer]["down"]), feed_scratch,
        )

    def fold_attend(layer):
        folds[layer, "out"], folds[layer, "qkv"] = fold_pair(
            wide_wire, line, (grad_out, grad_qkv),
            (finals[layer]["out"], finals[layer]["qkv"]), attend_scratch,
        )

    for layer in range(2):
        fold_feed(layer)
        fold_attend(layer)
        full = fulls[layer]
        spreads[layer, "up"], spreads[layer, "down"] = spread_feed(
            wide_wire, line, full["up"], full["down"]
        )
        spreads[layer, "out"], spreads[layer, "qkv"] = spread_attend(
            wide_wire, line, full["out"], full["qkv"]
        )

    def go_home(layer, names):
        final, full = finals[layer], fulls[layer]

        def action():
            for name in names:
                folds[layer, name].end()
            if names == ("down",):
                waits[layer, names] = home(
                    wide_wire, line, final["down"], None, None, full["down"], None, None
                )
            else:
                waits[layer, names] = home(
                    wide_wire, line, None, final["out"], final["qkv"], None, full["out"], full["qkv"]
                )

        return action

    def come_home(layer, names):
        return lambda: waits[layer, names]()

    def spread_up(layer):
        def action():
            folds[layer, "up"].end()
            place_own(wide_wire, line, spreads[layer, "up"], finals[layer]["up"])
            spreads[layer, "up"].start()

        return action

    def fill(count):
        while len(sequence.chunks) < count:
            sequence.add([lambda way, role: None])

    def feed_fold_part(layer):
        sequence.before_next(folds[layer, "down"].start)
        chunks = folds[layer, "up"].chunks()
        sequence.add(chunks).add(folds[layer, "down"].chunks())
        sequence.after(chunks[-1], folds[layer, "up"].start_side)
        return len(sequence.chunks)

    def attend_fold_feed_spread_part(layer, feed_end):
        sequence.before_next(folds[layer, "qkv"].start)
        chunks = folds[layer, "out"].chunks()
        sequence.add(chunks)
        sequence.after(chunks[-1], folds[layer, "out"].start_side)
        sequence.actions.setdefault(feed_end - 1 + 3 * LATE, []).extend(
            [go_home(layer, ("down",)), spread_up(layer)]
        )
        fill(feed_end + 2 * LATE)
        qkv_chunks = folds[layer, "qkv"].chunks()
        sequence.add(qkv_chunks)
        qkv_end = len(sequence.chunks)
        fill(feed_end + 3 * LATE + 2)
        sequence.before_next(come_home(layer, ("down",)))
        sequence.add(spreads[layer, "down"].chunks()).add(spreads[layer, "up"].chunks())
        sequence.actions.setdefault(qkv_end - 1 + 3 * LATE, []).append(
            go_home(layer, ("out", "qkv"))
        )
        fill(qkv_end + 3 * LATE + 2)
        sequence.before_next(come_home(layer, ("out", "qkv")), spreads[layer, "out"].start)

    feed_end = feed_fold_part(1)
    in_attend_1 = len(sequence.chunks)
    attend_fold_feed_spread_part(1, feed_end)
    sequence.actions.setdefault(len(sequence.chunks) - 1, []).append(flow.greet)
    sequence.add(spreads[1, "qkv"].chunks()).add(spreads[1, "out"].chunks())
    sequence.before_next(flow.greeted)
    in_feed_0 = len(sequence.chunks)
    feed_end = feed_fold_part(0)
    in_attend_0 = len(sequence.chunks)
    attend_fold_feed_spread_part(0, feed_end)
    sequence.add(spreads[0, "qkv"].chunks()).add(spreads[0, "out"].chunks())
    flow.limits = {}

    def feed(layer, grad):
        held_now = {name: loads[layer, name] for name in FEED_NAMES + ("up",)}
        feed_back_body(
            wire, flow, grad, held_now["w"], held_now["h"], held_now["z"], gains[layer],
            held_now["inner"], held_now["e"], held_now["d"], held_now["up"], held_now["down"],
            grad_down, grad_up, biases[layer], norms[layer][0], dh, dz,
            second, hidden, held, own,
        )

    def attend(layer):
        names = {name: loads[layer, name] for name in ATTEND_NAMES}
        attend_back_body(
            wire, flow, dz, dh, names["x"], gains[layer], names["a"], names["q"], names["k"],
            names["v"], names["o"], logs[layer], start, loads[1, "cos"], loads[1, "sin"],
            names["qkv"], names["out"],
            grad_qkv, grad_out, norms[layer][1], dx,
            second, mixture, projected, dk, dv, held, own,
        )
        norms[layer][0][...] += norms[layer][1][...]

    feed(1, loads[1, "g"])
    flow.walk = sequence.steps()
    flow.open(in_attend_1 - 1)
    load_feed(0)
    attend(1)
    smalls = [small_steps(wide_wire, line, norms[1][0], biases[1], *small[1], totals[1])]
    flow.open(in_feed_0 - 1)
    load_attend(0)
    flow.limits = {"feed": feed_limit(in_attend_1)}
    feed(0, dx)
    flow.open(in_attend_0 - 1)
    flow.limits = {"attend": in_feed_0}
    flow.last = True
    attend(0)
    moved = pltpu.make_async_copy(dx, dx_out, local.at[len(held_names)])
    moved.start()
    grad_swap = swap_across(wide_wire, dx, grad_came, False)
    next(grad_swap)
    flow.open(len(sequence.chunks) + 3 * LATE + 1)
    smalls.append(small_steps(wide_wire, line, norms[0][0], biases[0], *small[0], totals[0]))
    while flow.walk is not None or smalls:
        flow()
        for steps in list(smalls):
            if next(steps, "end") == "end":
                smalls.remove(steps)
    for layer in range(2):
        spreads[layer, "down"].end()
        spreads[layer, "qkv"].end()
    next(result_swap, None)
    next(grad_swap, None)
    moved.wait()
    wide_wire.finish()
    assert wire.used <= sems.shape[0] and wide_wire.used <= wide_sems.shape[0]


def feed_limit(feed_end):
    return feed_end + 3 * LATE + 1


def backward_wide(grad, result, saved, weights, start, tables):
    size, width = grad.shape
    length, part = saved[0][2].shape
    hidden_count = saved[0][10].shape[1]
    shape = (size, length, width, hidden_count, part)
    operands, specs = [], []

    def give(array, large=True):
        operands.append(array)
        specs.append(pl.BlockSpec(memory_space=pl.ANY if large else pltpu.VMEM))

    w_up = weights[0][2][0]
    for array in (grad, result, w_up) + tables:
        give(array)
    give(start[None], False)
    for layer in range(2):
        w_qkv, w_out, _, _, w_down, gains, _ = weights[layer]
        resid, normed, query, keys, values, mixture, logs, branch, middle, inner, active, slope, second = saved[layer]
        give(gains, False)
        give(logs, False)
        for array in (second, middle, branch, inner, active, slope, w_down):
            give(array)
        for array in (resid, normed, query, keys, values, mixture, w_qkv, w_out):
            give(array)
    rows = ((size, width), BF16)
    outs = [rows] * 3 + [((16, part), F32)] * 2
    for _ in range(2):
        outs += [
            ((width, hidden_count), BF16),
            ((4, hidden_count, part), BF16),
            ((4, part, part), BF16),
            ((width, 3 * part), BF16),
        ]
    out_specs = [pl.BlockSpec(memory_space=pl.ANY)] * 3 + vmem(2)
    out_specs += [pl.BlockSpec(memory_space=pl.ANY)] * 8
    line_rows = ((size, width), F32)
    buffers = [
        rows, ((width, hidden_count), BF16), (tables[0].shape, F32), (tables[1].shape, F32),
        line_rows, line_rows, line_rows,
        ((length, width), BF16), ((length, hidden_count), BF16), ((length, hidden_count), BF16),
        ((hidden_count, width), BF16),
        rows, ((length, width), BF16),
    ]
    buffers += [((length, part), BF16)] * 4
    buffers += [((width, 3 * part), BF16), ((part, width), BF16)]
    buffers += [
        ((length, width), BF16), ((length, hidden_count), BF16), ((length, part), BF16),
        ((length, 3 * part), BF16), ((length, part), F32), ((length, part), F32),
        ((6, size, width), BF16), line_rows, line_rows, rows, rows,
    ]
    grads = [
        ((width, hidden_count), BF16), ((hidden_count, width), BF16),
        ((part, width), BF16), ((width, 3 * part), BF16),
    ]
    buffers += grads
    scratch = [pltpu.VMEM(*entry) for entry in buffers]
    for (first, _), (last, _) in (grads[0:2], grads[2:4]):
        scratch += Fold.scratch(*first, False) + Fold.scratch(*last, True)
    for _ in range(2):
        scratch += [pltpu.VMEM((rows // 4, columns), BF16) for (rows, columns), _ in grads]
    for _ in range(2):
        scratch += [
            pltpu.VMEM((4, 8, part), F32),
            pltpu.VMEM((16, part), F32),
            pltpu.VMEM((16, part), F32),
            pltpu.VMEM((4, 16, part), F32),
        ]
    scratch += [pltpu.VMEM((8, width), F32)] * 4
    scratch += [pltpu.VMEM((1, hidden_count), F32)] * 2
    scratch += [
        pltpu.SemaphoreType.DMA((88,)),
        pltpu.SemaphoreType.DMA((520,)),
        pltpu.SemaphoreType.DMA((20,)),
        pltpu.SemaphoreType.REGULAR((5,)),
    ]
    found = pl.pallas_call(
        functools.partial(backward_kernel, shape),
        in_specs=specs,
        out_specs=out_specs,
        out_shape=shaped(*outs),
        scratch_shapes=scratch,
        compiler_params=pltpu.CompilerParams(
            collective_id=3, has_side_effects=True, vmem_limit_bytes=62 * 2**20
        ),
        name="backward",
    )(*operands)
    grad, grad_came, result_came = found[:3]
    totals = found[3:5]

    def shards(layer):
        up, down, out, qkv = found[5 + 4 * layer : 9 + 4 * layer]
        out, down = (block.reshape(-1, block.shape[2]) for block in (out, down))
        total = totals[layer]
        return qkv, out, up, total[8:12].reshape(-1), down, total[:4], total[4:8]

    return grad, grad_came, result_came, (shards(0), shards(1))


class Quad:
    def __init__(self):
        at = lax.axis_index("wide")
        pair, turn = lax.rem(at, 2), at // 2
        odd = lax.rem(turn, 2)
        self.side = {"wide": at + 1 - 2 * pair}
        self.mate = {"wide": (turn + 1 - 2 * odd) * 2 + pair}
        self.mine = odd * 2 + pair
        self.from_side = odd * 2 + 1 - pair
        self.from_mate = (1 - odd) * 2 + pair
        halfway = lax.axis_size("wide") // 2
        self.first = at < halfway
        self.across = {"wide": lax.rem(at + halfway, 2 * halfway)}


class Fetch:
    def __init__(self, wire, shard, full, by_heads):
        self.wire, self.full, self.rows = wire, full, full.shape[0]
        at, odd, upper = wire.at, lax.rem(wire.at, 2), wire.at // 2
        part = shard.shape[1]

        def columns(block, count=1):
            return pl.ds(pl.multiple_of(block * 256, 256), 256 * count)

        if by_heads:
            self.far = [
                (
                    lambda rows: shard.at[rows, columns(2 - 2 * odd)],
                    lambda rows: full.at[rows, columns(2 * upper)],
                    wire.far,
                )
            ]
            self.relay = lambda rows: full.at[rows, columns(2 - 2 * upper)]
            self.near = (shard.at[:, columns(1)], full.at[:, columns(odd + upper)])
            self.own = (shard.at[:, columns(2 * odd)], full.at[:, columns((at + 1) // 2)])
        else:
            block = self.rows

            def away(peer):
                return (
                    lambda rows: shard.at[span(peer * block + rows.start, rows.size)],
                    lambda rows: full.at[rows, columns(at)],
                    peer,
                )

            self.far = [away(wire.far), away(wire.diagonal)]
            self.relay = lambda rows: full.at[rows, columns(2 - 2 * upper, 2)]
            self.near = (shard.at[span(wire.near * block, block)], full.at[:, columns(at)])
            self.own = (shard.at[span(at * block, block)], full.at[:, columns(at)])

    def quarter(self, which, half=0, halves=1):
        size = self.rows // 4
        return span(which * size + half * (size // halves), size // halves)


def fetch_steps(wire, quad, fetches, local):
    copies, sent, nears = [], [], []
    for at, fetch in enumerate(fetches):
        rows = fetch.quarter(quad.mine)
        for source, target, peer in fetch.far:
            sent.append(wire.send(source(rows), target(rows), {"narrow": peer}))
        nears.append(wire.send(*fetch.near, {"narrow": wire.near}))
        copies.append(pltpu.make_async_copy(*fetch.own, local.at[at]))
        copies[-1].start()
    yield
    for made in sent:
        made.wait_recv()
    sides, mates = [], []
    for fetch in fetches:
        held = fetch.relay(fetch.quarter(quad.mine))
        sides.append(wire.send(held, held, quad.side))
        mates.append(wire.send(held, held, quad.mate))
    yield
    last = []
    for fetch, side, mate in zip(fetches, sides, mates):
        side.wait_recv()
        held = fetch.relay(fetch.quarter(quad.from_side, 0, 2))
        last.append(wire.send(held, held, quad.mate))
        mate.wait_recv()
        held = fetch.relay(fetch.quarter(quad.from_mate, 1, 2))
        last.append(wire.send(held, held, quad.side))
    yield
    for made in last + nears:
        made.wait_recv()
    for copy in copies:
        copy.wait()


def greet(peers):
    barrier = pltpu.get_barrier_semaphore()
    for peer in peers:
        pl.semaphore_signal(barrier, inc=1, device_id=peer, device_id_type=MESH)
    pl.semaphore_wait(barrier, len(peers))


def quad_barrier(wire, quad, *others):
    narrow = [{"narrow": peer} for peer in (wire.near, wire.far, wire.diagonal)]
    greet(narrow + [quad.side, quad.mate] + list(others))


def begin_kernel(
    blocks_ref, w_qkv_ref, w_out_ref, norms_ref,
    qkv_ref, out_ref, full_norms_ref, x_ref, dy_ref,
    local, sems,
):
    wire, quad = Wire(sems), Quad()
    quad_barrier(wire, quad, quad.across)
    size = x_ref.shape[0]
    blocks = [blocks_ref.at[pl.ds(at * size, size)] for at in range(2)]
    second = jnp.logical_not(quad.first)
    x_swap = wire.copy(blocks[1], x_ref, quad.across, quad.first)
    dy_swap = wire.copy(blocks[0], dy_ref, quad.across, second)
    kept = local.at[3]

    @pl.when(quad.first)
    def _():
        x_swap.start()
        pltpu.make_async_copy(blocks[0], x_ref, kept).start()

    @pl.when(second)
    def _():
        dy_swap.start()
        pltpu.make_async_copy(blocks[1], dy_ref, kept).start()

    fetches = [
        Fetch(wire, w_qkv_ref.at[0], qkv_ref, True),
        Fetch(wire, w_out_ref.at[0], out_ref, False),
    ]
    part = norms_ref.shape[1]
    slot = full_norms_ref.at[:, pl.ds(pl.multiple_of(wire.at * part, part), part)]
    sent = [
        wire.send(norms_ref, slot, {"narrow": peer})
        for peer in (wire.diagonal, wire.far, wire.near)
    ]
    own = pltpu.make_async_copy(norms_ref, slot, local.at[len(fetches)])
    own.start()
    run(fetch_steps(wire, quad, fetches, local))
    for made in sent:
        made.wait_recv()
    own.wait()

    @pl.when(quad.first)
    def _():
        pltpu.make_async_copy(blocks[0], x_ref, kept).wait()
        dy_swap.wait_recv()

    @pl.when(second)
    def _():
        pltpu.make_async_copy(blocks[1], dy_ref, kept).wait()
        x_swap.wait_recv()

    wire.finish()


def anywhere(count):
    return [pl.BlockSpec(memory_space=pl.ANY)] * count


def begin(blocks, w_qkv, w_out, norms):
    width = blocks.shape[1]
    shapes = [
        (w_qkv.shape[1:], BF16),
        ((w_out.shape[2], width), BF16),
        ((norms.shape[0], width), BF16),
        ((blocks.shape[0] // 2, width), BF16),
        ((blocks.shape[0] // 2, width), BF16),
    ]
    return pl.pallas_call(
        begin_kernel,
        in_specs=anywhere(4),
        out_specs=anywhere(5),
        out_shape=shaped(*shapes),
        scratch_shapes=[pltpu.SemaphoreType.DMA((8,)), pltpu.SemaphoreType.DMA((40,))],
        compiler_params=pltpu.CompilerParams(collective_id=10, has_side_effects=True),
        name="begin",
    )(blocks, w_qkv, w_out, norms)


def fetch_rest_steps(wire, quad, refs, outs, scratch):
    w_qkv, w_out, w_down = refs
    down_0, qkv_1, out_1, down_1 = outs
    first = fetch_steps(wire, quad, [Fetch(wire, w_down.at[0], down_0, False)], scratch[0])
    rest = [
        Fetch(wire, w_qkv.at[1], qkv_1, True),
        Fetch(wire, w_out.at[1], out_1, False),
        Fetch(wire, w_down.at[1], down_1, False),
    ]
    second = fetch_steps(wire, quad, rest, scratch[1])
    next(first)
    yield
    next(first)
    next(second)
    yield
    next(first)
    next(second)
    yield
    next(first, None)
    next(second)
    yield
    next(second, None)


def swap(block, distance):
    count = lax.axis_size("narrow")
    return lax.ppermute(block, "narrow", [(i, i ^ distance) for i in range(count)])


def pick(stack, table, at):
    return lax.dynamic_index_in_dim(stack, jnp.asarray(table)[at], 0, keepdims=False)


def by_heads(block, at):
    parts = jnp.stack(jnp.split(block, 3, axis=1))
    own = pick(parts, [0, 2, 0, 2], at)
    near = swap(parts[1], 1)
    far = swap(pick(parts, [2, 0, 2, 0], at), 2)
    parts = jnp.stack([own, near, far])
    order = jnp.asarray([[0, 1, 2], [1, 0, 2], [2, 0, 1], [2, 1, 0]])[at]
    return jnp.concatenate(
        [lax.dynamic_index_in_dim(parts, order[i], 0, keepdims=False) for i in range(3)], axis=1
    )


def from_heads(block, at):
    parts = jnp.stack(jnp.split(block, 3, axis=1))
    own = pick(parts, [0, 1, 1, 2], at)
    near = swap(pick(parts, [1, 0, 2, 1], at), 1)
    far = swap(pick(parts, [2, 2, 0, 0], at), 2)
    parts = jnp.stack([own, near, far])
    order = jnp.asarray([[0, 1, 2], [2, 1, 0], [0, 1, 2], [2, 1, 0]])[at]
    return jnp.concatenate(
        [lax.dynamic_index_in_dim(parts, order[i], 0, keepdims=False) for i in range(3)], axis=1
    )


def to_rows(block):
    return lax.all_to_all(block, "narrow", split_axis=0, concat_axis=1, tiled=True)


def to_columns(block):
    return lax.all_to_all(block, "narrow", split_axis=1, concat_axis=0, tiled=True)


def layer_forward(resid, weights, start, tables, background=None):
    w_qkv, w_out, w_up, b_up, w_down, gains, shifts = weights
    (normed, query, keys, values, mixture, logs, branch, middle, inner), more = attend_half(
        background or Background(1), resid, gains, shifts, *tables, start[:, None], w_qkv, w_out
    )
    if background is not None:
        w_down = more[0]
    inner, active, slope, second, result = feed_half(
        20 + w_up[1], inner, middle, gains, shifts, w_up, b_up, w_down
    )
    return result, more, (
        resid, normed, query, keys, values, mixture, logs, branch, middle, inner, active, slope, second
    )


def feed_backward(background, grad, saved, weights):
    w_qkv, w_out, w_up, b_up, w_down, gains, shifts = weights
    _, _, _, _, _, _, _, branch, middle, inner, active, slope, second = saved
    (grad_down, grad_up, grad_b_up, norms, grad_middle, grad_branch), results = feed_back(
        background, grad, second, middle, branch, gains, inner, active, slope, w_up, w_down
    )
    return ((grad_up, grad_down), norms, grad_b_up, grad_middle, grad_branch), results


def attend_backward(background, grad_branch, grad_middle, saved, weights, start, tables):
    w_qkv, w_out, w_up, b_up, w_down, gains, shifts = weights
    resid, normed, query, keys, values, mixture, logs, _, _, _, _, _, _ = saved
    (grad_qkv, grad_out, norms, grad), results = attend_back(
        background, grad_branch, grad_middle, resid, gains, normed, query, keys, values, mixture,
        logs, start[None], *tables, w_qkv, w_out,
    )
    return ((grad_out, grad_qkv), norms, grad), results


def layer_backward(grad, saved, weights, start, tables):
    ((grad_up, grad_down), norms, grad_b_up, grad_middle, grad_branch), _ = feed_backward(
        Background(30 + weights[2][1]), grad, saved, weights
    )
    ((grad_out, grad_qkv), norms_too, grad), _ = attend_backward(
        Background(4), grad_branch, grad_middle, saved, weights, start, tables
    )
    return grad, (grad_qkv, grad_out, grad_up, grad_b_up, grad_down, norms + norms_too)


def reduce_grads(grads, at):
    def fold(block):
        return lax.psum_scatter(block, "wide", scatter_dimension=0, tiled=True)

    def spread(block):
        return lax.all_gather(block, "wide", axis=0, tiled=True)

    def spread_rows(block):
        wide, narrow = lax.axis_size("wide"), lax.axis_size("narrow")
        rows, width = block.shape
        full = spread(block).reshape(wide, narrow, rows // narrow, width)
        return full.transpose(1, 0, 2, 3).reshape(wide * rows, width)

    qkv, out, up, b_up, down, norms = grads
    qkv = spread(from_heads(fold(qkv), at))
    out = spread_rows(to_columns(fold(out)))
    up = spread(fold(up))
    down = spread_rows(to_columns(fold(down)))
    b_up = lax.psum(b_up[0], "wide")
    norms = lax.psum(norms, ("wide", "narrow"))
    part = norms.shape[1] // lax.axis_size("narrow")
    norms = lax.dynamic_slice_in_dim(norms, at * part, part, 1)
    return qkv, out, up, b_up, down, norms[:4], norms[4:]


def on_device(ends, lengths, w_qkv, w_out, w_up, b_up, w_down, norm_gain, norm_bias):
    wide = lax.axis_size("wide")
    narrow = lax.axis_size("narrow")
    halfway = wide // 2
    wide_at = lax.axis_index("wide")
    at = lax.axis_index("narrow")
    first = wide_at < halfway
    row_count = ends.shape[0] // 2
    length = row_count * narrow

    def route(block):
        pairs = [(i, (i + halfway) % wide) for i in range(wide)]
        return lax.ppermute(block, "wide", pairs)

    own_lengths = lengths[lax.rem(wide_at, halfway), wide_at // halfway]
    places = jnp.arange(length, dtype=jnp.int32)
    passed = (places[:, None] >= jnp.cumsum(own_lengths)[None, :]).astype(jnp.int32)
    start = jnp.sum(passed * own_lengths[None, :], axis=1)
    tables = rope_tables(places - start)
    b_up = b_up.astype(F32)[:, None]
    norms = jnp.concatenate([norm_gain, norm_bias]).reshape(16, -1)

    if wide == 8:
        qkv_0, out_0, norms, resid, upstream = begin(ends, w_qkv, w_out, norms)
    else:
        came = route(jnp.where(first, ends[row_count:], ends[:row_count]))
        norms = lax.all_gather(norms, "narrow", axis=1, tiled=True)
        qkv_0, out_0 = by_heads(w_qkv[0], at), to_rows(w_out[0])
        down_0, down_1 = to_rows(w_down[0]), to_rows(w_down[1])
        qkv_1, out_1 = by_heads(w_qkv[1], at), to_rows(w_out[1])
        resid = jnp.where(first, ends[:row_count], came)
        upstream = jnp.where(first, came, ends[row_count:])
    norms = norms.astype(F32)

    if wide == 8:
        width = ends.shape[1]
        part = w_out.shape[2]
        background = Background(
            11, [w_qkv, w_out, w_down],
            [
                ((w_up.shape[2], width), BF16),
                (w_qkv.shape[1:], BF16),
                ((part, width), BF16),
                ((w_up.shape[2], width), BF16),
            ],
            [pltpu.SemaphoreType.DMA((4,))] * 2, fetch_rest_steps, quad=True, semaphores=72,
        )
        weights_0 = (qkv_0, out_0, (w_up, 0), b_up[0], None, norms[0:4], norms[8:12])
        middle, more, saved_first = layer_forward(resid, weights_0, start, tables, background)
        down_0, qkv_1, out_1, down_1 = more
        weights_0 = weights_0[:4] + (down_0,) + weights_0[5:]
    else:
        weights_0 = (qkv_0, out_0, (w_up, 0), b_up[0], down_0, norms[0:4], norms[8:12])
        middle, _, saved_first = layer_forward(resid, weights_0, start, tables)
    weights_1 = (qkv_1, out_1, (w_up, 1), b_up[1], down_1, norms[4:8], norms[12:16])
    weights = (weights_0, weights_1)
    result, _, saved_second = layer_forward(middle, weights_1, start, tables)
    if wide == 8:
        grad, grad_came, result_came, (totals_first, totals_second) = backward_wide(
            upstream, result, (saved_first, saved_second), weights, start, tables
        )
    else:
        result_came = route(result)
        grad, grads_second = layer_backward(upstream, saved_second, weights_1, start, tables)
        totals_second = reduce_grads(grads_second, at)
        grad, grads_first = layer_backward(grad, saved_first, weights_0, start, tables)
        totals_first = reduce_grads(grads_first, at)
        grad_came = route(grad)

    ends_out = jnp.where(
        first, jnp.concatenate([grad, grad_came]), jnp.concatenate([result_came, result])
    )
    totals = [jnp.stack([a.astype(F32), b.astype(F32)]) for a, b in zip(totals_first, totals_second)]
    return (ends_out,) + tuple(totals)


def solution(mesh):
    placed = (
        P(("wide", "narrow"), None),
        P(),
        P(None, None, "narrow"),
        P(None, None, "narrow"),
        P(None, None, "narrow"),
        P(None, "narrow"),
        P(None, None, "narrow"),
        P(None, None, "narrow"),
        P(None, None, "narrow"),
    )
    return jax.shard_map(
        on_device,
        mesh=mesh,
        in_specs=placed,
        out_specs=(P(("wide", "narrow"), None),) + placed[2:],
        check_vma=False,
    )
```

```python
import functools
import math

import jax
import jax.numpy as jnp
from jax import lax
from jax.experimental import pallas as pl
from jax.experimental.pallas import tpu as pltpu
from jax.sharding import PartitionSpec as P

HD = 64
EPSILON = 1e-05
MASKED = -1e30
SCALE = HD ** (-0.5)
F32 = jnp.float32
BF16 = jnp.bfloat16


def layer_norm(values, gain_row, shift_row):
    center = jnp.mean(values, axis=-1, keepdims=True)
    centred = values - center
    spread = jnp.mean(centred * centred, axis=-1, keepdims=True)
    return centred * lax.rsqrt(spread + EPSILON) * gain_row + shift_row


def rope_tables(offsets):
    halfway = HD // 2
    ladder = jnp.arange(halfway, dtype=F32) * (2.0 / HD)
    inverse = jnp.exp(-math.log(10000.0) * ladder)
    angles = offsets.astype(F32)[:, None] * inverse[None, :]
    cosine, sine = jnp.cos(angles), jnp.sin(angles)
    return (
        jnp.concatenate([cosine, cosine] * 2, axis=1),
        jnp.concatenate([-sine, sine] * 2, axis=1),
    )


def dot(left, right):
    return jnp.dot(left, right, preferred_element_type=F32)


def dot_t(left, right):
    return lax.dot_general(left, right, (((1,), (1,)), ((), ())), preferred_element_type=F32)


def t_dot(left, right):
    return lax.dot_general(left, right, (((0,), (0,)), ((), ())), preferred_element_type=F32)


MESH = pl.DeviceIdType.MESH


def layer_norm_back(values, grad, gain_row):
    center = jnp.mean(values, axis=-1, keepdims=True)
    centred = values - center
    scale = lax.rsqrt(jnp.mean(centred * centred, axis=-1, keepdims=True) + EPSILON)
    unit = centred * scale
    inner = grad * gain_row
    mean = jnp.mean(inner, axis=-1, keepdims=True)
    slope = jnp.mean(inner * unit, axis=-1, keepdims=True)
    grad_values = scale * (inner - mean - unit * slope)
    return (
        grad_values,
        jnp.sum(grad * unit, axis=0, keepdims=True),
        jnp.sum(grad, axis=0, keepdims=True),
    )


class Copy:
    def __init__(self, wire, source, target, peer, when):
        self.when, self.settled = when, False
        source, target = (item.ref if isinstance(item, Staged) else item for item in (source, target))
        self.pieces = (source, target, wire.sems.at[wire.used], wire.sems.at[wire.used + 1], peer)
        wire.used += 2
        wire.made.append(self)

    def remote(self, source=None):
        own, target, send_sem, recv_sem, peer = self.pieces
        return pltpu.make_async_remote_copy(
            src_ref=own if source is None else source,
            dst_ref=target,
            send_sem=send_sem,
            recv_sem=recv_sem,
            device_id=peer if isinstance(peer, dict) else {"narrow": peer},
            device_id_type=MESH,
        )

    def start(self):
        self.remote().start()

    def start_from(self, source):
        self.remote(source).start()

    def wait_recv(self):
        self.remote().wait_recv()

    def wait_send_early(self, others):
        self.when = others
        self.remote().wait_send()

    def settle(self):
        if not self.settled:
            self.settled = True
            self.wait_send()

    def wait_send(self):
        if self.when is None:
            self.remote().wait_send()
        else:

            @pl.when(self.when)
            def _():
                self.remote().wait_send()


class Wire:
    def __init__(self, sems):
        self.sems, self.used, self.made = sems, 0, []
        self.at = lax.axis_index("narrow")
        self.near = self.at + 1 - 2 * lax.rem(self.at, 2)
        self.far = lax.rem(self.at + 2, 4)
        self.diagonal = lax.rem(self.near + 2, 4)

    def barrier(self):
        barrier = pltpu.get_barrier_semaphore()
        for peer in (self.near, self.far):
            pl.semaphore_signal(barrier, inc=1, device_id={"narrow": peer}, device_id_type=MESH)
        pl.semaphore_wait(barrier, 2)

    def copy(self, source, target, peer, when=None):
        return Copy(self, source, target, peer, when)

    def send(self, source, target, peer):
        made = self.copy(source, target, peer)
        made.start()
        return made

    def move(self, source, target):
        source = source.ref if isinstance(source, Staged) else source
        copy = pltpu.make_async_copy(source, target, self.sems.at[self.used])
        self.used += 1
        copy.start()
        copy.wait()

    def finish(self):
        for made in self.made:
            made.settle()


def block_rows(block, size, part=0, parts=1):
    step = size // parts
    return pl.ds(pl.multiple_of(block * size + part * step, step), step)


class Gather:
    def __init__(self, wire, full, size):
        self.wire, self.full, self.size = wire, full, size
        self.to_near, self.to_far, self.relayed = [], [], []

    def rows(self, block, part):
        return self.full.at[block_rows(block, self.size, part, 2)]

    def push(self, part):
        own = self.rows(self.wire.at, part)
        self.to_near.append(self.wire.send(own, own, self.wire.near))
        self.to_far.append(self.wire.send(own, own, self.wire.far))

    def wait_near(self):
        for made in self.to_near:
            made.wait_recv()

    def relay(self, part):
        self.to_far[part].wait_recv()
        held = self.rows(self.wire.far, part)
        self.relayed.append(self.wire.send(held, held, self.wire.near))

    def wait_diagonal(self, part):
        self.relayed[part].wait_recv()


class Scatter:
    def __init__(self, wire, held, own, parts):
        self.held, self.own = held, own
        self.size = own.shape[0]
        step = self.size // parts
        self.cuts = [pl.ds(i * step, step) for i in range(parts)]

        def copies(out, into, peer, cuts):
            return [wire.copy(held.at[out, cut], held.at[into, cut], peer) for cut in cuts]

        self.side = copies(0, 1, wire.near, self.cuts)
        self.cross = copies(2, 3, wire.far, self.cuts)
        self.home = copies(4, 5, wire.near, [pl.ds(0, self.size)])[0]

    def put_diagonal(self, partial, part):
        self.held[0, self.cuts[part]] = partial.astype(BF16)
        self.side[part].start()

    def put_far(self, partial, part):
        cut = self.cuts[part]
        self.side[part].wait_recv()
        self.held[2, cut] = (partial + self.held[1, cut].astype(F32)).astype(BF16)
        self.cross[part].start()

    def put_near(self, partial):
        self.held[4] = partial.astype(BF16)
        self.home.start()

    def total(self):
        self.home.wait_recv()
        for made in self.cross:
            made.wait_recv()
        return self.own[...] + self.held[5].astype(F32) + self.held[3].astype(F32)


def turn(field, cosine, sine):
    lane = lax.broadcasted_iota(jnp.int32, cosine.shape, 1)
    first = lax.rem(lane, HD) < HD // 2
    turned = []
    for at in range(0, field.shape[1], 128):
        part = field[:, at : at + 128]
        swapped = jnp.where(
            first, pltpu.roll(part, 128 - HD // 2, 1), pltpu.roll(part, HD // 2, 1)
        )
        turned.append(part * cosine + swapped * sine)
    return jnp.concatenate(turned, axis=1)


def vmem(count):
    return [pl.BlockSpec(memory_space=pltpu.VMEM)] * count


def shaped(*entries):
    return [jax.ShapeDtypeStruct(shape, kind) for shape, kind in entries]


class Poll:
    def __init__(self, steps):
        self.steps = steps

    def __call__(self, times=1):
        for _ in range(times):
            for step in list(self.steps):
                if next(step, "end") == "end":
                    self.steps.remove(step)

    def enter(self):
        pass

    def leave(self):
        pass

    def before(self, what):
        pass

    def graded(self, name):
        pass


SMALL = 2**16


class Staged:
    def __init__(self, ref, copy, is_result):
        self.ref, self.copy, self.is_result = ref, copy, is_result
        self.begun = self.ended = False
        self.shape, self.dtype = ref.shape, ref.dtype

    def begin(self):
        self.begun = True
        self.copy.start()

    def wait(self):
        if not self.ended:
            self.ended = True
            self.copy.wait()

    def check(self):
        assert self.is_result or self.ended

    @property
    def at(self):
        self.check()
        return self.ref.at

    def __getitem__(self, index):
        self.check()
        return self.ref[index]

    def __setitem__(self, index, value):
        self.ref[index] = value


class Pending(Staged):
    def __init__(self, ref, action):
        super().__init__(ref, None, False)
        self.action = action

    def wait(self):
        if not self.ended:
            self.ended = True
            self.action()

    def wait_part(self, part):
        self.ended = True
        self.action(part)


def ready(*refs):
    for ref in refs:
        if isinstance(ref, Staged):
            ref.wait()


def ready_part(ref, part):
    if isinstance(ref, Pending):
        ref.wait_part(part)
    else:
        ready(ref)


def done(*refs):
    for ref in refs:
        if isinstance(ref, Staged):
            ref.begin()


class Background:
    def __init__(
        self, number, operands=(), outs=(), scratch=(), steps=None, staged=0, quad=False,
        across=False, semaphores=24,
    ):
        self.semaphores = semaphores
        self.staged = staged
        self.number, self.operands, self.outs = number, list(operands), list(outs)
        self.scratch, self.steps, self.quad, self.across = list(scratch), steps, quad, across


def is_large(shape, kind):
    return math.prod(shape) * jnp.dtype(kind).itemsize > SMALL


def call_with(body, background, outs, scratch, flops, *operands):
    placed = len(operands)
    everything = list(operands) + background.operands
    arrays = [item[0] if isinstance(item, tuple) else item for item in everything]
    shapes = [
        (array.shape[1:] if isinstance(item, tuple) else array.shape, array.dtype)
        for array, item in zip(arrays, everything)
    ]
    results = list(outs) + background.outs
    copies_in = [
        is_large(*shape) and not (background.quad and at >= placed)
        for at, shape in enumerate(shapes)
    ]
    raw_in = [background.quad and at >= placed for at in range(len(shapes))]
    raw_out = [at >= len(outs) + background.staged for at in range(len(results))]
    copies_out = [is_large(*shape) and not raw for shape, raw in zip(results, raw_out)]
    staged = [shape for shape, copied in zip(shapes + results, copies_in + copies_out) if copied]

    def kernel(*refs):
        refs = list(refs)

        def take(count):
            taken = refs[:count]
            del refs[:count]
            return taken

        sources, targets = take(len(shapes)), take(len(results))
        body_scratch, more_scratch = take(len(scratch)), take(len(background.scratch))
        held = take(len(staged))
        sems, local = take(2)
        wire = Wire(sems)
        number = 0
        for at, item in enumerate(everything):
            if copies_in[at]:
                source = sources[at].at[item[1]] if isinstance(item, tuple) else sources[at]
                ref = held[number]
                copy = pltpu.make_async_copy(source, ref, local.at[number])
                sources[at] = Staged(ref, copy, False)
                sources[at].begin()
                number += 1
        for at in range(len(results)):
            if copies_out[at]:
                ref = held[number]
                copy = pltpu.make_async_copy(ref, targets[at], local.at[number])
                targets[at] = Staged(ref, copy, True)
                number += 1
        steps = []
        if background.steps is None:
            wire.barrier()
        else:
            if background.quad:
                place = Quad()
                quad_barrier(wire, place, *([place.across] if background.across else []))
            else:
                place = Line()
                wide_barrier(wire, place, *([Quad().across] if background.across else []))
            steps = [
                background.steps(
                    wire, place, sources[placed:], targets[len(outs) :], more_scratch
                )
            ]

        poll = Poll(steps)
        body(wire, poll, *sources[:placed], *targets[: len(outs)], *body_scratch)
        while steps:
            poll()
        for ref in sources:
            ready(ref)
        for ref in targets:
            if isinstance(ref, Staged) and not ref.begun:
                ref.begin()
        wire.finish()
        for ref in targets:
            ready(ref)

    kernel.__name__ = body.__name__ if background.steps is None else body.__name__ + "_wide"

    def spec(apart):
        return pl.BlockSpec(memory_space=pl.ANY if apart else pltpu.VMEM)

    found = pl.pallas_call(
        kernel,
        in_specs=[spec(raw or copied) for raw, copied in zip(raw_in, copies_in)],
        out_specs=[spec(raw or copied) for raw, copied in zip(raw_out, copies_out)],
        out_shape=shaped(*results),
        scratch_shapes=list(scratch)
        + background.scratch
        + [pltpu.VMEM(*shape) for shape in staged]
        + [pltpu.SemaphoreType.DMA((background.semaphores,))]
        + [pltpu.SemaphoreType.DMA((max(len(staged), 1),))],
        compiler_params=pltpu.CompilerParams(
            collective_id=background.number, has_side_effects=True, vmem_limit_bytes=56 * 2**20
        ),
        cost_estimate=pl.CostEstimate(flops=flops, bytes_accessed=2**24, transcendentals=0),
        name=kernel.__name__,
    )(*arrays)
    return found[: len(outs)], found[len(outs) :]


def attend_half_body(
    wire, poll,
    x_ref, gain_ref, shift_ref, cos_ref, sin_ref, start_ref, w_qkv_ref, w_out_ref,
    a_ref, q_ref, k_ref, v_ref, o_ref, lse_ref, z_ref, h_ref, c_ref,
    held, own,
):
    size = x_ref.shape[0]
    gather = Gather(wire, a_ref, size)
    poll.enter()
    for part in range(2):
        rows = pl.ds(part * (size // 2), size // 2)
        ready_part(x_ref, part)
        normed = layer_norm(x_ref[rows].astype(F32), gain_ref[0:1], shift_ref[0:1])
        a_ref[block_rows(wire.at, size, part, 2)] = normed.astype(BF16)
        gather.push(part)
        poll()
    width = q_ref.shape[1]

    def project(block):
        rows = block_rows(block, size)
        projected = dot(a_ref[rows], w_qkv_ref[...])
        cosine, sine = cos_ref[rows], sin_ref[rows]
        q_ref[rows] = turn(projected[:, :width], cosine, sine).astype(BF16)
        k_ref[rows] = turn(projected[:, width : 2 * width], cosine, sine).astype(BF16)
        v_ref[rows] = projected[:, 2 * width :].astype(BF16)

    ready(w_qkv_ref, cos_ref, sin_ref)
    project(wire.at)
    gather.wait_near()
    project(wire.near)
    gather.relay(0)
    gather.relay(1)
    project(wire.far)
    gather.wait_diagonal(0)
    gather.wait_diagonal(1)
    project(wire.diagonal)

    done(a_ref, q_ref, k_ref, v_ref)
    poll()
    ready(start_ref, w_out_ref)
    scatter = Scatter(wire, held, own, 1)
    for block in (3, 1, 2, 0):
        rows = slice(block * size, (block + 1) * size)
        reach = (block + 1) * size
        key = lax.broadcasted_iota(jnp.int32, (size, reach), 1)
        query = lax.broadcasted_iota(jnp.int32, (size, reach), 0) + block * size
        allowed = (key >= start_ref[rows, :]) & (key <= query)
        mixed, logs = [], jnp.zeros((size, 128), F32)
        lane = lax.broadcasted_iota(jnp.int32, (size, 128), 1)
        for head in range(width // HD):
            lanes = slice(head * HD, (head + 1) * HD)
            scores = dot_t(q_ref[rows, lanes] * SCALE, k_ref[:reach, lanes])
            scores = jnp.where(allowed, scores, MASKED)
            summit = jnp.max(scores, axis=1, keepdims=True)
            weights = jnp.exp(scores - summit)
            total = jnp.sum(weights, axis=1, keepdims=True)
            chances = (weights * (1.0 / total)).astype(BF16)
            mixed.append(dot(chances, v_ref[:reach, lanes]))
            logs = jnp.where(lane == head, summit + jnp.log(total), logs)
        o_ref[rows, :] = jnp.concatenate(mixed, axis=1).astype(BF16)
        lse_ref[:, rows] = logs.T[: lse_ref.shape[0]]
        partial = dot(o_ref[rows, :], w_out_ref[...])

        if block == 2:
            poll()

        @pl.when(wire.diagonal == block)
        def _():
            scatter.put_diagonal(partial, 0)

        @pl.when(wire.far == block)
        def _():
            scatter.put_far(partial, 0)

        @pl.when(wire.near == block)
        def _():
            scatter.put_near(partial)

        @pl.when(wire.at == block)
        def _():
            own[...] = partial

    done(o_ref, lse_ref)
    poll()
    branch = scatter.total()
    z_ref[...] = branch
    middle = x_ref[...].astype(F32) + layer_norm(branch, gain_ref[1:2], shift_ref[1:2])
    h_ref[...] = middle
    c_ref[...] = layer_norm(middle, gain_ref[2:3], shift_ref[2:3]).astype(BF16)
    done(z_ref, h_ref)
    poll.leave()


def attend_half(background, resid, gains, shifts, cosine, sine, start, w_qkv, w_out):
    size, width = resid.shape
    length, part = cosine.shape[0], w_out.shape[0]
    return call_with(
        attend_half_body,
        background,
        [((length, width), BF16)]
        + [((length, part), BF16)] * 4
        + [((8, length), F32), ((size, width), F32), ((size, width), F32), ((size, width), BF16)],
        [pltpu.VMEM((6, size, width), BF16), pltpu.VMEM((size, width), F32)],
        8 * length * width * part + 4 * length * length * part,
        resid, gains, shifts, cosine, sine, start, w_qkv, w_out,
    )


def feed_half_body(
    wire, poll,
    c_ref, h_ref, gain_ref, shift_ref, w_up_ref, b_up_ref, w_down_ref,
    inner_ref, e_ref, d_ref, w_ref, y_ref,
    held, own,
):
    size = c_ref.shape[0]
    half = size // 2
    ready(c_ref)
    gather = Gather(wire, inner_ref, size)
    poll.enter()
    for part in range(2):
        inner_ref[block_rows(wire.at, size, part, 2)] = c_ref[pl.ds(part * half, half)]
        gather.push(part)
    poll()
    scatter = Scatter(wire, held, own, 2)

    def feed(cuts):
        inner = jnp.concatenate([inner_ref[cut] for cut in cuts])
        hidden = dot(inner, w_up_ref[...]) + b_up_ref[...]
        below = 0.5 + 0.5 * lax.erf(hidden * (0.5**0.5))
        density = jnp.exp(-0.5 * hidden * hidden) * ((2.0 * math.pi) ** -0.5)
        active = (hidden * below).astype(BF16)
        slope = (below + hidden * density).astype(BF16)
        for at, cut in enumerate(cuts):
            step = inner.shape[0] // len(cuts)
            e_ref[cut] = active[at * step : (at + 1) * step]
            d_ref[cut] = slope[at * step : (at + 1) * step]
        return dot(active, w_down_ref[...])

    ready(w_up_ref, b_up_ref, w_down_ref)
    own[...] = feed([block_rows(wire.at, size)])
    gather.wait_near()
    scatter.put_near(feed([block_rows(wire.near, size)]))
    for part in range(2):
        gather.relay(part)
        gather.wait_diagonal(part)
        partial = feed(
            [block_rows(wire.diagonal, size, part, 2), block_rows(wire.far, size, part, 2)]
        )
        scatter.put_diagonal(partial[:half], part)
        scatter.put_far(partial[half:], part)
    done(inner_ref, e_ref, d_ref)
    ready(h_ref)
    second = scatter.total()
    w_ref[...] = second
    result = h_ref[...] + layer_norm(second, gain_ref[3:4], shift_ref[3:4])
    y_ref[...] = result.astype(BF16)
    done(w_ref, y_ref)
    poll.leave()


def feed_half(number, inner, middle, gains, shifts, w_up, b_up, w_down):
    size, width = inner.shape
    length, hidden = 4 * size, b_up.shape[1]
    return call_with(
        feed_half_body,
        Background(number),
        [((length, width), BF16)]
        + [((length, hidden), BF16)] * 2
        + [((size, width), F32), ((size, width), BF16)],
        [pltpu.VMEM((6, size, width), BF16), pltpu.VMEM((size, width), F32)],
        4 * length * width * hidden,
        inner, middle, gains, shifts, w_up, b_up, w_down,
    )[0]


def feed_back_body(
    wire, poll,
    g_ref, w_ref, h_ref, z_ref, gain_ref, inner_ref, e_ref, d_ref, w_up_ref, w_down_ref,
    grad_down_ref, grad_up_ref, grad_b_ref, norms_ref, dh_ref, dz_ref,
    second, hidden, held, own,
):
    size = g_ref.shape[0]
    half = size // 2
    ready(g_ref, w_ref)
    gather = Gather(wire, second, size)
    norms = [jnp.zeros((1, g_ref.shape[1]), F32)] * 2
    for part in range(2):
        rows = pl.ds(part * half, half)
        grad, gain, shift = layer_norm_back(w_ref[rows], g_ref[rows].astype(F32), gain_ref[3:4])
        if part == 0:
            poll.enter()
        second[block_rows(wire.at, size, part, 2)] = grad.astype(BF16)
        gather.push(part)
        norms = [norms[0] + gain, norms[1] + shift]
    norms_ref[3:4] = norms[0]
    norms_ref[7:8] = norms[1]
    norms_ref[0:1] = jnp.zeros_like(norms[0])
    norms_ref[4:5] = jnp.zeros_like(norms[0])
    scatter = Scatter(wire, held, own, 2)
    poll()

    def feed(cuts, first=False):
        grad = jnp.concatenate([second[cut] for cut in cuts])
        slope = jnp.concatenate([d_ref[cut] for cut in cuts]).astype(F32)
        grad = (slope * dot_t(grad, w_down_ref[...])).astype(BF16)
        for at, cut in enumerate(cuts):
            step = grad.shape[0] // len(cuts)
            hidden[cut] = grad[at * step : (at + 1) * step]
        bias = jnp.sum(grad.astype(F32), axis=0, keepdims=True)
        grad_b_ref[...] = bias if first else grad_b_ref[...] + bias
        return dot_t(grad, w_up_ref[...])

    ready(d_ref, w_down_ref, w_up_ref)
    own[...] = feed([block_rows(wire.at, size)], True)
    poll()
    gather.wait_near()
    scatter.put_near(feed([block_rows(wire.near, size)]))
    poll()
    for part in range(2):
        poll(2)
        gather.relay(part)
        gather.wait_diagonal(part)
        partial = feed(
            [block_rows(wire.diagonal, size, part, 2), block_rows(wire.far, size, part, 2)]
        )
        scatter.put_diagonal(partial[:half], part)
        scatter.put_far(partial[half:], part)
        poll()
    poll.before("feed")
    ready(e_ref, inner_ref)
    for at in range(0, inner_ref.shape[1], 256):
        cut = slice(at, at + 256)
        grad_up_ref[cut, :] = t_dot(inner_ref[:, cut], hidden[...]).astype(BF16)
        poll()
    done(grad_up_ref)
    poll.graded("up")
    for at in range(0, e_ref.shape[1], 256):
        cut = slice(at, at + 256)
        grad_down_ref[cut, :] = t_dot(e_ref[:, cut], second[...]).astype(BF16)
        poll()
    done(grad_down_ref)
    poll.graded("down")
    poll(3)
    ready(h_ref, z_ref)
    grad, gain, shift = layer_norm_back(h_ref[...], scatter.total(), gain_ref[2:3])
    norms_ref[2:3] = gain
    norms_ref[6:7] = shift
    grad = g_ref[...].astype(F32) + grad
    dh_ref[...] = grad
    grad, gain, shift = layer_norm_back(z_ref[...], grad, gain_ref[1:2])
    norms_ref[1:2] = gain
    norms_ref[5:6] = shift
    dz_ref[...] = grad.astype(BF16)
    poll.leave()


def feed_back(background, grad, second, middle, branch, gains, inner, active, slope, w_up, w_down):
    size, width = grad.shape
    length, hidden = 4 * size, active.shape[1]
    return call_with(
        feed_back_body,
        background,
        [
            ((hidden, width), BF16),
            ((width, hidden), BF16),
            ((1, hidden), F32),
            ((8, width), F32),
            ((size, width), F32),
            ((size, width), BF16),
        ],
        [
            pltpu.VMEM((length, width), BF16),
            pltpu.VMEM((length, hidden), BF16),
            pltpu.VMEM((6, size, width), BF16),
            pltpu.VMEM((size, width), F32),
        ],
        8 * length * width * hidden,
        grad, second, middle, branch, gains, inner, active, slope, w_up, w_down,
    )


def attend_back_body(
    wire, poll,
    dz_ref, dh_ref, x_ref, gain_ref, a_ref, q_ref, k_ref, v_ref, o_ref, lse_ref, start_ref,
    cos_ref, sin_ref, w_qkv_ref, w_out_ref,
    grad_qkv_ref, grad_out_ref, norms_ref, dx_ref,
    branch, mixture, projected, dk, dv, held, own,
):
    size = dz_ref.shape[0]
    length, width = q_ref.shape
    half = size // 2
    ready(dz_ref)
    gather = Gather(wire, branch, size)
    poll.enter()
    for part in range(2):
        branch[block_rows(wire.at, size, part, 2)] = dz_ref[pl.ds(part * half, half)]
        gather.push(part)

    def unmix(block):
        rows = block_rows(block, size)
        mixture[rows] = dot_t(branch[rows], w_out_ref[...]).astype(BF16)

    dk[...] = jnp.zeros_like(dk)
    dv[...] = jnp.zeros_like(dv)
    poll()
    ready(w_out_ref)
    unmix(wire.at)
    gather.wait_near()
    unmix(wire.near)
    poll()
    poll(2)
    gather.relay(0)
    poll(2)
    gather.relay(1)
    unmix(wire.far)
    gather.wait_diagonal(0)
    gather.wait_diagonal(1)
    unmix(wire.diagonal)
    ready(o_ref, q_ref, k_ref, v_ref, lse_ref, start_ref, cos_ref, sin_ref, w_qkv_ref)
    poll.before("attend")
    grad_out_ref[...] = t_dot(o_ref[...], branch[...]).astype(BF16)
    done(grad_out_ref)
    poll()

    pick_head = (
        lax.broadcasted_iota(jnp.int32, (8, width), 1) // HD
        == lax.broadcasted_iota(jnp.int32, (8, width), 0)
    ).astype(F32)
    for block in range(length // size):
        rows = slice(block * size, (block + 1) * size)
        reach = (block + 1) * size
        key = lax.broadcasted_iota(jnp.int32, (reach, size), 0)
        query = lax.broadcasted_iota(jnp.int32, (reach, size), 1) + block * size
        allowed = (key >= start_ref[:, rows]) & (key <= query)
        inner = lax.dot_general(
            pick_head,
            mixture[rows].astype(F32) * o_ref[rows].astype(F32),
            (((1,), (1,)), ((), ())),
            precision=lax.Precision.HIGHEST,
            preferred_element_type=F32,
        )
        dqs, dks, dvs = [], [], []
        for head in range(width // HD):
            lanes = slice(head * HD, (head + 1) * HD)
            k_head, g_head = k_ref[:reach, lanes], mixture[rows, lanes]
            q_head = q_ref[rows, lanes] * SCALE
            scores = dot_t(k_head, q_head) - lse_ref[head : head + 1, rows]
            chances = jnp.exp(jnp.where(allowed, scores, MASKED))
            grad_prob = dot_t(v_ref[:reach, lanes], g_head)
            grad_score = (chances * (grad_prob - inner[head : head + 1])).astype(BF16)
            dvs.append(dot(chances.astype(BF16), g_head))
            dks.append(dot(grad_score, q_head))
            dqs.append(t_dot(grad_score, k_head) * SCALE)
            if block > 0 and head % 2 == 1:
                poll()
        dq = jnp.concatenate(dqs, axis=1)
        projected[rows, :width] = turn(dq, cos_ref[rows], -sin_ref[rows]).astype(BF16)
        dk[:reach, :] += jnp.concatenate(dks, axis=1)
        dv[:reach, :] += jnp.concatenate(dvs, axis=1)
    for block in range(length // size):
        rows = slice(block * size, (block + 1) * size)
        turned = turn(dk[rows], cos_ref[rows], -sin_ref[rows])
        projected[rows, width : 2 * width] = turned.astype(BF16)
        projected[rows, 2 * width :] = dv[rows].astype(BF16)

    scatter = Scatter(wire, held, own, 2)

    def unproject(cut):
        return dot_t(projected[cut], w_qkv_ref[...])

    partial = unproject(block_rows(wire.diagonal, size))
    scatter.put_diagonal(partial[:half], 0)
    scatter.put_diagonal(partial[half:], 1)
    poll()
    partial = unproject(block_rows(wire.far, size))
    scatter.put_far(partial[:half], 0)
    scatter.put_far(partial[half:], 1)
    poll()
    scatter.put_near(unproject(block_rows(wire.near, size)))
    own[...] = unproject(block_rows(wire.at, size))
    ready(a_ref)
    for at in range(0, a_ref.shape[1], 256):
        cut = slice(at, at + 256)
        grad_qkv_ref[cut, :] = t_dot(a_ref[:, cut], projected[...]).astype(BF16)
        poll()
    done(grad_qkv_ref)
    poll.graded("qkv")
    poll(3)
    ready(x_ref, dh_ref)
    grad, gain, shift = layer_norm_back(x_ref[...].astype(F32), scatter.total(), gain_ref[0:1])
    norms_ref[...] = jnp.zeros_like(norms_ref)
    norms_ref[0:1] = gain
    norms_ref[4:5] = shift
    dx_ref[...] = (dh_ref[...] + grad).astype(BF16)
    poll.leave()


def attend_back(
    background,
    grad_branch, grad_middle, resid, gains, normed, query, keys, values, mixture, logs, start,
    cosine, sine, w_qkv, w_out,
):
    size, width = resid.shape
    length, part = query.shape
    return call_with(
        attend_back_body,
        background,
        [
            ((width, 3 * part), BF16),
            ((part, width), BF16),
            ((8, width), F32),
            ((size, width), BF16),
        ],
        [
            pltpu.VMEM((length, width), BF16),
            pltpu.VMEM((length, part), BF16),
            pltpu.VMEM((length, 3 * part), BF16),
            pltpu.VMEM((length, part), F32),
            pltpu.VMEM((length, part), F32),
            pltpu.VMEM((6, size, width), BF16),
            pltpu.VMEM((size, width), F32),
        ],
        16 * length * width * part + 10 * length * length * part,
        grad_branch, grad_middle, resid, gains, normed, query, keys, values, mixture, logs,
        start, cosine, sine, w_qkv, w_out,
    )


CHUNK = 64
LATE = 2


class Line:
    def __init__(self):
        at = lax.axis_index("wide")
        self.pair = lax.rem(at, 2)
        self.turn = at // 2
        self.upper = self.turn // 3
        self.up = {"wide": lax.rem(self.turn + 1, 4) * 2 + self.pair}
        self.down = {"wide": lax.rem(self.turn + 3, 4) * 2 + self.pair}
        self.side = {"wide": at + 1 - 2 * self.pair}
        self.bottom, self.top = self.turn == 0, self.turn == 3
        self.at_end = self.upper * 3 == self.turn
        self.inside = jnp.logical_not(self.at_end)
        not_bottom, not_top = self.turn > 0, self.turn < 3
        self.ways = (
            (self.up, self.bottom, self.top, not_bottom, not_top),
            (self.down, self.top, self.bottom, not_top, not_bottom),
        )

    def steps(self, chunks):
        for at in range(len(chunks) + 3 * LATE):
            for turn in range(4):

                @pl.when(self.turn == turn)
                def _():
                    for way, hops in sorted(((0, turn), (1, 3 - turn)), key=lambda item: item[1]):
                        chunk = at - hops * LATE
                        if not 0 <= chunk < len(chunks):
                            continue
                        if hops == 0:
                            if chunk >= 2:
                                chunks[chunk - 2](way, "sent")
                            chunks[chunk](way, "first")
                        else:
                            chunks[chunk](way, "last" if hops == 3 else "inner")

            yield


def span(start, size):
    return pl.ds(pl.multiple_of(start, 16), size)


class Fold:
    def __init__(self, wire, line, ref, by_side, into, across, final):
        self.wire, self.line, self.ref, self.by_side = wire, line, ref, by_side
        self.into, self.across, self.final = into, across, final
        rows = ref.shape[0]
        self.length = rows // 4 if by_side else rows // 2
        self.base = line.pair * (rows // 2) if by_side else 0
        self.count = self.length // CHUNK
        self.copies, self.sides = [], []
        for way, (peer, _, _, _, inner) in enumerate(line.ways):
            cuts = [into.at[way, pl.ds(c * CHUNK, CHUNK)] for c in range(self.count)]
            self.copies.append([wire.copy(cut, cut, peer, inner) for cut in cuts])

    @staticmethod
    def scratch(rows, columns, by_side):
        return [
            pltpu.VMEM((2, rows // 4 if by_side else rows // 2, columns), BF16),
            pltpu.VMEM((rows // 2 if by_side else rows // 4, columns), BF16),
        ]

    def place(self, way, chunk):
        return (self.length if way == 0 else 0) + chunk * CHUNK

    def start(self):
        line = self.line
        if self.by_side:
            away = (1 - line.pair) * (self.ref.shape[0] // 2)
            for chunk in range(self.count):
                pair = []
                for way in (0, 1):
                    place = self.place(way, chunk)
                    pair.append(
                        self.wire.send(
                            self.ref.at[span(away + place, CHUNK)],
                            self.across.at[pl.ds(place, CHUNK)],
                            line.side,
                        )
                    )
                self.sides.append(pair)

    def step(self, chunk, way, role):
        place = self.place(way, chunk)
        cut = pl.ds(chunk * CHUNK, CHUNK)
        made = self.copies[way][chunk]
        if role == "sent":
            made.wait_send_early(self.line.inside)
            return
        if self.by_side:
            self.sides[chunk][way].wait_recv()

        def own():
            total = self.ref[span(self.base + place, CHUNK)].astype(F32)
            if self.by_side:
                total = total + self.across[pl.ds(place, CHUNK)].astype(F32)
            return total

        if role == "first":
            if self.by_side:
                self.into[way, cut] = own().astype(BF16)
                made.start()
            else:
                made.start_from(self.ref.at[pl.ds(place, CHUNK)])
            return
        made.wait_recv()
        self.into[way, cut] = (own() + self.into[way, cut].astype(F32)).astype(BF16)
        if role == "inner":
            made.start()

    def chunks(self):
        return [functools.partial(self.step, chunk) for chunk in range(self.count)]

    def start_side(self):
        line = self.line
        half = self.length // 2
        source = self.into.at[1 - line.upper, span((1 - line.pair) * half, half)]
        self.side = self.wire.copy(source, self.across, line.side, line.at_end)

        @pl.when(line.at_end)
        def _():
            self.side.start()

    def end(self):
        line = self.line
        size = self.final.shape[0]

        @pl.when(line.at_end)
        def _():
            if not self.by_side:
                self.side.wait_recv()
            for at in range(0, size, CHUNK):
                if self.by_side:
                    self.final[pl.ds(at, CHUNK)] = self.into[1 - line.upper, pl.ds(at, CHUNK)]
                else:
                    own = self.into[1 - line.upper, span(line.pair * size + at, CHUNK)]
                    total = own.astype(F32) + self.across[pl.ds(at, CHUNK)].astype(F32)
                    self.final[pl.ds(at, CHUNK)] = total.astype(BF16)

        self.settle()
        if not self.by_side:
            self.side.settle()

    def settle(self):
        for made in sum(self.copies + self.sides, []):
            made.settle()


class Spread:
    def __init__(self, wire, line, view, rows, by_side):
        self.wire, self.line, self.view, self.by_side = wire, line, view, by_side
        pair, upper = line.pair, line.upper
        self.quarter = rows // 4
        if by_side:
            self.length, self.base = rows // 4, pair * (rows // 2)
            self.mine = self.base + upper * self.quarter
        else:
            self.length, self.base = rows // 2, 0
            self.mine = upper * (rows // 2) + pair * self.quarter
        self.count = self.length // CHUNK
        self.copies = []
        for way, (peer, _, _, _, inner) in enumerate(line.ways):
            cuts = [self.chunk(way, c) for c in range(self.count)]
            self.copies.append([wire.copy(cut, cut, peer, inner) for cut in cuts])
        self.sides = []
        if not by_side:
            self.side = wire.copy(self.own(), self.own(), line.side, line.at_end)

    def own(self):
        return self.view(span(self.mine, self.quarter))

    def chunk(self, way, chunk):
        start = self.base + (0 if way == 0 else self.length) + chunk * CHUNK
        return self.view(span(start, CHUNK))

    def start(self):
        if not self.by_side:

            @pl.when(self.line.at_end)
            def _():
                self.side.start()

    def step(self, chunk, way, role):
        made = self.copies[way][chunk]
        if role == "sent":
            made.wait_send_early(self.line.inside)
            return
        if role == "first":
            if not self.by_side and chunk == 0:
                self.side.wait_recv()
            made.start()
        else:
            made.wait_recv()
            if role == "inner":
                made.start()
        if self.by_side:
            self.sides[chunk][way].start()

    def chunks(self):
        if self.by_side:
            self.sides = []
            for chunk in range(self.count):
                cuts = [self.chunk(way, chunk) for way in (0, 1)]
                self.sides.append([self.wire.copy(cut, cut, self.line.side) for cut in cuts])
        return [functools.partial(self.step, chunk) for chunk in range(self.count)]

    def end(self):
        for pair in self.sides:
            for made in pair:
                made.wait_recv()


class Sequence:
    def __init__(self, line):
        self.line, self.chunks, self.actions = line, [], {}

    def add(self, *lists):
        total = max(len(chunks) for chunks in lists)
        placed = [
            ((at + 0.5) * total / len(chunks), which, chunk)
            for which, chunks in enumerate(lists)
            for at, chunk in enumerate(chunks)
        ]
        self.chunks += [chunk for _, _, chunk in sorted(placed, key=lambda item: item[:2])]
        return self

    def before_next(self, *actions):
        self.actions.setdefault(len(self.chunks) - 1, []).extend(actions)

    def after(self, chunk, *actions):
        self.actions.setdefault(self.chunks.index(chunk) + 3 * LATE, []).extend(actions)

    def steps(self):
        for action in self.actions.get(-1, []):
            action()
        for at, _ in enumerate(self.line.steps(self.chunks)):
            for action in self.actions.get(at, []):
                action()
            yield


def small_steps(wire, line, norms_ref, bias_ref, narrow_in, sums, side_in, slots, total_ref):
    part = total_ref.shape[1]
    made = []

    def columns(device):
        return pl.ds(pl.multiple_of(device * part, part), part)

    for peer in (wire.near, wire.far, wire.diagonal):
        made.append(
            wire.send(norms_ref.at[:, columns(peer)], narrow_in.at[wire.at], {"narrow": peer})
        )
    narrow_in[wire.at] = norms_ref[:, columns(wire.at)]
    yield
    for copy in made:
        copy.wait_recv()
    total = narrow_in[0] + narrow_in[1] + narrow_in[2] + narrow_in[3]
    lines = [bias_ref[:, at * part : (at + 1) * part] for at in range(4)]
    sums[...] = jnp.concatenate([total] + lines + [jnp.zeros((4, part), F32)], axis=0)
    side = wire.send(sums, side_in, line.side)
    yield
    side.wait_recv()
    slots[line.turn] = sums[...] + side_in[...]
    for step in range(3):
        sends = []
        for way, peer in enumerate((line.up, line.down)):
            place = line.turn if way == 0 else 3 - line.turn
            goes = (place >= step) & (place < 3)
            comes = place > step
            slot = slots.at[lax.rem(line.turn + (4 - step if way == 0 else step), 4)]
            copy = wire.copy(slot, slot, peer, goes)
            sends.append((copy, goes, comes))

            @pl.when(goes)
            def _():
                copy.start()

        yield
        for copy, goes, comes in sends:

            @pl.when(comes)
            def _():
                copy.wait_recv()

    total_ref[...] = slots[0] + slots[1] + slots[2] + slots[3]


def home(wire, line, down, out, qkv, full_down, full_out, full_qkv):
    part = (full_out if full_down is None else full_down).shape[2]
    made = []
    at = wire.at

    def columns(device):
        return pl.ds(pl.multiple_of(device * part, part), part)

    for final, full, by_side in ((down, full_down, True), (out, full_out, False)):
        if final is None:
            continue
        quarter = final.shape[0]
        if by_side:
            mine = line.pair * (2 * quarter) + line.upper * quarter
        else:
            mine = line.upper * (2 * quarter) + line.pair * quarter
        slot = full.at[at, span(mine, quarter)]
        for peer in (wire.diagonal, wire.far, wire.near):
            made.append(
                wire.copy(final.at[:, columns(peer)], slot, {"narrow": peer}, line.at_end)
            )

        @pl.when(line.at_end)
        def _():
            wire.move(final.at[:, columns(at)], slot)

    if qkv is not None:
        quarter = qkv.shape[0]
        rows = span(line.pair * (2 * quarter) + line.upper * quarter, quarter)
        odd, upper = lax.rem(at, 2), at // 2
        far_slot = columns(2 - 2 * odd)
        made.append(
            wire.copy(
                qkv.at[:, columns(2 - 2 * upper)], full_qkv.at[rows, far_slot],
                {"narrow": wire.far}, line.at_end,
            )
        )
        made.append(
            wire.copy(
                qkv.at[:, columns(1 - odd + upper)], full_qkv.at[rows, columns(1)],
                {"narrow": wire.near}, line.at_end,
            )
        )

        @pl.when(line.at_end)
        def _():
            wire.move(qkv.at[:, columns((at + 1) // 2)], full_qkv.at[rows, columns(2 * odd)])

    @pl.when(line.at_end)
    def _():
        for copy in made:
            copy.start()

    def wait():
        @pl.when(line.at_end)
        def _():
            for copy in made:
                copy.wait_recv()

    return wait


def wide_barrier(wire, line, *others):
    barrier = pltpu.get_barrier_semaphore()

    def greet(peer):
        pl.semaphore_signal(barrier, inc=1, device_id=peer, device_id_type=MESH)

    for peer in (line.side,) + others:
        greet(peer)
    for peer in (wire.near, wire.far, wire.diagonal):
        greet({"narrow": peer})

    @pl.when(line.turn < 3)
    def _():
        greet(line.up)

    @pl.when(line.turn > 0)
    def _():
        greet(line.down)

    @pl.when(line.at_end)
    def _():
        pl.semaphore_wait(barrier, 5 + len(others))

    @pl.when(line.inside)
    def _():
        pl.semaphore_wait(barrier, 6 + len(others))


def run(*steps):
    steps = list(steps)
    while steps:
        for at in list(steps):
            if next(at, "end") == "end":
                steps.remove(at)


def fold_pair(wire, line, refs, finals, scratch):
    return (
        Fold(wire, line, refs[0], False, *scratch[0:2], finals[0]),
        Fold(wire, line, refs[1], True, *scratch[2:4], finals[1]),
    )


def spread_feed(wire, line, full_up, full_down):
    return (
        Spread(wire, line, lambda rows: full_up.at[rows], full_up.shape[0], False),
        Spread(wire, line, lambda rows: full_down.at[:, rows], full_down.shape[1], True),
    )


def spread_attend(wire, line, full_out, full_qkv):
    return (
        Spread(wire, line, lambda rows: full_out.at[:, rows], full_out.shape[1], False),
        Spread(wire, line, lambda rows: full_qkv.at[rows], full_qkv.shape[0], True),
    )


def place_own(wire, line, spread, final):
    @pl.when(line.at_end)
    def _():
        wire.move(final, spread.own())


def swap_across(wire, source, target, first_sends):
    quad = Quad()
    second = jnp.logical_not(quad.first)
    sends, takes = (quad.first, second) if first_sends else (second, quad.first)
    made = wire.copy(source, target, quad.across, sends)

    @pl.when(sends)
    def _():
        made.start()

    yield

    @pl.when(takes)
    def _():
        made.wait_recv()


class Flow(Poll):
    def __init__(self, wire, wide_wire, line, free):
        super().__init__([])
        self.wire, self.wide_wire, self.line, self.free = wire, wide_wire, line, free
        self.sequence, self.done, self.limit, self.limits = Sequence(line), 0, 0, {}
        self.entered = self.last = False
        self.smalls, self.ticks = [], 0
        self.walk, self.on_grade = None, {}

    def __call__(self, times=1):
        for _ in range(times):
            if self.walk is not None and self.done < self.limit:
                self.done += 1
                if next(self.walk, "end") == "end":
                    self.walk = None
            self.ticks += 1
            if self.ticks % 4 == 0 or self.walk is None:
                for steps in list(self.smalls):
                    if next(steps, "end") == "end":
                        self.smalls.remove(steps)

    def until(self, count):
        while self.walk is not None and self.done < min(count, self.limit):
            self()

    def open(self, limit):
        self.limit = limit

    def graded(self, name):
        for action in self.on_grade.pop(name, []):
            action()

    def before(self, what):
        self.until(self.limits.get(what, 0))

    def enter(self):
        if self.entered:
            pl.semaphore_wait(self.free.at[0], 1)
            pl.semaphore_wait(self.free.at[1], 1)
        self.entered = True

    def leave(self):
        self.wire.finish()
        self.wire.made = []
        if self.last:
            return
        for at, peer in enumerate((self.wire.near, self.wire.far)):
            pl.semaphore_signal(
                self.free.at[at], inc=1, device_id={"narrow": peer}, device_id_type=MESH
            )

    def peers(self):
        line = self.line
        not_bottom, not_top = line.ways[0][3], line.ways[1][3]
        return (
            (2, line.up, not_top, not_bottom),
            (3, line.down, not_bottom, not_top),
            (4, line.side, None, None),
        )

    def greet(self):
        for at, peer, sends, _ in self.peers():
            signal = functools.partial(
                pl.semaphore_signal, self.free.at[at], inc=1, device_id=peer, device_id_type=MESH
            )
            signal() if sends is None else pl.when(sends)(lambda signal=signal: signal())

    def greeted(self):
        for at, _, _, comes in self.peers():
            wait = functools.partial(pl.semaphore_wait, self.free.at[at], 1)
            wait() if comes is None else pl.when(comes)(lambda wait=wait: wait())


FEED_NAMES = ("w", "h", "z", "inner", "e", "d", "down")
ATTEND_NAMES = ("x", "a", "q", "k", "v", "o", "qkv", "out")


def backward_kernel(shape, *refs):
    size, length, width, hidden_count, part = shape
    refs = list(refs)

    def take(count):
        taken = refs[:count]
        del refs[:count]
        return taken

    dy, result, up, cosine, sine, start = take(6)
    gains, logs, large = [], [], []
    for _ in range(2):
        gain, log = take(2)
        gains.append(gain)
        logs.append(log)
        large.append(dict(zip(FEED_NAMES + ATTEND_NAMES, take(15))))
    dx_out, grad_came, result_came = take(3)
    totals = take(2)
    fulls = [dict(zip(("up", "down", "out", "qkv"), take(4))) for _ in range(2)]
    held_names = ("g", "up", "cos", "sin") + FEED_NAMES + ATTEND_NAMES
    buffers = dict(zip(held_names, take(len(held_names))))
    second, hidden, mixture, projected, dk, dv, held, own, dh, dz, dx = take(11)
    grad_up, grad_down, grad_out, grad_qkv = take(4)
    feed_scratch, attend_scratch = take(4), take(4)
    finals = [dict(zip(("up", "down", "out", "qkv"), take(4))) for _ in range(2)]
    small = [take(4) for _ in range(2)]
    norms = [take(2) for _ in range(2)]
    biases = take(2)
    sems, wide_sems, local, free = take(4)

    loads = {}

    def load(layer, name, source):
        at = held_names.index(name)
        copy = pltpu.make_async_copy(source, buffers[name], local.at[at])
        loads[layer, name] = Staged(buffers[name], copy, False)
        loads[layer, name].begin()

    def load_feed(layer):
        load(layer, "up", up.at[layer])
        for name in ("w", "d", "down", "e", "inner", "h", "z"):
            load(layer, name, large[layer][name])

    def load_attend(layer):
        for name in ("out", "o", "q", "k", "v", "qkv", "a", "x"):
            load(layer, name, large[layer][name])

    load(1, "g", dy)
    load_feed(1)
    load_attend(1)
    load(1, "cos", cosine)
    load(1, "sin", sine)
    wire, wide_wire, line = Wire(sems), Wire(wide_sems), Line()
    wide_barrier(wide_wire, line, Quad().across)
    result_swap = swap_across(wide_wire, result, result_came, True)
    next(result_swap)

    flow = Flow(wire, wide_wire, line, free)
    sequence = flow.sequence
    folds, spreads, waits = {}, {}, {}

    def fold_feed(layer):
        folds[layer, "up"], folds[layer, "down"] = fold_pair(
            wide_wire, line, (grad_up, grad_down),
            (finals[layer]["up"], finals[layer]["down"]), feed_scratch,
        )

    def fold_attend(layer):
        folds[layer, "out"], folds[layer, "qkv"] = fold_pair(
            wide_wire, line, (grad_out, grad_qkv),
            (finals[layer]["out"], finals[layer]["qkv"]), attend_scratch,
        )

    for layer in range(2):
        fold_feed(layer)
        fold_attend(layer)
        full = fulls[layer]
        spreads[layer, "up"], spreads[layer, "down"] = spread_feed(
            wide_wire, line, full["up"], full["down"]
        )
        spreads[layer, "out"], spreads[layer, "qkv"] = spread_attend(
            wide_wire, line, full["out"], full["qkv"]
        )

    def go_home(layer, names):
        final, full = finals[layer], fulls[layer]

        def action():
            for name in names:
                folds[layer, name].end()
            if names == ("down",):
                waits[layer, names] = home(
                    wide_wire, line, final["down"], None, None, full["down"], None, None
                )
            else:
                waits[layer, names] = home(
                    wide_wire, line, None, final["out"], final["qkv"], None, full["out"], full["qkv"]
                )

        return action

    def come_home(layer, names):
        return lambda: waits[layer, names]()

    def spread_up(layer):
        def action():
            folds[layer, "up"].end()
            place_own(wide_wire, line, spreads[layer, "up"], finals[layer]["up"])
            spreads[layer, "up"].start()

        return action

    def fill(count):
        while len(sequence.chunks) < count:
            sequence.add([lambda way, role: None])

    def feed_fold_part(layer):
        if layer == 0:
            sequence.before_next(folds[layer, "down"].start)
        chunks = folds[layer, "up"].chunks()
        sequence.add(chunks).add(folds[layer, "down"].chunks())
        sequence.after(chunks[-1], folds[layer, "up"].start_side)
        return len(sequence.chunks)

    def attend_fold_feed_spread_part(layer, feed_end):
        sequence.before_next(folds[layer, "qkv"].start)
        chunks = folds[layer, "out"].chunks()
        sequence.add(chunks)
        sequence.after(chunks[-1], folds[layer, "out"].start_side)
        sequence.actions.setdefault(feed_end - 1 + 3 * LATE, []).extend(
            [go_home(layer, ("down",)), folds[layer, "up"].settle]
        )
        fill(feed_end + 3 * LATE + 2)
        sequence.before_next(come_home(layer, ("down",)))
        sequence.add(spreads[layer, "down"].chunks())
        sequence.before_next(spread_up(layer))
        sequence.add(folds[layer, "qkv"].chunks())
        qkv_end = len(sequence.chunks)
        sequence.add(spreads[layer, "up"].chunks())
        sequence.actions.setdefault(qkv_end - 1 + 3 * LATE, []).append(
            go_home(layer, ("out", "qkv"))
        )
        fill(qkv_end + 3 * LATE + 2)
        sequence.before_next(come_home(layer, ("out", "qkv")), spreads[layer, "out"].start)

    feed_end = feed_fold_part(1)
    in_attend_1 = len(sequence.chunks)
    attend_fold_feed_spread_part(1, feed_end)
    sequence.actions.setdefault(len(sequence.chunks) - 1, []).append(flow.greet)
    sequence.add(spreads[1, "qkv"].chunks()).add(spreads[1, "out"].chunks())
    sequence.before_next(flow.greeted)
    in_feed_0 = len(sequence.chunks)
    feed_end = feed_fold_part(0)
    in_attend_0 = len(sequence.chunks)
    attend_fold_feed_spread_part(0, feed_end)
    sequence.add(spreads[0, "qkv"].chunks()).add(spreads[0, "out"].chunks())
    flow.limits = {}

    def feed(layer, grad):
        held_now = {name: loads[layer, name] for name in FEED_NAMES + ("up",)}
        feed_back_body(
            wire, flow, grad, held_now["w"], held_now["h"], held_now["z"], gains[layer],
            held_now["inner"], held_now["e"], held_now["d"], held_now["up"], held_now["down"],
            grad_down, grad_up, biases[layer], norms[layer][0], dh, dz,
            second, hidden, held, own,
        )

    def attend(layer):
        names = {name: loads[layer, name] for name in ATTEND_NAMES}
        attend_back_body(
            wire, flow, dz, dh, names["x"], gains[layer], names["a"], names["q"], names["k"],
            names["v"], names["o"], logs[layer], start, loads[1, "cos"], loads[1, "sin"],
            names["qkv"], names["out"],
            grad_qkv, grad_out, norms[layer][1], dx,
            second, mixture, projected, dk, dv, held, own,
        )
        norms[layer][0][...] += norms[layer][1][...]

    def open_to(limit):
        return lambda: flow.open(limit)

    def set_out():
        flow.walk = sequence.steps()

    flow.on_grade = {
        "down": [set_out, folds[1, "down"].start, open_to(in_attend_1 - 1)],
        "qkv": [open_to(in_feed_0 - 1)],
    }
    feed(1, loads[1, "g"])
    load_feed(0)
    attend(1)
    flow.smalls.append(
        small_steps(wide_wire, line, norms[1][0], biases[1], *small[1], totals[1])
    )
    load_attend(0)
    flow.limits = {"feed": feed_limit(in_attend_1), "attend": in_feed_0}
    flow.on_grade = {
        "down": [open_to(in_attend_0 - 1)],
        "qkv": [open_to(len(sequence.chunks) + 3 * LATE + 1)],
    }
    feed(0, dx)
    flow.last = True
    attend(0)
    moved = pltpu.make_async_copy(dx, dx_out, local.at[len(held_names)])
    moved.start()
    grad_swap = swap_across(wide_wire, dx, grad_came, False)
    next(grad_swap)
    flow.smalls.append(
        small_steps(wide_wire, line, norms[0][0], biases[0], *small[0], totals[0])
    )
    while flow.walk is not None or flow.smalls:
        flow()
    for layer in range(2):
        spreads[layer, "down"].end()
        spreads[layer, "qkv"].end()
    next(result_swap, None)
    next(grad_swap, None)
    moved.wait()
    wide_wire.finish()
    assert wire.used <= sems.shape[0] and wide_wire.used <= wide_sems.shape[0]


def feed_limit(feed_end):
    return feed_end + 3 * LATE + 1


def backward_wide(grad, result, saved, weights, start, tables):
    size, width = grad.shape
    length, part = saved[0][2].shape
    hidden_count = saved[0][10].shape[1]
    shape = (size, length, width, hidden_count, part)
    operands, specs = [], []

    def give(array, large=True):
        operands.append(array)
        specs.append(pl.BlockSpec(memory_space=pl.ANY if large else pltpu.VMEM))

    w_up = weights[0][2][0]
    for array in (grad, result, w_up) + tables:
        give(array)
    give(start[None], False)
    for layer in range(2):
        w_qkv, w_out, _, _, w_down, gains, _ = weights[layer]
        resid, normed, query, keys, values, mixture, logs, branch, middle, inner, active, slope, second = saved[layer]
        give(gains, False)
        give(logs, False)
        for array in (second, middle, branch, inner, active, slope, w_down):
            give(array)
        for array in (resid, normed, query, keys, values, mixture, w_qkv, w_out):
            give(array)
    rows = ((size, width), BF16)
    outs = [rows] * 3 + [((16, part), F32)] * 2
    for _ in range(2):
        outs += [
            ((width, hidden_count), BF16),
            ((4, hidden_count, part), BF16),
            ((4, part, part), BF16),
            ((width, 3 * part), BF16),
        ]
    out_specs = [pl.BlockSpec(memory_space=pl.ANY)] * 3 + vmem(2)
    out_specs += [pl.BlockSpec(memory_space=pl.ANY)] * 8
    line_rows = ((size, width), F32)
    buffers = [
        rows, ((width, hidden_count), BF16), (tables[0].shape, F32), (tables[1].shape, F32),
        line_rows, line_rows, line_rows,
        ((length, width), BF16), ((length, hidden_count), BF16), ((length, hidden_count), BF16),
        ((hidden_count, width), BF16),
        rows, ((length, width), BF16),
    ]
    buffers += [((length, part), BF16)] * 4
    buffers += [((width, 3 * part), BF16), ((part, width), BF16)]
    buffers += [
        ((length, width), BF16), ((length, hidden_count), BF16), ((length, part), BF16),
        ((length, 3 * part), BF16), ((length, part), F32), ((length, part), F32),
        ((6, size, width), BF16), line_rows, line_rows, rows, rows,
    ]
    grads = [
        ((width, hidden_count), BF16), ((hidden_count, width), BF16),
        ((part, width), BF16), ((width, 3 * part), BF16),
    ]
    buffers += grads
    scratch = [pltpu.VMEM(*entry) for entry in buffers]
    for (first, _), (last, _) in (grads[0:2], grads[2:4]):
        scratch += Fold.scratch(*first, False) + Fold.scratch(*last, True)
    for _ in range(2):
        scratch += [pltpu.VMEM((rows // 4, columns), BF16) for (rows, columns), _ in grads]
    for _ in range(2):
        scratch += [
            pltpu.VMEM((4, 8, part), F32),
            pltpu.VMEM((16, part), F32),
            pltpu.VMEM((16, part), F32),
            pltpu.VMEM((4, 16, part), F32),
        ]
    scratch += [pltpu.VMEM((8, width), F32)] * 4
    scratch += [pltpu.VMEM((1, hidden_count), F32)] * 2
    scratch += [
        pltpu.SemaphoreType.DMA((88,)),
        pltpu.SemaphoreType.DMA((520,)),
        pltpu.SemaphoreType.DMA((20,)),
        pltpu.SemaphoreType.REGULAR((5,)),
    ]
    found = pl.pallas_call(
        functools.partial(backward_kernel, shape),
        in_specs=specs,
        out_specs=out_specs,
        out_shape=shaped(*outs),
        scratch_shapes=scratch,
        compiler_params=pltpu.CompilerParams(
            collective_id=3, has_side_effects=True, vmem_limit_bytes=62 * 2**20
        ),
        name="backward",
    )(*operands)
    grad, grad_came, result_came = found[:3]
    totals = found[3:5]

    sums = [
        jnp.stack([block.reshape(-1, block.shape[-1]).astype(F32) for block in pair])
        for pair in zip(found[5:9], found[9:13])
    ]
    bias = jnp.stack([total[8:12].reshape(-1) for total in totals])
    gains, shifts = (
        jnp.stack([total[at : at + 4] for total in totals]) for at in (0, 4)
    )
    up, down, out, qkv = sums
    return grad, grad_came, result_came, (qkv, out, up, bias, down, gains, shifts)


class Quad:
    def __init__(self):
        at = lax.axis_index("wide")
        pair, turn = lax.rem(at, 2), at // 2
        odd = lax.rem(turn, 2)
        self.side = {"wide": at + 1 - 2 * pair}
        self.mate = {"wide": (turn + 1 - 2 * odd) * 2 + pair}
        self.mine = odd * 2 + pair
        self.from_side = odd * 2 + 1 - pair
        self.from_mate = (1 - odd) * 2 + pair
        halfway = lax.axis_size("wide") // 2
        self.first = at < halfway
        self.across = {"wide": lax.rem(at + halfway, 2 * halfway)}


class Fetch:
    def __init__(self, wire, shard, full, by_heads):
        self.wire, self.full, self.rows = wire, full, full.shape[0]
        at, odd, upper = wire.at, lax.rem(wire.at, 2), wire.at // 2
        part = shard.shape[1]

        def columns(block, count=1):
            return pl.ds(pl.multiple_of(block * 256, 256), 256 * count)

        if by_heads:
            self.far = [
                (
                    lambda rows: shard.at[rows, columns(2 - 2 * odd)],
                    lambda rows: full.at[rows, columns(2 * upper)],
                    wire.far,
                )
            ]
            self.relay = lambda rows: full.at[rows, columns(2 - 2 * upper)]
            self.near = (shard.at[:, columns(1)], full.at[:, columns(odd + upper)])
            self.own = (shard.at[:, columns(2 * odd)], full.at[:, columns((at + 1) // 2)])
        else:
            block = self.rows

            def away(peer):
                return (
                    lambda rows: shard.at[span(peer * block + rows.start, rows.size)],
                    lambda rows: full.at[rows, columns(at)],
                    peer,
                )

            self.far = [away(wire.far), away(wire.diagonal)]
            self.relay = lambda rows: full.at[rows, columns(2 - 2 * upper, 2)]
            self.near = (shard.at[span(wire.near * block, block)], full.at[:, columns(at)])
            self.own = (shard.at[span(at * block, block)], full.at[:, columns(at)])

    def quarter(self, which, half=0, halves=1):
        size = self.rows // 4
        return span(which * size + half * (size // halves), size // halves)


def fetch_steps(wire, quad, fetches, local):
    copies, sent, nears = [], [], []
    for at, fetch in enumerate(fetches):
        rows = fetch.quarter(quad.mine)
        for source, target, peer in fetch.far:
            sent.append(wire.send(source(rows), target(rows), {"narrow": peer}))
        nears.append(wire.send(*fetch.near, {"narrow": wire.near}))
        copies.append(pltpu.make_async_copy(*fetch.own, local[at]))
        copies[-1].start()
    yield
    for made in sent:
        made.wait_recv()
    sides, mates = [], []
    for fetch in fetches:
        held = fetch.relay(fetch.quarter(quad.mine))
        sides.append(wire.send(held, held, quad.side))
        mates.append(wire.send(held, held, quad.mate))
    yield
    last = []
    for fetch, side, mate in zip(fetches, sides, mates):
        side.wait_recv()
        held = fetch.relay(fetch.quarter(quad.from_side, 0, 2))
        last.append(wire.send(held, held, quad.mate))
        mate.wait_recv()
        held = fetch.relay(fetch.quarter(quad.from_mate, 1, 2))
        last.append(wire.send(held, held, quad.side))
    yield
    for made in last + nears:
        made.wait_recv()
    for copy in copies:
        copy.wait()


def greet(peers):
    barrier = pltpu.get_barrier_semaphore()
    for peer in peers:
        pl.semaphore_signal(barrier, inc=1, device_id=peer, device_id_type=MESH)
    pl.semaphore_wait(barrier, len(peers))


def quad_barrier(wire, quad, *others):
    narrow = [{"narrow": peer} for peer in (wire.near, wire.far, wire.diagonal)]
    greet(narrow + [quad.side, quad.mate] + list(others))


class Hand(Poll):
    def __init__(self, wire, free, actions):
        super().__init__([])
        self.wire, self.free, self.actions = wire, free, list(actions)
        self.entered = self.last = False
        self.settled = ()

    def __call__(self, times=1):
        for _ in range(times):
            if self.actions:
                for action in self.actions.pop(0):
                    action()

    def enter(self):
        if self.entered:
            pl.semaphore_wait(self.free.at[0], 1)
            pl.semaphore_wait(self.free.at[1], 1)
        self.entered = True

    def leave(self):
        self.wire.finish()
        self.wire.made = []
        ready(*self.settled)
        if self.last:
            return
        for at, peer in enumerate((self.wire.near, self.wire.far)):
            pl.semaphore_signal(
                self.free.at[at], inc=1, device_id={"narrow": peer}, device_id_type=MESH
            )


WEIGHT_NAMES = ("qkv", "out", "down")
KEPT_NAMES = ("a", "q", "k", "v", "o", "lse", "z", "h", "inner", "e", "d", "w", "y")


def forward_kernel(size, *refs):
    refs = list(refs)

    def take(count):
        taken = refs[:count]
        del refs[:count]
        return taken

    ends, w_qkv, w_out, w_down, w_up, norms, b_up, cosine, sine, start = take(10)
    x_out, dy_out = take(2)
    gains, weights_out, kept_out = take(2), [], []
    for _ in range(2):
        weights_out.append(dict(zip(WEIGHT_NAMES, take(3))))
        kept_out.append(dict(zip(KEPT_NAMES, take(13))))
    full_norms, shift_0, shift_1, cos_held, sin_held, start_held, up_0, up_1, x_held = take(9)
    held_weights = [dict(zip(WEIGHT_NAMES, take(3))) for _ in range(2)]
    kept = dict(zip(KEPT_NAMES, take(13)))
    result, inner_own, held, own = take(4)
    sems, quad_sems, local, free = take(4)
    shifts, ups = (shift_0, shift_1), (up_0, up_1)
    locals_used = [0]

    def place():
        locals_used[0] += 1
        return local.at[locals_used[0] - 1]

    def load(source, ref):
        staged = Staged(ref, pltpu.make_async_copy(source, ref, place()), False)
        staged.begin()
        return staged

    def keep(ref, target):
        return Staged(ref, pltpu.make_async_copy(ref, target, place()), True)

    cos_held, sin_held = load(cosine, cos_held), load(sine, sin_held)
    start_held = load(start, start_held)
    ups = [load(w_up.at[layer], ups[layer]) for layer in range(2)]
    wire, quad_wire, quad = Wire(sems), Wire(quad_sems), Quad()
    second = jnp.logical_not(quad.first)
    half = size // 2
    own_x = pltpu.make_async_copy(ends.at[pl.ds(0, size)], x_held, place())
    own_dy = pltpu.make_async_copy(ends.at[pl.ds(size, size)], dy_out, place())

    @pl.when(quad.first)
    def _():
        own_x.start()

    @pl.when(second)
    def _():
        own_dy.start()

    quad_barrier(quad_wire, quad, quad.across)
    x_parts = [
        quad_wire.copy(
            ends.at[pl.ds(size + part * half, half)], x_held.at[pl.ds(part * half, half)],
            quad.across, quad.first,
        )
        for part in range(2)
    ]
    dy_swap = quad_wire.copy(ends.at[pl.ds(0, size)], dy_out, quad.across, second)

    @pl.when(quad.first)
    def _():
        x_parts[0].start()

    def start_later():
        @pl.when(quad.first)
        def _():
            x_parts[0].wait_send()
            x_parts[1].start()

        x_parts[0].settled = True

        @pl.when(second)
        def _():
            dy_swap.start()

    def x_arrives(part):
        if part == 0:

            @pl.when(quad.first)
            def _():
                own_x.wait()

        @pl.when(second)
        def _():
            x_parts[part].wait_recv()

    def fetches(layer, names):
        sources = {"qkv": w_qkv, "out": w_out, "down": w_down}
        wanted = [
            Fetch(quad_wire, sources[name].at[layer], held_weights[layer][name], name == "qkv")
            for name in names
        ]
        at = locals_used[0]
        locals_used[0] += len(names)
        steps = fetch_steps(quad_wire, quad, wanted, [local.at[at + i] for i in range(len(names))])
        outs = [keep(held_weights[layer][name], weights_out[layer][name]) for name in names]
        finished = []

        def step():
            if not finished and next(steps, "end") == "end":
                finished.append(True)
                done(*outs)

        def finish():
            while not finished:
                step()

        return step, finish, outs

    begin, begin_all, begin_outs = fetches(0, ("qkv", "out"))
    down, down_all, down_outs = fetches(0, ("down",))
    rest, rest_all, rest_outs = fetches(1, WEIGHT_NAMES)
    begin()
    part = norms.shape[1]
    columns = pl.ds(pl.multiple_of(wire.at * part, part), part)
    sent = [
        quad_wire.send(norms, full_norms.at[:, columns], {"narrow": peer})
        for peer in (wire.diagonal, wire.far, wire.near)
    ]
    full_norms[:, columns] = norms[...]
    begin()
    for made in sent:
        made.wait_recv()
    spread = full_norms[...].astype(F32)
    for layer in range(2):
        gains[layer][...] = spread[4 * layer : 4 * layer + 4]
        shifts[layer][...] = spread[8 + 4 * layer : 12 + 4 * layer]

    actions = [
        [begin, start_later],
        [begin_all, down],
        [down, rest],
        [down, rest],
        [down_all, rest],
        [rest_all],
    ]
    hand = Hand(wire, free, actions)
    x_now = Pending(x_held, x_arrives)
    before = {}
    for layer in range(2):
        now = {name: keep(kept[name], kept_out[layer][name]) for name in KEPT_NAMES}
        if layer == 0:
            now["y"] = keep(result, kept_out[layer]["y"])
        gather_weights = held_weights[layer]
        waits = {"qkv": begin_all, "out": begin_all, "down": down_all}
        weights = {
            name: Pending(ref, waits[name] if layer == 0 else rest_all)
            for name, ref in gather_weights.items()
        }
        ready(*(before[name] for name in ("q", "k", "v", "o", "lse", "z", "h") if before))
        hand.settled = [before["inner"]] if before else []
        attend_half_body(
            wire, hand, x_now, gains[layer], shifts[layer], cos_held, sin_held, start_held,
            weights["qkv"], weights["out"],
            now["a"], now["q"], now["k"], now["v"], now["o"], now["lse"], now["z"], now["h"],
            inner_own, held, own,
        )
        ready(*(before[name] for name in ("e", "d", "w") if before))
        hand.settled = [now["a"]]
        hand.last = layer == 1
        feed_half_body(
            wire, hand, inner_own, kept["h"], gains[layer], shifts[layer], ups[layer],
            b_up.at[layer], weights["down"],
            now["inner"], now["e"], now["d"], now["w"], now["y"],
            held, own,
        )
        if layer == 0:
            x_copy = keep(x_held, x_out)
            x_copy.begin()
            x_now = result
        else:
            ready(*before.values())
        before = now
    ready(x_copy, *before.values(), *begin_outs, *down_outs, *rest_outs)

    @pl.when(quad.first)
    def _():
        dy_swap.wait_recv()

    @pl.when(second)
    def _():
        own_dy.wait()

    quad_wire.finish()
    assert wire.used <= sems.shape[0] and quad_wire.used <= quad_sems.shape[0]
    assert locals_used[0] <= local.shape[0]


def forward(ends, w_qkv, w_out, w_down, w_up, norms, b_up, cosine, sine, start):
    size, width = ends.shape[0] // 2, ends.shape[1]
    part, hidden = w_out.shape[2], w_up.shape[2]
    length = cosine.shape[0]
    rows, line_rows = ((size, width), BF16), ((size, width), F32)
    weights = [((width, 3 * part), BF16), ((part, width), BF16), ((hidden, width), BF16)]
    kept = [((length, width), BF16)] + [((length, part), BF16)] * 4
    kept += [((8, length), F32), line_rows, line_rows]
    kept += [((length, width), BF16)] + [((length, hidden), BF16)] * 2 + [line_rows, rows]
    norm = ((4, width), F32)
    outs = [rows, rows] + [norm] * 2 + (weights + kept) * 2
    out_specs = [pl.BlockSpec(memory_space=pl.ANY)] * 2 + vmem(2)
    out_specs += [pl.BlockSpec(memory_space=pl.ANY)] * 32
    buffers = [
        ((norms.shape[0], width), BF16), norm, norm,
        (cosine.shape, F32), (sine.shape, F32), (start.shape, jnp.int32),
        ((width, hidden), BF16), ((width, hidden), BF16), rows,
    ]
    buffers += weights * 2 + kept + [rows, rows, ((6, size, width), BF16), line_rows]
    apart = pl.BlockSpec(memory_space=pl.ANY)
    found = pl.pallas_call(
        functools.partial(forward_kernel, size),
        in_specs=[apart] * 5 + vmem(2) + [apart] * 3,
        out_specs=out_specs,
        out_shape=shaped(*outs),
        scratch_shapes=[pltpu.VMEM(*entry) for entry in buffers]
        + [
            pltpu.SemaphoreType.DMA((88,)),
            pltpu.SemaphoreType.DMA((104,)),
            pltpu.SemaphoreType.DMA((56,)),
            pltpu.SemaphoreType.REGULAR((2,)),
        ],
        compiler_params=pltpu.CompilerParams(
            collective_id=1, has_side_effects=True, vmem_limit_bytes=58 * 2**20
        ),
        name="forward",
    )(ends, w_qkv, w_out, w_down, w_up, norms, b_up, cosine, sine, start)
    x, dy = found[:2]
    gains, found = found[2:4], found[4:]
    weights, saved = [], []
    resid = x
    for layer in range(2):
        qkv, out, down = found[16 * layer : 16 * layer + 3]
        a, q, k, v, o, lse, z, h, inner, e, d, w, y = found[16 * layer + 3 : 16 * layer + 16]
        weights.append((qkv, out, (w_up, layer), None, down, gains[layer], None))
        saved.append((resid, a, q, k, v, o, lse, z, h, inner, e, d, w))
        resid = y
    return dy, resid, weights, saved


def swap(block, distance):
    count = lax.axis_size("narrow")
    return lax.ppermute(block, "narrow", [(i, i ^ distance) for i in range(count)])


def pick(stack, table, at):
    return lax.dynamic_index_in_dim(stack, jnp.asarray(table)[at], 0, keepdims=False)


def by_heads(block, at):
    parts = jnp.stack(jnp.split(block, 3, axis=1))
    own = pick(parts, [0, 2, 0, 2], at)
    near = swap(parts[1], 1)
    far = swap(pick(parts, [2, 0, 2, 0], at), 2)
    parts = jnp.stack([own, near, far])
    order = jnp.asarray([[0, 1, 2], [1, 0, 2], [2, 0, 1], [2, 1, 0]])[at]
    return jnp.concatenate(
        [lax.dynamic_index_in_dim(parts, order[i], 0, keepdims=False) for i in range(3)], axis=1
    )


def from_heads(block, at):
    parts = jnp.stack(jnp.split(block, 3, axis=1))
    own = pick(parts, [0, 1, 1, 2], at)
    near = swap(pick(parts, [1, 0, 2, 1], at), 1)
    far = swap(pick(parts, [2, 2, 0, 0], at), 2)
    parts = jnp.stack([own, near, far])
    order = jnp.asarray([[0, 1, 2], [2, 1, 0], [0, 1, 2], [2, 1, 0]])[at]
    return jnp.concatenate(
        [lax.dynamic_index_in_dim(parts, order[i], 0, keepdims=False) for i in range(3)], axis=1
    )


def to_rows(block):
    return lax.all_to_all(block, "narrow", split_axis=0, concat_axis=1, tiled=True)


def to_columns(block):
    return lax.all_to_all(block, "narrow", split_axis=1, concat_axis=0, tiled=True)


def layer_forward(resid, weights, start, tables):
    w_qkv, w_out, w_up, b_up, w_down, gains, shifts = weights
    (normed, query, keys, values, mixture, logs, branch, middle, inner), _ = attend_half(
        Background(1), resid, gains, shifts, *tables, start[:, None], w_qkv, w_out
    )
    inner, active, slope, second, result = feed_half(
        20 + w_up[1], inner, middle, gains, shifts, w_up, b_up, w_down
    )
    return result, (
        resid, normed, query, keys, values, mixture, logs, branch, middle, inner, active, slope, second
    )


def feed_backward(background, grad, saved, weights):
    w_qkv, w_out, w_up, b_up, w_down, gains, shifts = weights
    _, _, _, _, _, _, _, branch, middle, inner, active, slope, second = saved
    (grad_down, grad_up, grad_b_up, norms, grad_middle, grad_branch), results = feed_back(
        background, grad, second, middle, branch, gains, inner, active, slope, w_up, w_down
    )
    return ((grad_up, grad_down), norms, grad_b_up, grad_middle, grad_branch), results


def attend_backward(background, grad_branch, grad_middle, saved, weights, start, tables):
    w_qkv, w_out, w_up, b_up, w_down, gains, shifts = weights
    resid, normed, query, keys, values, mixture, logs, _, _, _, _, _, _ = saved
    (grad_qkv, grad_out, norms, grad), results = attend_back(
        background, grad_branch, grad_middle, resid, gains, normed, query, keys, values, mixture,
        logs, start[None], *tables, w_qkv, w_out,
    )
    return ((grad_out, grad_qkv), norms, grad), results


def layer_backward(grad, saved, weights, start, tables):
    ((grad_up, grad_down), norms, grad_b_up, grad_middle, grad_branch), _ = feed_backward(
        Background(30 + weights[2][1]), grad, saved, weights
    )
    ((grad_out, grad_qkv), norms_too, grad), _ = attend_backward(
        Background(4), grad_branch, grad_middle, saved, weights, start, tables
    )
    return grad, (grad_qkv, grad_out, grad_up, grad_b_up, grad_down, norms + norms_too)


def reduce_grads(grads, at):
    def fold(block):
        return lax.psum_scatter(block, "wide", scatter_dimension=0, tiled=True)

    def spread(block):
        return lax.all_gather(block, "wide", axis=0, tiled=True)

    def spread_rows(block):
        wide, narrow = lax.axis_size("wide"), lax.axis_size("narrow")
        rows, width = block.shape
        full = spread(block).reshape(wide, narrow, rows // narrow, width)
        return full.transpose(1, 0, 2, 3).reshape(wide * rows, width)

    qkv, out, up, b_up, down, norms = grads
    qkv = spread(from_heads(fold(qkv), at))
    out = spread_rows(to_columns(fold(out)))
    up = spread(fold(up))
    down = spread_rows(to_columns(fold(down)))
    b_up = lax.psum(b_up[0], "wide")
    norms = lax.psum(norms, ("wide", "narrow"))
    part = norms.shape[1] // lax.axis_size("narrow")
    norms = lax.dynamic_slice_in_dim(norms, at * part, part, 1)
    return qkv, out, up, b_up, down, norms[:4], norms[4:]


def on_device(ends, lengths, w_qkv, w_out, w_up, b_up, w_down, norm_gain, norm_bias):
    wide = lax.axis_size("wide")
    narrow = lax.axis_size("narrow")
    halfway = wide // 2
    wide_at = lax.axis_index("wide")
    at = lax.axis_index("narrow")
    first = wide_at < halfway
    row_count = ends.shape[0] // 2
    length = row_count * narrow

    def route(block):
        pairs = [(i, (i + halfway) % wide) for i in range(wide)]
        return lax.ppermute(block, "wide", pairs)

    own_lengths = lengths[lax.rem(wide_at, halfway), wide_at // halfway]
    places = jnp.arange(length, dtype=jnp.int32)
    passed = (places[:, None] >= jnp.cumsum(own_lengths)[None, :]).astype(jnp.int32)
    start = jnp.sum(passed * own_lengths[None, :], axis=1)
    tables = rope_tables(places - start)
    b_up = b_up.astype(F32)[:, None]
    norms = jnp.concatenate([norm_gain, norm_bias]).reshape(16, -1)

    if wide == 8:
        upstream, result, weights, saved = forward(
            ends, w_qkv, w_out, w_down, w_up, norms, b_up, *tables, start[:, None]
        )
        grad, grad_came, result_came, totals = backward_wide(
            upstream, result, saved, weights, start, tables
        )
    else:
        came = route(jnp.where(first, ends[row_count:], ends[:row_count]))
        norms = lax.all_gather(norms, "narrow", axis=1, tiled=True).astype(F32)
        resid = jnp.where(first, ends[:row_count], came)
        upstream = jnp.where(first, came, ends[row_count:])

        def weights_of(layer):
            return (
                by_heads(w_qkv[layer], at), to_rows(w_out[layer]), (w_up, layer), b_up[layer],
                to_rows(w_down[layer]), norms[4 * layer : 4 * layer + 4],
                norms[8 + 4 * layer : 12 + 4 * layer],
            )

        weights = [weights_of(layer) for layer in range(2)]
        middle, saved_first = layer_forward(resid, weights[0], start, tables)
        result, saved_second = layer_forward(middle, weights[1], start, tables)
        result_came = route(result)
        grad, grads_second = layer_backward(upstream, saved_second, weights[1], start, tables)
        totals_second = reduce_grads(grads_second, at)
        grad, grads_first = layer_backward(grad, saved_first, weights[0], start, tables)
        totals_first = reduce_grads(grads_first, at)
        grad_came = route(grad)
        totals = [
            jnp.stack([a.astype(F32), b.astype(F32)])
            for a, b in zip(totals_first, totals_second)
        ]

    ends_out = jnp.where(
        first, jnp.concatenate([grad, grad_came]), jnp.concatenate([result_came, result])
    )
    return (ends_out,) + tuple(totals)


def solution(mesh):
    placed = (
        P(("wide", "narrow"), None),
        P(),
        P(None, None, "narrow"),
        P(None, None, "narrow"),
        P(None, None, "narrow"),
        P(None, "narrow"),
        P(None, None, "narrow"),
        P(None, None, "narrow"),
        P(None, None, "narrow"),
    )
    return jax.shard_map(
        on_device,
        mesh=mesh,
        in_specs=placed,
        out_specs=(P(("wide", "narrow"), None),) + placed[2:],
        check_vma=False,
    )
```

```python
import functools
import math

import jax
import jax.numpy as jnp
from jax import lax
from jax.experimental import pallas as pl
from jax.experimental.pallas import tpu as pltpu
from jax.sharding import PartitionSpec as P

HD = 64
EPSILON = 1e-05
MASKED = -1e30
SCALE = HD ** (-0.5)
F32 = jnp.float32
BF16 = jnp.bfloat16


def layer_norm(values, gain_row, shift_row):
    center = jnp.mean(values, axis=-1, keepdims=True)
    centred = values - center
    spread = jnp.mean(centred * centred, axis=-1, keepdims=True)
    return centred * lax.rsqrt(spread + EPSILON) * gain_row + shift_row


def rope_tables(offsets):
    halfway = HD // 2
    ladder = jnp.arange(halfway, dtype=F32) * (2.0 / HD)
    inverse = jnp.exp(-math.log(10000.0) * ladder)
    angles = offsets.astype(F32)[:, None] * inverse[None, :]
    cosine, sine = jnp.cos(angles), jnp.sin(angles)
    return (
        jnp.concatenate([cosine, cosine] * 2, axis=1),
        jnp.concatenate([-sine, sine] * 2, axis=1),
    )


def dot(left, right):
    return jnp.dot(left, right, preferred_element_type=F32)


def dot_t(left, right):
    return lax.dot_general(left, right, (((1,), (1,)), ((), ())), preferred_element_type=F32)


def t_dot(left, right):
    return lax.dot_general(left, right, (((0,), (0,)), ((), ())), preferred_element_type=F32)


MESH = pl.DeviceIdType.MESH


def layer_norm_back(values, grad, gain_row):
    center = jnp.mean(values, axis=-1, keepdims=True)
    centred = values - center
    scale = lax.rsqrt(jnp.mean(centred * centred, axis=-1, keepdims=True) + EPSILON)
    unit = centred * scale
    inner = grad * gain_row
    mean = jnp.mean(inner, axis=-1, keepdims=True)
    slope = jnp.mean(inner * unit, axis=-1, keepdims=True)
    grad_values = scale * (inner - mean - unit * slope)
    return (
        grad_values,
        jnp.sum(grad * unit, axis=0, keepdims=True),
        jnp.sum(grad, axis=0, keepdims=True),
    )


class Copy:
    def __init__(self, wire, source, target, peer, when):
        self.when, self.settled = when, False
        source, target = (item.ref if isinstance(item, Staged) else item for item in (source, target))
        self.pieces = (source, target, wire.sems.at[wire.used], wire.sems.at[wire.used + 1], peer)
        wire.used += 2
        wire.made.append(self)

    def remote(self, source=None):
        own, target, send_sem, recv_sem, peer = self.pieces
        return pltpu.make_async_remote_copy(
            src_ref=own if source is None else source,
            dst_ref=target,
            send_sem=send_sem,
            recv_sem=recv_sem,
            device_id=peer if isinstance(peer, dict) else {"narrow": peer},
            device_id_type=MESH,
        )

    def start(self):
        self.remote().start()

    def start_from(self, source):
        self.remote(source).start()

    def wait_recv(self):
        self.remote().wait_recv()

    def wait_send_early(self, others):
        self.when = others
        self.remote().wait_send()

    def settle(self):
        if not self.settled:
            self.settled = True
            self.wait_send()

    def wait_send(self):
        if self.when is None:
            self.remote().wait_send()
        else:

            @pl.when(self.when)
            def _():
                self.remote().wait_send()


class Wire:
    def __init__(self, sems):
        self.sems, self.used, self.made = sems, 0, []
        self.at = lax.axis_index("narrow")
        self.near = self.at + 1 - 2 * lax.rem(self.at, 2)
        self.far = lax.rem(self.at + 2, 4)
        self.diagonal = lax.rem(self.near + 2, 4)

    def barrier(self):
        barrier = pltpu.get_barrier_semaphore()
        for peer in (self.near, self.far):
            pl.semaphore_signal(barrier, inc=1, device_id={"narrow": peer}, device_id_type=MESH)
        pl.semaphore_wait(barrier, 2)

    def copy(self, source, target, peer, when=None):
        return Copy(self, source, target, peer, when)

    def send(self, source, target, peer):
        made = self.copy(source, target, peer)
        made.start()
        return made

    def move(self, source, target):
        source = source.ref if isinstance(source, Staged) else source
        copy = pltpu.make_async_copy(source, target, self.sems.at[self.used])
        self.used += 1
        copy.start()
        copy.wait()

    def finish(self):
        for made in self.made:
            made.settle()


def block_rows(block, size, part=0, parts=1):
    step = size // parts
    return pl.ds(pl.multiple_of(block * size + part * step, step), step)


class Gather:
    def __init__(self, wire, full, size):
        self.wire, self.full, self.size = wire, full, size
        self.to_near, self.to_far, self.relayed = [], [], []

    def rows(self, block, part):
        return self.full.at[block_rows(block, self.size, part, 2)]

    def push(self, part):
        own = self.rows(self.wire.at, part)
        self.to_near.append(self.wire.send(own, own, self.wire.near))
        self.to_far.append(self.wire.send(own, own, self.wire.far))

    def wait_near(self):
        for made in self.to_near:
            made.wait_recv()

    def relay(self, part):
        self.to_far[part].wait_recv()
        held = self.rows(self.wire.far, part)
        self.relayed.append(self.wire.send(held, held, self.wire.near))

    def wait_diagonal(self, part):
        self.relayed[part].wait_recv()


class Scatter:
    def __init__(self, wire, held, own, parts):
        self.held, self.own = held, own
        self.size = own.shape[0]
        step = self.size // parts
        self.cuts = [pl.ds(i * step, step) for i in range(parts)]

        def copies(out, into, peer, cuts):
            return [wire.copy(held.at[out, cut], held.at[into, cut], peer) for cut in cuts]

        self.side = copies(0, 1, wire.near, self.cuts)
        self.cross = copies(2, 3, wire.far, self.cuts)
        self.home = copies(4, 5, wire.near, [pl.ds(0, self.size)])[0]

    def put_diagonal(self, partial, part):
        self.held[0, self.cuts[part]] = partial.astype(BF16)
        self.side[part].start()

    def put_far(self, partial, part):
        cut = self.cuts[part]
        self.side[part].wait_recv()
        self.held[2, cut] = (partial + self.held[1, cut].astype(F32)).astype(BF16)
        self.cross[part].start()

    def put_near(self, partial):
        self.held[4] = partial.astype(BF16)
        self.home.start()

    def total(self):
        self.home.wait_recv()
        for made in self.cross:
            made.wait_recv()
        return self.own[...] + self.held[5].astype(F32) + self.held[3].astype(F32)


def turn(field, cosine, sine):
    lane = lax.broadcasted_iota(jnp.int32, cosine.shape, 1)
    first = lax.rem(lane, HD) < HD // 2
    turned = []
    for at in range(0, field.shape[1], 128):
        part = field[:, at : at + 128]
        swapped = jnp.where(
            first, pltpu.roll(part, 128 - HD // 2, 1), pltpu.roll(part, HD // 2, 1)
        )
        turned.append(part * cosine + swapped * sine)
    return jnp.concatenate(turned, axis=1)


def vmem(count):
    return [pl.BlockSpec(memory_space=pltpu.VMEM)] * count


def shaped(*entries):
    return [jax.ShapeDtypeStruct(shape, kind) for shape, kind in entries]


class Poll:
    def __init__(self, steps):
        self.steps = steps

    def __call__(self, times=1):
        for _ in range(times):
            for step in list(self.steps):
                if next(step, "end") == "end":
                    self.steps.remove(step)

    def enter(self):
        pass

    def leave(self):
        pass

    def before(self, what):
        pass

    def graded(self, name):
        pass


SMALL = 2**16


class Staged:
    def __init__(self, ref, copy, is_result):
        self.ref, self.copy, self.is_result = ref, copy, is_result
        self.begun = self.ended = False
        self.shape, self.dtype = ref.shape, ref.dtype

    def begin(self):
        self.begun = True
        self.copy.start()

    def wait(self):
        if not self.ended:
            self.ended = True
            self.copy.wait()

    def check(self):
        assert self.is_result or self.ended

    @property
    def at(self):
        self.check()
        return self.ref.at

    def __getitem__(self, index):
        self.check()
        return self.ref[index]

    def __setitem__(self, index, value):
        self.ref[index] = value


class Pending(Staged):
    def __init__(self, ref, action):
        super().__init__(ref, None, False)
        self.action = action

    def wait(self):
        if not self.ended:
            self.ended = True
            self.action()

    def wait_part(self, part):
        self.ended = True
        self.action(part)


def ready(*refs):
    for ref in refs:
        if isinstance(ref, Staged):
            ref.wait()


def ready_part(ref, part):
    if isinstance(ref, Pending):
        ref.wait_part(part)
    else:
        ready(ref)


def done(*refs):
    for ref in refs:
        if isinstance(ref, Staged):
            ref.begin()


class Background:
    def __init__(
        self, number, operands=(), outs=(), scratch=(), steps=None, staged=0, quad=False,
        across=False, semaphores=24,
    ):
        self.semaphores = semaphores
        self.staged = staged
        self.number, self.operands, self.outs = number, list(operands), list(outs)
        self.scratch, self.steps, self.quad, self.across = list(scratch), steps, quad, across


def is_large(shape, kind):
    return math.prod(shape) * jnp.dtype(kind).itemsize > SMALL


def call_with(body, background, outs, scratch, flops, *operands):
    placed = len(operands)
    everything = list(operands) + background.operands
    arrays = [item[0] if isinstance(item, tuple) else item for item in everything]
    shapes = [
        (array.shape[1:] if isinstance(item, tuple) else array.shape, array.dtype)
        for array, item in zip(arrays, everything)
    ]
    results = list(outs) + background.outs
    copies_in = [
        is_large(*shape) and not (background.quad and at >= placed)
        for at, shape in enumerate(shapes)
    ]
    raw_in = [background.quad and at >= placed for at in range(len(shapes))]
    raw_out = [at >= len(outs) + background.staged for at in range(len(results))]
    copies_out = [is_large(*shape) and not raw for shape, raw in zip(results, raw_out)]
    staged = [shape for shape, copied in zip(shapes + results, copies_in + copies_out) if copied]

    def kernel(*refs):
        refs = list(refs)

        def take(count):
            taken = refs[:count]
            del refs[:count]
            return taken

        sources, targets = take(len(shapes)), take(len(results))
        body_scratch, more_scratch = take(len(scratch)), take(len(background.scratch))
        held = take(len(staged))
        sems, local = take(2)
        wire = Wire(sems)
        number = 0
        for at, item in enumerate(everything):
            if copies_in[at]:
                source = sources[at].at[item[1]] if isinstance(item, tuple) else sources[at]
                ref = held[number]
                copy = pltpu.make_async_copy(source, ref, local.at[number])
                sources[at] = Staged(ref, copy, False)
                sources[at].begin()
                number += 1
        for at in range(len(results)):
            if copies_out[at]:
                ref = held[number]
                copy = pltpu.make_async_copy(ref, targets[at], local.at[number])
                targets[at] = Staged(ref, copy, True)
                number += 1
        steps = []
        if background.steps is None:
            wire.barrier()
        else:
            if background.quad:
                place = Quad()
                quad_barrier(wire, place, *([place.across] if background.across else []))
            else:
                place = Line()
                wide_barrier(wire, place, *([Quad().across] if background.across else []))
            steps = [
                background.steps(
                    wire, place, sources[placed:], targets[len(outs) :], more_scratch
                )
            ]

        poll = Poll(steps)
        body(wire, poll, *sources[:placed], *targets[: len(outs)], *body_scratch)
        while steps:
            poll()
        for ref in sources:
            ready(ref)
        for ref in targets:
            if isinstance(ref, Staged) and not ref.begun:
                ref.begin()
        wire.finish()
        for ref in targets:
            ready(ref)

    kernel.__name__ = body.__name__ if background.steps is None else body.__name__ + "_wide"

    def spec(apart):
        return pl.BlockSpec(memory_space=pl.ANY if apart else pltpu.VMEM)

    found = pl.pallas_call(
        kernel,
        in_specs=[spec(raw or copied) for raw, copied in zip(raw_in, copies_in)],
        out_specs=[spec(raw or copied) for raw, copied in zip(raw_out, copies_out)],
        out_shape=shaped(*results),
        scratch_shapes=list(scratch)
        + background.scratch
        + [pltpu.VMEM(*shape) for shape in staged]
        + [pltpu.SemaphoreType.DMA((background.semaphores,))]
        + [pltpu.SemaphoreType.DMA((max(len(staged), 1),))],
        compiler_params=pltpu.CompilerParams(
            collective_id=background.number, has_side_effects=True, vmem_limit_bytes=56 * 2**20
        ),
        cost_estimate=pl.CostEstimate(flops=flops, bytes_accessed=2**24, transcendentals=0),
        name=kernel.__name__,
    )(*arrays)
    return found[: len(outs)], found[len(outs) :]


def attend_half_body(
    wire, poll,
    x_ref, gain_ref, shift_ref, cos_ref, sin_ref, start_ref, w_qkv_ref, w_out_ref,
    a_ref, q_ref, k_ref, v_ref, o_ref, lse_ref, z_ref, h_ref, c_ref,
    held, own,
):
    size = x_ref.shape[0]
    gather = Gather(wire, a_ref, size)
    poll.enter()
    for part in range(2):
        rows = pl.ds(part * (size // 2), size // 2)
        ready_part(x_ref, part)
        normed = layer_norm(x_ref[rows].astype(F32), gain_ref[0:1], shift_ref[0:1])
        a_ref[block_rows(wire.at, size, part, 2)] = normed.astype(BF16)
        gather.push(part)
        poll()
    width = q_ref.shape[1]

    def project(block):
        rows = block_rows(block, size)
        projected = dot(a_ref[rows], w_qkv_ref[...])
        cosine, sine = cos_ref[rows], sin_ref[rows]
        q_ref[rows] = turn(projected[:, :width], cosine, sine).astype(BF16)
        k_ref[rows] = turn(projected[:, width : 2 * width], cosine, sine).astype(BF16)
        v_ref[rows] = projected[:, 2 * width :].astype(BF16)

    ready(w_qkv_ref, cos_ref, sin_ref)
    project(wire.at)
    gather.wait_near()
    project(wire.near)
    gather.relay(0)
    gather.relay(1)
    project(wire.far)
    gather.wait_diagonal(0)
    gather.wait_diagonal(1)
    project(wire.diagonal)

    done(a_ref, q_ref, k_ref, v_ref)
    poll()
    ready(start_ref, w_out_ref)
    scatter = Scatter(wire, held, own, 1)
    for block in (3, 1, 2, 0):
        rows = slice(block * size, (block + 1) * size)
        reach = (block + 1) * size
        key = lax.broadcasted_iota(jnp.int32, (size, reach), 1)
        query = lax.broadcasted_iota(jnp.int32, (size, reach), 0) + block * size
        allowed = (key >= start_ref[rows, :]) & (key <= query)
        mixed, logs = [], jnp.zeros((size, 128), F32)
        lane = lax.broadcasted_iota(jnp.int32, (size, 128), 1)
        for head in range(width // HD):
            lanes = slice(head * HD, (head + 1) * HD)
            scores = dot_t(q_ref[rows, lanes] * SCALE, k_ref[:reach, lanes])
            scores = jnp.where(allowed, scores, MASKED)
            summit = jnp.max(scores, axis=1, keepdims=True)
            weights = jnp.exp(scores - summit)
            total = jnp.sum(weights, axis=1, keepdims=True)
            chances = (weights * (1.0 / total)).astype(BF16)
            mixed.append(dot(chances, v_ref[:reach, lanes]))
            logs = jnp.where(lane == head, summit + jnp.log(total), logs)
        o_ref[rows, :] = jnp.concatenate(mixed, axis=1).astype(BF16)
        lse_ref[:, rows] = logs.T[: lse_ref.shape[0]]
        partial = dot(o_ref[rows, :], w_out_ref[...])

        if block == 2:
            poll()

        @pl.when(wire.diagonal == block)
        def _():
            scatter.put_diagonal(partial, 0)

        @pl.when(wire.far == block)
        def _():
            scatter.put_far(partial, 0)

        @pl.when(wire.near == block)
        def _():
            scatter.put_near(partial)

        @pl.when(wire.at == block)
        def _():
            own[...] = partial

    done(o_ref, lse_ref)
    poll()
    branch = scatter.total()
    z_ref[...] = branch
    middle = x_ref[...].astype(F32) + layer_norm(branch, gain_ref[1:2], shift_ref[1:2])
    h_ref[...] = middle
    c_ref[...] = layer_norm(middle, gain_ref[2:3], shift_ref[2:3]).astype(BF16)
    done(z_ref, h_ref)
    poll.leave()


def attend_half(background, resid, gains, shifts, cosine, sine, start, w_qkv, w_out):
    size, width = resid.shape
    length, part = cosine.shape[0], w_out.shape[0]
    return call_with(
        attend_half_body,
        background,
        [((length, width), BF16)]
        + [((length, part), BF16)] * 4
        + [((8, length), F32), ((size, width), F32), ((size, width), F32), ((size, width), BF16)],
        [pltpu.VMEM((6, size, width), BF16), pltpu.VMEM((size, width), F32)],
        8 * length * width * part + 4 * length * length * part,
        resid, gains, shifts, cosine, sine, start, w_qkv, w_out,
    )


def feed_half_body(
    wire, poll,
    c_ref, h_ref, gain_ref, shift_ref, w_up_ref, b_up_ref, w_down_ref,
    inner_ref, e_ref, d_ref, w_ref, y_ref,
    held, own,
):
    size = c_ref.shape[0]
    half = size // 2
    ready(c_ref)
    gather = Gather(wire, inner_ref, size)
    poll.enter()
    for part in range(2):
        inner_ref[block_rows(wire.at, size, part, 2)] = c_ref[pl.ds(part * half, half)]
        gather.push(part)
    poll()
    scatter = Scatter(wire, held, own, 2)

    def feed(cuts):
        inner = jnp.concatenate([inner_ref[cut] for cut in cuts])
        hidden = dot(inner, w_up_ref[...]) + b_up_ref[...]
        below = 0.5 + 0.5 * lax.erf(hidden * (0.5**0.5))
        density = jnp.exp(-0.5 * hidden * hidden) * ((2.0 * math.pi) ** -0.5)
        active = (hidden * below).astype(BF16)
        slope = (below + hidden * density).astype(BF16)
        for at, cut in enumerate(cuts):
            step = inner.shape[0] // len(cuts)
            e_ref[cut] = active[at * step : (at + 1) * step]
            d_ref[cut] = slope[at * step : (at + 1) * step]
        return dot(active, w_down_ref[...])

    ready(w_up_ref, b_up_ref, w_down_ref)
    own[...] = feed([block_rows(wire.at, size)])
    gather.wait_near()
    scatter.put_near(feed([block_rows(wire.near, size)]))
    for part in range(2):
        gather.relay(part)
        gather.wait_diagonal(part)
        partial = feed(
            [block_rows(wire.diagonal, size, part, 2), block_rows(wire.far, size, part, 2)]
        )
        scatter.put_diagonal(partial[:half], part)
        scatter.put_far(partial[half:], part)
    done(inner_ref, e_ref, d_ref)
    ready(h_ref)
    second = scatter.total()
    w_ref[...] = second
    result = h_ref[...] + layer_norm(second, gain_ref[3:4], shift_ref[3:4])
    y_ref[...] = result.astype(BF16)
    done(w_ref, y_ref)
    poll.leave()


def feed_half(number, inner, middle, gains, shifts, w_up, b_up, w_down):
    size, width = inner.shape
    length, hidden = 4 * size, b_up.shape[1]
    return call_with(
        feed_half_body,
        Background(number),
        [((length, width), BF16)]
        + [((length, hidden), BF16)] * 2
        + [((size, width), F32), ((size, width), BF16)],
        [pltpu.VMEM((6, size, width), BF16), pltpu.VMEM((size, width), F32)],
        4 * length * width * hidden,
        inner, middle, gains, shifts, w_up, b_up, w_down,
    )[0]


def feed_back_body(
    wire, poll,
    g_ref, w_ref, h_ref, z_ref, gain_ref, inner_ref, e_ref, d_ref, w_up_ref, w_down_ref,
    grad_down_ref, grad_up_ref, grad_b_ref, norms_ref, dh_ref, dz_ref,
    second, hidden, held, own,
):
    size = g_ref.shape[0]
    half = size // 2
    ready(g_ref, w_ref)
    gather = Gather(wire, second, size)
    norms = [jnp.zeros((1, g_ref.shape[1]), F32)] * 2
    for part in range(2):
        rows = pl.ds(part * half, half)
        grad, gain, shift = layer_norm_back(w_ref[rows], g_ref[rows].astype(F32), gain_ref[3:4])
        if part == 0:
            poll.enter()
        second[block_rows(wire.at, size, part, 2)] = grad.astype(BF16)
        gather.push(part)
        norms = [norms[0] + gain, norms[1] + shift]
    norms_ref[3:4] = norms[0]
    norms_ref[7:8] = norms[1]
    norms_ref[0:1] = jnp.zeros_like(norms[0])
    norms_ref[4:5] = jnp.zeros_like(norms[0])
    scatter = Scatter(wire, held, own, 2)
    poll()

    def feed(cuts, first=False):
        grad = jnp.concatenate([second[cut] for cut in cuts])
        slope = jnp.concatenate([d_ref[cut] for cut in cuts]).astype(F32)
        grad = (slope * dot_t(grad, w_down_ref[...])).astype(BF16)
        for at, cut in enumerate(cuts):
            step = grad.shape[0] // len(cuts)
            hidden[cut] = grad[at * step : (at + 1) * step]
        bias = jnp.sum(grad.astype(F32), axis=0, keepdims=True)
        grad_b_ref[...] = bias if first else grad_b_ref[...] + bias
        return dot_t(grad, w_up_ref[...])

    ready(d_ref, w_down_ref, w_up_ref)
    own[...] = feed([block_rows(wire.at, size)], True)
    poll()
    gather.wait_near()
    scatter.put_near(feed([block_rows(wire.near, size)]))
    poll()
    for part in range(2):
        poll(2)
        gather.relay(part)
        gather.wait_diagonal(part)
        partial = feed(
            [block_rows(wire.diagonal, size, part, 2), block_rows(wire.far, size, part, 2)]
        )
        scatter.put_diagonal(partial[:half], part)
        scatter.put_far(partial[half:], part)
        poll()
    poll.before("feed")
    ready(e_ref, inner_ref)
    for at in range(0, inner_ref.shape[1], 256):
        cut = slice(at, at + 256)
        grad_up_ref[cut, :] = t_dot(inner_ref[:, cut], hidden[...]).astype(BF16)
        poll()
    done(grad_up_ref)
    poll.graded("up")
    for at in range(0, e_ref.shape[1], 256):
        cut = slice(at, at + 256)
        grad_down_ref[cut, :] = t_dot(e_ref[:, cut], second[...]).astype(BF16)
        poll()
    done(grad_down_ref)
    poll.graded("down")
    poll(3)
    ready(h_ref, z_ref)
    grad, gain, shift = layer_norm_back(h_ref[...], scatter.total(), gain_ref[2:3])
    norms_ref[2:3] = gain
    norms_ref[6:7] = shift
    grad = g_ref[...].astype(F32) + grad
    dh_ref[...] = grad
    grad, gain, shift = layer_norm_back(z_ref[...], grad, gain_ref[1:2])
    norms_ref[1:2] = gain
    norms_ref[5:6] = shift
    dz_ref[...] = grad.astype(BF16)
    poll.leave()


def feed_back(background, grad, second, middle, branch, gains, inner, active, slope, w_up, w_down):
    size, width = grad.shape
    length, hidden = 4 * size, active.shape[1]
    return call_with(
        feed_back_body,
        background,
        [
            ((hidden, width), BF16),
            ((width, hidden), BF16),
            ((1, hidden), F32),
            ((8, width), F32),
            ((size, width), F32),
            ((size, width), BF16),
        ],
        [
            pltpu.VMEM((length, width), BF16),
            pltpu.VMEM((length, hidden), BF16),
            pltpu.VMEM((6, size, width), BF16),
            pltpu.VMEM((size, width), F32),
        ],
        8 * length * width * hidden,
        grad, second, middle, branch, gains, inner, active, slope, w_up, w_down,
    )


def attend_back_body(
    wire, poll,
    dz_ref, dh_ref, x_ref, gain_ref, a_ref, q_ref, k_ref, v_ref, o_ref, lse_ref, start_ref,
    cos_ref, sin_ref, w_qkv_ref, w_out_ref,
    grad_qkv_ref, grad_out_ref, norms_ref, dx_ref,
    branch, mixture, projected, dk, dv, held, own,
):
    size = dz_ref.shape[0]
    length, width = q_ref.shape
    half = size // 2
    ready(dz_ref)
    gather = Gather(wire, branch, size)
    poll.enter()
    for part in range(2):
        branch[block_rows(wire.at, size, part, 2)] = dz_ref[pl.ds(part * half, half)]
        gather.push(part)

    def unmix(block):
        rows = block_rows(block, size)
        mixture[rows] = dot_t(branch[rows], w_out_ref[...]).astype(BF16)

    dk[...] = jnp.zeros_like(dk)
    dv[...] = jnp.zeros_like(dv)
    poll()
    ready(w_out_ref)
    unmix(wire.at)
    gather.wait_near()
    unmix(wire.near)
    poll()
    poll(2)
    gather.relay(0)
    poll(2)
    gather.relay(1)
    unmix(wire.far)
    gather.wait_diagonal(0)
    gather.wait_diagonal(1)
    unmix(wire.diagonal)
    ready(o_ref, q_ref, k_ref, v_ref, lse_ref, start_ref, cos_ref, sin_ref, w_qkv_ref)
    poll.before("attend")
    grad_out_ref[...] = t_dot(o_ref[...], branch[...]).astype(BF16)
    done(grad_out_ref)
    poll()

    pick_head = (
        lax.broadcasted_iota(jnp.int32, (8, width), 1) // HD
        == lax.broadcasted_iota(jnp.int32, (8, width), 0)
    ).astype(F32)
    for block in range(length // size):
        rows = slice(block * size, (block + 1) * size)
        reach = (block + 1) * size
        key = lax.broadcasted_iota(jnp.int32, (reach, size), 0)
        query = lax.broadcasted_iota(jnp.int32, (reach, size), 1) + block * size
        allowed = (key >= start_ref[:, rows]) & (key <= query)
        inner = lax.dot_general(
            pick_head,
            mixture[rows].astype(F32) * o_ref[rows].astype(F32),
            (((1,), (1,)), ((), ())),
            precision=lax.Precision.HIGHEST,
            preferred_element_type=F32,
        )
        dqs, dks, dvs = [], [], []
        for head in range(width // HD):
            lanes = slice(head * HD, (head + 1) * HD)
            k_head, g_head = k_ref[:reach, lanes], mixture[rows, lanes]
            q_head = q_ref[rows, lanes] * SCALE
            scores = dot_t(k_head, q_head) - lse_ref[head : head + 1, rows]
            chances = jnp.exp(jnp.where(allowed, scores, MASKED))
            grad_prob = dot_t(v_ref[:reach, lanes], g_head)
            grad_score = (chances * (grad_prob - inner[head : head + 1])).astype(BF16)
            dvs.append(dot(chances.astype(BF16), g_head))
            dks.append(dot(grad_score, q_head))
            dqs.append(t_dot(grad_score, k_head) * SCALE)
            if block > 0 and head % 2 == 1:
                poll()
        dq = jnp.concatenate(dqs, axis=1)
        projected[rows, :width] = turn(dq, cos_ref[rows], -sin_ref[rows]).astype(BF16)
        dk[:reach, :] += jnp.concatenate(dks, axis=1)
        dv[:reach, :] += jnp.concatenate(dvs, axis=1)
    for block in range(length // size):
        rows = slice(block * size, (block + 1) * size)
        turned = turn(dk[rows], cos_ref[rows], -sin_ref[rows])
        projected[rows, width : 2 * width] = turned.astype(BF16)
        projected[rows, 2 * width :] = dv[rows].astype(BF16)

    scatter = Scatter(wire, held, own, 2)

    def unproject(cut):
        return dot_t(projected[cut], w_qkv_ref[...])

    partial = unproject(block_rows(wire.diagonal, size))
    scatter.put_diagonal(partial[:half], 0)
    scatter.put_diagonal(partial[half:], 1)
    poll()
    partial = unproject(block_rows(wire.far, size))
    scatter.put_far(partial[:half], 0)
    scatter.put_far(partial[half:], 1)
    poll()
    scatter.put_near(unproject(block_rows(wire.near, size)))
    own[...] = unproject(block_rows(wire.at, size))
    ready(a_ref)
    for at in range(0, a_ref.shape[1], 256):
        cut = slice(at, at + 256)
        grad_qkv_ref[cut, :] = t_dot(a_ref[:, cut], projected[...]).astype(BF16)
        poll()
    done(grad_qkv_ref)
    poll.graded("qkv")
    poll(3)
    ready(x_ref, dh_ref)
    grad, gain, shift = layer_norm_back(x_ref[...].astype(F32), scatter.total(), gain_ref[0:1])
    norms_ref[...] = jnp.zeros_like(norms_ref)
    norms_ref[0:1] = gain
    norms_ref[4:5] = shift
    dx_ref[...] = (dh_ref[...] + grad).astype(BF16)
    poll.leave()


def attend_back(
    background,
    grad_branch, grad_middle, resid, gains, normed, query, keys, values, mixture, logs, start,
    cosine, sine, w_qkv, w_out,
):
    size, width = resid.shape
    length, part = query.shape
    return call_with(
        attend_back_body,
        background,
        [
            ((width, 3 * part), BF16),
            ((part, width), BF16),
            ((8, width), F32),
            ((size, width), BF16),
        ],
        [
            pltpu.VMEM((length, width), BF16),
            pltpu.VMEM((length, part), BF16),
            pltpu.VMEM((length, 3 * part), BF16),
            pltpu.VMEM((length, part), F32),
            pltpu.VMEM((length, part), F32),
            pltpu.VMEM((6, size, width), BF16),
            pltpu.VMEM((size, width), F32),
        ],
        16 * length * width * part + 10 * length * length * part,
        grad_branch, grad_middle, resid, gains, normed, query, keys, values, mixture, logs,
        start, cosine, sine, w_qkv, w_out,
    )


CHUNK = 64
LATE = 2


class Line:
    def __init__(self):
        at = lax.axis_index("wide")
        self.pair = lax.rem(at, 2)
        self.turn = at // 2
        self.upper = self.turn // 3
        self.up = {"wide": lax.rem(self.turn + 1, 4) * 2 + self.pair}
        self.down = {"wide": lax.rem(self.turn + 3, 4) * 2 + self.pair}
        self.side = {"wide": at + 1 - 2 * self.pair}
        self.bottom, self.top = self.turn == 0, self.turn == 3
        self.at_end = self.upper * 3 == self.turn
        self.inside = jnp.logical_not(self.at_end)
        not_bottom, not_top = self.turn > 0, self.turn < 3
        self.ways = (
            (self.up, self.bottom, self.top, not_bottom, not_top),
            (self.down, self.top, self.bottom, not_top, not_bottom),
        )

    def steps(self, chunks):
        for at in range(len(chunks) + 3 * LATE):
            for turn in range(4):

                @pl.when(self.turn == turn)
                def _():
                    for way, hops in sorted(((0, turn), (1, 3 - turn)), key=lambda item: item[1]):
                        chunk = at - hops * LATE
                        if not 0 <= chunk < len(chunks):
                            continue
                        if hops == 0:
                            if chunk >= 2:
                                chunks[chunk - 2](way, "sent")
                            chunks[chunk](way, "first")
                        else:
                            chunks[chunk](way, "last" if hops == 3 else "inner")

            yield


def span(start, size):
    return pl.ds(pl.multiple_of(start, 16), size)


class Fold:
    def __init__(self, wire, line, ref, by_side, into, across, final=None):
        self.wire, self.line, self.ref, self.by_side = wire, line, ref, by_side
        self.into, self.across, self.final = into, across, final
        rows = ref.shape[0]
        self.length = rows // 4 if by_side else rows // 2
        self.base = line.pair * (rows // 2) if by_side else 0
        self.count = self.length // CHUNK
        self.copies, self.sides = [], []
        for way, (peer, _, _, _, inner) in enumerate(line.ways):
            cuts = [into.at[way, pl.ds(c * CHUNK, CHUNK)] for c in range(self.count)]
            self.copies.append([wire.copy(cut, cut, peer, inner) for cut in cuts])
        self.pairs = []
        if final is None:
            for cut in (pl.ds(c * CHUNK, CHUNK) for c in range(self.count)):
                source = into.at[1 - line.upper, cut]
                self.pairs.append(wire.copy(source, across.at[cut], line.side, line.at_end))

    @staticmethod
    def scratch(rows, columns, by_side, streams=False):
        return [
            pltpu.VMEM((2, rows // 4 if by_side else rows // 2, columns), BF16),
            pltpu.VMEM((rows // 2 if by_side or streams else rows // 4, columns), BF16),
        ]

    def place(self, way, chunk):
        return (self.length if way == 0 else 0) + chunk * CHUNK

    def start(self):
        line = self.line
        if self.by_side:
            away = (1 - line.pair) * (self.ref.shape[0] // 2)
            for chunk in range(self.count):
                pair = []
                for way in (0, 1):
                    place = self.place(way, chunk)
                    pair.append(
                        self.wire.send(
                            self.ref.at[span(away + place, CHUNK)],
                            self.across.at[pl.ds(place, CHUNK)],
                            line.side,
                        )
                    )
                self.sides.append(pair)

    def step(self, chunk, way, role):
        place = self.place(way, chunk)
        cut = pl.ds(chunk * CHUNK, CHUNK)
        made = self.copies[way][chunk]
        if role == "sent":
            made.wait_send_early(self.line.inside)
            return
        if self.by_side:
            self.sides[chunk][way].wait_recv()

        def own():
            total = self.ref[span(self.base + place, CHUNK)].astype(F32)
            if self.by_side:
                total = total + self.across[pl.ds(place, CHUNK)].astype(F32)
            return total

        if role == "first":
            if self.by_side:
                self.into[way, cut] = own().astype(BF16)
                made.start()
            else:
                made.start_from(self.ref.at[pl.ds(place, CHUNK)])
            return
        made.wait_recv()
        self.into[way, cut] = (own() + self.into[way, cut].astype(F32)).astype(BF16)
        if role == "inner":
            made.start()
        elif self.pairs:
            self.pairs[chunk].start()

    def chunks(self):
        return [functools.partial(self.step, chunk) for chunk in range(self.count)]

    def start_side(self):
        line = self.line
        half = self.length // 2
        source = self.into.at[1 - line.upper, span((1 - line.pair) * half, half)]
        self.side = self.wire.copy(source, self.across, line.side, line.at_end)

        @pl.when(line.at_end)
        def _():
            self.side.start()

    def end(self):
        line = self.line
        size = self.final.shape[0]

        @pl.when(line.at_end)
        def _():
            if not self.by_side:
                self.side.wait_recv()
            for at in range(0, size, CHUNK):
                if self.by_side:
                    self.final[pl.ds(at, CHUNK)] = self.into[1 - line.upper, pl.ds(at, CHUNK)]
                else:
                    own = self.into[1 - line.upper, span(line.pair * size + at, CHUNK)]
                    total = own.astype(F32) + self.across[pl.ds(at, CHUNK)].astype(F32)
                    self.final[pl.ds(at, CHUNK)] = total.astype(BF16)

        self.settle()
        if not self.by_side:
            self.side.settle()

    def settle(self):
        for made in sum(self.copies + self.sides, []):
            made.settle()


class Spread:
    def __init__(self, wire, line, view, rows, by_side):
        self.wire, self.line, self.view, self.by_side = wire, line, view, by_side
        pair, upper = line.pair, line.upper
        self.quarter = rows // 4
        if by_side:
            self.length, self.base = rows // 4, pair * (rows // 2)
            self.mine = self.base + upper * self.quarter
        else:
            self.length, self.base = rows // 2, 0
            self.mine = upper * (rows // 2) + pair * self.quarter
        self.count = self.length // CHUNK
        self.copies = []
        for way, (peer, _, _, _, inner) in enumerate(line.ways):
            cuts = [self.chunk(way, c) for c in range(self.count)]
            self.copies.append([wire.copy(cut, cut, peer, inner) for cut in cuts])
        self.sides = []
        if not by_side:
            self.side = wire.copy(self.own(), self.own(), line.side, line.at_end)

    def own(self):
        return self.view(span(self.mine, self.quarter))

    def chunk(self, way, chunk):
        start = self.base + (0 if way == 0 else self.length) + chunk * CHUNK
        return self.view(span(start, CHUNK))

    def start(self):
        if not self.by_side:

            @pl.when(self.line.at_end)
            def _():
                self.side.start()

    def step(self, chunk, way, role):
        made = self.copies[way][chunk]
        if role == "sent":
            made.wait_send_early(self.line.inside)
            return
        if role == "first":
            if not self.by_side and chunk == 0:
                self.side.wait_recv()
            made.start()
        else:
            made.wait_recv()
            if role == "inner":
                made.start()
        if self.by_side:
            self.sides[chunk][way].start()

    def chunks(self):
        if self.by_side:
            self.sides = []
            for chunk in range(self.count):
                cuts = [self.chunk(way, chunk) for way in (0, 1)]
                self.sides.append([self.wire.copy(cut, cut, self.line.side) for cut in cuts])
        return [functools.partial(self.step, chunk) for chunk in range(self.count)]

    def end(self):
        for pair in self.sides:
            for made in pair:
                made.wait_recv()


class Stream(Spread):
    def __init__(self, wire, line, view, rows, fold):
        super().__init__(wire, line, view, rows, False)
        self.fold, self.own_copies = fold, []
        wire.made.remove(self.side)
        for way in (0, 1):
            self.own_copies.append([])
            for chunk in range(self.count):
                source = fold.across.at[pl.ds(chunk * CHUNK, CHUNK)]
                copy = pltpu.make_async_copy(source, self.chunk(way, chunk), wire.sems.at[wire.used])
                wire.used += 1
                self.own_copies[way].append(copy)

    def start(self):
        pass

    def step(self, chunk, way, role):
        if role != "first":
            super().step(chunk, way, role)
            return
        fold, cut = self.fold, pl.ds(chunk * CHUNK, CHUNK)
        fold.pairs[chunk].wait_recv()
        total = fold.into[1 - way, cut].astype(F32) + fold.across[cut].astype(F32)
        fold.across[cut] = total.astype(BF16)
        self.copies[way][chunk].start_from(fold.across.at[cut])
        self.own_copies[way][chunk].start()

    def settle(self):
        for made in sum(self.copies, []) + self.fold.pairs:
            made.settle()
        for way, copies in enumerate(self.own_copies):

            @pl.when(self.line.ways[way][1])
            def _():
                for copy in copies:
                    copy.wait()


class Sequence:
    def __init__(self, line):
        self.line, self.chunks, self.actions = line, [], {}

    def add(self, *lists):
        total = max(len(chunks) for chunks in lists)
        placed = [
            ((at + 0.5) * total / len(chunks), which, chunk)
            for which, chunks in enumerate(lists)
            for at, chunk in enumerate(chunks)
        ]
        self.chunks += [chunk for _, _, chunk in sorted(placed, key=lambda item: item[:2])]
        return self

    def before_next(self, *actions):
        self.actions.setdefault(len(self.chunks) - 1, []).extend(actions)

    def after(self, chunk, *actions):
        self.actions.setdefault(self.chunks.index(chunk) + 3 * LATE, []).extend(actions)

    def steps(self):
        for action in self.actions.get(-1, []):
            action()
        for at, _ in enumerate(self.line.steps(self.chunks)):
            for action in self.actions.get(at, []):
                action()
            yield


def small_steps(wire, line, norms_ref, bias_ref, narrow_in, sums, side_in, slots, total_ref):
    part = total_ref.shape[1]
    made = []

    def columns(device):
        return pl.ds(pl.multiple_of(device * part, part), part)

    for peer in (wire.near, wire.far, wire.diagonal):
        made.append(
            wire.send(norms_ref.at[:, columns(peer)], narrow_in.at[wire.at], {"narrow": peer})
        )
    narrow_in[wire.at] = norms_ref[:, columns(wire.at)]
    yield
    for copy in made:
        copy.wait_recv()
    total = narrow_in[0] + narrow_in[1] + narrow_in[2] + narrow_in[3]
    lines = [bias_ref[:, at * part : (at + 1) * part] for at in range(4)]
    sums[...] = jnp.concatenate([total] + lines + [jnp.zeros((4, part), F32)], axis=0)
    side = wire.send(sums, side_in, line.side)
    yield
    side.wait_recv()
    slots[line.turn] = sums[...] + side_in[...]
    for step in range(3):
        sends = []
        for way, peer in enumerate((line.up, line.down)):
            place = line.turn if way == 0 else 3 - line.turn
            goes = (place >= step) & (place < 3)
            comes = place > step
            slot = slots.at[lax.rem(line.turn + (4 - step if way == 0 else step), 4)]
            copy = wire.copy(slot, slot, peer, goes)
            sends.append((copy, goes, comes))

            @pl.when(goes)
            def _():
                copy.start()

        yield
        for copy, goes, comes in sends:

            @pl.when(comes)
            def _():
                copy.wait_recv()

    total_ref[...] = slots[0] + slots[1] + slots[2] + slots[3]


def home(wire, line, down, out, qkv, full_down, full_out, full_qkv):
    part = (full_out if full_down is None else full_down).shape[2]
    made = []
    at = wire.at

    def columns(device):
        return pl.ds(pl.multiple_of(device * part, part), part)

    for final, full, by_side in ((down, full_down, True), (out, full_out, False)):
        if final is None:
            continue
        quarter = final.shape[0]
        if by_side:
            mine = line.pair * (2 * quarter) + line.upper * quarter
        else:
            mine = line.upper * (2 * quarter) + line.pair * quarter
        slot = full.at[at, span(mine, quarter)]
        for peer in (wire.diagonal, wire.far, wire.near):
            made.append(
                wire.copy(final.at[:, columns(peer)], slot, {"narrow": peer}, line.at_end)
            )

        @pl.when(line.at_end)
        def _():
            wire.move(final.at[:, columns(at)], slot)

    if qkv is not None:
        quarter = qkv.shape[0]
        rows = span(line.pair * (2 * quarter) + line.upper * quarter, quarter)
        odd, upper = lax.rem(at, 2), at // 2
        far_slot = columns(2 - 2 * odd)
        made.append(
            wire.copy(
                qkv.at[:, columns(2 - 2 * upper)], full_qkv.at[rows, far_slot],
                {"narrow": wire.far}, line.at_end,
            )
        )
        made.append(
            wire.copy(
                qkv.at[:, columns(1 - odd + upper)], full_qkv.at[rows, columns(1)],
                {"narrow": wire.near}, line.at_end,
            )
        )

        @pl.when(line.at_end)
        def _():
            wire.move(qkv.at[:, columns((at + 1) // 2)], full_qkv.at[rows, columns(2 * odd)])

    @pl.when(line.at_end)
    def _():
        for copy in made:
            copy.start()

    def wait():
        @pl.when(line.at_end)
        def _():
            for copy in made:
                copy.wait_recv()

    return wait


def wide_barrier(wire, line, *others):
    barrier = pltpu.get_barrier_semaphore()

    def greet(peer):
        pl.semaphore_signal(barrier, inc=1, device_id=peer, device_id_type=MESH)

    for peer in (line.side,) + others:
        greet(peer)
    for peer in (wire.near, wire.far, wire.diagonal):
        greet({"narrow": peer})

    @pl.when(line.turn < 3)
    def _():
        greet(line.up)

    @pl.when(line.turn > 0)
    def _():
        greet(line.down)

    @pl.when(line.at_end)
    def _():
        pl.semaphore_wait(barrier, 5 + len(others))

    @pl.when(line.inside)
    def _():
        pl.semaphore_wait(barrier, 6 + len(others))


def run(*steps):
    steps = list(steps)
    while steps:
        for at in list(steps):
            if next(at, "end") == "end":
                steps.remove(at)


def fold_pair(wire, line, refs, finals, scratch):
    return (
        Fold(wire, line, refs[0], False, *scratch[0:2], finals[0]),
        Fold(wire, line, refs[1], True, *scratch[2:4], finals[1]),
    )


def rows_of(ref):
    return lambda rows: ref.at[rows]


def spread_down(wire, line, full_down):
    return Spread(wire, line, lambda rows: full_down.at[:, rows], full_down.shape[1], True)


def spread_attend(wire, line, full_out, full_qkv):
    return (
        Spread(wire, line, lambda rows: full_out.at[:, rows], full_out.shape[1], False),
        Spread(wire, line, lambda rows: full_qkv.at[rows], full_qkv.shape[0], True),
    )


def swap_across(wire, source, target, first_sends):
    quad = Quad()
    second = jnp.logical_not(quad.first)
    sends, takes = (quad.first, second) if first_sends else (second, quad.first)
    made = wire.copy(source, target, quad.across, sends)

    @pl.when(sends)
    def _():
        made.start()

    yield

    @pl.when(takes)
    def _():
        made.wait_recv()


class Flow(Poll):
    def __init__(self, wire, wide_wire, line, free):
        super().__init__([])
        self.wire, self.wide_wire, self.line, self.free = wire, wide_wire, line, free
        self.sequence, self.done, self.limit, self.limits = Sequence(line), 0, 0, {}
        self.entered = self.last = False
        self.smalls, self.ticks = [], 0
        self.walk, self.on_grade = None, {}

    def __call__(self, times=1):
        for _ in range(times):
            if self.walk is not None and self.done < self.limit:
                self.done += 1
                if next(self.walk, "end") == "end":
                    self.walk = None
            self.ticks += 1
            if self.ticks % 4 == 0 or self.walk is None:
                for steps in list(self.smalls):
                    if next(steps, "end") == "end":
                        self.smalls.remove(steps)

    def until(self, count):
        while self.walk is not None and self.done < min(count, self.limit):
            self()

    def open(self, limit):
        self.limit = limit

    def graded(self, name):
        for action in self.on_grade.pop(name, []):
            action()

    def before(self, what):
        self.until(self.limits.get(what, 0))

    def enter(self):
        if self.entered:
            pl.semaphore_wait(self.free.at[0], 1)
            pl.semaphore_wait(self.free.at[1], 1)
        self.entered = True

    def leave(self):
        self.wire.finish()
        self.wire.made = []
        if self.last:
            return
        for at, peer in enumerate((self.wire.near, self.wire.far)):
            pl.semaphore_signal(
                self.free.at[at], inc=1, device_id={"narrow": peer}, device_id_type=MESH
            )

    def peers(self):
        line = self.line
        not_bottom, not_top = line.ways[0][3], line.ways[1][3]
        return (
            (2, line.up, not_top, not_bottom),
            (3, line.down, not_bottom, not_top),
            (4, line.side, None, None),
        )

    def greet(self):
        for at, peer, sends, _ in self.peers():
            signal = functools.partial(
                pl.semaphore_signal, self.free.at[at], inc=1, device_id=peer, device_id_type=MESH
            )
            signal() if sends is None else pl.when(sends)(lambda signal=signal: signal())

    def greeted(self):
        for at, _, _, comes in self.peers():
            wait = functools.partial(pl.semaphore_wait, self.free.at[at], 1)
            wait() if comes is None else pl.when(comes)(lambda wait=wait: wait())


FEED_NAMES = ("w", "h", "z", "inner", "e", "d", "down")
ATTEND_NAMES = ("x", "a", "q", "k", "v", "o", "qkv", "out")


def backward_kernel(shape, *refs):
    size, length, width, hidden_count, part = shape
    refs = list(refs)

    def take(count):
        taken = refs[:count]
        del refs[:count]
        return taken

    dy, result, up, cosine, sine, start = take(6)
    gains, logs, large = [], [], []
    for _ in range(2):
        gain, log = take(2)
        gains.append(gain)
        logs.append(log)
        large.append(dict(zip(FEED_NAMES + ATTEND_NAMES, take(15))))
    dx_out, grad_came, result_came = take(3)
    totals = take(2)
    fulls = [dict(zip(("up", "down", "out", "qkv"), take(4))) for _ in range(2)]
    held_names = ("g", "up", "cos", "sin") + FEED_NAMES + ATTEND_NAMES
    buffers = dict(zip(held_names, take(len(held_names))))
    second, hidden, mixture, projected, dk, dv, held, own, dh, dz, dx = take(11)
    grad_up, grad_down, grad_out, grad_qkv = take(4)
    feed_scratch, attend_scratch = take(4), take(4)
    finals = [dict(zip(("down", "out", "qkv"), take(3))) for _ in range(2)]
    small = [take(4) for _ in range(2)]
    norms = [take(2) for _ in range(2)]
    biases = take(2)
    sems, wide_sems, local, free = take(4)

    loads = {}

    def load(layer, name, source):
        at = held_names.index(name)
        copy = pltpu.make_async_copy(source, buffers[name], local.at[at])
        loads[layer, name] = Staged(buffers[name], copy, False)
        loads[layer, name].begin()

    def load_feed(layer):
        load(layer, "up", up.at[layer])
        for name in ("w", "d", "down", "e", "inner", "h", "z"):
            load(layer, name, large[layer][name])

    def load_attend(layer):
        for name in ("out", "o", "q", "k", "v", "qkv", "a", "x"):
            load(layer, name, large[layer][name])

    load(1, "g", dy)
    load_feed(1)
    load_attend(1)
    load(1, "cos", cosine)
    load(1, "sin", sine)
    wire, wide_wire, line = Wire(sems), Wire(wide_sems), Line()
    wide_barrier(wide_wire, line, Quad().across)
    result_swap = swap_across(wide_wire, result, result_came, True)
    next(result_swap)

    flow = Flow(wire, wide_wire, line, free)
    sequence = flow.sequence
    folds, spreads, waits = {}, {}, {}

    def fold_feed(layer):
        folds[layer, "up"], folds[layer, "down"] = fold_pair(
            wide_wire, line, (grad_up, grad_down), (None, finals[layer]["down"]), feed_scratch,
        )

    def fold_attend(layer):
        folds[layer, "out"], folds[layer, "qkv"] = fold_pair(
            wide_wire, line, (grad_out, grad_qkv),
            (finals[layer]["out"], finals[layer]["qkv"]), attend_scratch,
        )

    for layer in range(2):
        fold_feed(layer)
        fold_attend(layer)
        full = fulls[layer]
        spreads[layer, "up"] = Stream(
            wide_wire, line, rows_of(full["up"]), grad_up.shape[0], folds[layer, "up"]
        )
        spreads[layer, "down"] = spread_down(wide_wire, line, full["down"])
        spreads[layer, "out"], spreads[layer, "qkv"] = spread_attend(
            wide_wire, line, full["out"], full["qkv"]
        )

    def go_home(layer, names):
        final, full = finals[layer], fulls[layer]

        def action():
            for name in names:
                folds[layer, name].end()
            if names == ("down",):
                waits[layer, names] = home(
                    wide_wire, line, final["down"], None, None, full["down"], None, None
                )
            else:
                waits[layer, names] = home(
                    wide_wire, line, None, final["out"], final["qkv"], None, full["out"], full["qkv"]
                )

        return action

    def come_home(layer, names):
        return lambda: waits[layer, names]()

    def fill(count):
        while len(sequence.chunks) < count:
            sequence.add([lambda way, role: None])

    def feed_fold_part(layer):
        if layer == 0:
            sequence.before_next(folds[layer, "down"].start)
        sequence.add(folds[layer, "up"].chunks()).add(folds[layer, "down"].chunks())
        return len(sequence.chunks)

    def attend_fold_feed_spread_part(layer, feed_end):
        sequence.before_next(folds[layer, "qkv"].start)
        chunks = folds[layer, "out"].chunks()
        sequence.add(chunks)
        sequence.after(chunks[-1], folds[layer, "out"].start_side)
        sequence.actions.setdefault(feed_end - 1 + 3 * LATE, []).extend(
            [go_home(layer, ("down",)), folds[layer, "up"].settle]
        )
        fill(feed_end + 2 * LATE)
        stream = spreads[layer, "up"].chunks()
        sequence.add(stream[:6]).add(folds[layer, "qkv"].chunks())
        qkv_end = len(sequence.chunks)
        sequence.add(stream[6:])
        fill(feed_end + 3 * LATE + 2)
        sequence.before_next(come_home(layer, ("down",)))
        sequence.add(spreads[layer, "down"].chunks())
        sequence.actions.setdefault(qkv_end - 1 + 3 * LATE, []).append(
            go_home(layer, ("out", "qkv"))
        )
        fill(qkv_end + 3 * LATE + 2)
        sequence.before_next(come_home(layer, ("out", "qkv")), spreads[layer, "out"].start)
        sequence.after(stream[-1], spreads[layer, "up"].settle)

    feed_end = feed_fold_part(1)
    in_attend_1 = len(sequence.chunks)
    attend_fold_feed_spread_part(1, feed_end)
    settled = max(
        at
        for at, actions in sequence.actions.items()
        if spreads[1, "up"].settle in actions or at == len(sequence.chunks) - 1
    )
    sequence.actions.setdefault(settled, []).append(flow.greet)
    sequence.add(spreads[1, "qkv"].chunks()).add(spreads[1, "out"].chunks())
    sequence.before_next(flow.greeted)
    in_feed_0 = len(sequence.chunks)
    feed_end = feed_fold_part(0)
    in_attend_0 = len(sequence.chunks)
    attend_fold_feed_spread_part(0, feed_end)
    sequence.add(spreads[0, "qkv"].chunks()).add(spreads[0, "out"].chunks())
    flow.limits = {}

    def feed(layer, grad):
        held_now = {name: loads[layer, name] for name in FEED_NAMES + ("up",)}
        feed_back_body(
            wire, flow, grad, held_now["w"], held_now["h"], held_now["z"], gains[layer],
            held_now["inner"], held_now["e"], held_now["d"], held_now["up"], held_now["down"],
            grad_down, grad_up, biases[layer], norms[layer][0], dh, dz,
            second, hidden, held, own,
        )

    def attend(layer):
        names = {name: loads[layer, name] for name in ATTEND_NAMES}
        attend_back_body(
            wire, flow, dz, dh, names["x"], gains[layer], names["a"], names["q"], names["k"],
            names["v"], names["o"], logs[layer], start, loads[1, "cos"], loads[1, "sin"],
            names["qkv"], names["out"],
            grad_qkv, grad_out, norms[layer][1], dx,
            second, mixture, projected, dk, dv, held, own,
        )
        norms[layer][0][...] += norms[layer][1][...]

    def open_to(limit):
        return lambda: flow.open(limit)

    def set_out():
        flow.walk = sequence.steps()

    flow.on_grade = {
        "down": [set_out, folds[1, "down"].start, open_to(in_attend_1 - 1)],
        "qkv": [open_to(in_feed_0 - 1)],
    }
    feed(1, loads[1, "g"])
    load_feed(0)
    attend(1)
    flow.smalls.append(
        small_steps(wide_wire, line, norms[1][0], biases[1], *small[1], totals[1])
    )
    load_attend(0)
    flow.limits = {"feed": feed_limit(in_attend_1), "attend": in_feed_0}
    flow.on_grade = {
        "down": [open_to(in_attend_0 - 1)],
        "qkv": [open_to(len(sequence.chunks) + 3 * LATE + 1)],
    }
    feed(0, dx)
    flow.last = True
    attend(0)
    moved = pltpu.make_async_copy(dx, dx_out, local.at[len(held_names)])
    moved.start()
    grad_swap = swap_across(wide_wire, dx, grad_came, False)
    next(grad_swap)
    flow.smalls.append(
        small_steps(wide_wire, line, norms[0][0], biases[0], *small[0], totals[0])
    )
    while flow.walk is not None or flow.smalls:
        flow()
    for layer in range(2):
        spreads[layer, "down"].end()
        spreads[layer, "qkv"].end()
    next(result_swap, None)
    next(grad_swap, None)
    moved.wait()
    wide_wire.finish()
    assert wire.used <= sems.shape[0] and wide_wire.used <= wide_sems.shape[0]


def feed_limit(feed_end):
    return feed_end + 3 * LATE + 1


def backward_wide(grad, result, saved, weights, start, tables):
    size, width = grad.shape
    length, part = saved[0][2].shape
    hidden_count = saved[0][10].shape[1]
    shape = (size, length, width, hidden_count, part)
    operands, specs = [], []

    def give(array, large=True):
        operands.append(array)
        specs.append(pl.BlockSpec(memory_space=pl.ANY if large else pltpu.VMEM))

    w_up = weights[0][2][0]
    for array in (grad, result, w_up) + tables:
        give(array)
    give(start[None], False)
    for layer in range(2):
        w_qkv, w_out, _, _, w_down, gains, _ = weights[layer]
        resid, normed, query, keys, values, mixture, logs, branch, middle, inner, active, slope, second = saved[layer]
        give(gains, False)
        give(logs, False)
        for array in (second, middle, branch, inner, active, slope, w_down):
            give(array)
        for array in (resid, normed, query, keys, values, mixture, w_qkv, w_out):
            give(array)
    rows = ((size, width), BF16)
    outs = [rows] * 3 + [((16, part), F32)] * 2
    for _ in range(2):
        outs += [
            ((width, hidden_count), BF16),
            ((4, hidden_count, part), BF16),
            ((4, part, part), BF16),
            ((width, 3 * part), BF16),
        ]
    out_specs = [pl.BlockSpec(memory_space=pl.ANY)] * 3 + vmem(2)
    out_specs += [pl.BlockSpec(memory_space=pl.ANY)] * 8
    line_rows = ((size, width), F32)
    buffers = [
        rows, ((width, hidden_count), BF16), (tables[0].shape, F32), (tables[1].shape, F32),
        line_rows, line_rows, line_rows,
        ((length, width), BF16), ((length, hidden_count), BF16), ((length, hidden_count), BF16),
        ((hidden_count, width), BF16),
        rows, ((length, width), BF16),
    ]
    buffers += [((length, part), BF16)] * 4
    buffers += [((width, 3 * part), BF16), ((part, width), BF16)]
    buffers += [
        ((length, width), BF16), ((length, hidden_count), BF16), ((length, part), BF16),
        ((length, 3 * part), BF16), ((length, part), F32), ((length, part), F32),
        ((6, size, width), BF16), line_rows, line_rows, rows, rows,
    ]
    grads = [
        ((width, hidden_count), BF16), ((hidden_count, width), BF16),
        ((part, width), BF16), ((width, 3 * part), BF16),
    ]
    buffers += grads
    scratch = [pltpu.VMEM(*entry) for entry in buffers]
    for streams, ((first, _), (last, _)) in ((True, grads[0:2]), (False, grads[2:4])):
        scratch += Fold.scratch(*first, False, streams) + Fold.scratch(*last, True)
    for _ in range(2):
        scratch += [pltpu.VMEM((rows // 4, columns), BF16) for (rows, columns), _ in grads[1:]]
    for _ in range(2):
        scratch += [
            pltpu.VMEM((4, 8, part), F32),
            pltpu.VMEM((16, part), F32),
            pltpu.VMEM((16, part), F32),
            pltpu.VMEM((4, 16, part), F32),
        ]
    scratch += [pltpu.VMEM((8, width), F32)] * 4
    scratch += [pltpu.VMEM((1, hidden_count), F32)] * 2
    scratch += [
        pltpu.SemaphoreType.DMA((88,)),
        pltpu.SemaphoreType.DMA((600,)),
        pltpu.SemaphoreType.DMA((20,)),
        pltpu.SemaphoreType.REGULAR((5,)),
    ]
    found = pl.pallas_call(
        functools.partial(backward_kernel, shape),
        in_specs=specs,
        out_specs=out_specs,
        out_shape=shaped(*outs),
        scratch_shapes=scratch,
        compiler_params=pltpu.CompilerParams(
            collective_id=3, has_side_effects=True, vmem_limit_bytes=62 * 2**20
        ),
        name="backward",
    )(*operands)
    grad, grad_came, result_came = found[:3]
    totals = found[3:5]

    sums = [
        jnp.stack([block.reshape(-1, block.shape[-1]).astype(F32) for block in pair])
        for pair in zip(found[5:9], found[9:13])
    ]
    bias = jnp.stack([total[8:12].reshape(-1) for total in totals])
    gains, shifts = (
        jnp.stack([total[at : at + 4] for total in totals]) for at in (0, 4)
    )
    up, down, out, qkv = sums
    return grad, grad_came, result_came, (qkv, out, up, bias, down, gains, shifts)


class Quad:
    def __init__(self):
        at = lax.axis_index("wide")
        pair, turn = lax.rem(at, 2), at // 2
        odd = lax.rem(turn, 2)
        self.side = {"wide": at + 1 - 2 * pair}
        self.mate = {"wide": (turn + 1 - 2 * odd) * 2 + pair}
        self.mine = odd * 2 + pair
        self.from_side = odd * 2 + 1 - pair
        self.from_mate = (1 - odd) * 2 + pair
        halfway = lax.axis_size("wide") // 2
        self.first = at < halfway
        self.across = {"wide": lax.rem(at + halfway, 2 * halfway)}


class Fetch:
    def __init__(self, wire, shard, full, by_heads):
        self.wire, self.full, self.rows = wire, full, full.shape[0]
        at, odd, upper = wire.at, lax.rem(wire.at, 2), wire.at // 2
        part = shard.shape[1]

        def columns(block, count=1):
            return pl.ds(pl.multiple_of(block * 256, 256), 256 * count)

        if by_heads:
            self.far = [
                (
                    lambda rows: shard.at[rows, columns(2 - 2 * odd)],
                    lambda rows: full.at[rows, columns(2 * upper)],
                    wire.far,
                )
            ]
            self.relay = lambda rows: full.at[rows, columns(2 - 2 * upper)]
            self.near = (shard.at[:, columns(1)], full.at[:, columns(odd + upper)])
            self.own = (shard.at[:, columns(2 * odd)], full.at[:, columns((at + 1) // 2)])
        else:
            block = self.rows

            def away(peer):
                return (
                    lambda rows: shard.at[span(peer * block + rows.start, rows.size)],
                    lambda rows: full.at[rows, columns(at)],
                    peer,
                )

            self.far = [away(wire.far), away(wire.diagonal)]
            self.relay = lambda rows: full.at[rows, columns(2 - 2 * upper, 2)]
            self.near = (shard.at[span(wire.near * block, block)], full.at[:, columns(at)])
            self.own = (shard.at[span(at * block, block)], full.at[:, columns(at)])

    def quarter(self, which, half=0, halves=1):
        size = self.rows // 4
        return span(which * size + half * (size // halves), size // halves)


def fetch_steps(wire, quad, fetches, local):
    copies, sent, nears = [], [], []
    for at, fetch in enumerate(fetches):
        rows = fetch.quarter(quad.mine)
        for source, target, peer in fetch.far:
            sent.append(wire.send(source(rows), target(rows), {"narrow": peer}))
        nears.append(wire.send(*fetch.near, {"narrow": wire.near}))
        copies.append(pltpu.make_async_copy(*fetch.own, local[at]))
        copies[-1].start()
    yield
    for made in sent:
        made.wait_recv()
    sides, mates = [], []
    for fetch in fetches:
        held = fetch.relay(fetch.quarter(quad.mine))
        sides.append(wire.send(held, held, quad.side))
        mates.append(wire.send(held, held, quad.mate))
    yield
    last = []
    for fetch, side, mate in zip(fetches, sides, mates):
        side.wait_recv()
        held = fetch.relay(fetch.quarter(quad.from_side, 0, 2))
        last.append(wire.send(held, held, quad.mate))
        mate.wait_recv()
        held = fetch.relay(fetch.quarter(quad.from_mate, 1, 2))
        last.append(wire.send(held, held, quad.side))
    yield
    for made in last + nears:
        made.wait_recv()
    for copy in copies:
        copy.wait()


def greet(peers):
    barrier = pltpu.get_barrier_semaphore()
    for peer in peers:
        pl.semaphore_signal(barrier, inc=1, device_id=peer, device_id_type=MESH)
    pl.semaphore_wait(barrier, len(peers))


def quad_barrier(wire, quad, *others):
    narrow = [{"narrow": peer} for peer in (wire.near, wire.far, wire.diagonal)]
    greet(narrow + [quad.side, quad.mate] + list(others))


class Hand(Poll):
    def __init__(self, wire, free, actions):
        super().__init__([])
        self.wire, self.free, self.actions = wire, free, list(actions)
        self.entered = self.last = False
        self.settled = ()

    def __call__(self, times=1):
        for _ in range(times):
            if self.actions:
                for action in self.actions.pop(0):
                    action()

    def enter(self):
        if self.entered:
            pl.semaphore_wait(self.free.at[0], 1)
            pl.semaphore_wait(self.free.at[1], 1)
        self.entered = True

    def leave(self):
        self.wire.finish()
        self.wire.made = []
        ready(*self.settled)
        if self.last:
            return
        for at, peer in enumerate((self.wire.near, self.wire.far)):
            pl.semaphore_signal(
                self.free.at[at], inc=1, device_id={"narrow": peer}, device_id_type=MESH
            )


WEIGHT_NAMES = ("qkv", "out", "down")
KEPT_NAMES = ("a", "q", "k", "v", "o", "lse", "z", "h", "inner", "e", "d", "w", "y")


def forward_kernel(size, *refs):
    refs = list(refs)

    def take(count):
        taken = refs[:count]
        del refs[:count]
        return taken

    ends, w_qkv, w_out, w_down, w_up, norms, b_up, cosine, sine, start = take(10)
    x_out, dy_out = take(2)
    gains, weights_out, kept_out = take(2), [], []
    for _ in range(2):
        weights_out.append(dict(zip(WEIGHT_NAMES, take(3))))
        kept_out.append(dict(zip(KEPT_NAMES, take(13))))
    full_norms, shift_0, shift_1, cos_held, sin_held, start_held, up_0, up_1, x_held = take(9)
    held_weights = [dict(zip(WEIGHT_NAMES, take(3))) for _ in range(2)]
    kept = dict(zip(KEPT_NAMES, take(13)))
    result, inner_own, held, own = take(4)
    sems, quad_sems, local, free = take(4)
    shifts, ups = (shift_0, shift_1), (up_0, up_1)
    locals_used = [0]

    def place():
        locals_used[0] += 1
        return local.at[locals_used[0] - 1]

    def load(source, ref):
        staged = Staged(ref, pltpu.make_async_copy(source, ref, place()), False)
        staged.begin()
        return staged

    def keep(ref, target):
        return Staged(ref, pltpu.make_async_copy(ref, target, place()), True)

    cos_held, sin_held = load(cosine, cos_held), load(sine, sin_held)
    start_held = load(start, start_held)
    ups = [load(w_up.at[layer], ups[layer]) for layer in range(2)]
    wire, quad_wire, quad = Wire(sems), Wire(quad_sems), Quad()
    second = jnp.logical_not(quad.first)
    half = size // 2
    own_x = pltpu.make_async_copy(ends.at[pl.ds(0, size)], x_held, place())
    own_dy = pltpu.make_async_copy(ends.at[pl.ds(size, size)], dy_out, place())

    @pl.when(quad.first)
    def _():
        own_x.start()

    @pl.when(second)
    def _():
        own_dy.start()

    quad_barrier(quad_wire, quad, quad.across)
    x_parts = [
        quad_wire.copy(
            ends.at[pl.ds(size + part * half, half)], x_held.at[pl.ds(part * half, half)],
            quad.across, quad.first,
        )
        for part in range(2)
    ]
    dy_swap = quad_wire.copy(ends.at[pl.ds(0, size)], dy_out, quad.across, second)

    @pl.when(quad.first)
    def _():
        x_parts[0].start()

    def start_later():
        @pl.when(quad.first)
        def _():
            x_parts[0].wait_send()
            x_parts[1].start()

        x_parts[0].settled = True

        @pl.when(second)
        def _():
            dy_swap.start()

    def x_arrives(part):
        if part == 0:

            @pl.when(quad.first)
            def _():
                own_x.wait()

        @pl.when(second)
        def _():
            x_parts[part].wait_recv()

    def fetches(layer, names):
        sources = {"qkv": w_qkv, "out": w_out, "down": w_down}
        wanted = [
            Fetch(quad_wire, sources[name].at[layer], held_weights[layer][name], name == "qkv")
            for name in names
        ]
        at = locals_used[0]
        locals_used[0] += len(names)
        steps = fetch_steps(quad_wire, quad, wanted, [local.at[at + i] for i in range(len(names))])
        outs = [keep(held_weights[layer][name], weights_out[layer][name]) for name in names]
        finished = []

        def step():
            if not finished and next(steps, "end") == "end":
                finished.append(True)
                done(*outs)

        def finish():
            while not finished:
                step()

        return step, finish, outs

    begin, begin_all, begin_outs = fetches(0, ("qkv", "out"))
    down, down_all, down_outs = fetches(0, ("down",))
    rest, rest_all, rest_outs = fetches(1, WEIGHT_NAMES)
    begin()
    part = norms.shape[1]
    columns = pl.ds(pl.multiple_of(wire.at * part, part), part)
    sent = [
        quad_wire.send(norms, full_norms.at[:, columns], {"narrow": peer})
        for peer in (wire.diagonal, wire.far, wire.near)
    ]
    full_norms[:, columns] = norms[...]
    begin()
    for made in sent:
        made.wait_recv()
    spread = full_norms[...].astype(F32)
    for layer in range(2):
        gains[layer][...] = spread[4 * layer : 4 * layer + 4]
        shifts[layer][...] = spread[8 + 4 * layer : 12 + 4 * layer]

    actions = [
        [begin, start_later],
        [begin_all, down],
        [down, rest],
        [down, rest],
        [down_all, rest],
        [rest_all],
    ]
    hand = Hand(wire, free, actions)
    x_now = Pending(x_held, x_arrives)
    before = {}
    for layer in range(2):
        now = {name: keep(kept[name], kept_out[layer][name]) for name in KEPT_NAMES}
        if layer == 0:
            now["y"] = keep(result, kept_out[layer]["y"])
        gather_weights = held_weights[layer]
        waits = {"qkv": begin_all, "out": begin_all, "down": down_all}
        weights = {
            name: Pending(ref, waits[name] if layer == 0 else rest_all)
            for name, ref in gather_weights.items()
        }
        ready(*(before[name] for name in ("q", "k", "v", "o", "lse", "z", "h") if before))
        hand.settled = [before["inner"]] if before else []
        attend_half_body(
            wire, hand, x_now, gains[layer], shifts[layer], cos_held, sin_held, start_held,
            weights["qkv"], weights["out"],
            now["a"], now["q"], now["k"], now["v"], now["o"], now["lse"], now["z"], now["h"],
            inner_own, held, own,
        )
        ready(*(before[name] for name in ("e", "d", "w") if before))
        hand.settled = [now["a"]]
        hand.last = layer == 1
        feed_half_body(
            wire, hand, inner_own, kept["h"], gains[layer], shifts[layer], ups[layer],
            b_up.at[layer], weights["down"],
            now["inner"], now["e"], now["d"], now["w"], now["y"],
            held, own,
        )
        if layer == 0:
            x_copy = keep(x_held, x_out)
            x_copy.begin()
            x_now = result
        else:
            ready(*before.values())
        before = now
    ready(x_copy, *before.values(), *begin_outs, *down_outs, *rest_outs)

    @pl.when(quad.first)
    def _():
        dy_swap.wait_recv()

    @pl.when(second)
    def _():
        own_dy.wait()

    quad_wire.finish()
    assert wire.used <= sems.shape[0] and quad_wire.used <= quad_sems.shape[0]
    assert locals_used[0] <= local.shape[0]


def forward(ends, w_qkv, w_out, w_down, w_up, norms, b_up, cosine, sine, start):
    size, width = ends.shape[0] // 2, ends.shape[1]
    part, hidden = w_out.shape[2], w_up.shape[2]
    length = cosine.shape[0]
    rows, line_rows = ((size, width), BF16), ((size, width), F32)
    weights = [((width, 3 * part), BF16), ((part, width), BF16), ((hidden, width), BF16)]
    kept = [((length, width), BF16)] + [((length, part), BF16)] * 4
    kept += [((8, length), F32), line_rows, line_rows]
    kept += [((length, width), BF16)] + [((length, hidden), BF16)] * 2 + [line_rows, rows]
    norm = ((4, width), F32)
    outs = [rows, rows] + [norm] * 2 + (weights + kept) * 2
    out_specs = [pl.BlockSpec(memory_space=pl.ANY)] * 2 + vmem(2)
    out_specs += [pl.BlockSpec(memory_space=pl.ANY)] * 32
    buffers = [
        ((norms.shape[0], width), BF16), norm, norm,
        (cosine.shape, F32), (sine.shape, F32), (start.shape, jnp.int32),
        ((width, hidden), BF16), ((width, hidden), BF16), rows,
    ]
    buffers += weights * 2 + kept + [rows, rows, ((6, size, width), BF16), line_rows]
    apart = pl.BlockSpec(memory_space=pl.ANY)
    found = pl.pallas_call(
        functools.partial(forward_kernel, size),
        in_specs=[apart] * 5 + vmem(2) + [apart] * 3,
        out_specs=out_specs,
        out_shape=shaped(*outs),
        scratch_shapes=[pltpu.VMEM(*entry) for entry in buffers]
        + [
            pltpu.SemaphoreType.DMA((88,)),
            pltpu.SemaphoreType.DMA((104,)),
            pltpu.SemaphoreType.DMA((56,)),
            pltpu.SemaphoreType.REGULAR((2,)),
        ],
        compiler_params=pltpu.CompilerParams(
            collective_id=1, has_side_effects=True, vmem_limit_bytes=58 * 2**20
        ),
        name="forward",
    )(ends, w_qkv, w_out, w_down, w_up, norms, b_up, cosine, sine, start)
    x, dy = found[:2]
    gains, found = found[2:4], found[4:]
    weights, saved = [], []
    resid = x
    for layer in range(2):
        qkv, out, down = found[16 * layer : 16 * layer + 3]
        a, q, k, v, o, lse, z, h, inner, e, d, w, y = found[16 * layer + 3 : 16 * layer + 16]
        weights.append((qkv, out, (w_up, layer), None, down, gains[layer], None))
        saved.append((resid, a, q, k, v, o, lse, z, h, inner, e, d, w))
        resid = y
    return dy, resid, weights, saved


def swap(block, distance):
    count = lax.axis_size("narrow")
    return lax.ppermute(block, "narrow", [(i, i ^ distance) for i in range(count)])


def pick(stack, table, at):
    return lax.dynamic_index_in_dim(stack, jnp.asarray(table)[at], 0, keepdims=False)


def by_heads(block, at):
    parts = jnp.stack(jnp.split(block, 3, axis=1))
    own = pick(parts, [0, 2, 0, 2], at)
    near = swap(parts[1], 1)
    far = swap(pick(parts, [2, 0, 2, 0], at), 2)
    parts = jnp.stack([own, near, far])
    order = jnp.asarray([[0, 1, 2], [1, 0, 2], [2, 0, 1], [2, 1, 0]])[at]
    return jnp.concatenate(
        [lax.dynamic_index_in_dim(parts, order[i], 0, keepdims=False) for i in range(3)], axis=1
    )


def from_heads(block, at):
    parts = jnp.stack(jnp.split(block, 3, axis=1))
    own = pick(parts, [0, 1, 1, 2], at)
    near = swap(pick(parts, [1, 0, 2, 1], at), 1)
    far = swap(pick(parts, [2, 2, 0, 0], at), 2)
    parts = jnp.stack([own, near, far])
    order = jnp.asarray([[0, 1, 2], [2, 1, 0], [0, 1, 2], [2, 1, 0]])[at]
    return jnp.concatenate(
        [lax.dynamic_index_in_dim(parts, order[i], 0, keepdims=False) for i in range(3)], axis=1
    )


def to_rows(block):
    return lax.all_to_all(block, "narrow", split_axis=0, concat_axis=1, tiled=True)


def to_columns(block):
    return lax.all_to_all(block, "narrow", split_axis=1, concat_axis=0, tiled=True)


def layer_forward(resid, weights, start, tables):
    w_qkv, w_out, w_up, b_up, w_down, gains, shifts = weights
    (normed, query, keys, values, mixture, logs, branch, middle, inner), _ = attend_half(
        Background(1), resid, gains, shifts, *tables, start[:, None], w_qkv, w_out
    )
    inner, active, slope, second, result = feed_half(
        20 + w_up[1], inner, middle, gains, shifts, w_up, b_up, w_down
    )
    return result, (
        resid, normed, query, keys, values, mixture, logs, branch, middle, inner, active, slope, second
    )


def feed_backward(background, grad, saved, weights):
    w_qkv, w_out, w_up, b_up, w_down, gains, shifts = weights
    _, _, _, _, _, _, _, branch, middle, inner, active, slope, second = saved
    (grad_down, grad_up, grad_b_up, norms, grad_middle, grad_branch), results = feed_back(
        background, grad, second, middle, branch, gains, inner, active, slope, w_up, w_down
    )
    return ((grad_up, grad_down), norms, grad_b_up, grad_middle, grad_branch), results


def attend_backward(background, grad_branch, grad_middle, saved, weights, start, tables):
    w_qkv, w_out, w_up, b_up, w_down, gains, shifts = weights
    resid, normed, query, keys, values, mixture, logs, _, _, _, _, _, _ = saved
    (grad_qkv, grad_out, norms, grad), results = attend_back(
        background, grad_branch, grad_middle, resid, gains, normed, query, keys, values, mixture,
        logs, start[None], *tables, w_qkv, w_out,
    )
    return ((grad_out, grad_qkv), norms, grad), results


def layer_backward(grad, saved, weights, start, tables):
    ((grad_up, grad_down), norms, grad_b_up, grad_middle, grad_branch), _ = feed_backward(
        Background(30 + weights[2][1]), grad, saved, weights
    )
    ((grad_out, grad_qkv), norms_too, grad), _ = attend_backward(
        Background(4), grad_branch, grad_middle, saved, weights, start, tables
    )
    return grad, (grad_qkv, grad_out, grad_up, grad_b_up, grad_down, norms + norms_too)


def reduce_grads(grads, at):
    def fold(block):
        return lax.psum_scatter(block, "wide", scatter_dimension=0, tiled=True)

    def spread(block):
        return lax.all_gather(block, "wide", axis=0, tiled=True)

    def spread_rows(block):
        wide, narrow = lax.axis_size("wide"), lax.axis_size("narrow")
        rows, width = block.shape
        full = spread(block).reshape(wide, narrow, rows // narrow, width)
        return full.transpose(1, 0, 2, 3).reshape(wide * rows, width)

    qkv, out, up, b_up, down, norms = grads
    qkv = spread(from_heads(fold(qkv), at))
    out = spread_rows(to_columns(fold(out)))
    up = spread(fold(up))
    down = spread_rows(to_columns(fold(down)))
    b_up = lax.psum(b_up[0], "wide")
    norms = lax.psum(norms, ("wide", "narrow"))
    part = norms.shape[1] // lax.axis_size("narrow")
    norms = lax.dynamic_slice_in_dim(norms, at * part, part, 1)
    return qkv, out, up, b_up, down, norms[:4], norms[4:]


def on_device(ends, lengths, w_qkv, w_out, w_up, b_up, w_down, norm_gain, norm_bias):
    wide = lax.axis_size("wide")
    narrow = lax.axis_size("narrow")
    halfway = wide // 2
    wide_at = lax.axis_index("wide")
    at = lax.axis_index("narrow")
    first = wide_at < halfway
    row_count = ends.shape[0] // 2
    length = row_count * narrow

    def route(block):
        pairs = [(i, (i + halfway) % wide) for i in range(wide)]
        return lax.ppermute(block, "wide", pairs)

    own_lengths = lengths[lax.rem(wide_at, halfway), wide_at // halfway]
    places = jnp.arange(length, dtype=jnp.int32)
    passed = (places[:, None] >= jnp.cumsum(own_lengths)[None, :]).astype(jnp.int32)
    start = jnp.sum(passed * own_lengths[None, :], axis=1)
    tables = rope_tables(places - start)
    b_up = b_up.astype(F32)[:, None]
    norms = jnp.concatenate([norm_gain, norm_bias]).reshape(16, -1)

    if wide == 8:
        upstream, result, weights, saved = forward(
            ends, w_qkv, w_out, w_down, w_up, norms, b_up, *tables, start[:, None]
        )
        grad, grad_came, result_came, totals = backward_wide(
            upstream, result, saved, weights, start, tables
        )
    else:
        came = route(jnp.where(first, ends[row_count:], ends[:row_count]))
        norms = lax.all_gather(norms, "narrow", axis=1, tiled=True).astype(F32)
        resid = jnp.where(first, ends[:row_count], came)
        upstream = jnp.where(first, came, ends[row_count:])

        def weights_of(layer):
            return (
                by_heads(w_qkv[layer], at), to_rows(w_out[layer]), (w_up, layer), b_up[layer],
                to_rows(w_down[layer]), norms[4 * layer : 4 * layer + 4],
                norms[8 + 4 * layer : 12 + 4 * layer],
            )

        weights = [weights_of(layer) for layer in range(2)]
        middle, saved_first = layer_forward(resid, weights[0], start, tables)
        result, saved_second = layer_forward(middle, weights[1], start, tables)
        result_came = route(result)
        grad, grads_second = layer_backward(upstream, saved_second, weights[1], start, tables)
        totals_second = reduce_grads(grads_second, at)
        grad, grads_first = layer_backward(grad, saved_first, weights[0], start, tables)
        totals_first = reduce_grads(grads_first, at)
        grad_came = route(grad)
        totals = [
            jnp.stack([a.astype(F32), b.astype(F32)])
            for a, b in zip(totals_first, totals_second)
        ]

    ends_out = jnp.where(
        first, jnp.concatenate([grad, grad_came]), jnp.concatenate([result_came, result])
    )
    return (ends_out,) + tuple(totals)


def solution(mesh):
    placed = (
        P(("wide", "narrow"), None),
        P(),
        P(None, None, "narrow"),
        P(None, None, "narrow"),
        P(None, None, "narrow"),
        P(None, "narrow"),
        P(None, None, "narrow"),
        P(None, None, "narrow"),
        P(None, None, "narrow"),
    )
    return jax.shard_map(
        on_device,
        mesh=mesh,
        in_specs=placed,
        out_specs=(P(("wide", "narrow"), None),) + placed[2:],
        check_vma=False,
    )
```

```python
import functools
import math

import jax
import jax.numpy as jnp
from jax import lax
from jax.experimental import pallas as pl
from jax.experimental.pallas import tpu as pltpu
from jax.sharding import PartitionSpec as P

HD = 64
EPSILON = 1e-05
MASKED = -1e30
SCALE = HD ** (-0.5)
F32 = jnp.float32
BF16 = jnp.bfloat16


def layer_norm(values, gain_row, shift_row):
    center = jnp.mean(values, axis=-1, keepdims=True)
    centred = values - center
    spread = jnp.mean(centred * centred, axis=-1, keepdims=True)
    return centred * lax.rsqrt(spread + EPSILON) * gain_row + shift_row


def rope_tables(offsets):
    halfway = HD // 2
    ladder = jnp.arange(halfway, dtype=F32) * (2.0 / HD)
    inverse = jnp.exp(-math.log(10000.0) * ladder)
    angles = offsets.astype(F32)[:, None] * inverse[None, :]
    cosine, sine = jnp.cos(angles), jnp.sin(angles)
    return (
        jnp.concatenate([cosine, cosine] * 2, axis=1),
        jnp.concatenate([-sine, sine] * 2, axis=1),
    )


def dot(left, right):
    return jnp.dot(left, right, preferred_element_type=F32)


def dot_t(left, right):
    return lax.dot_general(left, right, (((1,), (1,)), ((), ())), preferred_element_type=F32)


def t_dot(left, right):
    return lax.dot_general(left, right, (((0,), (0,)), ((), ())), preferred_element_type=F32)


MESH = pl.DeviceIdType.MESH


def layer_norm_back(values, grad, gain_row):
    center = jnp.mean(values, axis=-1, keepdims=True)
    centred = values - center
    scale = lax.rsqrt(jnp.mean(centred * centred, axis=-1, keepdims=True) + EPSILON)
    unit = centred * scale
    inner = grad * gain_row
    mean = jnp.mean(inner, axis=-1, keepdims=True)
    slope = jnp.mean(inner * unit, axis=-1, keepdims=True)
    grad_values = scale * (inner - mean - unit * slope)
    return (
        grad_values,
        jnp.sum(grad * unit, axis=0, keepdims=True),
        jnp.sum(grad, axis=0, keepdims=True),
    )


class Copy:
    def __init__(self, wire, source, target, peer, when):
        self.when, self.settled = when, False
        source, target = (item.ref if isinstance(item, Staged) else item for item in (source, target))
        self.pieces = (source, target, wire.sems.at[wire.used], wire.sems.at[wire.used + 1], peer)
        wire.used += 2
        wire.made.append(self)

    def remote(self, source=None):
        own, target, send_sem, recv_sem, peer = self.pieces
        return pltpu.make_async_remote_copy(
            src_ref=own if source is None else source,
            dst_ref=target,
            send_sem=send_sem,
            recv_sem=recv_sem,
            device_id=peer if isinstance(peer, dict) else {"narrow": peer},
            device_id_type=MESH,
        )

    def start(self):
        self.remote().start()

    def start_from(self, source):
        self.remote(source).start()

    def wait_recv(self):
        self.remote().wait_recv()

    def wait_send_early(self, others):
        self.when = others
        self.remote().wait_send()

    def settle(self):
        if not self.settled:
            self.settled = True
            self.wait_send()

    def wait_send(self):
        if self.when is None:
            self.remote().wait_send()
        else:

            @pl.when(self.when)
            def _():
                self.remote().wait_send()


class Wire:
    def __init__(self, sems):
        self.sems, self.used, self.made = sems, 0, []
        self.at = lax.axis_index("narrow")
        self.near = self.at + 1 - 2 * lax.rem(self.at, 2)
        self.far = lax.rem(self.at + 2, 4)
        self.diagonal = lax.rem(self.near + 2, 4)

    def barrier(self):
        barrier = pltpu.get_barrier_semaphore()
        for peer in (self.near, self.far):
            pl.semaphore_signal(barrier, inc=1, device_id={"narrow": peer}, device_id_type=MESH)
        pl.semaphore_wait(barrier, 2)

    def copy(self, source, target, peer, when=None):
        return Copy(self, source, target, peer, when)

    def send(self, source, target, peer):
        made = self.copy(source, target, peer)
        made.start()
        return made

    def move(self, source, target):
        source = source.ref if isinstance(source, Staged) else source
        copy = pltpu.make_async_copy(source, target, self.sems.at[self.used])
        self.used += 1
        copy.start()
        copy.wait()

    def finish(self):
        for made in self.made:
            made.settle()


def block_rows(block, size, part=0, parts=1):
    step = size // parts
    return pl.ds(pl.multiple_of(block * size + part * step, step), step)


class Gather:
    def __init__(self, wire, full, size):
        self.wire, self.full, self.size = wire, full, size
        self.to_near, self.to_far, self.relayed = [], [], []

    def rows(self, block, part):
        return self.full.at[block_rows(block, self.size, part, 2)]

    def push(self, part):
        own = self.rows(self.wire.at, part)
        self.to_near.append(self.wire.send(own, own, self.wire.near))
        self.to_far.append(self.wire.send(own, own, self.wire.far))

    def wait_near(self):
        for made in self.to_near:
            made.wait_recv()

    def relay(self, part):
        self.to_far[part].wait_recv()
        held = self.rows(self.wire.far, part)
        self.relayed.append(self.wire.send(held, held, self.wire.near))

    def wait_diagonal(self, part):
        self.relayed[part].wait_recv()


class Scatter:
    def __init__(self, wire, held, own, parts):
        self.held, self.own = held, own
        self.size = own.shape[0]
        step = self.size // parts
        self.cuts = [pl.ds(i * step, step) for i in range(parts)]

        def copies(out, into, peer, cuts):
            return [wire.copy(held.at[out, cut], held.at[into, cut], peer) for cut in cuts]

        self.side = copies(0, 1, wire.near, self.cuts)
        self.cross = copies(2, 3, wire.far, self.cuts)
        self.home = copies(4, 5, wire.near, [pl.ds(0, self.size)])[0]

    def put_diagonal(self, partial, part):
        self.held[0, self.cuts[part]] = partial.astype(BF16)
        self.side[part].start()

    def put_far(self, partial, part):
        cut = self.cuts[part]
        self.side[part].wait_recv()
        self.held[2, cut] = (partial + self.held[1, cut].astype(F32)).astype(BF16)
        self.cross[part].start()

    def put_near(self, partial):
        self.held[4] = partial.astype(BF16)
        self.home.start()

    def total(self):
        self.home.wait_recv()
        for made in self.cross:
            made.wait_recv()
        return self.own[...] + self.held[5].astype(F32) + self.held[3].astype(F32)


def turn(field, cosine, sine):
    lane = lax.broadcasted_iota(jnp.int32, cosine.shape, 1)
    first = lax.rem(lane, HD) < HD // 2
    turned = []
    for at in range(0, field.shape[1], 128):
        part = field[:, at : at + 128]
        swapped = jnp.where(
            first, pltpu.roll(part, 128 - HD // 2, 1), pltpu.roll(part, HD // 2, 1)
        )
        turned.append(part * cosine + swapped * sine)
    return jnp.concatenate(turned, axis=1)


def vmem(count):
    return [pl.BlockSpec(memory_space=pltpu.VMEM)] * count


def shaped(*entries):
    return [jax.ShapeDtypeStruct(shape, kind) for shape, kind in entries]


class Poll:
    def __init__(self, steps):
        self.steps = steps

    def __call__(self, times=1):
        for _ in range(times):
            for step in list(self.steps):
                if next(step, "end") == "end":
                    self.steps.remove(step)

    def enter(self):
        pass

    def leave(self):
        pass

    def before(self, what):
        pass

    def graded(self, name):
        pass


SMALL = 2**16


class Staged:
    def __init__(self, ref, copy, is_result):
        self.ref, self.copy, self.is_result = ref, copy, is_result
        self.begun = self.ended = False
        self.shape, self.dtype = ref.shape, ref.dtype

    def begin(self):
        self.begun = True
        self.copy.start()

    def wait(self):
        if not self.ended:
            self.ended = True
            self.copy.wait()

    def check(self):
        assert self.is_result or self.ended

    @property
    def at(self):
        self.check()
        return self.ref.at

    def __getitem__(self, index):
        self.check()
        return self.ref[index]

    def __setitem__(self, index, value):
        self.ref[index] = value


class Pending(Staged):
    def __init__(self, ref, action):
        super().__init__(ref, None, False)
        self.action = action

    def wait(self):
        if not self.ended:
            self.ended = True
            self.action()

    def wait_part(self, part):
        self.ended = True
        self.action(part)


def ready(*refs):
    for ref in refs:
        if isinstance(ref, Staged):
            ref.wait()


def ready_part(ref, part):
    if isinstance(ref, Pending):
        ref.wait_part(part)
    else:
        ready(ref)


def done(*refs):
    for ref in refs:
        if isinstance(ref, Staged):
            ref.begin()


class Background:
    def __init__(
        self, number, operands=(), outs=(), scratch=(), steps=None, staged=0, quad=False,
        across=False, semaphores=24,
    ):
        self.semaphores = semaphores
        self.staged = staged
        self.number, self.operands, self.outs = number, list(operands), list(outs)
        self.scratch, self.steps, self.quad, self.across = list(scratch), steps, quad, across


def is_large(shape, kind):
    return math.prod(shape) * jnp.dtype(kind).itemsize > SMALL


def call_with(body, background, outs, scratch, flops, *operands):
    placed = len(operands)
    everything = list(operands) + background.operands
    arrays = [item[0] if isinstance(item, tuple) else item for item in everything]
    shapes = [
        (array.shape[1:] if isinstance(item, tuple) else array.shape, array.dtype)
        for array, item in zip(arrays, everything)
    ]
    results = list(outs) + background.outs
    copies_in = [
        is_large(*shape) and not (background.quad and at >= placed)
        for at, shape in enumerate(shapes)
    ]
    raw_in = [background.quad and at >= placed for at in range(len(shapes))]
    raw_out = [at >= len(outs) + background.staged for at in range(len(results))]
    copies_out = [is_large(*shape) and not raw for shape, raw in zip(results, raw_out)]
    staged = [shape for shape, copied in zip(shapes + results, copies_in + copies_out) if copied]

    def kernel(*refs):
        refs = list(refs)

        def take(count):
            taken = refs[:count]
            del refs[:count]
            return taken

        sources, targets = take(len(shapes)), take(len(results))
        body_scratch, more_scratch = take(len(scratch)), take(len(background.scratch))
        held = take(len(staged))
        sems, local = take(2)
        wire = Wire(sems)
        number = 0
        for at, item in enumerate(everything):
            if copies_in[at]:
                source = sources[at].at[item[1]] if isinstance(item, tuple) else sources[at]
                ref = held[number]
                copy = pltpu.make_async_copy(source, ref, local.at[number])
                sources[at] = Staged(ref, copy, False)
                sources[at].begin()
                number += 1
        for at in range(len(results)):
            if copies_out[at]:
                ref = held[number]
                copy = pltpu.make_async_copy(ref, targets[at], local.at[number])
                targets[at] = Staged(ref, copy, True)
                number += 1
        steps = []
        if background.steps is None:
            wire.barrier()
        else:
            if background.quad:
                place = Quad()
                quad_barrier(wire, place, *([place.across] if background.across else []))
            else:
                place = Line()
                wide_barrier(wire, place, *([Quad().across] if background.across else []))
            steps = [
                background.steps(
                    wire, place, sources[placed:], targets[len(outs) :], more_scratch
                )
            ]

        poll = Poll(steps)
        body(wire, poll, *sources[:placed], *targets[: len(outs)], *body_scratch)
        while steps:
            poll()
        for ref in sources:
            ready(ref)
        for ref in targets:
            if isinstance(ref, Staged) and not ref.begun:
                ref.begin()
        wire.finish()
        for ref in targets:
            ready(ref)

    kernel.__name__ = body.__name__ if background.steps is None else body.__name__ + "_wide"

    def spec(apart):
        return pl.BlockSpec(memory_space=pl.ANY if apart else pltpu.VMEM)

    found = pl.pallas_call(
        kernel,
        in_specs=[spec(raw or copied) for raw, copied in zip(raw_in, copies_in)],
        out_specs=[spec(raw or copied) for raw, copied in zip(raw_out, copies_out)],
        out_shape=shaped(*results),
        scratch_shapes=list(scratch)
        + background.scratch
        + [pltpu.VMEM(*shape) for shape in staged]
        + [pltpu.SemaphoreType.DMA((background.semaphores,))]
        + [pltpu.SemaphoreType.DMA((max(len(staged), 1),))],
        compiler_params=pltpu.CompilerParams(
            collective_id=background.number, has_side_effects=True, vmem_limit_bytes=56 * 2**20
        ),
        cost_estimate=pl.CostEstimate(flops=flops, bytes_accessed=2**24, transcendentals=0),
        name=kernel.__name__,
    )(*arrays)
    return found[: len(outs)], found[len(outs) :]


def attend_half_body(
    wire, poll,
    x_ref, gain_ref, shift_ref, cos_ref, sin_ref, start_ref, w_qkv_ref, w_out_ref,
    a_ref, q_ref, k_ref, v_ref, o_ref, lse_ref, z_ref, h_ref, c_ref,
    held, own,
):
    size = x_ref.shape[0]
    gather = Gather(wire, a_ref, size)
    poll.enter()
    for part in range(2):
        rows = pl.ds(part * (size // 2), size // 2)
        ready_part(x_ref, part)
        normed = layer_norm(x_ref[rows].astype(F32), gain_ref[0:1], shift_ref[0:1])
        a_ref[block_rows(wire.at, size, part, 2)] = normed.astype(BF16)
        gather.push(part)
        poll()
    width = q_ref.shape[1]

    def project(block):
        rows = block_rows(block, size)
        projected = dot(a_ref[rows], w_qkv_ref[...])
        cosine, sine = cos_ref[rows], sin_ref[rows]
        q_ref[rows] = turn(projected[:, :width], cosine, sine).astype(BF16)
        k_ref[rows] = turn(projected[:, width : 2 * width], cosine, sine).astype(BF16)
        v_ref[rows] = projected[:, 2 * width :].astype(BF16)

    ready(w_qkv_ref, cos_ref, sin_ref)
    project(wire.at)
    gather.wait_near()
    project(wire.near)
    gather.relay(0)
    gather.relay(1)
    project(wire.far)
    gather.wait_diagonal(0)
    gather.wait_diagonal(1)
    project(wire.diagonal)

    done(a_ref, q_ref, k_ref, v_ref)
    poll()
    ready(start_ref, w_out_ref)
    scatter = Scatter(wire, held, own, 1)
    for block in (3, 1, 2, 0):
        rows = slice(block * size, (block + 1) * size)
        reach = (block + 1) * size
        key = lax.broadcasted_iota(jnp.int32, (size, reach), 1)
        query = lax.broadcasted_iota(jnp.int32, (size, reach), 0) + block * size
        allowed = (key >= start_ref[rows, :]) & (key <= query)
        mixed, logs = [], jnp.zeros((size, 128), F32)
        lane = lax.broadcasted_iota(jnp.int32, (size, 128), 1)
        for head in range(width // HD):
            lanes = slice(head * HD, (head + 1) * HD)
            scores = dot_t(q_ref[rows, lanes] * SCALE, k_ref[:reach, lanes])
            scores = jnp.where(allowed, scores, MASKED)
            summit = jnp.max(scores, axis=1, keepdims=True)
            weights = jnp.exp(scores - summit)
            total = jnp.sum(weights, axis=1, keepdims=True)
            chances = (weights * (1.0 / total)).astype(BF16)
            mixed.append(dot(chances, v_ref[:reach, lanes]))
            logs = jnp.where(lane == head, summit + jnp.log(total), logs)
        o_ref[rows, :] = jnp.concatenate(mixed, axis=1).astype(BF16)
        lse_ref[:, rows] = logs.T[: lse_ref.shape[0]]
        partial = dot(o_ref[rows, :], w_out_ref[...])

        if block == 2:
            poll()

        @pl.when(wire.diagonal == block)
        def _():
            scatter.put_diagonal(partial, 0)

        @pl.when(wire.far == block)
        def _():
            scatter.put_far(partial, 0)

        @pl.when(wire.near == block)
        def _():
            scatter.put_near(partial)

        @pl.when(wire.at == block)
        def _():
            own[...] = partial

    done(o_ref, lse_ref)
    poll()
    branch = scatter.total()
    z_ref[...] = branch
    middle = x_ref[...].astype(F32) + layer_norm(branch, gain_ref[1:2], shift_ref[1:2])
    h_ref[...] = middle
    c_ref[...] = layer_norm(middle, gain_ref[2:3], shift_ref[2:3]).astype(BF16)
    done(z_ref, h_ref)
    poll.leave()


def attend_half(background, resid, gains, shifts, cosine, sine, start, w_qkv, w_out):
    size, width = resid.shape
    length, part = cosine.shape[0], w_out.shape[0]
    return call_with(
        attend_half_body,
        background,
        [((length, width), BF16)]
        + [((length, part), BF16)] * 4
        + [((8, length), F32), ((size, width), F32), ((size, width), F32), ((size, width), BF16)],
        [pltpu.VMEM((6, size, width), BF16), pltpu.VMEM((size, width), F32)],
        8 * length * width * part + 4 * length * length * part,
        resid, gains, shifts, cosine, sine, start, w_qkv, w_out,
    )


def feed_half_body(
    wire, poll,
    c_ref, h_ref, gain_ref, shift_ref, w_up_ref, b_up_ref, w_down_ref,
    inner_ref, e_ref, d_ref, w_ref, y_ref,
    held, own,
):
    size = c_ref.shape[0]
    half = size // 2
    ready(c_ref)
    gather = Gather(wire, inner_ref, size)
    poll.enter()
    for part in range(2):
        inner_ref[block_rows(wire.at, size, part, 2)] = c_ref[pl.ds(part * half, half)]
        gather.push(part)
    poll()
    scatter = Scatter(wire, held, own, 2)

    def feed(cuts):
        inner = jnp.concatenate([inner_ref[cut] for cut in cuts])
        hidden = dot(inner, w_up_ref[...]) + b_up_ref[...]
        below = 0.5 + 0.5 * lax.erf(hidden * (0.5**0.5))
        density = jnp.exp(-0.5 * hidden * hidden) * ((2.0 * math.pi) ** -0.5)
        active = (hidden * below).astype(BF16)
        slope = (below + hidden * density).astype(BF16)
        for at, cut in enumerate(cuts):
            step = inner.shape[0] // len(cuts)
            e_ref[cut] = active[at * step : (at + 1) * step]
            d_ref[cut] = slope[at * step : (at + 1) * step]
        return dot(active, w_down_ref[...])

    ready(w_up_ref, b_up_ref, w_down_ref)
    own[...] = feed([block_rows(wire.at, size)])
    gather.wait_near()
    scatter.put_near(feed([block_rows(wire.near, size)]))
    for part in range(2):
        gather.relay(part)
        gather.wait_diagonal(part)
        partial = feed(
            [block_rows(wire.diagonal, size, part, 2), block_rows(wire.far, size, part, 2)]
        )
        scatter.put_diagonal(partial[:half], part)
        scatter.put_far(partial[half:], part)
    done(inner_ref, e_ref, d_ref)
    ready(h_ref)
    second = scatter.total()
    w_ref[...] = second
    result = h_ref[...] + layer_norm(second, gain_ref[3:4], shift_ref[3:4])
    y_ref[...] = result.astype(BF16)
    done(w_ref, y_ref)
    poll.leave()


def feed_half(number, inner, middle, gains, shifts, w_up, b_up, w_down):
    size, width = inner.shape
    length, hidden = 4 * size, b_up.shape[1]
    return call_with(
        feed_half_body,
        Background(number),
        [((length, width), BF16)]
        + [((length, hidden), BF16)] * 2
        + [((size, width), F32), ((size, width), BF16)],
        [pltpu.VMEM((6, size, width), BF16), pltpu.VMEM((size, width), F32)],
        4 * length * width * hidden,
        inner, middle, gains, shifts, w_up, b_up, w_down,
    )[0]


def feed_back_body(
    wire, poll,
    g_ref, w_ref, h_ref, z_ref, gain_ref, inner_ref, e_ref, d_ref, w_up_ref, w_down_ref,
    grad_down_ref, grad_up_ref, grad_b_ref, norms_ref, dh_ref, dz_ref,
    second, hidden, held, own,
):
    size = g_ref.shape[0]
    half = size // 2
    ready(g_ref, w_ref)
    gather = Gather(wire, second, size)
    norms = [jnp.zeros((1, g_ref.shape[1]), F32)] * 2
    for part in range(2):
        rows = pl.ds(part * half, half)
        grad, gain, shift = layer_norm_back(w_ref[rows], g_ref[rows].astype(F32), gain_ref[3:4])
        if part == 0:
            poll.enter()
        second[block_rows(wire.at, size, part, 2)] = grad.astype(BF16)
        gather.push(part)
        norms = [norms[0] + gain, norms[1] + shift]
    norms_ref[3:4] = norms[0]
    norms_ref[7:8] = norms[1]
    norms_ref[0:1] = jnp.zeros_like(norms[0])
    norms_ref[4:5] = jnp.zeros_like(norms[0])
    scatter = Scatter(wire, held, own, 2)
    poll()

    def feed(cuts, first=False):
        grad = jnp.concatenate([second[cut] for cut in cuts])
        slope = jnp.concatenate([d_ref[cut] for cut in cuts]).astype(F32)
        grad = (slope * dot_t(grad, w_down_ref[...])).astype(BF16)
        for at, cut in enumerate(cuts):
            step = grad.shape[0] // len(cuts)
            hidden[cut] = grad[at * step : (at + 1) * step]
        bias = jnp.sum(grad.astype(F32), axis=0, keepdims=True)
        grad_b_ref[...] = bias if first else grad_b_ref[...] + bias
        return dot_t(grad, w_up_ref[...])

    ready(d_ref, w_down_ref, w_up_ref)
    own[...] = feed([block_rows(wire.at, size)], True)
    poll()
    gather.wait_near()
    scatter.put_near(feed([block_rows(wire.near, size)]))
    poll()
    for part in range(2):
        poll(2)
        gather.relay(part)
        gather.wait_diagonal(part)
        partial = feed(
            [block_rows(wire.diagonal, size, part, 2), block_rows(wire.far, size, part, 2)]
        )
        scatter.put_diagonal(partial[:half], part)
        scatter.put_far(partial[half:], part)
        poll()
    poll.before("feed")
    ready(e_ref, inner_ref)
    for at in range(0, inner_ref.shape[1], 256):
        cut = slice(at, at + 256)
        grad_up_ref[cut, :] = t_dot(inner_ref[:, cut], hidden[...]).astype(BF16)
        poll()
    done(grad_up_ref)
    poll.graded("up")
    for at in range(0, e_ref.shape[1], 256):
        cut = slice(at, at + 256)
        grad_down_ref[cut, :] = t_dot(e_ref[:, cut], second[...]).astype(BF16)
        poll()
    done(grad_down_ref)
    poll.graded("down")
    poll(3)
    ready(h_ref, z_ref)
    grad, gain, shift = layer_norm_back(h_ref[...], scatter.total(), gain_ref[2:3])
    norms_ref[2:3] = gain
    norms_ref[6:7] = shift
    grad = g_ref[...].astype(F32) + grad
    dh_ref[...] = grad
    grad, gain, shift = layer_norm_back(z_ref[...], grad, gain_ref[1:2])
    norms_ref[1:2] = gain
    norms_ref[5:6] = shift
    dz_ref[...] = grad.astype(BF16)
    poll.leave()


def feed_back(background, grad, second, middle, branch, gains, inner, active, slope, w_up, w_down):
    size, width = grad.shape
    length, hidden = 4 * size, active.shape[1]
    return call_with(
        feed_back_body,
        background,
        [
            ((hidden, width), BF16),
            ((width, hidden), BF16),
            ((1, hidden), F32),
            ((8, width), F32),
            ((size, width), F32),
            ((size, width), BF16),
        ],
        [
            pltpu.VMEM((length, width), BF16),
            pltpu.VMEM((length, hidden), BF16),
            pltpu.VMEM((6, size, width), BF16),
            pltpu.VMEM((size, width), F32),
        ],
        8 * length * width * hidden,
        grad, second, middle, branch, gains, inner, active, slope, w_up, w_down,
    )


def attend_back_body(
    wire, poll,
    dz_ref, dh_ref, x_ref, gain_ref, a_ref, q_ref, k_ref, v_ref, o_ref, lse_ref, start_ref,
    cos_ref, sin_ref, w_qkv_ref, w_out_ref,
    grad_qkv_ref, grad_out_ref, norms_ref, dx_ref,
    branch, mixture, projected, dk, dv, held, own,
):
    size = dz_ref.shape[0]
    length, width = q_ref.shape
    half = size // 2
    ready(dz_ref)
    gather = Gather(wire, branch, size)
    poll.enter()
    for part in range(2):
        branch[block_rows(wire.at, size, part, 2)] = dz_ref[pl.ds(part * half, half)]
        gather.push(part)

    def unmix(block):
        rows = block_rows(block, size)
        mixture[rows] = dot_t(branch[rows], w_out_ref[...]).astype(BF16)

    dk[...] = jnp.zeros_like(dk)
    dv[...] = jnp.zeros_like(dv)
    poll()
    ready(w_out_ref)
    unmix(wire.at)
    gather.wait_near()
    unmix(wire.near)
    poll()
    poll(2)
    gather.relay(0)
    poll(2)
    gather.relay(1)
    unmix(wire.far)
    gather.wait_diagonal(0)
    gather.wait_diagonal(1)
    unmix(wire.diagonal)
    ready(o_ref, q_ref, k_ref, v_ref, lse_ref, start_ref, cos_ref, sin_ref, w_qkv_ref)
    poll.before("attend")
    grad_out_ref[...] = t_dot(o_ref[...], branch[...]).astype(BF16)
    done(grad_out_ref)
    poll()

    pick_head = (
        lax.broadcasted_iota(jnp.int32, (8, width), 1) // HD
        == lax.broadcasted_iota(jnp.int32, (8, width), 0)
    ).astype(F32)
    for block in range(length // size):
        rows = slice(block * size, (block + 1) * size)
        reach = (block + 1) * size
        key = lax.broadcasted_iota(jnp.int32, (reach, size), 0)
        query = lax.broadcasted_iota(jnp.int32, (reach, size), 1) + block * size
        allowed = (key >= start_ref[:, rows]) & (key <= query)
        inner = lax.dot_general(
            pick_head,
            mixture[rows].astype(F32) * o_ref[rows].astype(F32),
            (((1,), (1,)), ((), ())),
            precision=lax.Precision.HIGHEST,
            preferred_element_type=F32,
        )
        dqs, dks, dvs = [], [], []
        for head in range(width // HD):
            lanes = slice(head * HD, (head + 1) * HD)
            k_head, g_head = k_ref[:reach, lanes], mixture[rows, lanes]
            q_head = q_ref[rows, lanes] * SCALE
            scores = dot_t(k_head, q_head) - lse_ref[head : head + 1, rows]
            chances = jnp.exp(jnp.where(allowed, scores, MASKED))
            grad_prob = dot_t(v_ref[:reach, lanes], g_head)
            grad_score = (chances * (grad_prob - inner[head : head + 1])).astype(BF16)
            dvs.append(dot(chances.astype(BF16), g_head))
            dks.append(dot(grad_score, q_head))
            dqs.append(t_dot(grad_score, k_head) * SCALE)
            if block > 0 and head % 2 == 1:
                poll()
        dq = jnp.concatenate(dqs, axis=1)
        projected[rows, :width] = turn(dq, cos_ref[rows], -sin_ref[rows]).astype(BF16)
        dk[:reach, :] += jnp.concatenate(dks, axis=1)
        dv[:reach, :] += jnp.concatenate(dvs, axis=1)
    for block in range(length // size):
        rows = slice(block * size, (block + 1) * size)
        turned = turn(dk[rows], cos_ref[rows], -sin_ref[rows])
        projected[rows, width : 2 * width] = turned.astype(BF16)
        projected[rows, 2 * width :] = dv[rows].astype(BF16)

    scatter = Scatter(wire, held, own, 2)

    def unproject(cut):
        return dot_t(projected[cut], w_qkv_ref[...])

    partial = unproject(block_rows(wire.diagonal, size))
    scatter.put_diagonal(partial[:half], 0)
    scatter.put_diagonal(partial[half:], 1)
    poll()
    partial = unproject(block_rows(wire.far, size))
    scatter.put_far(partial[:half], 0)
    scatter.put_far(partial[half:], 1)
    poll()
    scatter.put_near(unproject(block_rows(wire.near, size)))
    own[...] = unproject(block_rows(wire.at, size))
    ready(a_ref)
    for at in range(0, a_ref.shape[1], 256):
        cut = slice(at, at + 256)
        grad_qkv_ref[cut, :] = t_dot(a_ref[:, cut], projected[...]).astype(BF16)
        poll()
    done(grad_qkv_ref)
    poll.graded("qkv")
    poll(3)
    ready(x_ref, dh_ref)
    grad, gain, shift = layer_norm_back(x_ref[...].astype(F32), scatter.total(), gain_ref[0:1])
    norms_ref[...] = jnp.zeros_like(norms_ref)
    norms_ref[0:1] = gain
    norms_ref[4:5] = shift
    dx_ref[...] = (dh_ref[...] + grad).astype(BF16)
    poll.leave()


def attend_back(
    background,
    grad_branch, grad_middle, resid, gains, normed, query, keys, values, mixture, logs, start,
    cosine, sine, w_qkv, w_out,
):
    size, width = resid.shape
    length, part = query.shape
    return call_with(
        attend_back_body,
        background,
        [
            ((width, 3 * part), BF16),
            ((part, width), BF16),
            ((8, width), F32),
            ((size, width), BF16),
        ],
        [
            pltpu.VMEM((length, width), BF16),
            pltpu.VMEM((length, part), BF16),
            pltpu.VMEM((length, 3 * part), BF16),
            pltpu.VMEM((length, part), F32),
            pltpu.VMEM((length, part), F32),
            pltpu.VMEM((6, size, width), BF16),
            pltpu.VMEM((size, width), F32),
        ],
        16 * length * width * part + 10 * length * length * part,
        grad_branch, grad_middle, resid, gains, normed, query, keys, values, mixture, logs,
        start, cosine, sine, w_qkv, w_out,
    )


CHUNK = 64
LATE = 3


class Line:
    def __init__(self):
        at = lax.axis_index("wide")
        self.pair = lax.rem(at, 2)
        self.turn = at // 2
        self.upper = self.turn // 3
        self.up = {"wide": lax.rem(self.turn + 1, 4) * 2 + self.pair}
        self.down = {"wide": lax.rem(self.turn + 3, 4) * 2 + self.pair}
        self.side = {"wide": at + 1 - 2 * self.pair}
        self.bottom, self.top = self.turn == 0, self.turn == 3
        self.at_end = self.upper * 3 == self.turn
        self.inside = jnp.logical_not(self.at_end)
        not_bottom, not_top = self.turn > 0, self.turn < 3
        self.ways = (
            (self.up, self.bottom, self.top, not_bottom, not_top),
            (self.down, self.top, self.bottom, not_top, not_bottom),
        )

    def steps(self, chunks):
        for at in range(len(chunks) + 3 * LATE):
            for turn in range(4):

                @pl.when(self.turn == turn)
                def _():
                    for way, hops in sorted(((0, turn), (1, 3 - turn)), key=lambda item: item[1]):
                        chunk = at - hops * LATE
                        if not 0 <= chunk < len(chunks):
                            continue
                        if hops == 0:
                            if chunk >= 2:
                                chunks[chunk - 2](way, "sent")
                            chunks[chunk](way, "first")
                        else:
                            chunks[chunk](way, "last" if hops == 3 else "inner")

            yield


def span(start, size):
    return pl.ds(pl.multiple_of(start, 16), size)


class Fold:
    def __init__(self, wire, line, ref, by_side, into, across, final=None):
        self.wire, self.line, self.ref, self.by_side = wire, line, ref, by_side
        self.into, self.across, self.final = into, across, final
        rows = ref.shape[0]
        self.length = rows // 4 if by_side else rows // 2
        self.base = line.pair * (rows // 2) if by_side else 0
        self.count = self.length // CHUNK
        self.copies, self.sides = [], []
        for way, (peer, _, _, _, inner) in enumerate(line.ways):
            cuts = [into.at[way, pl.ds(c * CHUNK, CHUNK)] for c in range(self.count)]
            self.copies.append([wire.copy(cut, cut, peer, inner) for cut in cuts])
        self.pairs = []
        if final is None:
            for cut in (pl.ds(c * CHUNK, CHUNK) for c in range(self.count)):
                source = into.at[1 - line.upper, cut]
                self.pairs.append(wire.copy(source, across.at[cut], line.side, line.at_end))

    @staticmethod
    def scratch(rows, columns, by_side, streams=False):
        return [
            pltpu.VMEM((2, rows // 4 if by_side else rows // 2, columns), BF16),
            pltpu.VMEM((rows // 2 if by_side or streams else rows // 4, columns), BF16),
        ]

    def place(self, way, chunk):
        return (self.length if way == 0 else 0) + chunk * CHUNK

    def start(self):
        line = self.line
        if self.by_side:
            away = (1 - line.pair) * (self.ref.shape[0] // 2)
            for chunk in range(self.count):
                pair = []
                for way in (0, 1):
                    place = self.place(way, chunk)
                    pair.append(
                        self.wire.send(
                            self.ref.at[span(away + place, CHUNK)],
                            self.across.at[pl.ds(place, CHUNK)],
                            line.side,
                        )
                    )
                self.sides.append(pair)

    def step(self, chunk, way, role):
        place = self.place(way, chunk)
        cut = pl.ds(chunk * CHUNK, CHUNK)
        made = self.copies[way][chunk]
        if role == "sent":
            made.wait_send_early(self.line.inside)
            return
        if self.by_side:
            self.sides[chunk][way].wait_recv()

        def own():
            total = self.ref[span(self.base + place, CHUNK)].astype(F32)
            if self.by_side:
                total = total + self.across[pl.ds(place, CHUNK)].astype(F32)
            return total

        if role == "first":
            if self.by_side:
                self.into[way, cut] = own().astype(BF16)
                made.start()
            else:
                made.start_from(self.ref.at[pl.ds(place, CHUNK)])
            return
        made.wait_recv()
        self.into[way, cut] = (own() + self.into[way, cut].astype(F32)).astype(BF16)
        if role == "inner":
            made.start()
        elif self.pairs:
            self.pairs[chunk].start()

    def chunks(self):
        return [functools.partial(self.step, chunk) for chunk in range(self.count)]

    def start_side(self):
        line = self.line
        half = self.length // 2
        source = self.into.at[1 - line.upper, span((1 - line.pair) * half, half)]
        self.side = self.wire.copy(source, self.across, line.side, line.at_end)

        @pl.when(line.at_end)
        def _():
            self.side.start()

    def end(self):
        line = self.line
        size = self.final.shape[0]

        @pl.when(line.at_end)
        def _():
            if not self.by_side:
                self.side.wait_recv()
            for at in range(0, size, CHUNK):
                if self.by_side:
                    self.final[pl.ds(at, CHUNK)] = self.into[1 - line.upper, pl.ds(at, CHUNK)]
                else:
                    own = self.into[1 - line.upper, span(line.pair * size + at, CHUNK)]
                    total = own.astype(F32) + self.across[pl.ds(at, CHUNK)].astype(F32)
                    self.final[pl.ds(at, CHUNK)] = total.astype(BF16)

        self.settle()
        if not self.by_side:
            self.side.settle()

    def settle(self):
        for made in sum(self.copies + self.sides, []):
            made.settle()


class Spread:
    def __init__(self, wire, line, view, rows, by_side):
        self.wire, self.line, self.view, self.by_side = wire, line, view, by_side
        pair, upper = line.pair, line.upper
        self.quarter = rows // 4
        if by_side:
            self.length, self.base = rows // 4, pair * (rows // 2)
            self.mine = self.base + upper * self.quarter
        else:
            self.length, self.base = rows // 2, 0
            self.mine = upper * (rows // 2) + pair * self.quarter
        self.count = self.length // CHUNK
        self.copies = []
        for way, (peer, _, _, _, inner) in enumerate(line.ways):
            cuts = [self.chunk(way, c) for c in range(self.count)]
            self.copies.append([wire.copy(cut, cut, peer, inner) for cut in cuts])
        self.sides = []
        if not by_side:
            self.side = wire.copy(self.own(), self.own(), line.side, line.at_end)

    def own(self):
        return self.view(span(self.mine, self.quarter))

    def chunk(self, way, chunk):
        start = self.base + (0 if way == 0 else self.length) + chunk * CHUNK
        return self.view(span(start, CHUNK))

    def start(self):
        if not self.by_side:

            @pl.when(self.line.at_end)
            def _():
                self.side.start()

    def step(self, chunk, way, role):
        made = self.copies[way][chunk]
        if role == "sent":
            made.wait_send_early(self.line.inside)
            return
        if role == "first":
            if not self.by_side and chunk == 0:
                self.side.wait_recv()
            made.start()
        else:
            made.wait_recv()
            if role == "inner":
                made.start()
        if self.by_side:
            self.sides[chunk][way].start()

    def chunks(self):
        if self.by_side:
            self.sides = []
            for chunk in range(self.count):
                cuts = [self.chunk(way, chunk) for way in (0, 1)]
                self.sides.append([self.wire.copy(cut, cut, self.line.side) for cut in cuts])
        return [functools.partial(self.step, chunk) for chunk in range(self.count)]

    def end(self):
        for pair in self.sides:
            for made in pair:
                made.wait_recv()


class Stream(Spread):
    def __init__(self, wire, line, view, rows, fold):
        super().__init__(wire, line, view, rows, False)
        self.fold, self.own_copies = fold, []
        wire.made.remove(self.side)
        for way in (0, 1):
            self.own_copies.append([])
            for chunk in range(self.count):
                source = fold.across.at[pl.ds(chunk * CHUNK, CHUNK)]
                copy = pltpu.make_async_copy(source, self.chunk(way, chunk), wire.sems.at[wire.used])
                wire.used += 1
                self.own_copies[way].append(copy)

    def start(self):
        pass

    def step(self, chunk, way, role):
        if role != "first":
            super().step(chunk, way, role)
            return
        fold, cut = self.fold, pl.ds(chunk * CHUNK, CHUNK)
        fold.pairs[chunk].wait_recv()
        total = fold.into[1 - way, cut].astype(F32) + fold.across[cut].astype(F32)
        fold.across[cut] = total.astype(BF16)
        self.copies[way][chunk].start_from(fold.across.at[cut])
        self.own_copies[way][chunk].start()

    def settle(self):
        for made in sum(self.copies, []) + self.fold.pairs:
            made.settle()
        for way, copies in enumerate(self.own_copies):

            @pl.when(self.line.ways[way][1])
            def _():
                for copy in copies:
                    copy.wait()


class Sequence:
    def __init__(self, line):
        self.line, self.chunks, self.actions = line, [], {}

    def add(self, *lists):
        total = max(len(chunks) for chunks in lists)
        placed = [
            ((at + 0.5) * total / len(chunks), which, chunk)
            for which, chunks in enumerate(lists)
            for at, chunk in enumerate(chunks)
        ]
        self.chunks += [chunk for _, _, chunk in sorted(placed, key=lambda item: item[:2])]
        return self

    def before_next(self, *actions):
        self.actions.setdefault(len(self.chunks) - 1, []).extend(actions)

    def after(self, chunk, *actions):
        self.actions.setdefault(self.chunks.index(chunk) + 3 * LATE, []).extend(actions)

    def steps(self):
        for action in self.actions.get(-1, []):
            action()
        for at, _ in enumerate(self.line.steps(self.chunks)):
            for action in self.actions.get(at, []):
                action()
            yield


def small_steps(wire, line, norms_ref, bias_ref, narrow_in, sums, side_in, slots, total_ref):
    part = total_ref.shape[1]
    made = []

    def columns(device):
        return pl.ds(pl.multiple_of(device * part, part), part)

    for peer in (wire.near, wire.far, wire.diagonal):
        made.append(
            wire.send(norms_ref.at[:, columns(peer)], narrow_in.at[wire.at], {"narrow": peer})
        )
    narrow_in[wire.at] = norms_ref[:, columns(wire.at)]
    yield
    for copy in made:
        copy.wait_recv()
    total = narrow_in[0] + narrow_in[1] + narrow_in[2] + narrow_in[3]
    lines = [bias_ref[:, at * part : (at + 1) * part] for at in range(4)]
    sums[...] = jnp.concatenate([total] + lines + [jnp.zeros((4, part), F32)], axis=0)
    side = wire.send(sums, side_in, line.side)
    yield
    side.wait_recv()
    slots[line.turn] = sums[...] + side_in[...]
    for step in range(3):
        sends = []
        for way, peer in enumerate((line.up, line.down)):
            place = line.turn if way == 0 else 3 - line.turn
            goes = (place >= step) & (place < 3)
            comes = place > step
            slot = slots.at[lax.rem(line.turn + (4 - step if way == 0 else step), 4)]
            copy = wire.copy(slot, slot, peer, goes)
            sends.append((copy, goes, comes))

            @pl.when(goes)
            def _():
                copy.start()

        yield
        for copy, goes, comes in sends:

            @pl.when(comes)
            def _():
                copy.wait_recv()

    total_ref[...] = slots[0] + slots[1] + slots[2] + slots[3]


def home(wire, line, down, out, qkv, full_down, full_out, full_qkv):
    part = (full_out if full_down is None else full_down).shape[2]
    made = []
    at = wire.at

    def columns(device):
        return pl.ds(pl.multiple_of(device * part, part), part)

    for final, full, by_side in ((down, full_down, True), (out, full_out, False)):
        if final is None:
            continue
        quarter = final.shape[0]
        if by_side:
            mine = line.pair * (2 * quarter) + line.upper * quarter
        else:
            mine = line.upper * (2 * quarter) + line.pair * quarter
        slot = full.at[at, span(mine, quarter)]
        for peer in (wire.diagonal, wire.far, wire.near):
            made.append(
                wire.copy(final.at[:, columns(peer)], slot, {"narrow": peer}, line.at_end)
            )

        @pl.when(line.at_end)
        def _():
            wire.move(final.at[:, columns(at)], slot)

    if qkv is not None:
        quarter = qkv.shape[0]
        rows = span(line.pair * (2 * quarter) + line.upper * quarter, quarter)
        odd, upper = lax.rem(at, 2), at // 2
        far_slot = columns(2 - 2 * odd)
        made.append(
            wire.copy(
                qkv.at[:, columns(2 - 2 * upper)], full_qkv.at[rows, far_slot],
                {"narrow": wire.far}, line.at_end,
            )
        )
        made.append(
            wire.copy(
                qkv.at[:, columns(1 - odd + upper)], full_qkv.at[rows, columns(1)],
                {"narrow": wire.near}, line.at_end,
            )
        )

        @pl.when(line.at_end)
        def _():
            wire.move(qkv.at[:, columns((at + 1) // 2)], full_qkv.at[rows, columns(2 * odd)])

    @pl.when(line.at_end)
    def _():
        for copy in made:
            copy.start()

    def wait():
        @pl.when(line.at_end)
        def _():
            for copy in made:
                copy.wait_recv()

    return wait


def wide_barrier(wire, line, *others):
    barrier = pltpu.get_barrier_semaphore()

    def greet(peer):
        pl.semaphore_signal(barrier, inc=1, device_id=peer, device_id_type=MESH)

    for peer in (line.side,) + others:
        greet(peer)
    for peer in (wire.near, wire.far, wire.diagonal):
        greet({"narrow": peer})

    @pl.when(line.turn < 3)
    def _():
        greet(line.up)

    @pl.when(line.turn > 0)
    def _():
        greet(line.down)

    @pl.when(line.at_end)
    def _():
        pl.semaphore_wait(barrier, 5 + len(others))

    @pl.when(line.inside)
    def _():
        pl.semaphore_wait(barrier, 6 + len(others))


def run(*steps):
    steps = list(steps)
    while steps:
        for at in list(steps):
            if next(at, "end") == "end":
                steps.remove(at)


def fold_pair(wire, line, refs, finals, scratch):
    return (
        Fold(wire, line, refs[0], False, *scratch[0:2], finals[0]),
        Fold(wire, line, refs[1], True, *scratch[2:4], finals[1]),
    )


def rows_of(ref):
    return lambda rows: ref.at[rows]


def spread_down(wire, line, full_down):
    return Spread(wire, line, lambda rows: full_down.at[:, rows], full_down.shape[1], True)


def spread_attend(wire, line, full_out, full_qkv):
    return (
        Spread(wire, line, lambda rows: full_out.at[:, rows], full_out.shape[1], False),
        Spread(wire, line, lambda rows: full_qkv.at[rows], full_qkv.shape[0], True),
    )


def swap_across(wire, source, target, first_sends):
    quad = Quad()
    second = jnp.logical_not(quad.first)
    sends, takes = (quad.first, second) if first_sends else (second, quad.first)
    made = wire.copy(source, target, quad.across, sends)

    @pl.when(sends)
    def _():
        made.start()

    yield

    @pl.when(takes)
    def _():
        made.wait_recv()


class Flow(Poll):
    def __init__(self, wire, wide_wire, line, free):
        super().__init__([])
        self.wire, self.wide_wire, self.line, self.free = wire, wide_wire, line, free
        self.sequence, self.done, self.limit, self.limits = Sequence(line), 0, 0, {}
        self.entered = self.last = False
        self.smalls, self.ticks = [], 0
        self.walk, self.on_grade = None, {}

    def __call__(self, times=1):
        for _ in range(times):
            if self.walk is not None and self.done < self.limit:
                self.done += 1
                if next(self.walk, "end") == "end":
                    self.walk = None
            self.ticks += 1
            if self.ticks % 4 == 0 or self.walk is None:
                for steps in list(self.smalls):
                    if next(steps, "end") == "end":
                        self.smalls.remove(steps)

    def until(self, count):
        while self.walk is not None and self.done < min(count, self.limit):
            self()

    def open(self, limit):
        self.limit = limit

    def graded(self, name):
        for action in self.on_grade.pop(name, []):
            action()

    def before(self, what):
        self.until(self.limits.get(what, 0))

    def enter(self):
        if self.entered:
            pl.semaphore_wait(self.free.at[0], 1)
            pl.semaphore_wait(self.free.at[1], 1)
        self.entered = True

    def leave(self):
        self.wire.finish()
        self.wire.made = []
        if self.last:
            return
        for at, peer in enumerate((self.wire.near, self.wire.far)):
            pl.semaphore_signal(
                self.free.at[at], inc=1, device_id={"narrow": peer}, device_id_type=MESH
            )

    def peers(self):
        line = self.line
        not_bottom, not_top = line.ways[0][3], line.ways[1][3]
        return (
            (2, line.up, not_top, not_bottom),
            (3, line.down, not_bottom, not_top),
            (4, line.side, None, None),
        )

    def greet(self):
        for at, peer, sends, _ in self.peers():
            signal = functools.partial(
                pl.semaphore_signal, self.free.at[at], inc=1, device_id=peer, device_id_type=MESH
            )
            signal() if sends is None else pl.when(sends)(lambda signal=signal: signal())

    def greeted(self):
        for at, _, _, comes in self.peers():
            wait = functools.partial(pl.semaphore_wait, self.free.at[at], 1)
            wait() if comes is None else pl.when(comes)(lambda wait=wait: wait())


FEED_NAMES = ("w", "h", "z", "inner", "e", "d", "down")
ATTEND_NAMES = ("x", "a", "q", "k", "v", "o", "qkv", "out")


def backward_kernel(shape, *refs):
    size, length, width, hidden_count, part = shape
    refs = list(refs)

    def take(count):
        taken = refs[:count]
        del refs[:count]
        return taken

    dy, result, up, cosine, sine, start = take(6)
    gains, logs, large = [], [], []
    for _ in range(2):
        gain, log = take(2)
        gains.append(gain)
        logs.append(log)
        large.append(dict(zip(FEED_NAMES + ATTEND_NAMES, take(15))))
    dx_out, grad_came, result_came = take(3)
    totals = take(2)
    fulls = [dict(zip(("up", "down", "out", "qkv"), take(4))) for _ in range(2)]
    held_names = ("g", "up", "cos", "sin") + FEED_NAMES + ATTEND_NAMES
    buffers = dict(zip(held_names, take(len(held_names))))
    second, hidden, mixture, projected, dk, dv, held, own, dh, dz, dx = take(11)
    grad_up, grad_down, grad_out, grad_qkv = take(4)
    feed_scratch, attend_scratch = take(4), take(4)
    finals = [dict(zip(("down", "out", "qkv"), take(3))) for _ in range(2)]
    small = [take(4) for _ in range(2)]
    norms = [take(2) for _ in range(2)]
    biases = take(2)
    sems, wide_sems, local, free = take(4)

    loads = {}

    def load(layer, name, source):
        at = held_names.index(name)
        copy = pltpu.make_async_copy(source, buffers[name], local.at[at])
        loads[layer, name] = Staged(buffers[name], copy, False)
        loads[layer, name].begin()

    def load_feed(layer):
        load(layer, "up", up.at[layer])
        for name in ("w", "d", "down", "e", "inner", "h", "z"):
            load(layer, name, large[layer][name])

    def load_attend(layer):
        for name in ("out", "o", "q", "k", "v", "qkv", "a", "x"):
            load(layer, name, large[layer][name])

    load(1, "g", dy)
    load_feed(1)
    load_attend(1)
    load(1, "cos", cosine)
    load(1, "sin", sine)
    wire, wide_wire, line = Wire(sems), Wire(wide_sems), Line()
    wide_barrier(wide_wire, line, Quad().across)
    result_swap = swap_across(wide_wire, result, result_came, True)
    next(result_swap)

    flow = Flow(wire, wide_wire, line, free)
    sequence = flow.sequence
    folds, spreads, waits = {}, {}, {}

    def fold_feed(layer):
        folds[layer, "up"], folds[layer, "down"] = fold_pair(
            wide_wire, line, (grad_up, grad_down), (None, finals[layer]["down"]), feed_scratch,
        )

    def fold_attend(layer):
        folds[layer, "out"], folds[layer, "qkv"] = fold_pair(
            wide_wire, line, (grad_out, grad_qkv),
            (finals[layer]["out"], finals[layer]["qkv"]), attend_scratch,
        )

    for layer in range(2):
        fold_feed(layer)
        fold_attend(layer)
        full = fulls[layer]
        spreads[layer, "up"] = Stream(
            wide_wire, line, rows_of(full["up"]), grad_up.shape[0], folds[layer, "up"]
        )
        spreads[layer, "down"] = spread_down(wide_wire, line, full["down"])
        spreads[layer, "out"], spreads[layer, "qkv"] = spread_attend(
            wide_wire, line, full["out"], full["qkv"]
        )

    def go_home(layer, names):
        final, full = finals[layer], fulls[layer]

        def action():
            for name in names:
                folds[layer, name].end()
            if names == ("down",):
                waits[layer, names] = home(
                    wide_wire, line, final["down"], None, None, full["down"], None, None
                )
            else:
                waits[layer, names] = home(
                    wide_wire, line, None, final["out"], final["qkv"], None, full["out"], full["qkv"]
                )

        return action

    def come_home(layer, names):
        return lambda: waits[layer, names]()

    def fill(count):
        while len(sequence.chunks) < count:
            sequence.add([lambda way, role: None])

    def feed_fold_part(layer):
        if layer == 0:
            sequence.before_next(folds[layer, "down"].start)
        sequence.add(folds[layer, "up"].chunks()).add(folds[layer, "down"].chunks())
        return len(sequence.chunks)

    def attend_fold_feed_spread_part(layer, feed_end):
        sequence.before_next(folds[layer, "qkv"].start)
        chunks = folds[layer, "out"].chunks()
        sequence.add(chunks)
        sequence.after(chunks[-1], folds[layer, "out"].start_side)
        sequence.actions.setdefault(feed_end - 1 + 3 * LATE, []).extend(
            [go_home(layer, ("down",)), folds[layer, "up"].settle]
        )
        fill(feed_end + 2 * LATE)
        stream = spreads[layer, "up"].chunks()
        sequence.add(stream[:6]).add(folds[layer, "qkv"].chunks())
        qkv_end = len(sequence.chunks)
        sequence.add(stream[6:])
        fill(feed_end + 3 * LATE + 2)
        sequence.before_next(come_home(layer, ("down",)))
        sequence.add(spreads[layer, "down"].chunks())
        sequence.actions.setdefault(qkv_end - 1 + 3 * LATE, []).append(
            go_home(layer, ("out", "qkv"))
        )
        fill(qkv_end + 3 * LATE + 2)
        sequence.before_next(come_home(layer, ("out", "qkv")), spreads[layer, "out"].start)
        sequence.after(stream[-1], spreads[layer, "up"].settle)

    feed_end = feed_fold_part(1)
    in_attend_1 = len(sequence.chunks)
    attend_fold_feed_spread_part(1, feed_end)
    settled = max(
        at
        for at, actions in sequence.actions.items()
        if spreads[1, "up"].settle in actions or at == len(sequence.chunks) - 1
    )
    sequence.actions.setdefault(settled, []).append(flow.greet)
    sequence.add(spreads[1, "qkv"].chunks()).add(spreads[1, "out"].chunks())
    sequence.before_next(flow.greeted)
    in_feed_0 = len(sequence.chunks)
    feed_end = feed_fold_part(0)
    in_attend_0 = len(sequence.chunks)
    attend_fold_feed_spread_part(0, feed_end)
    sequence.add(spreads[0, "qkv"].chunks()).add(spreads[0, "out"].chunks())
    flow.limits = {}

    def feed(layer, grad):
        held_now = {name: loads[layer, name] for name in FEED_NAMES + ("up",)}
        feed_back_body(
            wire, flow, grad, held_now["w"], held_now["h"], held_now["z"], gains[layer],
            held_now["inner"], held_now["e"], held_now["d"], held_now["up"], held_now["down"],
            grad_down, grad_up, biases[layer], norms[layer][0], dh, dz,
            second, hidden, held, own,
        )

    def attend(layer):
        names = {name: loads[layer, name] for name in ATTEND_NAMES}
        attend_back_body(
            wire, flow, dz, dh, names["x"], gains[layer], names["a"], names["q"], names["k"],
            names["v"], names["o"], logs[layer], start, loads[1, "cos"], loads[1, "sin"],
            names["qkv"], names["out"],
            grad_qkv, grad_out, norms[layer][1], dx,
            second, mixture, projected, dk, dv, held, own,
        )
        norms[layer][0][...] += norms[layer][1][...]

    def open_to(limit):
        return lambda: flow.open(limit)

    def set_out():
        flow.walk = sequence.steps()

    flow.on_grade = {
        "down": [set_out, folds[1, "down"].start, open_to(in_attend_1 - 1)],
        "qkv": [open_to(in_feed_0 - 1)],
    }
    feed(1, loads[1, "g"])
    load_feed(0)
    attend(1)
    flow.smalls.append(
        small_steps(wide_wire, line, norms[1][0], biases[1], *small[1], totals[1])
    )
    load_attend(0)
    flow.limits = {"feed": feed_limit(in_attend_1), "attend": in_feed_0}
    flow.on_grade = {
        "down": [open_to(in_attend_0 - 1)],
        "qkv": [open_to(len(sequence.chunks) + 3 * LATE + 1)],
    }
    feed(0, dx)
    flow.last = True
    attend(0)
    moved = pltpu.make_async_copy(dx, dx_out, local.at[len(held_names)])
    moved.start()
    grad_swap = swap_across(wide_wire, dx, grad_came, False)
    next(grad_swap)
    flow.smalls.append(
        small_steps(wide_wire, line, norms[0][0], biases[0], *small[0], totals[0])
    )
    while flow.walk is not None or flow.smalls:
        flow()
    for layer in range(2):
        spreads[layer, "down"].end()
        spreads[layer, "qkv"].end()
    next(result_swap, None)
    next(grad_swap, None)
    moved.wait()
    wide_wire.finish()
    assert wire.used <= sems.shape[0] and wide_wire.used <= wide_sems.shape[0]


def feed_limit(feed_end):
    return feed_end + 3 * LATE + 1


def backward_wide(grad, result, saved, weights, start, tables):
    size, width = grad.shape
    length, part = saved[0][2].shape
    hidden_count = saved[0][10].shape[1]
    shape = (size, length, width, hidden_count, part)
    operands, specs = [], []

    def give(array, large=True):
        operands.append(array)
        specs.append(pl.BlockSpec(memory_space=pl.ANY if large else pltpu.VMEM))

    w_up = weights[0][2][0]
    for array in (grad, result, w_up) + tables:
        give(array)
    give(start[None], False)
    for layer in range(2):
        w_qkv, w_out, _, _, w_down, gains, _ = weights[layer]
        resid, normed, query, keys, values, mixture, logs, branch, middle, inner, active, slope, second = saved[layer]
        give(gains, False)
        give(logs, False)
        for array in (second, middle, branch, inner, active, slope, w_down):
            give(array)
        for array in (resid, normed, query, keys, values, mixture, w_qkv, w_out):
            give(array)
    rows = ((size, width), BF16)
    outs = [rows] * 3 + [((16, part), F32)] * 2
    for _ in range(2):
        outs += [
            ((width, hidden_count), BF16),
            ((4, hidden_count, part), BF16),
            ((4, part, part), BF16),
            ((width, 3 * part), BF16),
        ]
    out_specs = [pl.BlockSpec(memory_space=pl.ANY)] * 3 + vmem(2)
    out_specs += [pl.BlockSpec(memory_space=pl.ANY)] * 8
    line_rows = ((size, width), F32)
    buffers = [
        rows, ((width, hidden_count), BF16), (tables[0].shape, F32), (tables[1].shape, F32),
        line_rows, line_rows, line_rows,
        ((length, width), BF16), ((length, hidden_count), BF16), ((length, hidden_count), BF16),
        ((hidden_count, width), BF16),
        rows, ((length, width), BF16),
    ]
    buffers += [((length, part), BF16)] * 4
    buffers += [((width, 3 * part), BF16), ((part, width), BF16)]
    buffers += [
        ((length, width), BF16), ((length, hidden_count), BF16), ((length, part), BF16),
        ((length, 3 * part), BF16), ((length, part), F32), ((length, part), F32),
        ((6, size, width), BF16), line_rows, line_rows, rows, rows,
    ]
    grads = [
        ((width, hidden_count), BF16), ((hidden_count, width), BF16),
        ((part, width), BF16), ((width, 3 * part), BF16),
    ]
    buffers += grads
    scratch = [pltpu.VMEM(*entry) for entry in buffers]
    for streams, ((first, _), (last, _)) in ((True, grads[0:2]), (False, grads[2:4])):
        scratch += Fold.scratch(*first, False, streams) + Fold.scratch(*last, True)
    for _ in range(2):
        scratch += [pltpu.VMEM((rows // 4, columns), BF16) for (rows, columns), _ in grads[1:]]
    for _ in range(2):
        scratch += [
            pltpu.VMEM((4, 8, part), F32),
            pltpu.VMEM((16, part), F32),
            pltpu.VMEM((16, part), F32),
            pltpu.VMEM((4, 16, part), F32),
        ]
    scratch += [pltpu.VMEM((8, width), F32)] * 4
    scratch += [pltpu.VMEM((1, hidden_count), F32)] * 2
    scratch += [
        pltpu.SemaphoreType.DMA((88,)),
        pltpu.SemaphoreType.DMA((600,)),
        pltpu.SemaphoreType.DMA((20,)),
        pltpu.SemaphoreType.REGULAR((5,)),
    ]
    found = pl.pallas_call(
        functools.partial(backward_kernel, shape),
        in_specs=specs,
        out_specs=out_specs,
        out_shape=shaped(*outs),
        scratch_shapes=scratch,
        compiler_params=pltpu.CompilerParams(
            collective_id=3, has_side_effects=True, vmem_limit_bytes=62 * 2**20
        ),
        name="backward",
    )(*operands)
    grad, grad_came, result_came = found[:3]
    totals = found[3:5]

    sums = [
        jnp.stack([block.reshape(-1, block.shape[-1]).astype(F32) for block in pair])
        for pair in zip(found[5:9], found[9:13])
    ]
    bias = jnp.stack([total[8:12].reshape(-1) for total in totals])
    gains, shifts = (
        jnp.stack([total[at : at + 4] for total in totals]) for at in (0, 4)
    )
    up, down, out, qkv = sums
    return grad, grad_came, result_came, (qkv, out, up, bias, down, gains, shifts)


class Quad:
    def __init__(self):
        at = lax.axis_index("wide")
        pair, turn = lax.rem(at, 2), at // 2
        odd = lax.rem(turn, 2)
        self.side = {"wide": at + 1 - 2 * pair}
        self.mate = {"wide": (turn + 1 - 2 * odd) * 2 + pair}
        self.mine = odd * 2 + pair
        self.from_side = odd * 2 + 1 - pair
        self.from_mate = (1 - odd) * 2 + pair
        halfway = lax.axis_size("wide") // 2
        self.first = at < halfway
        self.across = {"wide": lax.rem(at + halfway, 2 * halfway)}


class Fetch:
    def __init__(self, wire, shard, full, by_heads):
        self.wire, self.full, self.rows = wire, full, full.shape[0]
        at, odd, upper = wire.at, lax.rem(wire.at, 2), wire.at // 2
        part = shard.shape[1]

        def columns(block, count=1):
            return pl.ds(pl.multiple_of(block * 256, 256), 256 * count)

        if by_heads:
            self.far = [
                (
                    lambda rows: shard.at[rows, columns(2 - 2 * odd)],
                    lambda rows: full.at[rows, columns(2 * upper)],
                    wire.far,
                )
            ]
            self.relay = lambda rows: full.at[rows, columns(2 - 2 * upper)]
            self.near = (shard.at[:, columns(1)], full.at[:, columns(odd + upper)])
            self.own = (shard.at[:, columns(2 * odd)], full.at[:, columns((at + 1) // 2)])
        else:
            block = self.rows

            def away(peer):
                return (
                    lambda rows: shard.at[span(peer * block + rows.start, rows.size)],
                    lambda rows: full.at[rows, columns(at)],
                    peer,
                )

            self.far = [away(wire.far), away(wire.diagonal)]
            self.relay = lambda rows: full.at[rows, columns(2 - 2 * upper, 2)]
            self.near = (shard.at[span(wire.near * block, block)], full.at[:, columns(at)])
            self.own = (shard.at[span(at * block, block)], full.at[:, columns(at)])

    def quarter(self, which, half=0, halves=1):
        size = self.rows // 4
        return span(which * size + half * (size // halves), size // halves)


def fetch_steps(wire, quad, fetches, local):
    copies, sent, nears = [], [], []
    for at, fetch in enumerate(fetches):
        rows = fetch.quarter(quad.mine)
        for source, target, peer in fetch.far:
            sent.append(wire.send(source(rows), target(rows), {"narrow": peer}))
        nears.append(wire.send(*fetch.near, {"narrow": wire.near}))
        copies.append(pltpu.make_async_copy(*fetch.own, local[at]))
        copies[-1].start()
    yield
    for made in sent:
        made.wait_recv()
    sides, mates = [], []
    for fetch in fetches:
        held = fetch.relay(fetch.quarter(quad.mine))
        sides.append(wire.send(held, held, quad.side))
        mates.append(wire.send(held, held, quad.mate))
    yield
    last = []
    for fetch, side, mate in zip(fetches, sides, mates):
        side.wait_recv()
        held = fetch.relay(fetch.quarter(quad.from_side, 0, 2))
        last.append(wire.send(held, held, quad.mate))
        mate.wait_recv()
        held = fetch.relay(fetch.quarter(quad.from_mate, 1, 2))
        last.append(wire.send(held, held, quad.side))
    yield
    for made in last + nears:
        made.wait_recv()
    for copy in copies:
        copy.wait()


def greet(peers):
    barrier = pltpu.get_barrier_semaphore()
    for peer in peers:
        pl.semaphore_signal(barrier, inc=1, device_id=peer, device_id_type=MESH)
    pl.semaphore_wait(barrier, len(peers))


def quad_barrier(wire, quad, *others):
    narrow = [{"narrow": peer} for peer in (wire.near, wire.far, wire.diagonal)]
    greet(narrow + [quad.side, quad.mate] + list(others))


class Hand(Poll):
    def __init__(self, wire, free, actions):
        super().__init__([])
        self.wire, self.free, self.actions = wire, free, list(actions)
        self.entered = self.last = False
        self.settled = ()

    def __call__(self, times=1):
        for _ in range(times):
            if self.actions:
                for action in self.actions.pop(0):
                    action()

    def enter(self):
        if self.entered:
            pl.semaphore_wait(self.free.at[0], 1)
            pl.semaphore_wait(self.free.at[1], 1)
        self.entered = True

    def leave(self):
        self.wire.finish()
        self.wire.made = []
        ready(*self.settled)
        if self.last:
            return
        for at, peer in enumerate((self.wire.near, self.wire.far)):
            pl.semaphore_signal(
                self.free.at[at], inc=1, device_id={"narrow": peer}, device_id_type=MESH
            )


WEIGHT_NAMES = ("qkv", "out", "down")
KEPT_NAMES = ("a", "q", "k", "v", "o", "lse", "z", "h", "inner", "e", "d", "w", "y")


def forward_kernel(size, *refs):
    refs = list(refs)

    def take(count):
        taken = refs[:count]
        del refs[:count]
        return taken

    ends, w_qkv, w_out, w_down, w_up, norms, b_up, cosine, sine, start = take(10)
    x_out, dy_out = take(2)
    gains, weights_out, kept_out = take(2), [], []
    for _ in range(2):
        weights_out.append(dict(zip(WEIGHT_NAMES, take(3))))
        kept_out.append(dict(zip(KEPT_NAMES, take(13))))
    full_norms, shift_0, shift_1, cos_held, sin_held, start_held, up_0, up_1, x_held = take(9)
    held_weights = [dict(zip(WEIGHT_NAMES, take(3))) for _ in range(2)]
    kept = dict(zip(KEPT_NAMES, take(13)))
    result, inner_own, held, own = take(4)
    sems, quad_sems, local, free = take(4)
    shifts, ups = (shift_0, shift_1), (up_0, up_1)
    locals_used = [0]

    def place():
        locals_used[0] += 1
        return local.at[locals_used[0] - 1]

    def load(source, ref):
        staged = Staged(ref, pltpu.make_async_copy(source, ref, place()), False)
        staged.begin()
        return staged

    def keep(ref, target):
        return Staged(ref, pltpu.make_async_copy(ref, target, place()), True)

    cos_held, sin_held = load(cosine, cos_held), load(sine, sin_held)
    start_held = load(start, start_held)
    ups = [load(w_up.at[layer], ups[layer]) for layer in range(2)]
    wire, quad_wire, quad = Wire(sems), Wire(quad_sems), Quad()
    second = jnp.logical_not(quad.first)
    half = size // 2
    own_x = pltpu.make_async_copy(ends.at[pl.ds(0, size)], x_held, place())
    own_dy = pltpu.make_async_copy(ends.at[pl.ds(size, size)], dy_out, place())

    @pl.when(quad.first)
    def _():
        own_x.start()

    @pl.when(second)
    def _():
        own_dy.start()

    quad_barrier(quad_wire, quad, quad.across)
    x_parts = [
        quad_wire.copy(
            ends.at[pl.ds(size + part * half, half)], x_held.at[pl.ds(part * half, half)],
            quad.across, quad.first,
        )
        for part in range(2)
    ]
    dy_swap = quad_wire.copy(ends.at[pl.ds(0, size)], dy_out, quad.across, second)

    @pl.when(quad.first)
    def _():
        x_parts[0].start()

    def start_later():
        @pl.when(quad.first)
        def _():
            x_parts[0].wait_send()
            x_parts[1].start()

        x_parts[0].settled = True

        @pl.when(second)
        def _():
            dy_swap.start()

    def x_arrives(part):
        if part == 0:

            @pl.when(quad.first)
            def _():
                own_x.wait()

        @pl.when(second)
        def _():
            x_parts[part].wait_recv()

    def fetches(layer, names):
        sources = {"qkv": w_qkv, "out": w_out, "down": w_down}
        wanted = [
            Fetch(quad_wire, sources[name].at[layer], held_weights[layer][name], name == "qkv")
            for name in names
        ]
        at = locals_used[0]
        locals_used[0] += len(names)
        steps = fetch_steps(quad_wire, quad, wanted, [local.at[at + i] for i in range(len(names))])
        outs = [keep(held_weights[layer][name], weights_out[layer][name]) for name in names]
        finished = []

        def step():
            if not finished and next(steps, "end") == "end":
                finished.append(True)
                done(*outs)

        def finish():
            while not finished:
                step()

        return step, finish, outs

    begin, begin_all, begin_outs = fetches(0, ("qkv", "out"))
    down, down_all, down_outs = fetches(0, ("down",))
    rest, rest_all, rest_outs = fetches(1, WEIGHT_NAMES)
    begin()
    part = norms.shape[1]
    columns = pl.ds(pl.multiple_of(wire.at * part, part), part)
    sent = [
        quad_wire.send(norms, full_norms.at[:, columns], {"narrow": peer})
        for peer in (wire.diagonal, wire.far, wire.near)
    ]
    full_norms[:, columns] = norms[...]
    begin()
    for made in sent:
        made.wait_recv()
    spread = full_norms[...].astype(F32)
    for layer in range(2):
        gains[layer][...] = spread[4 * layer : 4 * layer + 4]
        shifts[layer][...] = spread[8 + 4 * layer : 12 + 4 * layer]

    actions = [
        [begin, start_later],
        [begin_all, down],
        [down, rest],
        [down, rest],
        [down_all, rest],
        [rest_all],
    ]
    hand = Hand(wire, free, actions)
    x_now = Pending(x_held, x_arrives)
    before = {}
    for layer in range(2):
        now = {name: keep(kept[name], kept_out[layer][name]) for name in KEPT_NAMES}
        if layer == 0:
            now["y"] = keep(result, kept_out[layer]["y"])
        gather_weights = held_weights[layer]
        waits = {"qkv": begin_all, "out": begin_all, "down": down_all}
        weights = {
            name: Pending(ref, waits[name] if layer == 0 else rest_all)
            for name, ref in gather_weights.items()
        }
        ready(*(before[name] for name in ("q", "k", "v", "o", "lse", "z", "h") if before))
        hand.settled = [before["inner"]] if before else []
        attend_half_body(
            wire, hand, x_now, gains[layer], shifts[layer], cos_held, sin_held, start_held,
            weights["qkv"], weights["out"],
            now["a"], now["q"], now["k"], now["v"], now["o"], now["lse"], now["z"], now["h"],
            inner_own, held, own,
        )
        ready(*(before[name] for name in ("e", "d", "w") if before))
        hand.settled = [now["a"]]
        hand.last = layer == 1
        feed_half_body(
            wire, hand, inner_own, kept["h"], gains[layer], shifts[layer], ups[layer],
            b_up.at[layer], weights["down"],
            now["inner"], now["e"], now["d"], now["w"], now["y"],
            held, own,
        )
        if layer == 0:
            x_copy = keep(x_held, x_out)
            x_copy.begin()
            x_now = result
        else:
            ready(*before.values())
        before = now
    ready(x_copy, *before.values(), *begin_outs, *down_outs, *rest_outs)

    @pl.when(quad.first)
    def _():
        dy_swap.wait_recv()

    @pl.when(second)
    def _():
        own_dy.wait()

    quad_wire.finish()
    assert wire.used <= sems.shape[0] and quad_wire.used <= quad_sems.shape[0]
    assert locals_used[0] <= local.shape[0]


def forward(ends, w_qkv, w_out, w_down, w_up, norms, b_up, cosine, sine, start):
    size, width = ends.shape[0] // 2, ends.shape[1]
    part, hidden = w_out.shape[2], w_up.shape[2]
    length = cosine.shape[0]
    rows, line_rows = ((size, width), BF16), ((size, width), F32)
    weights = [((width, 3 * part), BF16), ((part, width), BF16), ((hidden, width), BF16)]
    kept = [((length, width), BF16)] + [((length, part), BF16)] * 4
    kept += [((8, length), F32), line_rows, line_rows]
    kept += [((length, width), BF16)] + [((length, hidden), BF16)] * 2 + [line_rows, rows]
    norm = ((4, width), F32)
    outs = [rows, rows] + [norm] * 2 + (weights + kept) * 2
    out_specs = [pl.BlockSpec(memory_space=pl.ANY)] * 2 + vmem(2)
    out_specs += [pl.BlockSpec(memory_space=pl.ANY)] * 32
    buffers = [
        ((norms.shape[0], width), BF16), norm, norm,
        (cosine.shape, F32), (sine.shape, F32), (start.shape, jnp.int32),
        ((width, hidden), BF16), ((width, hidden), BF16), rows,
    ]
    buffers += weights * 2 + kept + [rows, rows, ((6, size, width), BF16), line_rows]
    apart = pl.BlockSpec(memory_space=pl.ANY)
    found = pl.pallas_call(
        functools.partial(forward_kernel, size),
        in_specs=[apart] * 5 + vmem(2) + [apart] * 3,
        out_specs=out_specs,
        out_shape=shaped(*outs),
        scratch_shapes=[pltpu.VMEM(*entry) for entry in buffers]
        + [
            pltpu.SemaphoreType.DMA((88,)),
            pltpu.SemaphoreType.DMA((104,)),
            pltpu.SemaphoreType.DMA((56,)),
            pltpu.SemaphoreType.REGULAR((2,)),
        ],
        compiler_params=pltpu.CompilerParams(
            collective_id=1, has_side_effects=True, vmem_limit_bytes=58 * 2**20
        ),
        name="forward",
    )(ends, w_qkv, w_out, w_down, w_up, norms, b_up, cosine, sine, start)
    x, dy = found[:2]
    gains, found = found[2:4], found[4:]
    weights, saved = [], []
    resid = x
    for layer in range(2):
        qkv, out, down = found[16 * layer : 16 * layer + 3]
        a, q, k, v, o, lse, z, h, inner, e, d, w, y = found[16 * layer + 3 : 16 * layer + 16]
        weights.append((qkv, out, (w_up, layer), None, down, gains[layer], None))
        saved.append((resid, a, q, k, v, o, lse, z, h, inner, e, d, w))
        resid = y
    return dy, resid, weights, saved


def swap(block, distance):
    count = lax.axis_size("narrow")
    return lax.ppermute(block, "narrow", [(i, i ^ distance) for i in range(count)])


def pick(stack, table, at):
    return lax.dynamic_index_in_dim(stack, jnp.asarray(table)[at], 0, keepdims=False)


def by_heads(block, at):
    parts = jnp.stack(jnp.split(block, 3, axis=1))
    own = pick(parts, [0, 2, 0, 2], at)
    near = swap(parts[1], 1)
    far = swap(pick(parts, [2, 0, 2, 0], at), 2)
    parts = jnp.stack([own, near, far])
    order = jnp.asarray([[0, 1, 2], [1, 0, 2], [2, 0, 1], [2, 1, 0]])[at]
    return jnp.concatenate(
        [lax.dynamic_index_in_dim(parts, order[i], 0, keepdims=False) for i in range(3)], axis=1
    )


def from_heads(block, at):
    parts = jnp.stack(jnp.split(block, 3, axis=1))
    own = pick(parts, [0, 1, 1, 2], at)
    near = swap(pick(parts, [1, 0, 2, 1], at), 1)
    far = swap(pick(parts, [2, 2, 0, 0], at), 2)
    parts = jnp.stack([own, near, far])
    order = jnp.asarray([[0, 1, 2], [2, 1, 0], [0, 1, 2], [2, 1, 0]])[at]
    return jnp.concatenate(
        [lax.dynamic_index_in_dim(parts, order[i], 0, keepdims=False) for i in range(3)], axis=1
    )


def to_rows(block):
    return lax.all_to_all(block, "narrow", split_axis=0, concat_axis=1, tiled=True)


def to_columns(block):
    return lax.all_to_all(block, "narrow", split_axis=1, concat_axis=0, tiled=True)


def layer_forward(resid, weights, start, tables):
    w_qkv, w_out, w_up, b_up, w_down, gains, shifts = weights
    (normed, query, keys, values, mixture, logs, branch, middle, inner), _ = attend_half(
        Background(1), resid, gains, shifts, *tables, start[:, None], w_qkv, w_out
    )
    inner, active, slope, second, result = feed_half(
        20 + w_up[1], inner, middle, gains, shifts, w_up, b_up, w_down
    )
    return result, (
        resid, normed, query, keys, values, mixture, logs, branch, middle, inner, active, slope, second
    )


def feed_backward(background, grad, saved, weights):
    w_qkv, w_out, w_up, b_up, w_down, gains, shifts = weights
    _, _, _, _, _, _, _, branch, middle, inner, active, slope, second = saved
    (grad_down, grad_up, grad_b_up, norms, grad_middle, grad_branch), results = feed_back(
        background, grad, second, middle, branch, gains, inner, active, slope, w_up, w_down
    )
    return ((grad_up, grad_down), norms, grad_b_up, grad_middle, grad_branch), results


def attend_backward(background, grad_branch, grad_middle, saved, weights, start, tables):
    w_qkv, w_out, w_up, b_up, w_down, gains, shifts = weights
    resid, normed, query, keys, values, mixture, logs, _, _, _, _, _, _ = saved
    (grad_qkv, grad_out, norms, grad), results = attend_back(
        background, grad_branch, grad_middle, resid, gains, normed, query, keys, values, mixture,
        logs, start[None], *tables, w_qkv, w_out,
    )
    return ((grad_out, grad_qkv), norms, grad), results


def layer_backward(grad, saved, weights, start, tables):
    ((grad_up, grad_down), norms, grad_b_up, grad_middle, grad_branch), _ = feed_backward(
        Background(30 + weights[2][1]), grad, saved, weights
    )
    ((grad_out, grad_qkv), norms_too, grad), _ = attend_backward(
        Background(4), grad_branch, grad_middle, saved, weights, start, tables
    )
    return grad, (grad_qkv, grad_out, grad_up, grad_b_up, grad_down, norms + norms_too)


def reduce_grads(grads, at):
    def fold(block):
        return lax.psum_scatter(block, "wide", scatter_dimension=0, tiled=True)

    def spread(block):
        return lax.all_gather(block, "wide", axis=0, tiled=True)

    def spread_rows(block):
        wide, narrow = lax.axis_size("wide"), lax.axis_size("narrow")
        rows, width = block.shape
        full = spread(block).reshape(wide, narrow, rows // narrow, width)
        return full.transpose(1, 0, 2, 3).reshape(wide * rows, width)

    qkv, out, up, b_up, down, norms = grads
    qkv = spread(from_heads(fold(qkv), at))
    out = spread_rows(to_columns(fold(out)))
    up = spread(fold(up))
    down = spread_rows(to_columns(fold(down)))
    b_up = lax.psum(b_up[0], "wide")
    norms = lax.psum(norms, ("wide", "narrow"))
    part = norms.shape[1] // lax.axis_size("narrow")
    norms = lax.dynamic_slice_in_dim(norms, at * part, part, 1)
    return qkv, out, up, b_up, down, norms[:4], norms[4:]


def on_device(ends, lengths, w_qkv, w_out, w_up, b_up, w_down, norm_gain, norm_bias):
    wide = lax.axis_size("wide")
    narrow = lax.axis_size("narrow")
    halfway = wide // 2
    wide_at = lax.axis_index("wide")
    at = lax.axis_index("narrow")
    first = wide_at < halfway
    row_count = ends.shape[0] // 2
    length = row_count * narrow

    def route(block):
        pairs = [(i, (i + halfway) % wide) for i in range(wide)]
        return lax.ppermute(block, "wide", pairs)

    own_lengths = lengths[lax.rem(wide_at, halfway), wide_at // halfway]
    places = jnp.arange(length, dtype=jnp.int32)
    passed = (places[:, None] >= jnp.cumsum(own_lengths)[None, :]).astype(jnp.int32)
    start = jnp.sum(passed * own_lengths[None, :], axis=1)
    tables = rope_tables(places - start)
    b_up = b_up.astype(F32)[:, None]
    norms = jnp.concatenate([norm_gain, norm_bias]).reshape(16, -1)

    if wide == 8:
        upstream, result, weights, saved = forward(
            ends, w_qkv, w_out, w_down, w_up, norms, b_up, *tables, start[:, None]
        )
        grad, grad_came, result_came, totals = backward_wide(
            upstream, result, saved, weights, start, tables
        )
    else:
        came = route(jnp.where(first, ends[row_count:], ends[:row_count]))
        norms = lax.all_gather(norms, "narrow", axis=1, tiled=True).astype(F32)
        resid = jnp.where(first, ends[:row_count], came)
        upstream = jnp.where(first, came, ends[row_count:])

        def weights_of(layer):
            return (
                by_heads(w_qkv[layer], at), to_rows(w_out[layer]), (w_up, layer), b_up[layer],
                to_rows(w_down[layer]), norms[4 * layer : 4 * layer + 4],
                norms[8 + 4 * layer : 12 + 4 * layer],
            )

        weights = [weights_of(layer) for layer in range(2)]
        middle, saved_first = layer_forward(resid, weights[0], start, tables)
        result, saved_second = layer_forward(middle, weights[1], start, tables)
        result_came = route(result)
        grad, grads_second = layer_backward(upstream, saved_second, weights[1], start, tables)
        totals_second = reduce_grads(grads_second, at)
        grad, grads_first = layer_backward(grad, saved_first, weights[0], start, tables)
        totals_first = reduce_grads(grads_first, at)
        grad_came = route(grad)
        totals = [
            jnp.stack([a.astype(F32), b.astype(F32)])
            for a, b in zip(totals_first, totals_second)
        ]

    ends_out = jnp.where(
        first, jnp.concatenate([grad, grad_came]), jnp.concatenate([result_came, result])
    )
    return (ends_out,) + tuple(totals)


def solution(mesh):
    placed = (
        P(("wide", "narrow"), None),
        P(),
        P(None, None, "narrow"),
        P(None, None, "narrow"),
        P(None, None, "narrow"),
        P(None, "narrow"),
        P(None, None, "narrow"),
        P(None, None, "narrow"),
        P(None, None, "narrow"),
    )
    return jax.shard_map(
        on_device,
        mesh=mesh,
        in_specs=placed,
        out_specs=(P(("wide", "narrow"), None),) + placed[2:],
        check_vma=False,
    )
```
